32 devices in a mesh: seq: 8 (over y, x, core), head: 4 (over z).
Axes of the slice: x: 2, y: 2, z: 4, core: 2. Of those that a mesh axis runs over, the one named last changes fastest.
Arguments:
- x_input: bfloat16 [1024, 16384], P('seq', 'head'), may hold values from -6 to 6
- z_input: bfloat16 [1024, 16384], P('seq', 'head'), may hold values from -52 to 52
- bc_input: bfloat16 [2, 1024, 128], P(None, 'seq'), may hold values from -2.09375 to 2.09375
- dt_raw: float32 [128, 1024], P('head', 'seq'), may hold values from -1.5 to 4.5
- dt_bias: float32 [128], P('head'), may hold values from -4.2 to 0.3
- a_log: float32 [128], P('head')
- d_skip: float32 [128], P('head'), may hold values from 0.5 to 1.5
- conv_x: float32 [4, 16384], P(None, 'head'), may hold values from -3 to 3
- convolution_bc_taps: float32 [2, 4, 128], replicated, may hold values from -3 to 3
- rescale_factor: float32 [16384], P('head'), may hold values from 0.5 to 1.5
- grad_out: bfloat16 [1024, 16384], P('seq', 'head'), may hold values from -40 to 40
Outputs:
- grad_x: bfloat16 [1024, 16384], P('seq', 'head')
- grad_z: bfloat16 [1024, 16384], P('seq', 'head')
- grad_bc: bfloat16 [2, 1024, 128], P(None, ('seq', 'head'))
- grad_dt: float32 [128, 1024], P('head', 'seq')
The draws below stay inside these ranges and needn't reach their ends.
All inputs are finite; a program needn't handle non-finite values.
Results may differ from the reference program's by a relative error of at most 0.0086.
Values may be sent and summed in bfloat16 or wider, within the bound.
No kernel may reach another device: no remote copies, remote signals or barrier semaphores. Data moves between devices by JAX's collectives and lax.ppermute only.
A program may use at most 64 MiB of HBM per device.

```python
import math
import jax
import jax.numpy as jnp
from jax import lax

HEADS = 128
HEAD_DIM = 128
NSTATE = 128
KCONV = 4
TOK_DEV = 128
STREAM_LENGTH = 1024
INNER = 16384
N_SEQ = 8


def head_kinds(key):
    slow_share = 0.5
    return jax.random.uniform(jax.random.fold_in(key, 101), (HEADS,)) < slow_share


def draw_a_log(key, part):
    slow_heads = head_kinds(key)
    slow_log = math.log(1.0 / (0.0215 * STREAM_LENGTH)) + jax.random.uniform(jax.random.fold_in(key, 102), (HEADS,), minval=math.log(0.3), maxval=math.log(1.5))
    fast_log = jax.random.uniform(jax.random.fold_in(key, 103), (HEADS,), minval=math.log(0.028), maxval=math.log(0.05))
    return jnp.where(slow_heads, slow_log, fast_log).astype(jnp.float32)


def draw_dt_bias(key, part):
    slow_heads = head_kinds(key)
    slow_bias = jax.random.uniform(jax.random.fold_in(key, 104), (HEADS,), minval=-4.2, maxval=-3.8)
    fast_bias = jax.random.uniform(jax.random.fold_in(key, 105), (HEADS,), minval=-0.3, maxval=0.3)
    return jnp.where(slow_heads, slow_bias, fast_bias).astype(jnp.float32)


def draw_dt_raw(key, part):
    spread = 1.0
    equal_fraction = jax.random.uniform(jax.random.fold_in(key, 110), (HEADS, STREAM_LENGTH), minval=-spread, maxval=spread)
    position_cells = jax.random.randint(jax.random.fold_in(key, 111), (4,), 0, STREAM_LENGTH)
    device_batches = jnp.any(jnp.arange(STREAM_LENGTH)[None, :] == position_cells[:, None], axis=0)
    return (equal_fraction + 3.0 * device_batches[None, :].astype(jnp.float32)).astype(jnp.float32)


def scaled_sample(key, base, column_range):
    column_scale = 10.0 ** (column_range * jnp.arange(INNER, dtype=jnp.float32) / INNER)
    row_scale = 10.0 ** (jax.random.uniform(jax.random.fold_in(key, 121), (STREAM_LENGTH, 1)) - 0.5)
    sample = jnp.clip(jax.random.normal(jax.random.fold_in(key, 123), (STREAM_LENGTH, INNER)), -4.0, 4.0)
    return base * sample * column_scale[None, :] * row_scale


def draw_z_input(key, part):
    column_range = 1.0
    return scaled_sample(jax.random.fold_in(key, 130), 0.4, column_range).astype(jnp.bfloat16)


def draw_grad_out(key, part):
    column_range = 0.5
    return scaled_sample(jax.random.fold_in(key, 140), 0.7, column_range).astype(jnp.bfloat16)


def steps_of(key, shape, pieces, low, top_value):
    def one(dim, shards_of):
        draws = jax.random.uniform(jax.random.fold_in(jax.random.fold_in(key, 6), dim), (shards_of,), jnp.float32, low / len(pieces), top_value / len(pieces))
        return jnp.repeat(jnp.exp(draws), shape[dim] // shards_of).reshape((-1,) + (1,) * (len(shape) - dim - 1))

    gain = one(*pieces[0])
    for cut in pieces[1:]:
        gain = gain * one(*cut)
    return gain


def scatter_about(key, dims, deviation, most, split=(), kind=jnp.bfloat16):
    drawn = jax.random.normal(key, dims, jnp.float32) * deviation
    if len(split) > 0:
        drawn = steps_of(key, dims, split, -0.22, 0.18) * drawn
    return jnp.clip(drawn, min=-most, max=most).astype(kind)


def setup_inputs(seed: int = 0) -> dict:
    splits = jax.random.split(jax.random.key(seed), 12)
    x_input = scatter_about(splits[0], (STREAM_LENGTH, INNER), 1.0, 6.0, ((0, 8), (1, 4)))
    z_input = draw_z_input(jax.random.fold_in(splits[11], 71), 0)
    bc_input = scatter_about(splits[2], (2, STREAM_LENGTH, NSTATE), 0.35, 2.09375, ((1, 8),))
    dt_raw = draw_dt_raw(jax.random.fold_in(splits[11], 71), 0)
    dt_bias = draw_dt_bias(jax.random.fold_in(splits[11], 71), 0)
    a_log = draw_a_log(jax.random.fold_in(splits[11], 71), 0)
    d_skip = jnp.clip(0.5 + 1.0 * jax.random.uniform(splits[6], (HEADS,), jnp.float32) ** steps_of(splits[6], (HEADS,), ((0, 4),), -0.2, 0.2), 0.5, 1.5)
    conv_x = scatter_about(splits[7], (KCONV, INNER), KCONV ** -0.5, 3.0, ((1, 4),), jnp.float32)
    convolution_bc_taps = scatter_about(splits[8], (2, KCONV, NSTATE), KCONV ** -0.5, 3.0, (), jnp.float32)
    rescale_factor = jnp.clip(1.0 + 0.1 * jax.random.normal(splits[9], (INNER,), jnp.float32), 0.5, 1.5)
    grad_out = draw_grad_out(jax.random.fold_in(splits[11], 71), 0)
    return dict(x_input=x_input, z_input=z_input, bc_input=bc_input, dt_raw=dt_raw, dt_bias=dt_bias, a_log=a_log, d_skip=d_skip, conv_x=conv_x, convolution_bc_taps=convolution_bc_taps, rescale_factor=rescale_factor, grad_out=grad_out)


EPS = 1e-05

def silu_grad(value):
    sigma = jax.nn.sigmoid(value)
    return sigma * (1.0 + value * (1.0 - sigma))

def conv_rows(extended, weight_matrix):
    length = extended.shape[-2] - 3
    summed = weight_matrix[..., 0, :][..., None, :] * extended[..., 0:length, :]
    for offset in range(1, 4):
        summed = summed + weight_matrix[..., offset, :][..., None, :] * extended[..., offset:offset + length, :]
    return summed

def conv_back(extended, weight_matrix):
    length = extended.shape[-2] - 3
    summed = weight_matrix[..., 0, :][..., None, :] * extended[..., 3:3 + length, :]
    for offset in range(1, 4):
        summed = summed + weight_matrix[..., offset, :][..., None, :] * extended[..., 3 - offset:3 - offset + length, :]
    return summed

def decay_of(cumul, causal):
    between = cumul[:, None] - cumul[None, :]
    return jnp.where(causal, jnp.exp(jnp.minimum(between, 0.0)), 0.0)

def weighted_rows(trailing_decay, step_size, b_rows):
    return ((trailing_decay * step_size)[:, None] * b_rows.astype(jnp.float32)).astype(jnp.bfloat16)

def head_forward(cumul, step_size, gram_matrix, x_head, state_low, c_rows, skip_gain, causal):
    decay_matrix = decay_of(cumul, causal)
    mixer_low = (gram_matrix * decay_matrix * step_size[None, :]).astype(jnp.bfloat16)
    intra_out = jnp.dot(mixer_low, x_head, preferred_element_type=jnp.float32)
    handed_forward = jnp.dot(c_rows, state_low, preferred_element_type=jnp.float32)
    return intra_out + jnp.exp(cumul)[:, None] * handed_forward + skip_gain * x_head.astype(jnp.float32)

def head_backward(cumul, step_size, gram_matrix, x_head, grad_head, state_low, state_exact, out_low, out_exact, b_rows, c_rows, skip_gain, decay_rate, causal):
    decay_matrix = decay_of(cumul, causal)
    mixer_low = (gram_matrix * decay_matrix * step_size[None, :]).astype(jnp.bfloat16)
    grad_mix = jnp.dot(grad_head, x_head.T, preferred_element_type=jnp.float32)
    decayed_grad = grad_mix * decay_matrix
    weighted_grad = decayed_grad * step_size[None, :]
    gram_grad = weighted_grad * gram_matrix
    lifted = jnp.exp(cumul)
    handed_forward = jnp.dot(c_rows, state_low, preferred_element_type=jnp.float32)
    reached = jnp.dot(x_head, out_low.T, preferred_element_type=jnp.float32)
    trailing_decay = jnp.exp(cumul[-1] - cumul)
    inner_b = lax.optimization_barrier(jnp.sum(b_rows.astype(jnp.float32) * reached, axis=1))
    state_term = trailing_decay * step_size * inner_b
    grad_cumul = lax.optimization_barrier(jnp.sum(gram_grad, axis=1)) - lax.optimization_barrier(jnp.sum(gram_grad, axis=0))
    grad_cumul = grad_cumul + lifted * lax.optimization_barrier(jnp.sum(grad_head.astype(jnp.float32) * handed_forward, axis=1)) - state_term
    end_grad = jnp.sum(state_term) + jnp.exp(cumul[-1]) * jnp.sum(out_exact * state_exact)
    grad_cumul = grad_cumul.at[-1].add(end_grad)
    grad_log = jnp.cumsum(grad_cumul[::-1])[::-1]
    grad_step = lax.optimization_barrier(jnp.sum(decayed_grad * gram_matrix, axis=0)) + trailing_decay * inner_b + decay_rate * grad_log
    weighted_b = weighted_rows(trailing_decay, step_size, b_rows)
    grad_x = jnp.dot(mixer_low.T, grad_head, preferred_element_type=jnp.float32)
    grad_x = grad_x + skip_gain * grad_head.astype(jnp.float32) + jnp.dot(weighted_b, out_low, preferred_element_type=jnp.float32)
    grad_c = lifted[:, None] * jnp.dot(grad_head, state_low.T, preferred_element_type=jnp.float32)
    grad_b = (trailing_decay * step_size)[:, None] * reached
    return (grad_x, grad_step, grad_c, grad_b, weighted_grad)

def block_prep(x_rows, b_rows, step_size, decay_rate):
    length = x_rows.shape[0]
    head_count = step_size.shape[0]
    cumul = jnp.cumsum(decay_rate[:, None] * step_size, axis=1)
    trailing_decay = jnp.exp(cumul[:, -1:] - cumul)
    x_heads = jnp.moveaxis(x_rows.reshape(length, head_count, -1), 1, 0)

    def one_head(head_items):
        weighted_b = weighted_rows(head_items[0], head_items[1], b_rows)
        return jnp.dot(weighted_b.T, head_items[2], preferred_element_type=jnp.float32)
    local_state = lax.map(one_head, (trailing_decay, step_size, x_heads))
    return (cumul, x_heads, local_state)

def block_mix(cumul, step_size, gram_matrix, x_heads, state_low, c_rows, skip_gain, causal):

    def one_head(head_items):
        return head_forward(head_items[0], head_items[1], gram_matrix, head_items[2], head_items[3], c_rows, head_items[4], causal)
    outputs = lax.map(one_head, (cumul, step_size, x_heads, state_low, skip_gain))
    return jnp.moveaxis(outputs, 0, 1).reshape(outputs.shape[1], -1)

def carry_grad(cumul, c_rows, grad_heads):

    def one_head(head_items):
        lifted_c = (jnp.exp(head_items[0])[:, None] * c_rows.astype(jnp.float32)).astype(jnp.bfloat16)
        return jnp.dot(lifted_c.T, head_items[1], preferred_element_type=jnp.float32)
    return lax.map(one_head, (cumul, grad_heads))

def block_back(cumul, step_size, gram_matrix, x_heads, grad_heads, state_exact, out_exact, b_rows, c_rows, skip_gain, decay_rate, causal):
    length = b_rows.shape[0]
    nstate = b_rows.shape[1]
    state_low = state_exact.astype(jnp.bfloat16)
    out_low = out_exact.astype(jnp.bfloat16)

    def one_head(running, head_items):
        cumulative_head, step_head, x_head, grad_head, low_in, exact_in, low_out, exact_out, skip_head, rate_head = head_items
        grad_x, grad_step, grad_c, grad_b, weighted_grad = head_backward(cumulative_head, step_head, gram_matrix, x_head, grad_head, low_in, exact_in, low_out, exact_out, b_rows, c_rows, skip_head, rate_head, causal)
        return ((running[0] + weighted_grad, running[1] + grad_c, running[2] + grad_b), (grad_x, grad_step))
    initial = (jnp.zeros((length, length), jnp.float32), jnp.zeros((length, nstate), jnp.float32), jnp.zeros((length, nstate), jnp.float32))
    (grad_sum, c_sum, b_sum), (grad_xs, grad_steps) = lax.scan(one_head, initial, (cumul, step_size, x_heads, grad_heads, state_low, state_exact, out_low, out_exact, skip_gain, decay_rate))
    grad_c = c_sum + jnp.dot(grad_sum, b_rows.astype(jnp.float32), precision=lax.Precision.HIGHEST)
    grad_b = b_sum + jnp.dot(grad_sum.T, c_rows.astype(jnp.float32), precision=lax.Precision.HIGHEST)
    grad_x = jnp.moveaxis(grad_xs, 0, 1).reshape(length, -1)
    return (grad_x, jnp.stack([grad_b, grad_c]), grad_steps)

def reference(x_input, z_input, bc_input, dt_raw, dt_bias, a_log, d_skip, conv_x, convolution_bc_taps, rescale_factor, grad_out):
    length = TOK_DEV
    channels = x_input.shape[1]
    head_count = dt_raw.shape[0]
    nstate = bc_input.shape[2]
    decay_rate = -jnp.exp(a_log)
    step_all = jax.nn.softplus(dt_raw + dt_bias[:, None])
    input_extended_left = jnp.concatenate([jnp.zeros((3, channels), jnp.bfloat16), x_input], axis=0)
    bc_padded = jnp.concatenate([jnp.zeros((2, 3, nstate), jnp.bfloat16), bc_input], axis=1)
    causal = jnp.tril(jnp.ones((length, length), dtype=bool))

    def prepare(block_index):
        first_row = (block_index * length).astype(jnp.int32)
        x_ext = lax.dynamic_slice_in_dim(input_extended_left, first_row, length + 3, 0)
        bc_ext = lax.dynamic_slice_in_dim(bc_padded, first_row, length + 3, 1)
        step_size = lax.dynamic_slice_in_dim(step_all, first_row, length, 1)
        x_pre = conv_rows(x_ext.astype(jnp.float32), conv_x)
        bc_pre = conv_rows(bc_ext.astype(jnp.float32), convolution_bc_taps)
        x_rows = jax.nn.silu(x_pre).astype(jnp.bfloat16)
        bc_rows = jax.nn.silu(bc_pre).astype(jnp.bfloat16)
        gram_matrix = jnp.dot(bc_rows[1], bc_rows[0].T, preferred_element_type=jnp.float32)
        cumul, x_heads, local_state = block_prep(x_rows, bc_rows[0], step_size, decay_rate)
        return (first_row, x_pre, bc_pre, bc_rows, step_size, gram_matrix, cumul, x_heads, local_state)

    def forward_block(state_exact, block_index):
        first_row, x_pre, bc_pre, bc_rows, step_size, gram_matrix, cumul, x_heads, local_state = prepare(block_index)
        z_rows = lax.dynamic_slice_in_dim(z_input, first_row, length, 0).astype(jnp.float32)
        grad_rows = lax.dynamic_slice_in_dim(grad_out, first_row, length, 0).astype(jnp.float32)
        mixed_out = block_mix(cumul, step_size, gram_matrix, x_heads, state_exact.astype(jnp.bfloat16), bc_rows[1], d_skip, causal)
        gate_value = jax.nn.silu(z_rows)
        gated = mixed_out * gate_value
        inv_rms = lax.rsqrt(lax.optimization_barrier(jnp.sum(gated * gated, axis=1)) / INNER + EPS)
        normed = gated * inv_rms[:, None]
        scaled = grad_rows * rescale_factor
        mean_dot = lax.optimization_barrier(jnp.sum(scaled * normed, axis=1)) / INNER
        grad_gated = inv_rms[:, None] * (scaled - normed * mean_dot[:, None])
        grad_z = (grad_gated * mixed_out * silu_grad(z_rows)).astype(jnp.bfloat16)
        grad_mixed = (grad_gated * gate_value).astype(jnp.bfloat16)
        grad_heads = jnp.moveaxis(grad_mixed.reshape(length, head_count, -1), 1, 0)
        state_grad = carry_grad(cumul, bc_rows[1], grad_heads)
        totals = cumul[:, -1]
        state_next = jnp.exp(totals)[:, None, None] * state_exact + local_state
        return (state_next, (state_exact, state_grad, grad_z, grad_heads))
    zero_state = jnp.zeros((head_count, nstate, HEAD_DIM), jnp.float32)
    block_ids = jnp.arange(N_SEQ, dtype=jnp.int32)
    final_state, (states_in, state_grads, grad_z_blocks, grad_head_blocks) = lax.scan(forward_block, zero_state, block_ids)

    def backward_block(running, block_items):
        out_exact, rim_x, rim_bc = running
        block_index, state_exact, state_grad, grad_heads = block_items
        first_row, x_pre, bc_pre, bc_rows, step_size, gram_matrix, cumul, x_heads, unused_state = prepare(block_index)
        grad_x_rows, grad_bc_rows, grad_steps = block_back(cumul, step_size, gram_matrix, x_heads, grad_heads, state_exact, out_exact, bc_rows[0], bc_rows[1], d_skip, decay_rate, causal)
        grad_x_pre = grad_x_rows * silu_grad(x_pre)
        grad_bc_pre = grad_bc_rows * silu_grad(bc_pre)
        grad_x_block = conv_back(jnp.concatenate([grad_x_pre, rim_x], axis=0), conv_x).astype(jnp.bfloat16)
        grad_bc_block = conv_back(jnp.concatenate([grad_bc_pre, rim_bc], axis=1), convolution_bc_taps).astype(jnp.bfloat16)
        raw_rows = lax.dynamic_slice_in_dim(dt_raw, first_row, length, 1)
        grad_dt_block = grad_steps * jax.nn.sigmoid(raw_rows + dt_bias[:, None])
        totals = cumul[:, -1]
        out_prior = state_grad + jnp.exp(totals)[:, None, None] * out_exact
        return ((out_prior, grad_x_pre[:3], grad_bc_pre[:, :3]), (grad_x_block, grad_bc_block, grad_dt_block))
    initial = (zero_state, jnp.zeros((3, channels), jnp.float32), jnp.zeros((2, 3, nstate), jnp.float32))
    final_back, (input_slope_parts, grad_bc_blocks, grad_dt_blocks) = lax.scan(backward_block, initial, (block_ids, states_in, state_grads, grad_head_blocks), reverse=True)
    grad_x = input_slope_parts.reshape(STREAM_LENGTH, channels)
    grad_z = grad_z_blocks.reshape(STREAM_LENGTH, channels)
    grad_bc = jnp.moveaxis(grad_bc_blocks, 0, 1).reshape(2, STREAM_LENGTH, nstate)
    grad_dt = jnp.moveaxis(grad_dt_blocks, 0, 1).reshape(head_count, STREAM_LENGTH)
    return (grad_x, grad_z, grad_bc, grad_dt)
```

```python
import functools

import jax
import jax.numpy as jnp
from jax import lax
from jax.experimental import pallas as pl
from jax.experimental.pallas import tpu as pltpu
from jax.sharding import PartitionSpec as P

EPS = 1e-05
GROUP = 8
F32 = jnp.float32
BF16 = jnp.bfloat16
EXACT = lax.Precision.HIGHEST
VMEM_BYTES = 40 * 2**20


def sigmoid(value):
    return 0.5 + 0.5 * jnp.tanh(0.5 * value)


def dot(a, b, precision=None):
    return jnp.dot(a, b, preferred_element_type=F32, precision=precision)


def dot_rows(a, b):
    return lax.dot_general(a, b, (((1,), (1,)), ((), ())), preferred_element_type=F32)


def dot_columns(a, b):
    return lax.dot_general(a, b, (((0,), (0,)), ((), ())), preferred_element_type=F32)


def triangle(length, upper):
    first = lax.broadcasted_iota(jnp.int32, (length, length), 0)
    second = lax.broadcasted_iota(jnp.int32, (length, length), 1)
    return first <= second if upper else first >= second


def columns_of(rows):
    return rows.T


def call(body, outs, ins, *, base=None, grid=(), scratch=(), aliases=None, flops=0, moved=0):
    in_specs = [pl.BlockSpec(block, index) for _, block, index in ins]
    out_specs = [pl.BlockSpec(block, index) for _, _, block, index in outs]
    out_shape = [jax.ShapeDtypeStruct(shape, dtype) for shape, dtype, _, _ in outs]
    arrays = [array for array, _, _ in ins]
    moved = moved or sum(a.size * a.dtype.itemsize for a in arrays) + sum(
        o.size * o.dtype.itemsize for o in out_shape
    )
    return pl.pallas_call(
        body,
        out_shape=out_shape,
        grid_spec=pltpu.PrefetchScalarGridSpec(
            num_scalar_prefetch=1,
            grid=grid,
            in_specs=in_specs,
            out_specs=out_specs,
            scratch_shapes=list(scratch),
        ),
        input_output_aliases=aliases or {},
        cost_estimate=pl.CostEstimate(flops=flops, bytes_accessed=moved, transcendentals=0),
        compiler_params=pltpu.CompilerParams(vmem_limit_bytes=VMEM_BYTES),
    )(base, *arrays)


def steps_body(_, raw, bias, log_rate, skip, step_out, cumul_out, rows_out):
    heads, length = raw.shape
    shifted = raw[...] + bias[...]
    step = jnp.maximum(shifted, 0.0) + jnp.log1p(jnp.exp(-jnp.abs(shifted)))
    decay = -jnp.exp(log_rate[...]) * step
    cumul = dot(decay, triangle(length, True).astype(F32), EXACT)
    step_out[...] = step
    cumul_out[...] = cumul
    for head in range(heads):
        lanes = slice(head * 128, head * 128 + 128)
        rows_out[0:1, lanes] = jnp.broadcast_to(cumul[head : head + 1, length - 1 :], (1, 128))
        rows_out[1:2, lanes] = jnp.broadcast_to(skip[head : head + 1, :], (1, 128))


def weights_body(place, own, core, across, diagonal, *outs):
    t0, t1 = own[0:1, :], core[...]
    e0, e1, own_chip = jnp.exp(t0), jnp.exp(t1), jnp.exp(t0 + t1)
    ex, ed = jnp.exp(across[...]), jnp.exp(diagonal[...])
    both = own_chip * ed
    one = jnp.ones_like(e0)
    zero = jnp.zeros_like(e0)
    for out, reverse in zip(outs, (False, True)):
        y, x, c = (
            (1 - place[i] if reverse else place[i]) == 1 for i in range(3)
        )
        pick = lambda test, yes, no: jnp.where(test, yes, no)
        rows = [pick(c, one, e1), pick(c, e0, one)]
        rows += [pick(x, one, ex), pick(x, own_chip, one)]
        rows += [
            pick(jnp.logical_and(x, y), zero, one),
            pick(y, pick(x, one, both), zero),
        ]
        second_in, second_take = pick(c, e1, one), pick(c, one, zero)
        first_send, first_take = pick(c, one, e0), pick(c, zero, one)
        a, b = pick(x, one, zero), pick(y, pick(x, ex, one), zero)
        rows += [second_in * a, second_in * b, second_take]
        rows += [first_send * a, first_send * b, first_take]
        a = pick(y, pick(x, ex, ed), zero)
        b = pick(jnp.logical_or(x, y), one, zero)
        rows += [second_in * a, second_in * b, second_take]
        rows += [first_send * a, first_send * b, first_take]
        for index, row in enumerate(rows):
            out[index : index + 1, :] = row


def combine(base, groups, weights, outs):
    arrays, columns = [], []
    for slots in outs:
        for column, terms in slots:
            if column not in columns:
                columns.append(column)
            for _, (array, slot) in terms:
                if not any(array is a and slot == s for a, s in arrays):
                    arrays.append((array, slot))
    place = lambda array, slot: [
        i for i, (a, s) in enumerate(arrays) if a is array and s == slot
    ][0]
    plan = [
        [
            (columns.index(column), [(row, place(*source)) for row, source in terms])
            for column, terms in slots
        ]
        for slots in outs
    ]

    def body(_, *refs):
        rows, values = refs[: len(columns)], refs[len(columns) : len(columns) + len(arrays)]
        results = refs[len(columns) + len(arrays) :]
        width = rows[0].shape[1]
        for result, slots in zip(results, plan):
            for slot, (column, terms) in enumerate(slots):
                for start in range(0, width, 256):
                    lanes = slice(start, start + 256)
                    total = None
                    for row, index in terms:
                        term = rows[column][row : row + 1, lanes] * values[index][
                            0, :, lanes
                        ].astype(F32)
                        total = term if total is None else total + term
                    result[slot, :, lanes] = total.astype(BF16)

    length, width = arrays[0][0].shape[1:]
    ins = [
        (
            weights,
            (weights.shape[0], width),
            lambda g, b, column=column: (0, lax.rem(b[0] + column, groups)),
        )
        for column in columns
    ]
    ins += [
        (array, (1, length, width), lambda g, b, slot=slot: (slot, 0, 0))
        for array, slot in arrays
    ]
    results = [
        ((len(slots), length, width), BF16, (len(slots), length, width), lambda g, b: (0, 0, 0))
        for slots in outs
    ]
    return call(body, results, ins, base=base, grid=(1,))


def scan_blocks(base, groups, weights, local, reverse):
    count = lax.axis_size("seq")
    place = lambda position: count - 1 - position if reverse else position

    def swap(block, bit, keep):
        route = [(place(i), place(i ^ bit)) for i in range(count) if keep(i)]
        return lax.ppermute(block, "seq", route)

    taken = swap(local[2:4], 1, lambda i: True)
    first, second = combine(
        base,
        groups,
        weights,
        [
            [(0, [(0, (local, 0)), (1, (taken, 0))])],
            [(1, [(0, (local, 1)), (1, (taken, 1))])],
        ],
    )
    first_a = swap(first, 2, lambda i: i < 6)
    second_a = swap(second, 4, lambda i: i < 4)
    (first_sent,) = combine(base, groups, weights, [[(0, [(2, (first, 0)), (3, (first_a, 0))])]])
    first_b = swap(first_sent, 4, lambda i: i < 4)
    (second_sent,) = combine(
        base, groups, weights, [[(1, [(4, (second, 0)), (5, (second_a, 0))])]]
    )
    second_b = swap(second_sent, 2, lambda i: i < 2 or i > 3)
    mine, sent = combine(
        base,
        groups,
        weights,
        [
            [
                (0, [(6, (first_a, 0)), (7, (first_b, 0)), (8, (taken, 0))]),
                (1, [(12, (second_a, 0)), (13, (second_b, 0)), (14, (taken, 1))]),
            ],
            [
                (0, [(9, (first_a, 0)), (10, (first_b, 0)), (11, (local, 0))]),
                (1, [(15, (second_a, 0)), (16, (second_b, 0)), (17, (local, 1))]),
            ],
        ],
    )
    return mine, swap(sent, 1, lambda i: True)


def gather_blocks(totals, local, reverse):
    table = lax.all_gather(totals, "seq", axis=0, tiled=True)
    blocks = lax.all_gather(local[None], "seq", axis=0, tiled=True)
    own = lax.axis_index("seq")
    order = jnp.arange(table.shape[0], dtype=jnp.int32)
    if reverse:
        inside = (order[None, :] > own) & (order[None, :] < order[:, None])
        selected = order > own
    else:
        inside = (order[None, :] > order[:, None]) & (order[None, :] < own)
        selected = order < own
    exponent = jnp.sum(jnp.where(inside[:, :, None], table[None], 0.0), axis=1)
    factor = jnp.where(selected[:, None], jnp.exp(exponent), 0.0)
    factor = factor.reshape(factor.shape[0], local.shape[0], 1, local.shape[2])
    state = jnp.sum(factor * blocks.astype(F32), axis=0).astype(BF16)
    return state, state


def prepare_body(
    base,
    x_in,
    x_halo,
    taps,
    bc_in,
    bc_halo,
    bc_taps,
    step_in,
    cumul_in,
    x_out,
    slope_out,
    state_out,
    bc_out,
    bc_slope_out,
    gram_out,
    ext,
    bc_ext,
    b_turned,
):
    length, width = x_in.shape

    @pl.when(pl.program_id(0) == 0)
    def _():
        for j in range(2):
            bc_ext[5:8, :] = bc_halo[:, j * 128 : j * 128 + 128].astype(F32)
            bc_ext[8 : 8 + length, :] = bc_in[j].astype(F32)
            pre = bc_taps[j, 0:1, :] * bc_ext[5 : 5 + length, :]
            for k in range(1, 4):
                pre = pre + bc_taps[j, k : k + 1, :] * bc_ext[5 + k : 5 + k + length, :]
            sigma = sigmoid(pre)
            bc_out[j] = (pre * sigma).astype(BF16)
            bc_slope_out[j] = sigma * (1.0 + pre * (1.0 - sigma))
        b_turned[...] = bc_out[0].astype(F32).T
        gram_out[...] = jnp.where(triangle(length, False), dot_rows(bc_out[1], bc_out[0]), 0.0)

    tail_step = jnp.exp(cumul_in[:, length - 1 :] - cumul_in[...]) * step_in[...]
    for head in range(width // 128):
        lanes = slice(head * 128, head * 128 + 128)
        ext[5:8, :] = x_halo[:, lanes].astype(F32)
        ext[8 : 8 + length, :] = x_in[:, lanes].astype(F32)
        pre = taps[0:1, lanes] * ext[5 : 5 + length, :]
        for k in range(1, 4):
            pre = pre + taps[k : k + 1, lanes] * ext[5 + k : 5 + k + length, :]
        sigma = sigmoid(pre)
        x_low = (pre * sigma).astype(BF16)
        x_out[:, lanes] = x_low
        slope_out[:, lanes] = sigma * (1.0 + pre * (1.0 - sigma))
        weighted = (b_turned[...] * tail_step[head : head + 1, :]).astype(BF16)
        state_out[0, :, lanes] = dot(weighted, x_low).astype(BF16)


def inner_body(base, gram, step_in, cumul_in, x_in, rows, mixed_out):
    cumul = cumul_in[...]
    cumul_columns = columns_of(cumul)
    for head in range(x_in.shape[1] // 128):
        lanes = slice(head * 128, head * 128 + 128)
        row = cumul[head : head + 1, :]
        decay = jnp.exp(jnp.minimum(cumul_columns[:, head : head + 1] - row, 0.0))
        mixer = (gram[...] * decay * step_in[head : head + 1, :]).astype(BF16)
        x_head = x_in[:, lanes]
        mixed_out[:, lanes] = dot(mixer, x_head) + rows[1:2, lanes] * x_head.astype(F32)


def pick_state(own_half, mine, other):
    group = pl.program_id(0)
    return jnp.where(group < own_half, mine[0], other[0])


def mix_body(
    own_half,
    base,
    mixed_in,
    c_rows,
    cumul_in,
    mine,
    other,
    z_in,
    grad_in,
    gain,
    mixed_out,
    sums_out,
    squares,
    products,
):
    group = pl.program_id(0)

    @pl.when(group == 0)
    def _():
        squares[...] = jnp.zeros_like(squares)
        products[...] = jnp.zeros_like(products)

    carried = dot(c_rows[0], pick_state(own_half, mine, other))
    lifted = jnp.exp(columns_of(cumul_in[...]))
    square, product = squares[...], products[...]
    for head in range(mixed_in.shape[1] // 128):
        lanes = slice(head * 128, head * 128 + 128)
        mixed = mixed_in[:, lanes] + lifted[:, head : head + 1] * carried[:, lanes]
        mixed_out[:, lanes] = mixed
        z = z_in[:, lanes].astype(F32)
        gated = mixed * z * sigmoid(z)
        square = square + gated * gated
        product = product + grad_in[:, lanes].astype(F32) * gain[:, lanes] * gated
    squares[...] = square
    products[...] = product

    @pl.when(group == pl.num_programs(0) - 1)
    def _():
        sums_out[0:1, :] = jnp.sum(squares[...].T, axis=0, keepdims=True)
        sums_out[1:2, :] = jnp.sum(products[...].T, axis=0, keepdims=True)
        sums_out[2:8, :] = jnp.zeros_like(sums_out[2:8, :])


def gate_body(
    inner,
    parts,
    base,
    *refs,
):
    sums = refs[:parts]
    mixed_in, z_in, grad_in, gain, bc, cumul_in, grad_z, grad_mixed, state_out, c_turned = refs[
        parts:
    ]

    @pl.when(pl.program_id(0) == 0)
    def _():
        c_turned[...] = bc[1].astype(F32).T

    total = sums[0][...]
    for part in sums[1:]:
        total = total + part[...]
    inv_rms = lax.rsqrt(total[0:1, :] / inner + EPS)
    mean_dot = inv_rms * total[1:2, :] / inner
    scales = jnp.concatenate(
        [inv_rms, inv_rms * inv_rms * mean_dot, jnp.zeros((6, total.shape[1]), F32)], axis=0
    )
    columns = columns_of(scales)
    alpha, beta = columns[:, 0:1], columns[:, 1:2]
    lifted = jnp.exp(cumul_in[...])
    for head in range(mixed_in.shape[1] // 128):
        lanes = slice(head * 128, head * 128 + 128)
        z = z_in[:, lanes].astype(F32)
        sigma = sigmoid(z)
        gate = z * sigma
        mixed = mixed_in[:, lanes]
        scaled = grad_in[:, lanes].astype(F32) * gain[:, lanes]
        grad_gated = alpha * scaled - beta * (mixed * gate)
        grad_z[:, lanes] = (grad_gated * mixed * (sigma * (1.0 + z * (1.0 - sigma)))).astype(BF16)
        low = (grad_gated * gate).astype(BF16)
        grad_mixed[:, lanes] = low
        lifted_c = (c_turned[...] * lifted[head : head + 1, :]).astype(BF16)
        state_out[0, :, lanes] = dot(lifted_c, low).astype(BF16)


def inner_back_body(
    own_half,
    base,
    gram,
    bc,
    step_in,
    cumul_in,
    x_in,
    grad_in,
    mine,
    other,
    rows,
    grad_x,
    q_out,
    r_out,
    bc_out,
    z_sum,
    c_sum,
):
    group = pl.program_id(0)
    length = x_in.shape[0]

    @pl.when(group == 0)
    def _():
        z_sum[...] = jnp.zeros_like(z_sum)
        c_sum[...] = jnp.zeros_like(c_sum)

    cumul = cumul_in[...]
    cumul_columns = columns_of(cumul)
    lifted = jnp.exp(cumul_columns)
    state = pick_state(own_half, mine, other)
    c_rows = bc[1].astype(F32)
    lane = lax.broadcasted_iota(jnp.int32, (length, 128), 1)
    q_columns = jnp.zeros((length, 128), F32)
    for head in range(x_in.shape[1] // 128):
        lanes = slice(head * 128, head * 128 + 128)
        step = step_in[head : head + 1, :]
        decay = jnp.exp(
            jnp.minimum(cumul_columns[:, head : head + 1] - cumul[head : head + 1, :], 0.0)
        )
        gram_decay = gram[...] * decay
        mixer = (gram_decay * step).astype(BF16)
        x_head, grad_head = x_in[:, lanes], grad_in[:, lanes]
        product = dot_rows(grad_head, x_head)
        z_sum[...] += product * decay * step
        gram_grad = product * gram_decay
        r_out[head : head + 1, :] = jnp.sum(gram_grad, axis=0, keepdims=True)
        handed = lifted[:, head : head + 1] * dot_rows(grad_head, state[:, lanes])
        c_sum[...] += handed
        q = jnp.sum(gram_grad * step + c_rows * handed, axis=1, keepdims=True)
        q_columns = jnp.where(lane == head, q, q_columns)
        grad_x[:, lanes] = dot_columns(mixer, grad_head) + rows[1:2, lanes] * grad_head.astype(F32)
    q_out[...] = q_columns.T[:GROUP, :]

    @pl.when(group == pl.num_programs(0) - 1)
    def _():
        summed = jnp.where(triangle(length, False), z_sum[...], 0.0)
        bc_out[0] = dot(summed.T, c_rows, EXACT)
        bc_out[1] = c_sum[...] + dot(summed, bc[0].astype(F32), EXACT)


def finish_body(
    own_half,
    base,
    bc,
    raw,
    bias,
    log_rate,
    step_in,
    cumul_in,
    q_in,
    r_in,
    x_in,
    partial,
    slope,
    taps,
    state_mine,
    state_other,
    out_mine,
    out_other,
    bc_partial,
    bc_slope,
    grad_x,
    head_rows,
    tail_rows,
    grad_dt,
    bc_out,
    ext,
    b_sum,
    dots,
):
    group = pl.program_id(0)
    length, width = x_in.shape

    @pl.when(group == 0)
    def _():
        b_sum[...] = jnp.zeros_like(b_sum)

    cumul, step = cumul_in[...], step_in[...]
    tail = jnp.exp(cumul[:, length - 1 :] - cumul)
    tail_columns = columns_of(tail)
    weight_columns = columns_of(tail * step)
    state = pick_state(own_half, state_mine, state_other)
    out_low = pick_state(own_half, out_mine, out_other)
    b_rows = bc[0].astype(F32)
    returned = dot(bc[0], out_low)
    lane = lax.broadcasted_iota(jnp.int32, (length, 128), 1)
    w_columns = jnp.zeros((length, 128), F32)
    ext[length : length + 8, :] = jnp.zeros((8, 128), F32)
    for head in range(width // 128):
        lanes = slice(head * 128, head * 128 + 128)
        weight = weight_columns[:, head : head + 1]
        reached = dot_rows(x_in[:, lanes], out_low[:, lanes])
        b_sum[...] += weight * reached
        w = tail_columns[:, head : head + 1] * jnp.sum(b_rows * reached, axis=1, keepdims=True)
        w_columns = jnp.where(lane == head, w, w_columns)
        dots[head : head + 1, :] = jnp.sum(
            out_low[:, lanes].astype(F32) * state[:, lanes].astype(F32), axis=0, keepdims=True
        )
        grad_pre = (partial[:, lanes] + weight * returned[:, lanes]) * slope[:, lanes]
        ext[0:length, :] = grad_pre
        head_rows[:, lanes] = grad_pre[:8, :]
        total = taps[0:1, lanes] * ext[3 : 3 + length, :]
        for k in range(1, 4):
            total = total + taps[k : k + 1, lanes] * ext[3 - k : 3 - k + length, :]
        grad_x[:, lanes] = total.astype(BF16)
        tail_rows[:, lanes] = total[length - 16 :, :]

    q, r = q_in[...], r_in[...]
    w = w_columns.T[:GROUP, :]
    inside = jnp.sum(step * w, axis=1, keepdims=True)
    end = inside + jnp.exp(cumul[:, length - 1 :]) * jnp.sum(dots[...], axis=1, keepdims=True)
    last = lax.broadcasted_iota(jnp.int32, (GROUP, length), 1) == length - 1
    grad_cumul = q - step * (r + w) + jnp.where(last, end, 0.0)
    grad_log = dot(grad_cumul, triangle(length, False).astype(F32), EXACT)
    grad_step = r + w - jnp.exp(log_rate[...]) * grad_log
    grad_dt[...] = grad_step * sigmoid(raw[...] + bias[...])

    @pl.when(group == pl.num_programs(0) - 1)
    def _():
        bc_out[0] = (b_sum[...] + bc_partial[0]) * bc_slope[0]
        bc_out[1] = bc_partial[1] * bc_slope[1]


def patch_body(base, grad_x, tail_rows, halo, taps, out):
    length = tail_rows.shape[0]
    rows = lax.broadcasted_iota(jnp.int32, tail_rows.shape, 0)
    total = tail_rows[...]
    for row in range(3):
        added = None
        for k in range(4):
            source = row + 3 - k - 3
            if 0 <= source < 3:
                term = taps[k : k + 1, :] * halo[source : source + 1, :]
                added = term if added is None else added + term
        total = total + jnp.where(rows == length - 3 + row, added, 0.0)
    out[...] = total.astype(BF16)


def conv_back(extended, weights):
    length = extended.shape[-2] - 3
    summed = weights[..., 0, :][..., None, :] * extended[..., 3 : 3 + length, :]
    for k in range(1, 4):
        summed = (
            summed
            + weights[..., k, :][..., None, :] * extended[..., 3 - k : 3 - k + length, :]
        )
    return summed


def shards(
    x_input,
    z_input,
    bc_input,
    dt_raw,
    dt_bias,
    a_log,
    d_skip,
    conv_x,
    convolution_bc_taps,
    rescale_factor,
    grad_out,
):
    length, channels = x_input.shape
    heads = dt_raw.shape[0]
    groups = heads // GROUP
    width = GROUP * 128
    count, parts = lax.axis_size("seq"), lax.axis_size("head")
    inner = channels * parts
    own = lax.axis_index("seq")
    split = count == 8 and groups == 4
    own_half = groups // 2 if split else groups
    base = ((own % 2) * own_half if split else own * 0).astype(jnp.int32)[None]

    whole = lambda *shape: (shape, lambda g, b: (0,) * len(shape))
    turn = lambda g, b: lax.rem(g + b[0], groups)
    wide = ((length, width), lambda g, b: (0, turn(g, b)))
    rows8 = ((GROUP, length), lambda g, b: (turn(g, b), 0))
    column8 = ((GROUP, 1), lambda g, b: (turn(g, b), 0))
    lanes_of = lambda n: ((n, width), lambda g, b: (0, turn(g, b)))
    slot = ((1, length, width), lambda g, b: (g, 0, 0))
    mine_slot = ((1, length, width), lambda g, b: (jnp.minimum(g, own_half - 1), 0, 0))
    other_slot = ((1, length, width), lambda g, b: (jnp.maximum(g - own_half, 0), 0, 0))
    full = lambda array: (array,) + whole(*array.shape)
    grid = (groups,)

    bias, log_rate, skip = dt_bias[:, None], a_log[:, None], d_skip[:, None]
    gain = rescale_factor[None, :]

    bc_rim = jnp.moveaxis(bc_input[:, length - 3 :], 0, 1).reshape(3, 256)
    rim = jnp.concatenate([x_input[length - 3 :], bc_rim], axis=1)
    rim = lax.ppermute(rim, "seq", [(i - 1, i) for i in range(1, count)])

    step, cumul, rows = call(
        steps_body,
        [
            ((heads, length), F32) + whole(heads, length),
            ((heads, length), F32) + whole(heads, length),
            ((2, channels), F32) + whole(2, channels),
        ],
        [full(dt_raw), full(bias), full(log_rate), full(skip)],
        base=base,
        grid=(1,),
    )
    if split:
        swap = lambda block, bit: lax.ppermute(
            block, "seq", [(i, i ^ bit) for i in range(count)]
        )
        total = rows[0:1]
        total_core = swap(total, 1)
        total_across = swap(total + total_core, 2)
        total_diagonal = swap(total_across, 4)
        place = jnp.stack([own // 4, own // 2 % 2, own % 2]).astype(jnp.int32)
        weight_shape = ((24, channels), F32) + whole(24, channels)
        ahead, behind = call(
            weights_body,
            [weight_shape, weight_shape],
            [full(rows), full(total_core), full(total_across), full(total_diagonal)],
            base=place,
            grid=(1,),
        )

    def passed(local, reverse):
        if split:
            return scan_blocks(base, groups, behind if reverse else ahead, local, reverse)
        return gather_blocks(rows[0:1], local, reverse)

    x_low, slope, local, bc, bc_slope, gram = call(
        prepare_body,
        [
            ((length, channels), BF16) + wide,
            ((length, channels), F32) + wide,
            ((groups, length, width), BF16) + slot,
            ((2, length, 128), BF16) + whole(2, length, 128),
            ((2, length, 128), F32) + whole(2, length, 128),
            ((length, length), F32) + whole(length, length),
        ],
        [
            (x_input,) + wide,
            (rim,) + lanes_of(3),
            (conv_x,) + lanes_of(4),
            full(bc_input),
            (rim, (3, 256), lambda g, b: (0, channels // 256)),
            full(convolution_bc_taps),
            (step,) + rows8,
            (cumul,) + rows8,
        ],
        base=base,
        grid=grid,
        scratch=[
            pltpu.VMEM((length + 8, 128), F32),
            pltpu.VMEM((length + 8, 128), F32),
            pltpu.VMEM((128, length), F32),
        ],
        flops=2 * length * 128 * channels,
    )
    (mixed,) = call(
        inner_body,
        [((length, channels), F32) + wide],
        [
            full(gram),
            (step,) + rows8,
            (cumul,) + rows8,
            (x_low,) + wide,
            (rows,) + lanes_of(2),
        ],
        base=base,
        grid=grid,
        flops=2 * length * 128 * channels,
    )
    state_mine, state_other = passed(local, False)
    c_spec = ((1, length, 128), lambda g, b: (1, 0, 0))
    mixed, sums = call(
        functools.partial(mix_body, own_half),
        [
            ((length, channels), F32) + wide,
            ((8, length), F32) + whole(8, length),
        ],
        [
            (mixed,) + wide,
            (bc,) + c_spec,
            (cumul,) + rows8,
            (state_mine,) + mine_slot,
            (state_other,) + other_slot,
            (z_input,) + wide,
            (grad_out,) + wide,
            (gain,) + lanes_of(1),
        ],
        base=base,
        grid=grid,
        scratch=[pltpu.VMEM((length, 128), F32), pltpu.VMEM((length, 128), F32)],
        flops=2 * length * 128 * channels,
    )
    if parts <= 4:
        all_sums = [sums] + [
            lax.ppermute(sums, "head", [(i, (i + shift) % parts) for i in range(parts)])
            for shift in range(1, parts)
        ]
    else:
        all_sums = [lax.psum(sums, "head")]
    grad_z, grad_mixed, local_back = call(
        functools.partial(gate_body, inner, len(all_sums)),
        [
            ((length, channels), BF16) + wide,
            ((length, channels), BF16) + wide,
            ((groups, length, width), BF16) + slot,
        ],
        [full(part) for part in all_sums]
        + [
            (mixed,) + wide,
            (z_input,) + wide,
            (grad_out,) + wide,
            (gain,) + lanes_of(1),
            full(bc),
            (cumul,) + rows8,
        ],
        base=base,
        grid=grid,
        scratch=[pltpu.VMEM((128, length), F32)],
        flops=2 * length * 128 * channels,
    )
    partial, q_rows, r_rows, bc_partial = call(
        functools.partial(inner_back_body, own_half),
        [
            ((length, channels), F32) + wide,
            ((heads, length), F32) + rows8,
            ((heads, length), F32) + rows8,
            ((2, length, 128), F32) + whole(2, length, 128),
        ],
        [
            full(gram),
            full(bc),
            (step,) + rows8,
            (cumul,) + rows8,
            (x_low,) + wide,
            (grad_mixed,) + wide,
            (state_mine,) + mine_slot,
            (state_other,) + other_slot,
            (rows,) + lanes_of(2),
        ],
        base=base,
        grid=grid,
        scratch=[pltpu.VMEM((length, length), F32), pltpu.VMEM((length, 128), F32)],
        flops=6 * length * 128 * channels,
    )
    out_mine, out_other = passed(local_back, True)
    grad_x, head_rows, tail_rows, grad_dt, grad_bc_pre = call(
        functools.partial(finish_body, own_half),
        [
            ((length, channels), BF16) + wide,
            ((8, channels), F32) + lanes_of(8),
            ((16, channels), F32) + lanes_of(16),
            ((heads, length), F32) + rows8,
            ((2, length, 128), F32) + whole(2, length, 128),
        ],
        [
            full(bc),
            (dt_raw,) + rows8,
            (bias,) + column8,
            (log_rate,) + column8,
            (step,) + rows8,
            (cumul,) + rows8,
            (q_rows,) + rows8,
            (r_rows,) + rows8,
            (x_low,) + wide,
            (partial,) + wide,
            (slope,) + wide,
            (conv_x,) + lanes_of(4),
            (state_mine,) + mine_slot,
            (state_other,) + other_slot,
            (out_mine,) + mine_slot,
            (out_other,) + other_slot,
            full(bc_partial),
            full(bc_slope),
        ],
        base=base,
        grid=grid,
        scratch=[
            pltpu.VMEM((length + 8, 128), F32),
            pltpu.VMEM((length, 128), F32),
            pltpu.VMEM((GROUP, 128), F32),
        ],
        flops=4 * length * 128 * channels,
    )
    back_route = [(i, i - 1) for i in range(1, count)]
    rim_back = jnp.concatenate(
        [head_rows[:3], grad_bc_pre[0, :3], grad_bc_pre[1, :3]], axis=1
    )
    rim_back = lax.ppermute(rim_back, "seq", back_route)
    bc_rim_back = jnp.moveaxis(rim_back[:, channels:].reshape(3, 2, 128), 1, 0)
    bc_sum = conv_back(jnp.concatenate([grad_bc_pre, bc_rim_back], axis=1), convolution_bc_taps)
    share = length // parts
    place_head = lax.axis_index("head")
    take = lambda block, index: lax.dynamic_slice_in_dim(block, index * share, share, 1)
    if parts <= 4:
        grad_bc = take(bc_sum, place_head)
        for shift in range(1, parts):
            sent = take(bc_sum, (place_head + shift) % parts)
            grad_bc = grad_bc + lax.ppermute(
                sent, "head", [(i, (i + shift) % parts) for i in range(parts)]
            )
    else:
        grad_bc = take(lax.psum(bc_sum, "head"), place_head)
    grad_bc = grad_bc.astype(BF16)

    rows16 = ((16, channels), lambda g, b: (length // 16 - 1, 0))
    (grad_x,) = call(
        patch_body,
        [((length, channels), BF16) + rows16],
        [
            (grad_x,) + rows16,
            full(tail_rows),
            (rim_back, (3, channels), lambda g, b: (0, 0)),
            full(conv_x),
        ],
        base=base,
        grid=(1,),
        aliases={1: 0},
    )
    return (grad_x, grad_z, grad_bc, grad_dt)


def solution(mesh):
    return jax.shard_map(
        shards,
        mesh=mesh,
        in_specs=(
            P("seq", "head"),
            P("seq", "head"),
            P(None, "seq", None),
            P("head", "seq"),
            P("head"),
            P("head"),
            P("head"),
            P(None, "head"),
            P(),
            P("head"),
            P("seq", "head"),
        ),
        out_specs=(
            P("seq", "head"),
            P("seq", "head"),
            P(None, ("seq", "head"), None),
            P("head", "seq"),
        ),
        check_vma=False,
    )
```

```python
import functools

import jax
import jax.numpy as jnp
from jax import lax
from jax.experimental import pallas as pl
from jax.experimental.pallas import tpu as pltpu
from jax.sharding import PartitionSpec as P

EPS = 1e-05
GROUP = 8
F32 = jnp.float32
BF16 = jnp.bfloat16
EXACT = lax.Precision.HIGHEST
VMEM_BYTES = 40 * 2**20


def sigmoid(value):
    return 0.5 + 0.5 * jnp.tanh(0.5 * value)


def dot(a, b, precision=None):
    return jnp.dot(a, b, preferred_element_type=F32, precision=precision)


def dot_rows(a, b):
    return lax.dot_general(a, b, (((1,), (1,)), ((), ())), preferred_element_type=F32)


def dot_columns(a, b):
    return lax.dot_general(a, b, (((0,), (0,)), ((), ())), preferred_element_type=F32)


def triangle(length, upper):
    first = lax.broadcasted_iota(jnp.int32, (length, length), 0)
    second = lax.broadcasted_iota(jnp.int32, (length, length), 1)
    return first <= second if upper else first >= second


def columns_of(rows):
    return rows.T


def call(body, outs, ins, *, base=None, grid=(), scratch=(), aliases=None, after=(), flops=0):
    in_specs = [pl.BlockSpec(block, index) for _, block, index in ins]
    in_specs += [pl.BlockSpec(memory_space=pl.ANY) for _ in after]
    out_specs = [pl.BlockSpec(block, index) for _, _, block, index in outs]
    out_shape = [jax.ShapeDtypeStruct(shape, dtype) for shape, dtype, _, _ in outs]
    arrays = [array for array, _, _ in ins]
    moved = sum(a.size * a.dtype.itemsize for a in arrays + out_shape)
    read = 1 + len(arrays)

    def ordered(*refs):
        body(*refs[:read], *refs[read + len(after) :])

    return pl.pallas_call(
        ordered,
        out_shape=out_shape,
        grid_spec=pltpu.PrefetchScalarGridSpec(
            num_scalar_prefetch=1,
            grid=grid,
            in_specs=in_specs,
            out_specs=out_specs,
            scratch_shapes=list(scratch),
        ),
        input_output_aliases=aliases or {},
        cost_estimate=pl.CostEstimate(flops=flops, bytes_accessed=moved, transcendentals=0),
        compiler_params=pltpu.CompilerParams(vmem_limit_bytes=VMEM_BYTES),
    )(base, *arrays, *after)


def in_hbm(array):
    return pltpu.with_memory_space_constraint(array, pltpu.HBM)


def column_of(row):
    count = row.shape[1]
    first = lax.broadcasted_iota(jnp.int32, (count, count), 0)
    second = lax.broadcasted_iota(jnp.int32, (count, count), 1)
    return jnp.sum(jnp.where(first == second, row, 0.0), axis=1, keepdims=True)


def steps_body(
    _,
    raw,
    bias,
    log_rate,
    skip,
    x_tail,
    bc_tail,
    step_out,
    cumul_out,
    rate_out,
    slope_out,
    rows_out,
    rim_out,
):
    heads, length = raw.shape
    channels = x_tail.shape[1]
    rim_out[:, 0:channels] = x_tail[...].astype(F32)[13:16, :].astype(BF16)
    for j in range(2):
        start = channels + 128 * j
        rim_out[:, start : start + 128] = bc_tail[j].astype(F32)[13:16, :].astype(BF16)
    shifted = raw[...] + column_of(bias[...])
    step = jnp.maximum(shifted, 0.0) + jnp.log1p(jnp.exp(-jnp.abs(shifted)))
    rate = jnp.broadcast_to(-jnp.exp(column_of(log_rate[...])), step.shape)
    cumul = dot(rate * step, triangle(length, True).astype(F32), EXACT)
    step_out[...] = step
    cumul_out[...] = cumul
    rate_out[...] = rate
    slope_out[...] = sigmoid(shifted)
    skips = column_of(skip[...])
    for head in range(heads):
        lanes = slice(head * 128, head * 128 + 128)
        rows_out[0:1, lanes] = jnp.broadcast_to(cumul[head : head + 1, length - 1 :], (1, 128))
        rows_out[1:2, lanes] = jnp.broadcast_to(skips[head : head + 1, :], (1, 128))


def pick(test, yes, no):
    return jnp.where(test, yes, no)


def place_bits(place, reverse):
    return [(1 - place[i] if reverse else place[i]) == 1 for i in range(3)]


def chip_weights_body(place, own, core, *outs):
    t0, t1 = own[0:1, :], core[...]
    one = jnp.ones_like(t0)
    for out, reverse in zip(outs, (False, True)):
        _, _, c = place_bits(place, reverse)
        out[0:1, :] = pick(c, one, jnp.exp(t1))
        out[1:2, :] = pick(c, jnp.exp(t0), one)
    outs[2][...] = t0 + t1


def weights_body(place, own, core, across, diagonal, *outs):
    t0, t1 = own[0:1, :], core[...]
    e0, e1, own_chip = jnp.exp(t0), jnp.exp(t1), jnp.exp(t0 + t1)
    ex, ed = jnp.exp(across[...]), jnp.exp(diagonal[...])
    both = own_chip * ed
    one = jnp.ones_like(e0)
    zero = jnp.zeros_like(e0)
    x_first = place[2] == 0
    for out, reverse in zip(outs, (False, True)):
        y, x, c = place_bits(place, reverse)
        rows = [
            pick(x_first, pick(x, one, ex), pick(jnp.logical_and(x, y), zero, one)),
            pick(x_first, pick(x, own_chip, one), pick(y, pick(x, one, both), zero)),
        ]
        a = pick(x_first, pick(x, one, zero), pick(y, pick(x, ex, ed), zero))
        b = pick(
            x_first, pick(y, pick(x, ex, one), zero), pick(jnp.logical_or(x, y), one, zero)
        )
        into, send = pick(c, e1, one), pick(c, one, e0)
        rows += [into * a, into * b, pick(c, one, zero)]
        rows += [send * a, send * b, pick(c, zero, one)]
        for index, row in enumerate(rows):
            out[index : index + 1, :] = row


def combine(base, groups, weights, outs, after=()):
    arrays, columns = [], []
    for slots in outs:
        for column, terms in slots:
            if column not in columns:
                columns.append(column)
            for _, (array, slot) in terms:
                if not any(array is a and slot == s for a, s in arrays):
                    arrays.append((array, slot))
    place = lambda array, slot: [
        i for i, (a, s) in enumerate(arrays) if a is array and s == slot
    ][0]
    plan = [
        [
            (columns.index(column), [(row, place(*source)) for row, source in terms])
            for column, terms in slots
        ]
        for slots in outs
    ]

    def body(_, *refs):
        rows, values = refs[: len(columns)], refs[len(columns) : len(columns) + len(arrays)]
        results = refs[len(columns) + len(arrays) :]
        width = rows[0].shape[1]
        for result, slots in zip(results, plan):
            for slot, (column, terms) in enumerate(slots):
                for start in range(0, width, 256):
                    lanes = slice(start, start + 256)
                    total = None
                    for row, index in terms:
                        term = rows[column][row : row + 1, lanes] * values[index][
                            0, :, lanes
                        ].astype(F32)
                        total = term if total is None else total + term
                    result[slot, :, lanes] = total.astype(BF16)

    length, width = arrays[0][0].shape[1:]
    ins = [
        (
            weights,
            (weights.shape[0], width),
            lambda g, b, column=column: (0, lax.rem(b[0] + column, groups)),
        )
        for column in columns
    ]
    ins += [
        (array, (1, length, width), lambda g, b, slot=slot: (slot, 0, 0))
        for array, slot in arrays
    ]
    results = [
        ((len(slots), length, width), BF16, (len(slots), length, width), lambda g, b: (0, 0, 0))
        for slots in outs
    ]
    return call(body, results, ins, base=base, grid=(1,), after=after)


def scan_blocks(base, groups, chip_weights, weights, local, reverse, beside):
    count = lax.axis_size("seq")
    place = lambda position: count - 1 - position if reverse else position

    def swap(block, bit_of, keep):
        route = [
            (place(i), place(i ^ bit_of(place(i) % 2)))
            for i in range(count)
            if keep(i, place(i) % 2)
        ]
        return lax.ppermute(block, "seq", route)

    def both(rows, sources):
        return [
            (slot, [(row, (array, slot)) for row, array in zip(rows, sources)])
            for slot in range(2)
        ]

    def merge(table, *plans, after=()):
        return combine(base, groups, table, [both(*plan) for plan in plans], after)

    everyone = lambda i, core: True
    taken = swap(local[2:4], lambda core: 1, everyone)
    (chip,) = merge(chip_weights, ((0, 1), (local, taken)))
    chip_a = swap(
        chip, lambda core: 4 if core else 2, lambda i, core: i < 4 if core else i < 6
    )
    after_a = beside[0](chip)
    (sent,) = merge(weights, ((0, 1), (chip, chip_a)), after=[after_a])
    chip_b = swap(
        sent, lambda core: 2 if core else 4, lambda i, core: i not in (2, 3) if core else i < 4
    )
    after_b = beside[1](sent)
    mine, handed = merge(
        weights,
        ((2, 3, 4), (chip_a, chip_b, taken)),
        ((5, 6, 7), (chip_a, chip_b, local)),
        after=[after_b],
    )
    return mine, swap(handed, lambda core: 1, everyone)


def gather_blocks(totals, local, reverse):
    table = lax.all_gather(totals, "seq", axis=0, tiled=True)
    blocks = lax.all_gather(local[None], "seq", axis=0, tiled=True)
    own = lax.axis_index("seq")
    order = jnp.arange(table.shape[0], dtype=jnp.int32)
    if reverse:
        inside = (order[None, :] > own) & (order[None, :] < order[:, None])
        selected = order > own
    else:
        inside = (order[None, :] > order[:, None]) & (order[None, :] < own)
        selected = order < own
    exponent = jnp.sum(jnp.where(inside[:, :, None], table[None], 0.0), axis=1)
    factor = jnp.where(selected[:, None], jnp.exp(exponent), 0.0)
    factor = factor.reshape(factor.shape[0], local.shape[0], 1, local.shape[2])
    state = jnp.sum(factor * blocks.astype(F32), axis=0).astype(BF16)
    return state, state


def prepare_body(
    base,
    x_in,
    x_halo,
    taps,
    bc_in,
    bc_halo,
    bc_taps,
    step_in,
    cumul_in,
    x_out,
    slope_out,
    state_out,
    bc_out,
    bc_slope_out,
    gram_out,
    ext,
    bc_ext,
    b_turned,
):
    length, width = x_in.shape

    @pl.when(pl.program_id(0) == 0)
    def _():
        for j in range(2):
            bc_ext[5:8, :] = bc_halo[:, j * 128 : j * 128 + 128].astype(F32)
            bc_ext[8 : 8 + length, :] = bc_in[j].astype(F32)
            pre = bc_taps[j, 0:1, :] * bc_ext[5 : 5 + length, :]
            for k in range(1, 4):
                pre = pre + bc_taps[j, k : k + 1, :] * bc_ext[5 + k : 5 + k + length, :]
            sigma = sigmoid(pre)
            bc_out[j] = (pre * sigma).astype(BF16)
            bc_slope_out[j] = sigma * (1.0 + pre * (1.0 - sigma))
        b_turned[...] = bc_out[0].astype(F32).T
        gram_out[...] = jnp.where(triangle(length, False), dot_rows(bc_out[1], bc_out[0]), 0.0)

    tail_step = jnp.exp(cumul_in[:, length - 1 :] - cumul_in[...]) * step_in[...]
    for head in range(width // 128):
        lanes = slice(head * 128, head * 128 + 128)
        ext[5:8, :] = x_halo[:, lanes].astype(F32)
        ext[8 : 8 + length, :] = x_in[:, lanes].astype(F32)
        pre = taps[0:1, lanes] * ext[5 : 5 + length, :]
        for k in range(1, 4):
            pre = pre + taps[k : k + 1, lanes] * ext[5 + k : 5 + k + length, :]
        sigma = sigmoid(pre)
        x_low = (pre * sigma).astype(BF16)
        x_out[:, lanes] = x_low
        slope_out[:, lanes] = sigma * (1.0 + pre * (1.0 - sigma))
        weighted = (b_turned[...] * tail_step[head : head + 1, :]).astype(BF16)
        state_out[0, :, lanes] = dot(weighted, x_low).astype(BF16)


def inner_body(base, gram, step_in, cumul_in, x_in, rows, mixed_out):
    cumul = cumul_in[...]
    cumul_columns = columns_of(cumul)
    for head in range(x_in.shape[1] // 128):
        lanes = slice(head * 128, head * 128 + 128)
        row = cumul[head : head + 1, :]
        decay = jnp.exp(jnp.minimum(cumul_columns[:, head : head + 1] - row, 0.0))
        mixer = (gram[...] * decay * step_in[head : head + 1, :]).astype(BF16)
        x_head = x_in[:, lanes]
        mixed_out[:, lanes] = dot(mixer, x_head) + rows[1:2, lanes] * x_head.astype(F32)


def pick_state(own_half, mine, other):
    group = pl.program_id(0)
    return jnp.where(group < own_half, mine[0], other[0])


def gate_body(base, z_in, grad_in, gain, gate_out, scaled_out):
    for start in range(0, z_in.shape[1], 128):
        lanes = slice(start, start + 128)
        z = z_in[:, lanes].astype(F32)
        gate = z * sigmoid(z)
        gate_out[:, lanes] = gate
        scaled_out[:, lanes] = grad_in[:, lanes].astype(F32) * gain[:, lanes] * gate


def mix_body(
    own_half,
    base,
    mixed_in,
    c_rows,
    cumul_in,
    mine,
    other,
    gate_in,
    scaled_in,
    mixed_out,
    sums_out,
    squares,
    products,
):
    group = pl.program_id(0)

    @pl.when(group == 0)
    def _():
        squares[...] = jnp.zeros_like(squares)
        products[...] = jnp.zeros_like(products)

    carried = dot(c_rows[0], pick_state(own_half, mine, other))
    lifted = jnp.exp(columns_of(cumul_in[...]))
    square, product = squares[...], products[...]
    for head in range(mixed_in.shape[1] // 128):
        lanes = slice(head * 128, head * 128 + 128)
        mixed = mixed_in[:, lanes] + lifted[:, head : head + 1] * carried[:, lanes]
        mixed_out[:, lanes] = mixed
        gated = mixed * gate_in[:, lanes]
        square = square + gated * gated
        product = product + mixed * scaled_in[:, lanes]
    squares[...] = square
    products[...] = product

    @pl.when(group == pl.num_programs(0) - 1)
    def _():
        sums_out[0:1, :] = jnp.sum(squares[...].T, axis=0, keepdims=True)
        sums_out[1:2, :] = jnp.sum(products[...].T, axis=0, keepdims=True)
        sums_out[2:8, :] = jnp.zeros_like(sums_out[2:8, :])


def norm_columns(inner, sums):
    total = sums[0][...]
    for part in sums[1:]:
        total = total + part[...]
    inv_rms = lax.rsqrt(total[0:1, :] / inner + EPS)
    mean_dot = inv_rms * total[1:2, :] / inner
    scales = jnp.concatenate(
        [inv_rms, inv_rms * inv_rms * mean_dot, jnp.zeros((6, total.shape[1]), F32)], axis=0
    )
    columns = columns_of(scales)
    return columns[:, 0:1], columns[:, 1:2]


def grad_mixed_body(inner, parts, base, *refs):
    sums = refs[:parts]
    mixed_in, gate_in, scaled_in, bc, cumul_in, grad_mixed, state_out, c_turned = refs[parts:]

    @pl.when(pl.program_id(0) == 0)
    def _():
        c_turned[...] = bc[1].astype(F32).T

    alpha, beta = norm_columns(inner, sums)
    lifted = jnp.exp(cumul_in[...])
    for head in range(mixed_in.shape[1] // 128):
        lanes = slice(head * 128, head * 128 + 128)
        gate = gate_in[:, lanes]
        low = (
            alpha * scaled_in[:, lanes] - beta * (mixed_in[:, lanes] * gate * gate)
        ).astype(BF16)
        grad_mixed[:, lanes] = low
        lifted_c = (c_turned[...] * lifted[head : head + 1, :]).astype(BF16)
        state_out[0, :, lanes] = dot(lifted_c, low).astype(BF16)


def grad_z_body(inner, parts, base, *refs):
    sums = refs[:parts]
    mixed_in, z_in, grad_in, gain, grad_z = refs[parts:]
    alpha, beta = norm_columns(inner, sums)
    for start in range(0, z_in.shape[1], 128):
        lanes = slice(start, start + 128)
        z = z_in[:, lanes].astype(F32)
        sigma = sigmoid(z)
        mixed = mixed_in[:, lanes]
        scaled = grad_in[:, lanes].astype(F32) * gain[:, lanes]
        grad_gated = alpha * scaled - beta * (mixed * (z * sigma))
        grad_z[:, lanes] = (grad_gated * mixed * (sigma * (1.0 + z * (1.0 - sigma)))).astype(BF16)


def inner_back_body(
    own_half,
    base,
    gram,
    bc,
    step_in,
    cumul_in,
    x_in,
    grad_in,
    mine,
    other,
    rows,
    grad_x,
    q_out,
    r_out,
    weighted_x,
    bc_out,
    z_sum,
    c_sum,
):
    group = pl.program_id(0)
    length = x_in.shape[0]

    @pl.when(group == 0)
    def _():
        z_sum[...] = jnp.zeros_like(z_sum)
        c_sum[...] = jnp.zeros_like(c_sum)

    cumul = cumul_in[...]
    cumul_columns = columns_of(cumul)
    lifted = jnp.exp(cumul_columns)
    weights = columns_of(jnp.exp(cumul[:, length - 1 :] - cumul) * step_in[...])
    state = pick_state(own_half, mine, other)
    c_rows = bc[1].astype(F32)
    lane = lax.broadcasted_iota(jnp.int32, (length, 128), 1)
    q_columns = jnp.zeros((length, 128), F32)
    for head in range(x_in.shape[1] // 128):
        lanes = slice(head * 128, head * 128 + 128)
        step = step_in[head : head + 1, :]
        decay = jnp.exp(
            jnp.minimum(cumul_columns[:, head : head + 1] - cumul[head : head + 1, :], 0.0)
        )
        gram_decay = gram[...] * decay
        mixer = (gram_decay * step).astype(BF16)
        x_head, grad_head = x_in[:, lanes], grad_in[:, lanes]
        product = dot_rows(grad_head, x_head)
        z_sum[...] += product * decay * step
        gram_grad = product * gram_decay
        r_out[head : head + 1, :] = jnp.sum(gram_grad, axis=0, keepdims=True)
        handed = lifted[:, head : head + 1] * dot_rows(grad_head, state[:, lanes])
        c_sum[...] += handed
        q = jnp.sum(gram_grad * step + c_rows * handed, axis=1, keepdims=True)
        q_columns = jnp.where(lane == head, q, q_columns)
        weighted_x[:, lanes] = (weights[:, head : head + 1] * x_head.astype(F32)).astype(BF16)
        grad_x[:, lanes] = dot_columns(mixer, grad_head) + rows[1:2, lanes] * grad_head.astype(F32)
    q_out[...] = q_columns.T[:GROUP, :]

    @pl.when(group == pl.num_programs(0) - 1)
    def _():
        summed = jnp.where(triangle(length, False), z_sum[...], 0.0)
        bc_out[0] = dot(summed.T, c_rows, EXACT)
        bc_out[1] = c_sum[...] + dot(summed, bc[0].astype(F32), EXACT)


def block_weights(step, cumul):
    return columns_of(jnp.exp(cumul[:, cumul.shape[1] - 1 :] - cumul) * step)


def rim_body(
    own_half,
    base,
    bc,
    step_in,
    cumul_in,
    weighted_x,
    partial,
    slope,
    out_mine,
    out_other,
    bc_partial,
    bc_slope,
    rim_out,
    bc_out,
    b_sum,
):
    group = pl.program_id(0)

    @pl.when(group == 0)
    def _():
        b_sum[...] = jnp.zeros_like(b_sum)

    out_low = pick_state(own_half, out_mine, out_other)
    b_sum[...] += dot_rows(weighted_x[...], out_low)
    weights = block_weights(step_in[...], cumul_in[...])[0:8, :]
    returned = dot(bc[0][0:16, :], out_low)[0:8, :]
    for head in range(weighted_x.shape[1] // 128):
        lanes = slice(head * 128, head * 128 + 128)
        weight = weights[:, head : head + 1]
        rim_out[:, lanes] = (partial[:, lanes] + weight * returned[:, lanes]) * slope[:, lanes]

    @pl.when(group == pl.num_programs(0) - 1)
    def _():
        bc_out[0] = (b_sum[...] + bc_partial[0]) * bc_slope[0]
        bc_out[1] = bc_partial[1] * bc_slope[1]


def grad_dt_body(
    own_half,
    base,
    bc,
    rate,
    dt_slope,
    step_in,
    cumul_in,
    q_in,
    r_in,
    x_in,
    state_mine,
    state_other,
    out_mine,
    out_other,
    grad_dt,
    selector,
    products,
):
    length, width = x_in.shape

    @pl.when(pl.program_id(0) == 0)
    def _():
        row = lax.broadcasted_iota(jnp.int32, (width, 128), 0)
        lane = lax.broadcasted_iota(jnp.int32, (width, 128), 1)
        selector[...] = (row // 128 == lane).astype(BF16)

    cumul, step = cumul_in[...], step_in[...]
    state = pick_state(own_half, state_mine, state_other)
    out_low = pick_state(own_half, out_mine, out_other)
    returned = dot(bc[0], out_low)
    for start in range(0, width, 128):
        lanes = slice(start, start + 128)
        products[:, lanes] = (x_in[:, lanes].astype(F32) * returned[:, lanes]).astype(BF16)
    inner_b = dot(products[...], selector[...]).T[:GROUP, :]
    w = jnp.exp(cumul[:, length - 1 :] - cumul) * inner_b
    dots = dot(jnp.ones((16, length), BF16), state * out_low)[:GROUP, :]
    row = lax.broadcasted_iota(jnp.int32, (GROUP, width), 0)
    lane = lax.broadcasted_iota(jnp.int32, (GROUP, width), 1)
    dots = jnp.sum(jnp.where(lane // 128 == row, dots, 0.0), axis=1, keepdims=True)
    q, r = q_in[...], r_in[...]
    inside = jnp.sum(step * w, axis=1, keepdims=True)
    end = inside + jnp.exp(cumul[:, length - 1 :]) * dots
    last = lax.broadcasted_iota(jnp.int32, (GROUP, length), 1) == length - 1
    grad_cumul = q - step * (r + w) + jnp.where(last, end, 0.0)
    grad_log = dot(grad_cumul, triangle(length, False).astype(F32), EXACT)
    grad_dt[...] = (r + w + rate[...] * grad_log) * dt_slope[...]


def grad_x_body(
    own_half,
    base,
    bc,
    step_in,
    cumul_in,
    partial,
    slope,
    taps,
    halo,
    out_mine,
    out_other,
    grad_x,
    ext,
):
    length, width = partial.shape
    weights = block_weights(step_in[...], cumul_in[...])
    returned = dot(bc[0], pick_state(own_half, out_mine, out_other))
    for head in range(width // 128):
        lanes = slice(head * 128, head * 128 + 128)
        weight = weights[:, head : head + 1]
        ext[0:length, :] = (partial[:, lanes] + weight * returned[:, lanes]) * slope[:, lanes]
        ext[length : length + 3, :] = halo[:, lanes]
        total = taps[0:1, lanes] * ext[3 : 3 + length, :]
        for k in range(1, 4):
            total = total + taps[k : k + 1, lanes] * ext[3 - k : 3 - k + length, :]
        grad_x[:, lanes] = total.astype(BF16)


def conv_back(extended, weights):
    length = extended.shape[-2] - 3
    summed = weights[..., 0, :][..., None, :] * extended[..., 3 : 3 + length, :]
    for k in range(1, 4):
        summed = (
            summed
            + weights[..., k, :][..., None, :] * extended[..., 3 - k : 3 - k + length, :]
        )
    return summed


def shards(
    x_input,
    z_input,
    bc_input,
    dt_raw,
    dt_bias,
    a_log,
    d_skip,
    conv_x,
    convolution_bc_taps,
    rescale_factor,
    grad_out,
):
    length, channels = x_input.shape
    heads = dt_raw.shape[0]
    groups = heads // GROUP
    width = GROUP * 128
    count, parts = lax.axis_size("seq"), lax.axis_size("head")
    inner = channels * parts
    own = lax.axis_index("seq")
    split = count == 8 and groups == 4
    own_half = groups // 2 if split else groups
    base = ((own % 2) * own_half if split else own * 0).astype(jnp.int32)[None]

    whole = lambda *shape: (shape, lambda g, b: (0,) * len(shape))
    turn = lambda g, b: lax.rem(g + b[0], groups)
    wide = ((length, width), lambda g, b: (0, turn(g, b)))
    rows8 = ((GROUP, length), lambda g, b: (turn(g, b), 0))
    lanes_of = lambda n: ((n, width), lambda g, b: (0, turn(g, b)))
    slot = ((1, length, width), lambda g, b: (g, 0, 0))
    mine_slot = ((1, length, width), lambda g, b: (jnp.minimum(g, own_half - 1), 0, 0))
    other_slot = ((1, length, width), lambda g, b: (jnp.maximum(g - own_half, 0), 0, 0))
    full = lambda array: (array,) + whole(*array.shape)
    grid = (groups,)

    gain = rescale_factor[None, :]
    f32 = lambda *shape: (shape, F32)
    low = lambda *shape: (shape, BF16)

    step, cumul, rate, dt_slope, rows, rim = call(
        steps_body,
        [
            f32(heads, length) + whole(heads, length),
            f32(heads, length) + whole(heads, length),
            f32(heads, length) + whole(heads, length),
            f32(heads, length) + whole(heads, length),
            f32(2, channels) + whole(2, channels),
            low(3, channels + 256) + whole(3, channels + 256),
        ],
        [
            full(in_hbm(dt_raw)),
            full(dt_bias[None, :]),
            full(a_log[None, :]),
            full(d_skip[None, :]),
            (in_hbm(x_input), (16, channels), lambda g, b: (length // 16 - 1, 0)),
            (in_hbm(bc_input), (2, 16, 128), lambda g, b: (0, length // 16 - 1, 0)),
        ],
        base=base,
        grid=(1,),
    )
    rim = lax.ppermute(rim, "seq", [(i - 1, i) for i in range(1, count)])
    if split:
        swap = lambda block, bit: lax.ppermute(
            block, "seq", [(i, i ^ bit) for i in range(count)]
        )
        total_core = swap(rows[0:1], 1)
        place = jnp.stack([own // 4, own // 2 % 2, own % 2]).astype(jnp.int32)
        pair = f32(2, channels) + whole(2, channels)
        chip_ahead, chip_behind, chip_total = call(
            chip_weights_body,
            [pair, pair, f32(1, channels) + whole(1, channels)],
            [full(rows), full(total_core)],
            base=place,
            grid=(1,),
        )
        total_across = swap(chip_total, 2)
        total_diagonal = swap(chip_total, 6)
        eight = f32(8, channels) + whole(8, channels)
        ahead, behind = call(
            weights_body,
            [eight, eight],
            [full(rows), full(total_core), full(total_across), full(total_diagonal)],
            base=place,
            grid=(1,),
        )

    def passed(local, reverse, beside):
        if split:
            chip = chip_behind if reverse else chip_ahead
            table = behind if reverse else ahead
            return scan_blocks(base, groups, chip, table, local, reverse, beside)
        for work in beside:
            work(local)
        return gather_blocks(rows[0:1], local, reverse)

    x_low, slope, local, bc, bc_slope, gram = call(
        prepare_body,
        [
            low(length, channels) + wide,
            f32(length, channels) + wide,
            low(groups, length, width) + slot,
            low(2, length, 128) + whole(2, length, 128),
            f32(2, length, 128) + whole(2, length, 128),
            f32(length, length) + whole(length, length),
        ],
        [
            (in_hbm(x_input),) + wide,
            (rim,) + lanes_of(3),
            (in_hbm(conv_x),) + lanes_of(4),
            full(in_hbm(bc_input)),
            (rim, (3, 256), lambda g, b: (0, channels // 256)),
            full(in_hbm(convolution_bc_taps)),
            (step,) + rows8,
            (cumul,) + rows8,
        ],
        base=base,
        grid=grid,
        scratch=[
            pltpu.VMEM((length + 8, 128), F32),
            pltpu.VMEM((length + 8, 128), F32),
            pltpu.VMEM((128, length), F32),
        ],
        flops=2 * length * 128 * channels,
    )
    done = {}

    def mix_inside(ready):
        (done["mixed"],) = call(
            inner_body,
            [f32(length, channels) + wide],
            [
                full(gram),
                (step,) + rows8,
                (cumul,) + rows8,
                (x_low,) + wide,
                (rows,) + lanes_of(2),
            ],
            base=base,
            grid=grid,
            after=[ready],
            flops=2 * length * 128 * channels,
        )
        return done["mixed"]

    def gates(ready):
        done["gate"], done["scaled"] = call(
            gate_body,
            [f32(length, channels) + wide, f32(length, channels) + wide],
            [(z_input,) + wide, (grad_out,) + wide, (gain,) + lanes_of(1)],
            base=base,
            grid=grid,
            after=[ready],
        )
        return done["gate"]

    state_mine, state_other = passed(local, False, (mix_inside, gates))
    gate, scaled = done["gate"], done["scaled"]
    c_spec = ((1, length, 128), lambda g, b: (1, 0, 0))
    mixed, sums = call(
        functools.partial(mix_body, own_half),
        [f32(length, channels) + wide, f32(8, length) + whole(8, length)],
        [
            (done["mixed"],) + wide,
            (bc,) + c_spec,
            (cumul,) + rows8,
            (state_mine,) + mine_slot,
            (state_other,) + other_slot,
            (gate,) + wide,
            (scaled,) + wide,
        ],
        base=base,
        grid=grid,
        scratch=[pltpu.VMEM((length, 128), F32), pltpu.VMEM((length, 128), F32)],
        flops=2 * length * 128 * channels,
    )
    turn_head = lambda block, bit: lax.ppermute(
        block, "head", [(i, i ^ bit) for i in range(parts)]
    )
    if parts == 4:
        sums = sums + turn_head(sums, 1)
        all_sums = [sums, turn_head(sums, 2)]
    else:
        all_sums = [lax.psum(sums, "head")]
    grad_mixed, local_back = call(
        functools.partial(grad_mixed_body, inner, len(all_sums)),
        [low(length, channels) + wide, low(groups, length, width) + slot],
        [full(part) for part in all_sums]
        + [
            (mixed,) + wide,
            (gate,) + wide,
            (scaled,) + wide,
            full(bc),
            (cumul,) + rows8,
        ],
        base=base,
        grid=grid,
        scratch=[pltpu.VMEM((128, length), F32)],
        flops=2 * length * 128 * channels,
    )

    def back_inside(ready):
        done["back"] = call(
            functools.partial(inner_back_body, own_half),
            [
                f32(length, channels) + wide,
                f32(heads, length) + rows8,
                f32(heads, length) + rows8,
                low(length, channels) + wide,
                f32(2, length, 128) + whole(2, length, 128),
            ],
            [
                full(gram),
                full(bc),
                (step,) + rows8,
                (cumul,) + rows8,
                (x_low,) + wide,
                (grad_mixed,) + wide,
                (state_mine,) + mine_slot,
                (state_other,) + other_slot,
                (rows,) + lanes_of(2),
            ],
            base=base,
            grid=grid,
            scratch=[pltpu.VMEM((length, length), F32), pltpu.VMEM((length, 128), F32)],
            after=[ready],
            flops=6 * length * 128 * channels,
        )
        return done["back"][1]

    def back_gates(ready):
        (done["grad_z"],) = call(
            functools.partial(grad_z_body, inner, len(all_sums)),
            [low(length, channels) + wide],
            [full(part) for part in all_sums]
            + [
                (mixed,) + wide,
                (z_input,) + wide,
                (grad_out,) + wide,
                (gain,) + lanes_of(1),
            ],
            base=base,
            grid=grid,
            after=[ready],
        )
        return done["grad_z"]

    out_mine, out_other = passed(local_back, True, (back_inside, back_gates))
    partial, q_rows, r_rows, weighted_x, bc_partial = done["back"]
    first_rows = ((8, width), lambda g, b: (0, turn(g, b)))
    outs_in = [(out_mine,) + mine_slot, (out_other,) + other_slot]
    rim_back, grad_bc_pre = call(
        functools.partial(rim_body, own_half),
        [f32(8, channels) + lanes_of(8), f32(2, length, 128) + whole(2, length, 128)],
        [
            full(bc),
            (step,) + rows8,
            (cumul,) + rows8,
            (weighted_x,) + wide,
            (partial,) + first_rows,
            (slope,) + first_rows,
        ]
        + outs_in
        + [full(bc_partial), full(bc_slope)],
        base=base,
        grid=grid,
        scratch=[pltpu.VMEM((length, 128), F32)],
        flops=2 * length * 128 * channels,
    )
    rim_back = jnp.concatenate([rim_back[:3], grad_bc_pre[0, :3], grad_bc_pre[1, :3]], axis=1)
    rim_back = lax.ppermute(rim_back, "seq", [(i, i - 1) for i in range(1, count)])
    (grad_dt,) = call(
        functools.partial(grad_dt_body, own_half),
        [f32(heads, length) + rows8],
        [
            full(bc),
            (rate,) + rows8,
            (dt_slope,) + rows8,
            (step,) + rows8,
            (cumul,) + rows8,
            (q_rows,) + rows8,
            (r_rows,) + rows8,
            (x_low,) + wide,
            (state_mine,) + mine_slot,
            (state_other,) + other_slot,
        ]
        + outs_in,
        base=base,
        grid=grid,
        scratch=[pltpu.VMEM((width, 128), BF16), pltpu.VMEM((length, width), BF16)],
        after=[grad_bc_pre],
        flops=4 * length * 128 * channels,
    )
    bc_rim_back = jnp.moveaxis(rim_back[:, channels:].reshape(3, 2, 128), 1, 0)
    bc_sum = conv_back(jnp.concatenate([grad_bc_pre, bc_rim_back], axis=1), convolution_bc_taps)
    place_head = lax.axis_index("head")
    take = lambda block, index, rows: lax.dynamic_slice_in_dim(block, index * rows, rows, 1)
    if parts == 4:
        half, share = length // 2, length // 4
        high, odd = place_head // 2, place_head % 2
        bc_half = take(bc_sum, high, half) + turn_head(take(bc_sum, 1 - high, half), 2)
        grad_bc = take(bc_half, odd, share) + turn_head(take(bc_half, 1 - odd, share), 1)
    else:
        grad_bc = take(lax.psum(bc_sum, "head"), place_head, length // parts)
    grad_bc = grad_bc.astype(BF16)
    (grad_x,) = call(
        functools.partial(grad_x_body, own_half),
        [low(length, channels) + wide],
        [
            full(bc),
            (step,) + rows8,
            (cumul,) + rows8,
            (partial,) + wide,
            (slope,) + wide,
            (conv_x,) + lanes_of(4),
            (rim_back,) + lanes_of(3),
        ]
        + outs_in,
        base=base,
        grid=grid,
        scratch=[pltpu.VMEM((length + 8, 128), F32)],
        flops=2 * length * 128 * channels,
    )
    return (grad_x, done["grad_z"], grad_bc, grad_dt)


def solution(mesh):
    return jax.shard_map(
        shards,
        mesh=mesh,
        in_specs=(
            P("seq", "head"),
            P("seq", "head"),
            P(None, "seq", None),
            P("head", "seq"),
            P("head"),
            P("head"),
            P("head"),
            P(None, "head"),
            P(),
            P("head"),
            P("seq", "head"),
        ),
        out_specs=(
            P("seq", "head"),
            P("seq", "head"),
            P(None, ("seq", "head"), None),
            P("head", "seq"),
        ),
        check_vma=False,
    )
```

```python
import functools

import jax
import jax.numpy as jnp
from jax import lax
from jax.experimental import pallas as pl
from jax.experimental.pallas import tpu as pltpu
from jax.sharding import PartitionSpec as P

EPS = 1e-05
GROUP = 8
F32 = jnp.float32
BF16 = jnp.bfloat16
VMEM_BYTES = 16 * 2**20


def sigmoid(value):
    return 0.5 + 0.5 * jnp.tanh(0.5 * value)


def dot(a, b):
    return jnp.dot(a, b, preferred_element_type=F32)


def dot_split(a, b):
    high = a.astype(BF16)
    rest = a - high.astype(F32)
    middle = rest.astype(BF16)
    low = (rest - middle.astype(F32)).astype(BF16)
    return dot(high, b) + (dot(middle, b) + dot(low, b))


def dot_rows(a, b):
    return lax.dot_general(a, b, (((1,), (1,)), ((), ())), preferred_element_type=F32)


def dot_columns(a, b):
    return lax.dot_general(a, b, (((0,), (0,)), ((), ())), preferred_element_type=F32)


def triangle(length, upper):
    first = lax.broadcasted_iota(jnp.int32, (length, length), 0)
    second = lax.broadcasted_iota(jnp.int32, (length, length), 1)
    return first <= second if upper else first >= second


def columns_of(rows):
    return rows.T


def call(body, outs, ins, *, base=None, grid=(), scratch=(), after=(), token=False, flops=0):
    in_specs = [pl.BlockSpec(block, index) for _, block, index in ins]
    in_specs += [pl.BlockSpec(memory_space=pl.ANY) for _ in after]
    outs = list(outs)
    if token:
        outs.append(((8, 128), F32, (8, 128), lambda *_: (0, 0)))
    out_specs = [pl.BlockSpec(block, index) for _, _, block, index in outs]
    out_shape = [jax.ShapeDtypeStruct(shape, dtype) for shape, dtype, _, _ in outs]
    arrays = [array for array, _, _ in ins]
    moved = sum(a.size * a.dtype.itemsize for a in arrays + out_shape)
    read = 1 + len(arrays)

    def ordered(*refs):
        results = refs[read + len(after) :]
        if token:
            results[len(outs) - 1][...] = jnp.zeros((8, 128), F32)
            results = results[: len(outs) - 1] + results[len(outs) :]
        body(*refs[:read], *results)

    return pl.pallas_call(
        ordered,
        out_shape=out_shape,
        grid_spec=pltpu.PrefetchScalarGridSpec(
            num_scalar_prefetch=1,
            grid=grid,
            in_specs=in_specs,
            out_specs=out_specs,
            scratch_shapes=list(scratch),
        ),
        cost_estimate=pl.CostEstimate(flops=flops, bytes_accessed=moved, transcendentals=0),
        compiler_params=pltpu.CompilerParams(vmem_limit_bytes=VMEM_BYTES),
    )(base, *arrays, *after)


def in_hbm(array):
    return pltpu.with_memory_space_constraint(array, pltpu.HBM)


def column_of(row):
    count = row.shape[1]
    first = lax.broadcasted_iota(jnp.int32, (count, count), 0)
    second = lax.broadcasted_iota(jnp.int32, (count, count), 1)
    return jnp.sum(jnp.where(first == second, row, 0.0), axis=1, keepdims=True)


def steps_body(
    _,
    raw,
    bias,
    log_rate,
    skip,
    x_tail,
    bc_tail,
    step_out,
    cumul_out,
    rate_out,
    slope_out,
    rows_out,
    rim_out,
):
    heads, length = raw.shape
    channels = x_tail.shape[1]
    rim_out[:, 0:channels] = x_tail[...].astype(F32)[13:16, :].astype(BF16)
    for j in range(2):
        start = channels + 128 * j
        rim_out[:, start : start + 128] = bc_tail[j].astype(F32)[13:16, :].astype(BF16)
    shifted = raw[...] + column_of(bias[...])
    step = jnp.maximum(shifted, 0.0) + jnp.log1p(jnp.exp(-jnp.abs(shifted)))
    rate = jnp.broadcast_to(-jnp.exp(column_of(log_rate[...])), step.shape)
    cumul = dot_split(rate * step, triangle(length, True).astype(BF16))
    step_out[...] = step
    cumul_out[...] = cumul
    rate_out[...] = rate
    slope_out[...] = sigmoid(shifted)
    skips = column_of(skip[...])
    for head in range(heads):
        lanes = slice(head * 128, head * 128 + 128)
        rows_out[0:1, lanes] = jnp.broadcast_to(cumul[head : head + 1, length - 1 :], (1, 128))
        rows_out[1:2, lanes] = jnp.broadcast_to(skips[head : head + 1, :], (1, 128))


def pick(test, yes, no):
    return jnp.where(test, yes, no)


def place_bits(place, reverse):
    return [(1 - place[i] if reverse else place[i]) == 1 for i in range(3)]


def chip_weights_body(place, own, core, *outs):
    t0, t1 = own[0:1, :], core[...]
    one = jnp.ones_like(t0)
    for out, reverse in zip(outs, (False, True)):
        _, _, c = place_bits(place, reverse)
        out[0:1, :] = pick(c, one, jnp.exp(t1))
        out[1:2, :] = pick(c, jnp.exp(t0), one)
    outs[2][...] = t0 + t1


def weights_body(place, own, core, across, diagonal, *outs):
    t0, t1 = own[0:1, :], core[...]
    e0, e1, own_chip = jnp.exp(t0), jnp.exp(t1), jnp.exp(t0 + t1)
    ex, ed = jnp.exp(across[...]), jnp.exp(diagonal[...])
    both = own_chip * ed
    one = jnp.ones_like(e0)
    zero = jnp.zeros_like(e0)
    x_first = place[2] == 0
    for out, reverse in zip(outs, (False, True)):
        y, x, c = place_bits(place, reverse)
        rows = [
            pick(x_first, pick(x, one, ex), pick(jnp.logical_and(x, y), zero, one)),
            pick(x_first, pick(x, own_chip, one), pick(y, pick(x, one, both), zero)),
        ]
        a = pick(x_first, pick(x, one, zero), pick(y, pick(x, ex, ed), zero))
        b = pick(
            x_first, pick(y, pick(x, ex, one), zero), pick(jnp.logical_or(x, y), one, zero)
        )
        into, send = pick(c, e1, one), pick(c, one, e0)
        rows += [into * a, into * b, pick(c, one, zero)]
        rows += [send * a, send * b, pick(c, zero, one)]
        for index, row in enumerate(rows):
            out[index : index + 1, :] = row


def combine(base, groups, weights, outs, after=()):
    arrays, columns = [], []
    for slots in outs:
        for column, terms in slots:
            if column not in columns:
                columns.append(column)
            for _, (array, slot) in terms:
                if not any(array is a and slot == s for a, s in arrays):
                    arrays.append((array, slot))
    place = lambda array, slot: [
        i for i, (a, s) in enumerate(arrays) if a is array and s == slot
    ][0]
    plan = [
        [
            (columns.index(column), [(row, place(*source)) for row, source in terms])
            for column, terms in slots
        ]
        for slots in outs
    ]

    def body(_, *refs):
        rows, values = refs[: len(columns)], refs[len(columns) : len(columns) + len(arrays)]
        results = refs[len(columns) + len(arrays) :]
        width = rows[0].shape[1]
        for result, slots in zip(results, plan):
            for slot, (column, terms) in enumerate(slots):
                for start in range(0, width, 256):
                    lanes = slice(start, start + 256)
                    total = None
                    for row, index in terms:
                        term = rows[column][row : row + 1, lanes] * values[index][
                            0, :, lanes
                        ].astype(F32)
                        total = term if total is None else total + term
                    result[slot, :, lanes] = total.astype(BF16)

    length, width = arrays[0][0].shape[1:]
    ins = [
        (
            weights,
            (weights.shape[0], width),
            lambda g, b, column=column: (0, lax.rem(b[0] + column, groups)),
        )
        for column in columns
    ]
    ins += [
        (array, (1, length, width), lambda g, b, slot=slot: (slot, 0, 0))
        for array, slot in arrays
    ]
    results = [
        ((len(slots), length, width), BF16, (len(slots), length, width), lambda g, b: (0, 0, 0))
        for slots in outs
    ]
    return call(body, results, ins, base=base, grid=(1,), after=after)


def scan_blocks(base, groups, chip_weights, weights, local, reverse, beside, first):
    count = lax.axis_size("seq")
    place = lambda position: count - 1 - position if reverse else position

    def swap(block, bit_of, keep):
        route = [
            (place(i), place(i ^ bit_of(place(i) % 2)))
            for i in range(count)
            if keep(i, place(i) % 2)
        ]
        return lax.ppermute(block, "seq", route)

    def both(rows, sources):
        return [
            (slot, [(row, (array, slot)) for row, array in zip(rows, sources)])
            for slot in range(2)
        ]

    def merge(table, *plans, after=()):
        return combine(base, groups, table, [both(*plan) for plan in plans], after)

    everyone = lambda i, core: True
    taken = swap(local[2:4], lambda core: 1, everyone)
    (chip,) = merge(chip_weights, ((0, 1), (local, taken)), after=first)
    chip_a = swap(
        chip, lambda core: 4 if core else 2, lambda i, core: i < 4 if core else i < 6
    )
    after_a = beside[0](chip)
    (sent,) = merge(weights, ((0, 1), (chip, chip_a)), after=[after_a])
    chip_b = swap(
        sent, lambda core: 2 if core else 4, lambda i, core: i not in (2, 3) if core else i < 4
    )
    after_b = beside[1](sent)
    mine, handed = merge(
        weights,
        ((2, 3, 4), (chip_a, chip_b, taken)),
        ((5, 6, 7), (chip_a, chip_b, local)),
        after=[after_b],
    )
    return mine, swap(handed, lambda core: 1, everyone)


def gather_blocks(totals, local, reverse):
    table = lax.all_gather(totals, "seq", axis=0, tiled=True)
    blocks = lax.all_gather(local[None], "seq", axis=0, tiled=True)
    own = lax.axis_index("seq")
    order = jnp.arange(table.shape[0], dtype=jnp.int32)
    if reverse:
        inside = (order[None, :] > own) & (order[None, :] < order[:, None])
        selected = order > own
    else:
        inside = (order[None, :] > order[:, None]) & (order[None, :] < own)
        selected = order < own
    exponent = jnp.sum(jnp.where(inside[:, :, None], table[None], 0.0), axis=1)
    factor = jnp.where(selected[:, None], jnp.exp(exponent), 0.0)
    factor = factor.reshape(factor.shape[0], local.shape[0], 1, local.shape[2])
    state = jnp.sum(factor * blocks.astype(F32), axis=0).astype(BF16)
    return state, state


def prepare_body(
    base,
    x_in,
    x_halo,
    taps,
    bc_in,
    bc_halo,
    bc_taps,
    step_in,
    cumul_in,
    x_out,
    slope_out,
    state_out,
    bc_out,
    bc_slope_out,
    gram_out,
    ext,
    bc_ext,
    b_turned,
):
    length, width = x_in.shape

    @pl.when(pl.program_id(0) == 0)
    def _():
        for j in range(2):
            bc_ext[5:8, :] = bc_halo[:, j * 128 : j * 128 + 128].astype(F32)
            bc_ext[8 : 8 + length, :] = bc_in[j].astype(F32)
            pre = bc_taps[j, 0:1, :] * bc_ext[5 : 5 + length, :]
            for k in range(1, 4):
                pre = pre + bc_taps[j, k : k + 1, :] * bc_ext[5 + k : 5 + k + length, :]
            sigma = sigmoid(pre)
            bc_out[j] = (pre * sigma).astype(BF16)
            bc_slope_out[j] = sigma * (1.0 + pre * (1.0 - sigma))
        b_turned[...] = bc_out[0].astype(F32).T
        gram_out[...] = jnp.where(triangle(length, False), dot_rows(bc_out[1], bc_out[0]), 0.0)

    tail_step = jnp.exp(cumul_in[:, length - 1 :] - cumul_in[...]) * step_in[...]
    for head in range(width // 128):
        lanes = slice(head * 128, head * 128 + 128)
        ext[5:8, :] = x_halo[:, lanes].astype(F32)
        ext[8 : 8 + length, :] = x_in[:, lanes].astype(F32)
        pre = taps[0:1, lanes] * ext[5 : 5 + length, :]
        for k in range(1, 4):
            pre = pre + taps[k : k + 1, lanes] * ext[5 + k : 5 + k + length, :]
        sigma = sigmoid(pre)
        x_low = (pre * sigma).astype(BF16)
        x_out[:, lanes] = x_low
        slope_out[:, lanes] = sigma * (1.0 + pre * (1.0 - sigma))
        weighted = (b_turned[...] * tail_step[head : head + 1, :]).astype(BF16)
        state_out[0, :, lanes] = dot(weighted, x_low).astype(BF16)


def inner_body(base, gram, step_in, cumul_in, x_in, rows, mixed_out):
    cumul = cumul_in[...]
    cumul_columns = columns_of(cumul)
    for head in range(x_in.shape[1] // 128):
        lanes = slice(head * 128, head * 128 + 128)
        row = cumul[head : head + 1, :]
        decay = jnp.exp(jnp.minimum(cumul_columns[:, head : head + 1] - row, 0.0))
        mixer = (gram[...] * decay * step_in[head : head + 1, :]).astype(BF16)
        x_head = x_in[:, lanes]
        mixed_out[:, lanes] = dot(mixer, x_head) + rows[1:2, lanes] * x_head.astype(F32)


def pick_state(own_half, mine, other):
    group = pl.program_id(0)
    return jnp.where(group < own_half, mine[0], other[0])


def gate_body(base, z_in, grad_in, gain, gate_out, scaled_out):
    for start in range(0, z_in.shape[1], 128):
        lanes = slice(start, start + 128)
        z = z_in[:, lanes].astype(F32)
        gate = z * sigmoid(z)
        gate_out[:, lanes] = gate
        scaled_out[:, lanes] = grad_in[:, lanes].astype(F32) * gain[:, lanes] * gate


def mix_body(
    own_half,
    base,
    mixed_in,
    c_rows,
    cumul_in,
    mine,
    other,
    gate_in,
    scaled_in,
    mixed_out,
    sums_out,
    squares,
    products,
):
    group = pl.program_id(0)

    @pl.when(group == 0)
    def _():
        squares[...] = jnp.zeros_like(squares)
        products[...] = jnp.zeros_like(products)

    carried = dot(c_rows[0], pick_state(own_half, mine, other))
    lifted = jnp.exp(columns_of(cumul_in[...]))
    square, product = squares[...], products[...]
    for head in range(mixed_in.shape[1] // 128):
        lanes = slice(head * 128, head * 128 + 128)
        mixed = mixed_in[:, lanes] + lifted[:, head : head + 1] * carried[:, lanes]
        mixed_out[:, lanes] = mixed
        gated = mixed * gate_in[:, lanes]
        square = square + gated * gated
        product = product + mixed * scaled_in[:, lanes]
    squares[...] = square
    products[...] = product

    @pl.when(group == pl.num_programs(0) - 1)
    def _():
        sums_out[0:1, :] = jnp.sum(squares[...].T, axis=0, keepdims=True)
        sums_out[1:2, :] = jnp.sum(products[...].T, axis=0, keepdims=True)
        sums_out[2:8, :] = jnp.zeros_like(sums_out[2:8, :])


def norm_columns(inner, sums):
    total = sums[0][...]
    for part in sums[1:]:
        total = total + part[...]
    inv_rms = lax.rsqrt(total[0:1, :] / inner + EPS)
    mean_dot = inv_rms * total[1:2, :] / inner
    scales = jnp.concatenate(
        [inv_rms, inv_rms * inv_rms * mean_dot, jnp.zeros((6, total.shape[1]), F32)], axis=0
    )
    columns = columns_of(scales)
    return columns[:, 0:1], columns[:, 1:2]


def between_body(base, bc, step_in, cumul_in, x_in, mixed_in, gate_in, *outs):
    weighted_x, squared, lifted_out, c_turned = outs

    @pl.when(pl.program_id(0) == 0)
    def _():
        c_turned[...] = bc[1].astype(F32).T

    weights = block_weights(step_in[...], cumul_in[...])
    lifted = jnp.exp(cumul_in[...])
    for head in range(x_in.shape[1] // 128):
        lanes = slice(head * 128, head * 128 + 128)
        weight = weights[:, head : head + 1]
        weighted_x[:, lanes] = (weight * x_in[:, lanes].astype(F32)).astype(BF16)
        gate = gate_in[:, lanes]
        squared[:, lanes] = mixed_in[:, lanes] * gate * gate
        lifted_out[:, lanes] = (c_turned[...] * lifted[head : head + 1, :]).astype(BF16)


def grad_mixed_body(inner, parts, base, *refs):
    sums = refs[:parts]
    squared, scaled_in, lifted_c, grad_mixed, state_out = refs[parts:]
    alpha, beta = norm_columns(inner, sums)
    for start in range(0, squared.shape[1], 128):
        lanes = slice(start, start + 128)
        low = (alpha * scaled_in[:, lanes] - beta * squared[:, lanes]).astype(BF16)
        grad_mixed[:, lanes] = low
        state_out[0, :, lanes] = dot(lifted_c[:, lanes], low).astype(BF16)


def grad_z_body(inner, parts, base, *refs):
    sums = refs[:parts]
    mixed_in, z_in, grad_in, gain, grad_z = refs[parts:]
    alpha, beta = norm_columns(inner, sums)
    for start in range(0, z_in.shape[1], 128):
        lanes = slice(start, start + 128)
        z = z_in[:, lanes].astype(F32)
        sigma = sigmoid(z)
        mixed = mixed_in[:, lanes]
        scaled = grad_in[:, lanes].astype(F32) * gain[:, lanes]
        grad_gated = alpha * scaled - beta * (mixed * (z * sigma))
        grad_z[:, lanes] = (grad_gated * mixed * (sigma * (1.0 + z * (1.0 - sigma)))).astype(BF16)


def inner_back_body(
    own_half,
    base,
    gram,
    bc,
    step_in,
    cumul_in,
    x_in,
    grad_in,
    mine,
    other,
    rows,
    grad_x,
    q_out,
    r_out,
    bc_out,
    z_sum,
    c_sum,
):
    group = pl.program_id(0)
    length = x_in.shape[0]

    @pl.when(group == 0)
    def _():
        z_sum[...] = jnp.zeros_like(z_sum)
        c_sum[...] = jnp.zeros_like(c_sum)

    cumul = cumul_in[...]
    cumul_columns = columns_of(cumul)
    lifted = jnp.exp(cumul_columns)
    state = pick_state(own_half, mine, other)
    c_rows = bc[1].astype(F32)
    lane = lax.broadcasted_iota(jnp.int32, (length, 128), 1)
    q_columns = jnp.zeros((length, 128), F32)
    for head in range(x_in.shape[1] // 128):
        lanes = slice(head * 128, head * 128 + 128)
        step = step_in[head : head + 1, :]
        decay = jnp.exp(
            jnp.minimum(cumul_columns[:, head : head + 1] - cumul[head : head + 1, :], 0.0)
        )
        gram_decay = gram[...] * decay
        mixer = (gram_decay * step).astype(BF16)
        x_head, grad_head = x_in[:, lanes], grad_in[:, lanes]
        product = dot_rows(grad_head, x_head)
        z_sum[...] += product * decay * step
        gram_grad = product * gram_decay
        r_out[head : head + 1, :] = jnp.sum(gram_grad, axis=0, keepdims=True)
        handed = lifted[:, head : head + 1] * dot_rows(grad_head, state[:, lanes])
        c_sum[...] += handed
        q = jnp.sum(gram_grad * step + c_rows * handed, axis=1, keepdims=True)
        q_columns = jnp.where(lane == head, q, q_columns)
        grad_x[:, lanes] = dot_columns(mixer, grad_head) + rows[1:2, lanes] * grad_head.astype(F32)
    q_out[...] = q_columns.T[:GROUP, :]

    @pl.when(group == pl.num_programs(0) - 1)
    def _():
        summed = jnp.where(triangle(length, False), z_sum[...], 0.0)
        bc_out[0] = dot_split(summed.T, bc[1])
        bc_out[1] = c_sum[...] + dot_split(summed, bc[0])


def block_weights(step, cumul):
    return columns_of(jnp.exp(cumul[:, cumul.shape[1] - 1 :] - cumul) * step)


def rim_body(
    own_half,
    base,
    bc,
    step_in,
    cumul_in,
    weighted_x,
    partial,
    slope,
    out_mine,
    out_other,
    bc_partial,
    bc_slope,
    rim_out,
    bc_out,
    b_sum,
):
    group, groups = pl.program_id(0), pl.num_programs(0)
    width = weighted_x.shape[1]

    @pl.when(group == 0)
    def _():
        b_sum[...] = jnp.zeros_like(b_sum)

    out_low = pick_state(own_half, out_mine, out_other)
    b_sum[...] += dot_rows(weighted_x[...], out_low)
    weights = block_weights(step_in[...], cumul_in[...])[0:8, :]
    returned = dot(bc[0][0:16, :], out_low)[0:8, :]
    for head in range(width // 128):
        lanes = slice(head * 128, head * 128 + 128)
        weight = weights[:, head : head + 1]
        rows = (partial[:, lanes] + weight * returned[:, lanes]) * slope[:, lanes]
        place = pl.multiple_of(lax.rem(group + base[0], groups) * width + head * 128, 128)
        rim_out[:, pl.ds(place, 128)] = rows[0:3, :]

    @pl.when(group == groups - 1)
    def _():
        bc_out[0] = (b_sum[...] + bc_partial[0]) * bc_slope[0]
        bc_out[1] = bc_partial[1] * bc_slope[1]
        for j in range(2):
            start = rim_out.shape[1] - 256 + 128 * j
            rim_out[:, start : start + 128] = bc_out[j, 0:3, :]


def grad_dt_body(
    own_half,
    base,
    bc,
    rate,
    dt_slope,
    step_in,
    cumul_in,
    q_in,
    r_in,
    x_in,
    state_mine,
    state_other,
    out_mine,
    out_other,
    grad_dt,
    selector,
    products,
):
    length, width = x_in.shape

    @pl.when(pl.program_id(0) == 0)
    def _():
        row = lax.broadcasted_iota(jnp.int32, (width, 128), 0)
        lane = lax.broadcasted_iota(jnp.int32, (width, 128), 1)
        selector[...] = (row // 128 == lane).astype(BF16)

    cumul, step = cumul_in[...], step_in[...]
    state = pick_state(own_half, state_mine, state_other)
    out_low = pick_state(own_half, out_mine, out_other)
    returned = dot(bc[0], out_low)
    for start in range(0, width, 128):
        lanes = slice(start, start + 128)
        products[:, lanes] = (x_in[:, lanes].astype(F32) * returned[:, lanes]).astype(BF16)
    inner_b = dot(products[...], selector[...]).T[:GROUP, :]
    w = jnp.exp(cumul[:, length - 1 :] - cumul) * inner_b
    dots = dot(jnp.ones((16, length), BF16), state * out_low)[:GROUP, :]
    row = lax.broadcasted_iota(jnp.int32, (GROUP, width), 0)
    lane = lax.broadcasted_iota(jnp.int32, (GROUP, width), 1)
    dots = jnp.sum(jnp.where(lane // 128 == row, dots, 0.0), axis=1, keepdims=True)
    q, r = q_in[...], r_in[...]
    inside = jnp.sum(step * w, axis=1, keepdims=True)
    end = inside + jnp.exp(cumul[:, length - 1 :]) * dots
    last = lax.broadcasted_iota(jnp.int32, (GROUP, length), 1) == length - 1
    grad_cumul = q - step * (r + w) + jnp.where(last, end, 0.0)
    grad_log = dot_split(grad_cumul, triangle(length, False).astype(BF16))
    grad_dt[...] = (r + w + rate[...] * grad_log) * dt_slope[...]


def grad_x_body(
    own_half,
    base,
    bc,
    step_in,
    cumul_in,
    partial,
    slope,
    taps,
    halo,
    out_mine,
    out_other,
    grad_x,
    ext,
):
    length, width = partial.shape
    weights = block_weights(step_in[...], cumul_in[...])
    returned = dot(bc[0], pick_state(own_half, out_mine, out_other))
    for head in range(width // 128):
        lanes = slice(head * 128, head * 128 + 128)
        weight = weights[:, head : head + 1]
        ext[0:length, :] = (partial[:, lanes] + weight * returned[:, lanes]) * slope[:, lanes]
        ext[length : length + 3, :] = halo[:, lanes]
        total = taps[0:1, lanes] * ext[3 : 3 + length, :]
        for k in range(1, 4):
            total = total + taps[k : k + 1, lanes] * ext[3 - k : 3 - k + length, :]
        grad_x[:, lanes] = total.astype(BF16)


def bc_back_body(place, grad_pre, halo, taps, kept, sent, ext, total):
    length, half = grad_pre.shape[1], kept.shape[1]
    for j in range(2):
        ext[0:length, :] = grad_pre[j]
        ext[length : length + 3, :] = halo[:, 128 * j : 128 * j + 128]
        summed = taps[j, 0:1, :] * ext[3 : 3 + length, :]
        for k in range(1, 4):
            summed = summed + taps[j, k : k + 1, :] * ext[3 - k : 3 - k + length, :]
        total[...] = summed
        kept[j] = total[pl.ds(pl.multiple_of(place[0] * half, half), half), :]
        sent[j] = total[pl.ds(pl.multiple_of((1 - place[0]) * half, half), half), :]


def bc_half_body(place, mine, taken, kept, sent, total):
    half = kept.shape[1]
    for j in range(2):
        total[...] = mine[j] + taken[j]
        kept[j] = total[pl.ds(pl.multiple_of(place[1] * half, half), half), :]
        sent[j] = total[pl.ds(pl.multiple_of((1 - place[1]) * half, half), half), :]


def bc_last_body(_, mine, taken, out):
    out[...] = (mine[...] + taken[...]).astype(BF16)


def conv_back(extended, weights):
    length = extended.shape[-2] - 3
    summed = weights[..., 0, :][..., None, :] * extended[..., 3 : 3 + length, :]
    for k in range(1, 4):
        summed = (
            summed
            + weights[..., k, :][..., None, :] * extended[..., 3 - k : 3 - k + length, :]
        )
    return summed


def shards(
    x_input,
    z_input,
    bc_input,
    dt_raw,
    dt_bias,
    a_log,
    d_skip,
    conv_x,
    convolution_bc_taps,
    rescale_factor,
    grad_out,
):
    length, channels = x_input.shape
    heads = dt_raw.shape[0]
    groups = heads // GROUP
    width = GROUP * 128
    count, parts = lax.axis_size("seq"), lax.axis_size("head")
    inner = channels * parts
    own = lax.axis_index("seq")
    split = count == 8 and groups == 4
    own_half = groups // 2 if split else groups
    base = ((own % 2) * own_half if split else own * 0).astype(jnp.int32)[None]

    whole = lambda *shape: (shape, lambda g, b: (0,) * len(shape))
    turn = lambda g, b: lax.rem(g + b[0], groups)
    wide = ((length, width), lambda g, b: (0, turn(g, b)))
    rows8 = ((GROUP, length), lambda g, b: (turn(g, b), 0))
    lanes_of = lambda n: ((n, width), lambda g, b: (0, turn(g, b)))
    slot = ((1, length, width), lambda g, b: (g, 0, 0))
    mine_slot = ((1, length, width), lambda g, b: (jnp.minimum(g, own_half - 1), 0, 0))
    other_slot = ((1, length, width), lambda g, b: (jnp.maximum(g - own_half, 0), 0, 0))
    full = lambda array: (array,) + whole(*array.shape)
    grid = (groups,)

    gain = rescale_factor[None, :]
    f32 = lambda *shape: (shape, F32)
    low = lambda *shape: (shape, BF16)

    step, cumul, rate, dt_slope, rows, rim = call(
        steps_body,
        [
            f32(heads, length) + whole(heads, length),
            f32(heads, length) + whole(heads, length),
            f32(heads, length) + whole(heads, length),
            f32(heads, length) + whole(heads, length),
            f32(2, channels) + whole(2, channels),
            low(3, channels + 256) + whole(3, channels + 256),
        ],
        [
            full(in_hbm(dt_raw)),
            full(in_hbm(dt_bias[None, :])),
            full(in_hbm(a_log[None, :])),
            full(in_hbm(d_skip[None, :])),
            (in_hbm(x_input), (16, channels), lambda g, b: (length // 16 - 1, 0)),
            (in_hbm(bc_input), (2, 16, 128), lambda g, b: (0, length // 16 - 1, 0)),
        ],
        base=base,
        grid=(1,),
    )
    rim = lax.ppermute(rim, "seq", [(i - 1, i) for i in range(1, count)])
    if split:
        swap = lambda block, bit: lax.ppermute(
            block, "seq", [(i, i ^ bit) for i in range(count)]
        )
        total_core = swap(rows[0:1], 1)
        place = jnp.stack([own // 4, own // 2 % 2, own % 2]).astype(jnp.int32)
        pair = f32(2, channels) + whole(2, channels)
        chip_ahead, chip_behind, chip_total = call(
            chip_weights_body,
            [pair, pair, f32(1, channels) + whole(1, channels)],
            [full(rows), full(total_core)],
            base=place,
            grid=(1,),
        )
        total_across = swap(chip_total, 2)
        total_diagonal = swap(chip_total, 6)
        eight = f32(8, channels) + whole(8, channels)
        ahead, behind = call(
            weights_body,
            [eight, eight],
            [full(rows), full(total_core), full(total_across), full(total_diagonal)],
            base=place,
            grid=(1,),
        )

        early = [chip_total]
    else:
        early = []

    def passed(local, reverse, beside):
        if split:
            first = [] if reverse else [total_across, total_diagonal]
            chip = chip_behind if reverse else chip_ahead
            table = behind if reverse else ahead
            return scan_blocks(base, groups, chip, table, local, reverse, beside, first)
        for work in beside:
            work(local)
        return gather_blocks(rows[0:1], local, reverse)

    x_low, slope, local, bc, bc_slope, gram = call(
        prepare_body,
        [
            low(length, channels) + wide,
            f32(length, channels) + wide,
            low(groups, length, width) + slot,
            low(2, length, 128) + whole(2, length, 128),
            f32(2, length, 128) + whole(2, length, 128),
            f32(length, length) + whole(length, length),
        ],
        [
            (in_hbm(x_input),) + wide,
            (rim,) + lanes_of(3),
            (in_hbm(conv_x),) + lanes_of(4),
            full(in_hbm(bc_input)),
            (rim, (3, 256), lambda g, b: (0, channels // 256)),
            full(in_hbm(convolution_bc_taps)),
            (step,) + rows8,
            (cumul,) + rows8,
        ],
        base=base,
        grid=grid,
        scratch=[
            pltpu.VMEM((length + 8, 128), F32),
            pltpu.VMEM((length + 8, 128), F32),
            pltpu.VMEM((128, length), F32),
        ],
        after=early,
        flops=2 * length * 128 * channels,
    )
    done = {}

    def mix_inside(ready):
        done["mixed"], token = call(
            inner_body,
            [f32(length, channels) + wide],
            [
                full(gram),
                (step,) + rows8,
                (cumul,) + rows8,
                (x_low,) + wide,
                (rows,) + lanes_of(2),
            ],
            base=base,
            grid=grid,
            after=[ready],
            token=True,
            flops=2 * length * 128 * channels,
        )
        return token

    def gates(ready):
        done["gate"], done["scaled"], token = call(
            gate_body,
            [f32(length, channels) + wide, f32(length, channels) + wide],
            [(z_input,) + wide, (grad_out,) + wide, (gain,) + lanes_of(1)],
            base=base,
            grid=grid,
            after=[ready],
            token=True,
        )
        return token

    state_mine, state_other = passed(local, False, (mix_inside, gates))
    gate, scaled = done["gate"], done["scaled"]
    c_spec = ((1, length, 128), lambda g, b: (1, 0, 0))
    mixed, sums = call(
        functools.partial(mix_body, own_half),
        [f32(length, channels) + wide, f32(8, length) + whole(8, length)],
        [
            (done["mixed"],) + wide,
            (bc,) + c_spec,
            (cumul,) + rows8,
            (state_mine,) + mine_slot,
            (state_other,) + other_slot,
            (gate,) + wide,
            (scaled,) + wide,
        ],
        base=base,
        grid=grid,
        scratch=[pltpu.VMEM((length, 128), F32), pltpu.VMEM((length, 128), F32)],
        flops=2 * length * 128 * channels,
    )
    turn_head = lambda block, bit: lax.ppermute(
        block, "head", [(i, i ^ bit) for i in range(parts)]
    )
    if parts == 4:
        sums = sums + turn_head(sums, 1)
        all_sums = [sums, turn_head(sums, 2)]
    else:
        all_sums = [lax.psum(sums, "head")]
    weighted_x, squared, lifted_c = call(
        between_body,
        [low(length, channels) + wide, f32(length, channels) + wide, low(length, channels) + wide],
        [
            full(bc),
            (step,) + rows8,
            (cumul,) + rows8,
            (x_low,) + wide,
            (mixed,) + wide,
            (gate,) + wide,
        ],
        base=base,
        grid=grid,
        scratch=[pltpu.VMEM((128, length), F32)],
    )
    grad_mixed, local_back = call(
        functools.partial(grad_mixed_body, inner, len(all_sums)),
        [low(length, channels) + wide, low(groups, length, width) + slot],
        [full(part) for part in all_sums]
        + [(squared,) + wide, (scaled,) + wide, (lifted_c,) + wide],
        base=base,
        grid=grid,
        flops=2 * length * 128 * channels,
    )

    def back_inside(ready):
        done["back"] = call(
            functools.partial(inner_back_body, own_half),
            [
                f32(length, channels) + wide,
                f32(heads, length) + rows8,
                f32(heads, length) + rows8,
                f32(2, length, 128) + whole(2, length, 128),
            ],
            [
                full(gram),
                full(bc),
                (step,) + rows8,
                (cumul,) + rows8,
                (x_low,) + wide,
                (grad_mixed,) + wide,
                (state_mine,) + mine_slot,
                (state_other,) + other_slot,
                (rows,) + lanes_of(2),
            ],
            base=base,
            grid=grid,
            scratch=[pltpu.VMEM((length, length), F32), pltpu.VMEM((length, 128), F32)],
            after=[ready],
            flops=6 * length * 128 * channels,
        )
        return done["back"][1]

    def back_gates(ready):
        done["grad_z"], token = call(
            functools.partial(grad_z_body, inner, len(all_sums)),
            [low(length, channels) + wide],
            [full(part) for part in all_sums]
            + [
                (mixed,) + wide,
                (z_input,) + wide,
                (grad_out,) + wide,
                (gain,) + lanes_of(1),
            ],
            base=base,
            grid=grid,
            after=[ready],
            token=True,
        )
        return token

    out_mine, out_other = passed(local_back, True, (back_inside, back_gates))
    partial, q_rows, r_rows, bc_partial = done["back"]
    first_rows = ((8, width), lambda g, b: (0, turn(g, b)))
    outs_in = [(out_mine,) + mine_slot, (out_other,) + other_slot]
    rim_back, grad_bc_pre = call(
        functools.partial(rim_body, own_half),
        [
            f32(3, channels + 256) + whole(3, channels + 256),
            f32(2, length, 128) + whole(2, length, 128),
        ],
        [
            full(bc),
            (step,) + rows8,
            (cumul,) + rows8,
            (weighted_x,) + wide,
            (partial,) + first_rows,
            (slope,) + first_rows,
        ]
        + outs_in
        + [full(bc_partial), full(bc_slope)],
        base=base,
        grid=grid,
        scratch=[pltpu.VMEM((length, 128), F32)],
        flops=2 * length * 128 * channels,
    )
    rim_back = lax.ppermute(rim_back, "seq", [(i, i - 1) for i in range(1, count)])
    grad_dt, dt_token = call(
        functools.partial(grad_dt_body, own_half),
        [f32(heads, length) + rows8],
        [
            full(bc),
            (rate,) + rows8,
            (dt_slope,) + rows8,
            (step,) + rows8,
            (cumul,) + rows8,
            (q_rows,) + rows8,
            (r_rows,) + rows8,
            (x_low,) + wide,
            (state_mine,) + mine_slot,
            (state_other,) + other_slot,
        ]
        + outs_in,
        base=base,
        grid=grid,
        scratch=[pltpu.VMEM((width, 128), BF16), pltpu.VMEM((length, width), BF16)],
        after=[grad_bc_pre],
        token=True,
        flops=4 * length * 128 * channels,
    )
    if parts == 4:
        place_head = lax.axis_index("head")
        place_head = jnp.stack([place_head // 2, place_head % 2]).astype(jnp.int32)
        piece = lambda rows: f32(2, rows, 128) + whole(2, rows, 128)
        kept, sent = call(
            bc_back_body,
            [piece(length // 2), piece(length // 2)],
            [
                full(grad_bc_pre),
                (rim_back, (3, 256), lambda g, b: (0, channels // 256)),
                full(convolution_bc_taps),
            ],
            base=place_head,
            grid=(1,),
            scratch=[pltpu.VMEM((length + 8, 128), F32), pltpu.VMEM((length, 128), F32)],
            after=[dt_token],
        )
        taken = turn_head(sent, 2)
    grad_x, x_token = call(
        functools.partial(grad_x_body, own_half),
        [low(length, channels) + wide],
        [
            full(bc),
            (step,) + rows8,
            (cumul,) + rows8,
            (partial,) + wide,
            (slope,) + wide,
            (conv_x,) + lanes_of(4),
            (rim_back,) + lanes_of(3),
        ]
        + outs_in,
        base=base,
        grid=grid,
        scratch=[pltpu.VMEM((length + 8, 128), F32)],
        token=True,
        flops=2 * length * 128 * channels,
    )
    if parts == 4:
        kept, sent = call(
            bc_half_body,
            [piece(length // 4), piece(length // 4)],
            [full(kept), full(taken)],
            base=place_head,
            grid=(1,),
            scratch=[pltpu.VMEM((length // 2, 128), F32)],
            after=[x_token],
        )
        (grad_bc,) = call(
            bc_last_body,
            [low(2, length // 4, 128) + whole(2, length // 4, 128)],
            [full(kept), full(turn_head(sent, 1))],
            base=base,
            grid=(1,),
        )
    else:
        bc_halo = jnp.moveaxis(rim_back[:, channels:].reshape(3, 2, 128), 1, 0)
        bc_sum = conv_back(jnp.concatenate([grad_bc_pre, bc_halo], axis=1), convolution_bc_taps)
        share = length // parts
        first_row = lax.axis_index("head") * share
        bc_sum = lax.psum(bc_sum, "head")
        grad_bc = lax.dynamic_slice_in_dim(bc_sum, first_row, share, 1).astype(BF16)
    return (grad_x, done["grad_z"], grad_bc, grad_dt)


def solution(mesh):
    return jax.shard_map(
        shards,
        mesh=mesh,
        in_specs=(
            P("seq", "head"),
            P("seq", "head"),
            P(None, "seq", None),
            P("head", "seq"),
            P("head"),
            P("head"),
            P("head"),
            P(None, "head"),
            P(),
            P("head"),
            P("seq", "head"),
        ),
        out_specs=(
            P("seq", "head"),
            P("seq", "head"),
            P(None, ("seq", "head"), None),
            P("head", "seq"),
        ),
        check_vma=False,
    )
```

```python
import functools

import jax
import jax.numpy as jnp
from jax import lax
from jax.experimental import pallas as pl
from jax.experimental.pallas import tpu as pltpu
from jax.sharding import PartitionSpec as P

EPS = 1e-05
GROUP = 8
F32 = jnp.float32
BF16 = jnp.bfloat16
VMEM_BYTES = 16 * 2**20


def sigmoid(value):
    return 0.5 + 0.5 * jnp.tanh(0.5 * value)


def dot(a, b):
    return jnp.dot(a, b, preferred_element_type=F32)


def dot_split(a, b):
    high = a.astype(BF16)
    rest = a - high.astype(F32)
    middle = rest.astype(BF16)
    low = (rest - middle.astype(F32)).astype(BF16)
    return dot(high, b) + (dot(middle, b) + dot(low, b))


def dot_rows(a, b):
    return lax.dot_general(a, b, (((1,), (1,)), ((), ())), preferred_element_type=F32)


def dot_columns(a, b):
    return lax.dot_general(a, b, (((0,), (0,)), ((), ())), preferred_element_type=F32)


def triangle(length, upper):
    first = lax.broadcasted_iota(jnp.int32, (length, length), 0)
    second = lax.broadcasted_iota(jnp.int32, (length, length), 1)
    return first <= second if upper else first >= second


def columns_of(rows):
    return rows.T


def call(body, outs, ins, *, base=None, grid=(), scratch=(), after=(), carry=(), place=None, token=False, flops=0):
    aliases = {1 + len(ins) + len(after) + i: i for i in range(len(carry))}
    if place is not None:
        aliases[1 + place] = 0
    after = list(after) + list(carry)
    in_specs = [pl.BlockSpec(block, index) for _, block, index in ins]
    in_specs += [pl.BlockSpec(memory_space=pl.ANY) for _ in after]
    outs = list(outs)
    if token:
        outs.append(((8, 128), F32, (8, 128), lambda *_: (0, 0)))
    out_specs = [pl.BlockSpec(block, index) for _, _, block, index in outs]
    out_shape = [jax.ShapeDtypeStruct(shape, dtype) for shape, dtype, _, _ in outs]
    arrays = [array for array, _, _ in ins]
    moved = sum(a.size * a.dtype.itemsize for a in arrays + out_shape)
    read = 1 + len(arrays)

    def ordered(*refs):
        results = refs[read + len(after) :]
        if token:
            results[len(outs) - 1][...] = jnp.zeros((8, 128), F32)
            results = results[: len(outs) - 1] + results[len(outs) :]
        body(*refs[:read], *results)

    return pl.pallas_call(
        ordered,
        out_shape=out_shape,
        grid_spec=pltpu.PrefetchScalarGridSpec(
            num_scalar_prefetch=1,
            grid=grid,
            in_specs=in_specs,
            out_specs=out_specs,
            scratch_shapes=list(scratch),
        ),
        input_output_aliases=aliases,
        cost_estimate=pl.CostEstimate(flops=flops, bytes_accessed=moved, transcendentals=0),
        compiler_params=pltpu.CompilerParams(vmem_limit_bytes=VMEM_BYTES),
    )(base, *arrays, *after)


def in_hbm(array):
    return pltpu.with_memory_space_constraint(array, pltpu.HBM)


def column_of(row):
    count = row.shape[1]
    first = lax.broadcasted_iota(jnp.int32, (count, count), 0)
    second = lax.broadcasted_iota(jnp.int32, (count, count), 1)
    return jnp.sum(jnp.where(first == second, row, 0.0), axis=1, keepdims=True)


def steps_body(
    _,
    raw,
    bias,
    log_rate,
    skip,
    x_tail,
    bc_tail,
    step_out,
    cumul_out,
    rate_out,
    slope_out,
    rows_out,
    rim_out,
):
    heads, length = raw.shape
    channels = x_tail.shape[1]
    rim_out[:, 0:channels] = x_tail[...].astype(F32)[13:16, :].astype(BF16)
    for j in range(2):
        start = channels + 128 * j
        rim_out[:, start : start + 128] = bc_tail[j].astype(F32)[13:16, :].astype(BF16)
    shifted = raw[...] + column_of(bias[...])
    step = jnp.maximum(shifted, 0.0) + jnp.log1p(jnp.exp(-jnp.abs(shifted)))
    rate = jnp.broadcast_to(-jnp.exp(column_of(log_rate[...])), step.shape)
    cumul = dot_split(rate * step, triangle(length, True).astype(BF16))
    step_out[...] = step
    cumul_out[...] = cumul
    rate_out[...] = rate
    slope_out[...] = sigmoid(shifted)
    skips = column_of(skip[...])
    for head in range(heads):
        lanes = slice(head * 128, head * 128 + 128)
        rows_out[0:1, lanes] = jnp.broadcast_to(cumul[head : head + 1, length - 1 :], (1, 128))
        rows_out[1:2, lanes] = jnp.broadcast_to(skips[head : head + 1, :], (1, 128))


def pick(test, yes, no):
    return jnp.where(test, yes, no)


def weights_body(place, own, core, across, *outs):
    t0, t1 = own[0:1, :], core[...]
    e0, e1, own_chip, ex = jnp.exp(t0), jnp.exp(t1), jnp.exp(t0 + t1), jnp.exp(across[...])
    one = jnp.ones_like(e0)
    zero = jnp.zeros_like(e0)
    x_first = place[3] == 0
    for out, reverse in zip(outs, (False, True)):
        y, x, c = ((1 - place[i] if reverse else place[i]) == 1 for i in (1, 2, 3))
        either = jnp.logical_or(x, y)
        scale = pick(jnp.logical_or(x_first, either), one, ex)
        rows = [pick(c, one, e1), pick(c, e0, one)]
        rows += [rows[0] * scale, rows[1] * scale]
        rows += [
            pick(x_first, pick(x, one, ex), pick(jnp.logical_and(x, y), zero, one)),
            pick(x_first, pick(x, own_chip, one), pick(y, pick(x, one, own_chip), zero)),
        ]
        a = pick(x_first, pick(x, one, zero), pick(y, pick(x, ex, one), zero))
        b = pick(x_first, pick(y, pick(x, ex, one), zero), pick(either, one, zero))
        into, send = pick(c, e1, one), pick(c, one, e0)
        rows += [into * a, into * b, pick(c, one, zero)]
        rows += [send * a, send * b, pick(c, zero, one)]
        for index, row in enumerate(rows):
            out[index : index + 1, :] = row


def combine(base, groups, weights, outs, after=()):
    arrays, columns = [], []
    for slots in outs:
        for column, terms in slots:
            if column not in columns:
                columns.append(column)
            for _, (array, slot) in terms:
                if not any(array is a and slot == s for a, s in arrays):
                    arrays.append((array, slot))
    place = lambda array, slot: [
        i for i, (a, s) in enumerate(arrays) if a is array and s == slot
    ][0]
    plan = [
        [
            (columns.index(column), [(row, place(*source)) for row, source in terms])
            for column, terms in slots
        ]
        for slots in outs
    ]

    def body(_, *refs):
        rows, values = refs[: len(columns)], refs[len(columns) : len(columns) + len(arrays)]
        results = refs[len(columns) + len(arrays) :]
        width = rows[0].shape[1]
        for result, slots in zip(results, plan):
            for slot, (column, terms) in enumerate(slots):
                for start in range(0, width, 256):
                    lanes = slice(start, start + 256)
                    total = None
                    for row, index in terms:
                        term = rows[column][row : row + 1, lanes] * values[index][
                            0, :, lanes
                        ].astype(F32)
                        total = term if total is None else total + term
                    result[slot, :, lanes] = total.astype(BF16)

    length, width = arrays[0][0].shape[1:]
    ins = [
        (
            weights,
            (weights.shape[0], width),
            lambda g, b, column=column: (0, lax.rem(b[0] + column, groups)),
        )
        for column in columns
    ]
    ins += [
        (array, (1, length, width), lambda g, b, slot=slot: (slot, 0, 0))
        for array, slot in arrays
    ]
    results = [
        ((len(slots), length, width), BF16, (len(slots), length, width), lambda g, b: (0, 0, 0))
        for slots in outs
    ]
    return call(body, results, ins, base=base, grid=(1,), after=after)


def scan_blocks(base, groups, weights, local, local_sent, reverse, beside):
    count = lax.axis_size("seq")
    place = lambda position: count - 1 - position if reverse else position

    def swap(block, bit_of, keep):
        route = [
            (place(i), place(i ^ bit_of(place(i) % 2)))
            for i in range(count)
            if keep(i, place(i) % 2)
        ]
        return lax.ppermute(block, "seq", route)

    def merge(*plans, after=()):
        both = [
            [
                (slot, [(row, (array, slot)) for row, array in zip(rows, sources)])
                for slot in range(2)
            ]
            for rows, sources in plans
        ]
        return combine(base, groups, weights, both, after)

    everyone = lambda i, core: True
    taken = swap(local_sent, lambda core: 1, everyone)
    chip, chip_sent = merge(((0, 1), (local, taken)), ((2, 3), (local, taken)))
    chip_a = swap(
        chip_sent, lambda core: 4 if core else 2, lambda i, core: i < 4 if core else i < 6
    )
    after_a = beside[0](chip)
    (sent,) = merge(((4, 5), (chip, chip_a)), after=[after_a])
    chip_b = swap(
        sent, lambda core: 2 if core else 4, lambda i, core: i not in (2, 3) if core else i < 4
    )
    after_b = beside[1](sent)
    mine, handed = merge(
        ((6, 7, 8), (chip_a, chip_b, taken)),
        ((9, 10, 11), (chip_a, chip_b, local)),
        after=[after_b],
    )
    return mine, swap(handed, lambda core: 1, everyone)


def gather_blocks(totals, local, reverse):
    table = lax.all_gather(totals, "seq", axis=0, tiled=True)
    blocks = lax.all_gather(local[None], "seq", axis=0, tiled=True)
    own = lax.axis_index("seq")
    order = jnp.arange(table.shape[0], dtype=jnp.int32)
    if reverse:
        inside = (order[None, :] > own) & (order[None, :] < order[:, None])
        selected = order > own
    else:
        inside = (order[None, :] > order[:, None]) & (order[None, :] < own)
        selected = order < own
    exponent = jnp.sum(jnp.where(inside[:, :, None], table[None], 0.0), axis=1)
    factor = jnp.where(selected[:, None], jnp.exp(exponent), 0.0)
    factor = factor.reshape(factor.shape[0], local.shape[0], 1, local.shape[2])
    state = jnp.sum(factor * blocks.astype(F32), axis=0).astype(BF16)
    return state, state


def prepare_body(first, base, x_in, x_halo, taps, step_in, cumul_in, *refs):
    length, width = x_in.shape
    if first:
        bc_in, bc_halo, bc_taps, x_out, slope_out, state_out = refs[:6]
        bc_out, bc_slope_out, gram_out, b_turned, ext, bc_ext = refs[6:]

        @pl.when(pl.program_id(0) == 0)
        def _():
            for j in range(2):
                bc_ext[5:8, :] = bc_halo[:, j * 128 : j * 128 + 128].astype(F32)
                bc_ext[8 : 8 + length, :] = bc_in[j].astype(F32)
                pre = bc_taps[j, 0:1, :] * bc_ext[5 : 5 + length, :]
                for k in range(1, 4):
                    pre = pre + bc_taps[j, k : k + 1, :] * bc_ext[5 + k : 5 + k + length, :]
                sigma = sigmoid(pre)
                bc_out[j] = (pre * sigma).astype(BF16)
                bc_slope_out[j] = sigma * (1.0 + pre * (1.0 - sigma))
            b_turned[...] = bc_out[0].astype(F32).T
            gram_out[...] = jnp.where(
                triangle(length, False), dot_rows(bc_out[1], bc_out[0]), 0.0
            )

    else:
        b_turned, x_out, slope_out, state_out, ext = refs

    tail_step = jnp.exp(cumul_in[:, length - 1 :] - cumul_in[...]) * step_in[...]
    for head in range(width // 128):
        lanes = slice(head * 128, head * 128 + 128)
        ext[5:8, :] = x_halo[:, lanes].astype(F32)
        ext[8 : 8 + length, :] = x_in[:, lanes].astype(F32)
        pre = taps[0:1, lanes] * ext[5 : 5 + length, :]
        for k in range(1, 4):
            pre = pre + taps[k : k + 1, lanes] * ext[5 + k : 5 + k + length, :]
        sigma = sigmoid(pre)
        x_low = (pre * sigma).astype(BF16)
        x_out[:, lanes] = x_low
        slope_out[:, lanes] = sigma * (1.0 + pre * (1.0 - sigma))
        weighted = (b_turned[...] * tail_step[head : head + 1, :]).astype(BF16)
        state_out[0, :, lanes] = dot(weighted, x_low).astype(BF16)


def inner_body(base, gram, step_in, cumul_in, x_in, rows, mixed_out):
    cumul = cumul_in[...]
    cumul_columns = columns_of(cumul)
    for head in range(x_in.shape[1] // 128):
        lanes = slice(head * 128, head * 128 + 128)
        row = cumul[head : head + 1, :]
        decay = jnp.exp(jnp.minimum(cumul_columns[:, head : head + 1] - row, 0.0))
        mixer = (gram[...] * decay * step_in[head : head + 1, :]).astype(BF16)
        x_head = x_in[:, lanes]
        mixed_out[:, lanes] = dot(mixer, x_head) + rows[1:2, lanes] * x_head.astype(F32)


def pick_state(own_half, mine, other):
    group = pl.program_id(0)
    return jnp.where(group < own_half, mine[0], other[0])


def gate_body(
    base,
    z_in,
    grad_in,
    gain,
    bc,
    step_in,
    cumul_in,
    x_in,
    gate_out,
    scaled_out,
    weighted_x,
    lifted_out,
    c_turned,
):
    @pl.when(pl.program_id(0) == 0)
    def _():
        c_turned[...] = bc[1].astype(F32).T

    weights = block_weights(step_in[...], cumul_in[...])
    lifted = jnp.exp(cumul_in[...])
    for head in range(z_in.shape[1] // 128):
        lanes = slice(head * 128, head * 128 + 128)
        z = z_in[:, lanes].astype(F32)
        gate = z * sigmoid(z)
        gate_out[:, lanes] = gate
        scaled_out[:, lanes] = grad_in[:, lanes].astype(F32) * gain[:, lanes] * gate
        weight = weights[:, head : head + 1]
        weighted_x[:, lanes] = (weight * x_in[:, lanes].astype(F32)).astype(BF16)
        lifted_out[:, lanes] = (c_turned[...] * lifted[head : head + 1, :]).astype(BF16)


def mix_body(
    base, mixed_in, c_rows, cumul_in, state, gate_in, scaled_in, sums_in, *outs
):
    mixed_out, sums_out, squares, products = outs
    group = pl.program_id(0)

    @pl.when(group == 0)
    def _():
        squares[...] = jnp.zeros_like(squares)
        products[...] = jnp.zeros_like(products)

    carried = dot(c_rows[0], state[0])
    lifted = jnp.exp(columns_of(cumul_in[...]))
    square, product = squares[...], products[...]
    for head in range(mixed_in.shape[1] // 128):
        lanes = slice(head * 128, head * 128 + 128)
        mixed = mixed_in[:, lanes] + lifted[:, head : head + 1] * carried[:, lanes]
        mixed_out[:, lanes] = mixed
        gated = mixed * gate_in[:, lanes]
        square = square + gated * gated
        product = product + mixed * scaled_in[:, lanes]
    squares[...] = square
    products[...] = product

    @pl.when(group == pl.num_programs(0) - 1)
    def _():
        sums_out[...] = sums_in[...]
        sums_out[0:1, :] += jnp.sum(squares[...].T, axis=0, keepdims=True)
        sums_out[1:2, :] += jnp.sum(products[...].T, axis=0, keepdims=True)


def norm_columns(inner, sums):
    total = sums[0][...]
    for part in sums[1:]:
        total = total + part[...]
    inv_rms = lax.rsqrt(total[0:1, :] / inner + EPS)
    mean_dot = inv_rms * total[1:2, :] / inner
    scales = jnp.concatenate(
        [inv_rms, inv_rms * inv_rms * mean_dot, jnp.zeros((6, total.shape[1]), F32)], axis=0
    )
    columns = columns_of(scales)
    return columns[:, 0:1], columns[:, 1:2]


def square_body(base, mixed_in, gate_in, squared):
    for start in range(0, mixed_in.shape[1], 128):
        lanes = slice(start, start + 128)
        gate = gate_in[:, lanes]
        squared[:, lanes] = mixed_in[:, lanes] * gate * gate


def grad_mixed_body(inner, parts, base, *refs):
    sums = refs[:parts]
    squared, scaled_in, lifted_c, grad_mixed, state_out = refs[parts:]
    alpha, beta = norm_columns(inner, sums)
    for start in range(0, squared.shape[1], 128):
        lanes = slice(start, start + 128)
        low = (alpha * scaled_in[:, lanes] - beta * squared[:, lanes]).astype(BF16)
        grad_mixed[:, lanes] = low
        state_out[0, :, lanes] = dot(lifted_c[:, lanes], low).astype(BF16)


def grad_z_body(inner, parts, base, *refs):
    sums = refs[:parts]
    mixed_in, z_in, grad_in, gain, grad_z = refs[parts:]
    alpha, beta = norm_columns(inner, sums)
    for start in range(0, z_in.shape[1], 128):
        lanes = slice(start, start + 128)
        z = z_in[:, lanes].astype(F32)
        sigma = sigmoid(z)
        mixed = mixed_in[:, lanes]
        scaled = grad_in[:, lanes].astype(F32) * gain[:, lanes]
        grad_gated = alpha * scaled - beta * (mixed * (z * sigma))
        grad_z[:, lanes] = (grad_gated * mixed * (sigma * (1.0 + z * (1.0 - sigma)))).astype(BF16)


def inner_back_body(
    own_half,
    base,
    gram,
    bc,
    step_in,
    cumul_in,
    x_in,
    grad_in,
    mine,
    other,
    rows,
    grad_x,
    q_out,
    r_out,
    bc_out,
    z_sum,
    c_sum,
):
    group = pl.program_id(0)
    length = x_in.shape[0]

    @pl.when(group == 0)
    def _():
        z_sum[...] = jnp.zeros_like(z_sum)
        c_sum[...] = jnp.zeros_like(c_sum)

    cumul = cumul_in[...]
    cumul_columns = columns_of(cumul)
    lifted = jnp.exp(cumul_columns)
    state = pick_state(own_half, mine, other)
    c_rows = bc[1].astype(F32)
    lane = lax.broadcasted_iota(jnp.int32, (length, 128), 1)
    q_columns = jnp.zeros((length, 128), F32)
    for head in range(x_in.shape[1] // 128):
        lanes = slice(head * 128, head * 128 + 128)
        step = step_in[head : head + 1, :]
        decay = jnp.exp(
            jnp.minimum(cumul_columns[:, head : head + 1] - cumul[head : head + 1, :], 0.0)
        )
        gram_decay = gram[...] * decay
        mixer = (gram_decay * step).astype(BF16)
        x_head, grad_head = x_in[:, lanes], grad_in[:, lanes]
        product = dot_rows(grad_head, x_head)
        z_sum[...] += product * decay * step
        gram_grad = product * gram_decay
        r_out[head : head + 1, :] = jnp.sum(gram_grad, axis=0, keepdims=True)
        handed = lifted[:, head : head + 1] * dot_rows(grad_head, state[:, lanes])
        c_sum[...] += handed
        q = jnp.sum(gram_grad * step + c_rows * handed, axis=1, keepdims=True)
        q_columns = jnp.where(lane == head, q, q_columns)
        grad_x[:, lanes] = dot_columns(mixer, grad_head) + rows[1:2, lanes] * grad_head.astype(F32)
    q_out[...] = q_columns.T[:GROUP, :]

    @pl.when(group == pl.num_programs(0) - 1)
    def _():
        summed = jnp.where(triangle(length, False), z_sum[...], 0.0)
        bc_out[0] = dot_split(summed.T, bc[1])
        bc_out[1] = c_sum[...] + dot_split(summed, bc[0])


def block_weights(step, cumul):
    return columns_of(jnp.exp(cumul[:, cumul.shape[1] - 1 :] - cumul) * step)


def rim_body(
    own_half,
    base,
    bc,
    step_in,
    cumul_in,
    weighted_x,
    partial,
    slope,
    out_mine,
    out_other,
    bc_partial,
    bc_slope,
    rim_out,
    bc_out,
    b_sum,
):
    group, groups = pl.program_id(0), pl.num_programs(0)
    width = weighted_x.shape[1]

    @pl.when(group == 0)
    def _():
        b_sum[...] = jnp.zeros_like(b_sum)

    out_low = pick_state(own_half, out_mine, out_other)
    b_sum[...] += dot_rows(weighted_x[...], out_low)
    weights = block_weights(step_in[...], cumul_in[...])[0:8, :]
    returned = dot(bc[0][0:16, :], out_low)[0:8, :]
    for head in range(width // 128):
        lanes = slice(head * 128, head * 128 + 128)
        weight = weights[:, head : head + 1]
        rows = (partial[:, lanes] + weight * returned[:, lanes]) * slope[:, lanes]
        place = pl.multiple_of(lax.rem(group + base[0], groups) * width + head * 128, 128)
        rim_out[:, pl.ds(place, 128)] = rows[0:3, :]

    @pl.when(group == groups - 1)
    def _():
        bc_out[0] = (b_sum[...] + bc_partial[0]) * bc_slope[0]
        bc_out[1] = bc_partial[1] * bc_slope[1]
        for j in range(2):
            start = rim_out.shape[1] - 256 + 128 * j
            rim_out[:, start : start + 128] = bc_out[j, 0:3, :]


def grad_dt_body(
    own_half,
    base,
    bc,
    rate,
    dt_slope,
    step_in,
    cumul_in,
    q_in,
    r_in,
    x_in,
    state_mine,
    state_other,
    out_mine,
    out_other,
    grad_dt,
    selector,
    products,
):
    length, width = x_in.shape

    @pl.when(pl.program_id(0) == 0)
    def _():
        row = lax.broadcasted_iota(jnp.int32, (width, 128), 0)
        lane = lax.broadcasted_iota(jnp.int32, (width, 128), 1)
        selector[...] = (row // 128 == lane).astype(BF16)

    cumul, step = cumul_in[...], step_in[...]
    state = pick_state(own_half, state_mine, state_other)
    out_low = pick_state(own_half, out_mine, out_other)
    returned = dot(bc[0], out_low)
    for start in range(0, width, 128):
        lanes = slice(start, start + 128)
        products[:, lanes] = (x_in[:, lanes].astype(F32) * returned[:, lanes]).astype(BF16)
    inner_b = dot(products[...], selector[...]).T[:GROUP, :]
    w = jnp.exp(cumul[:, length - 1 :] - cumul) * inner_b
    dots = dot(jnp.ones((16, length), BF16), state * out_low)[:GROUP, :]
    row = lax.broadcasted_iota(jnp.int32, (GROUP, width), 0)
    lane = lax.broadcasted_iota(jnp.int32, (GROUP, width), 1)
    dots = jnp.sum(jnp.where(lane // 128 == row, dots, 0.0), axis=1, keepdims=True)
    q, r = q_in[...], r_in[...]
    inside = jnp.sum(step * w, axis=1, keepdims=True)
    end = inside + jnp.exp(cumul[:, length - 1 :]) * dots
    last = lax.broadcasted_iota(jnp.int32, (GROUP, length), 1) == length - 1
    grad_cumul = q - step * (r + w) + jnp.where(last, end, 0.0)
    grad_log = dot_split(grad_cumul, triangle(length, False).astype(BF16))
    grad_dt[...] = (r + w + rate[...] * grad_log) * dt_slope[...]


def grad_x_body(
    own_half,
    base,
    bc,
    step_in,
    cumul_in,
    partial,
    slope,
    taps,
    halo,
    out_mine,
    out_other,
    grad_x,
    ext,
):
    length, width = partial.shape
    weights = block_weights(step_in[...], cumul_in[...])
    returned = dot(bc[0], pick_state(own_half, out_mine, out_other))
    for head in range(width // 128):
        lanes = slice(head * 128, head * 128 + 128)
        weight = weights[:, head : head + 1]
        ext[0:length, :] = (partial[:, lanes] + weight * returned[:, lanes]) * slope[:, lanes]
        ext[length : length + 3, :] = halo[:, lanes]
        total = taps[0:1, lanes] * ext[3 : 3 + length, :]
        for k in range(1, 4):
            total = total + taps[k : k + 1, lanes] * ext[3 - k : 3 - k + length, :]
        grad_x[:, lanes] = total.astype(BF16)


def bc_back_body(place, grad_pre, halo, taps, kept, sent, ext, total):
    length, half = grad_pre.shape[1], kept.shape[1]
    for j in range(2):
        ext[0:length, :] = grad_pre[j]
        ext[length : length + 3, :] = halo[:, 128 * j : 128 * j + 128]
        summed = taps[j, 0:1, :] * ext[3 : 3 + length, :]
        for k in range(1, 4):
            summed = summed + taps[j, k : k + 1, :] * ext[3 - k : 3 - k + length, :]
        total[...] = summed
        kept[j] = total[pl.ds(pl.multiple_of(place[4] * half, half), half), :]
        sent[j] = total[pl.ds(pl.multiple_of((1 - place[4]) * half, half), half), :]


def bc_half_body(place, mine, taken, kept, sent, total):
    half = kept.shape[1]
    for j in range(2):
        total[...] = mine[j] + taken[j]
        kept[j] = total[pl.ds(pl.multiple_of(place[5] * half, half), half), :]
        sent[j] = total[pl.ds(pl.multiple_of((1 - place[5]) * half, half), half), :]


def bc_last_body(_, mine, taken, out):
    out[...] = (mine[...] + taken[...]).astype(BF16)


def conv_back(extended, weights):
    length = extended.shape[-2] - 3
    summed = weights[..., 0, :][..., None, :] * extended[..., 3 : 3 + length, :]
    for k in range(1, 4):
        summed = (
            summed
            + weights[..., k, :][..., None, :] * extended[..., 3 - k : 3 - k + length, :]
        )
    return summed


def shards(
    x_input,
    z_input,
    bc_input,
    dt_raw,
    dt_bias,
    a_log,
    d_skip,
    conv_x,
    convolution_bc_taps,
    rescale_factor,
    grad_out,
):
    length, channels = x_input.shape
    heads = dt_raw.shape[0]
    groups = heads // GROUP
    width = GROUP * 128
    count, parts = lax.axis_size("seq"), lax.axis_size("head")
    inner = channels * parts
    own = lax.axis_index("seq")
    split = count == 8 and groups == 4
    own_half = groups // 2 if split else groups
    bit = lambda value, place: lax.shift_right_logical(value, place) & 1
    high, odd = bit(lax.axis_index("head"), 1), bit(lax.axis_index("head"), 0)
    core = bit(own, 0)
    base = jnp.stack(
        [core * own_half if split else core * 0, bit(own, 2), bit(own, 1), core, high, odd]
    ).astype(jnp.int32)

    whole = lambda *shape: (shape, lambda g, b: (0,) * len(shape))
    turn = lambda g, b, off=0: lax.rem(g + off + b[0], groups)
    wide_at = lambda off: ((length, width), lambda g, b: (0, turn(g, b, off)))
    rows_at = lambda off: ((GROUP, length), lambda g, b: (turn(g, b, off), 0))
    lanes_at = lambda n, off: ((n, width), lambda g, b: (0, turn(g, b, off)))
    wide, rows8, lanes_of = wide_at(0), rows_at(0), lambda n: lanes_at(n, 0)
    slot = ((1, length, width), lambda g, b: (g, 0, 0))
    mine_slot = ((1, length, width), lambda g, b: (jnp.minimum(g, own_half - 1), 0, 0))
    other_slot = ((1, length, width), lambda g, b: (jnp.maximum(g - own_half, 0), 0, 0))
    full = lambda array: (array,) + whole(*array.shape)
    grid = (groups,)
    halves = [own_half, 0] if split else [0]
    half_grid = (own_half,)

    gain = rescale_factor[None, :]
    f32 = lambda *shape: (shape, F32)
    low = lambda *shape: (shape, BF16)

    step, cumul, rate, dt_slope, rows, rim = call(
        steps_body,
        [
            f32(heads, length) + whole(heads, length),
            f32(heads, length) + whole(heads, length),
            f32(heads, length) + whole(heads, length),
            f32(heads, length) + whole(heads, length),
            f32(2, channels) + whole(2, channels),
            low(3, channels + 256) + whole(3, channels + 256),
        ],
        [
            full(in_hbm(dt_raw)),
            full(in_hbm(dt_bias[None, :])),
            full(in_hbm(a_log[None, :])),
            full(in_hbm(d_skip[None, :])),
            (in_hbm(x_input), (16, channels), lambda g, b: (length // 16 - 1, 0)),
            (in_hbm(bc_input), (2, 16, 128), lambda g, b: (0, length // 16 - 1, 0)),
        ],
        base=base,
        grid=(1,),
    )
    rim = lax.ppermute(rim, "seq", [(i - 1, i) for i in range(1, count)])
    if split:
        swap = lambda block, bit: lax.ppermute(
            block, "seq", [(i, i ^ bit) for i in range(count)]
        )
        total = rows[0:1]
        total_core = swap(total, 1)
        chip_total = total + total_core
        total_across = swap(chip_total, 2)
        table = f32(16, channels) + whole(16, channels)
        ahead, behind = call(
            weights_body,
            [table, table],
            [full(rows), full(total_core), full(total_across)],
            base=base,
            grid=(1,),
        )

    def passed(locals_, reverse, beside):
        if split:
            local_sent, local = locals_
            weights = behind if reverse else ahead
            return scan_blocks(base, groups, weights, local, local_sent, reverse, beside)
        (local,) = locals_
        for work in beside:
            work(local)
        return gather_blocks(rows[0:1], local, reverse)

    carry, local = [], []
    for off in halves:
        first = off == halves[0]
        ins = [
            (in_hbm(x_input),) + wide_at(off),
            (rim,) + lanes_at(3, off),
            (in_hbm(conv_x),) + lanes_at(4, off),
            (step,) + rows_at(off),
            (cumul,) + rows_at(off),
        ]
        outs = [
            low(length, channels) + wide_at(off),
            f32(length, channels) + wide_at(off),
            low(own_half, length, width) + slot,
        ]
        scratch = [pltpu.VMEM((length + 8, 128), F32)]
        if first:
            ins += [
                full(in_hbm(bc_input)),
                (rim, (3, 256), lambda g, b: (0, channels // 256)),
                full(in_hbm(convolution_bc_taps)),
            ]
            outs += [
                low(2, length, 128) + whole(2, length, 128),
                f32(2, length, 128) + whole(2, length, 128),
                f32(length, length) + whole(length, length),
                f32(128, length) + whole(128, length),
            ]
            scratch += [pltpu.VMEM((length + 8, 128), F32)]
        else:
            ins += [full(b_turned)]
        result = call(
            functools.partial(prepare_body, first),
            outs,
            ins,
            base=base,
            grid=half_grid,
            scratch=scratch,
            carry=carry,
            flops=2 * length * 128 * channels,
        )
        if first:
            bc, bc_slope, gram, b_turned = result[3:]
        carry = result[:2]
        local.append(result[2])
    x_low, slope = carry
    done = {}

    def mix_inside(ready):
        done["mixed"], token = call(
            inner_body,
            [f32(length, channels) + wide],
            [
                full(gram),
                (step,) + rows8,
                (cumul,) + rows8,
                (x_low,) + wide,
                (rows,) + lanes_of(2),
            ],
            base=base,
            grid=grid,
            after=[ready],
            token=True,
            flops=2 * length * 128 * channels,
        )
        return token

    def gates(ready):
        done["gate"], done["scaled"], done["weighted_x"], done["lifted_c"], token = call(
            gate_body,
            [
                f32(length, channels) + wide,
                f32(length, channels) + wide,
                low(length, channels) + wide,
                low(length, channels) + wide,
            ],
            [
                (z_input,) + wide,
                (grad_out,) + wide,
                (gain,) + lanes_of(1),
                full(bc),
                (step,) + rows8,
                (cumul,) + rows8,
                (x_low,) + wide,
            ],
            base=base,
            grid=grid,
            scratch=[pltpu.VMEM((128, length), F32)],
            after=[ready],
            token=True,
        )
        return token

    state_mine, state_other = passed(local, False, (mix_inside, gates))
    gate, scaled = done["gate"], done["scaled"]
    c_spec = ((1, length, 128), lambda g, b: (1, 0, 0))
    mixed, sums = done["mixed"], jnp.zeros((8, length), F32)
    for off, state in zip(reversed(halves), (state_mine, state_other)):
        mixed, sums = call(
            mix_body,
            [f32(length, channels) + wide_at(off), f32(8, length) + whole(8, length)],
            [
                (mixed,) + wide_at(off),
                (bc,) + c_spec,
                (cumul,) + rows_at(off),
                (state,) + slot,
                (gate,) + wide_at(off),
                (scaled,) + wide_at(off),
                full(sums),
            ],
            base=base,
            grid=half_grid,
            scratch=[pltpu.VMEM((length, 128), F32), pltpu.VMEM((length, 128), F32)],
            place=0,
            flops=2 * length * 128 * channels,
        )
    turn_head = lambda block, bit: lax.ppermute(
        block, "head", [(i, i ^ bit) for i in range(parts)]
    )
    if parts == 4:
        sums = sums + turn_head(sums, 1)
        all_sums = [sums, turn_head(sums, 2)]
    else:
        all_sums = [lax.psum(sums, "head")]
    (squared,) = call(
        square_body,
        [f32(length, channels) + wide],
        [(mixed,) + wide, (gate,) + wide],
        base=base,
        grid=grid,
    )
    carry, local_back = [], []
    for off in halves:
        grad_mixed, state = call(
            functools.partial(grad_mixed_body, inner, len(all_sums)),
            [low(length, channels) + wide_at(off), low(own_half, length, width) + slot],
            [full(part) for part in all_sums]
            + [
                (squared,) + wide_at(off),
                (scaled,) + wide_at(off),
                (done["lifted_c"],) + wide_at(off),
            ],
            base=base,
            grid=half_grid,
            carry=carry,
            flops=2 * length * 128 * channels,
        )
        carry = [grad_mixed]
        local_back.append(state)

    def back_inside(ready):
        done["back"] = call(
            functools.partial(inner_back_body, own_half),
            [
                f32(length, channels) + wide,
                f32(heads, length) + rows8,
                f32(heads, length) + rows8,
                f32(2, length, 128) + whole(2, length, 128),
            ],
            [
                full(gram),
                full(bc),
                (step,) + rows8,
                (cumul,) + rows8,
                (x_low,) + wide,
                (grad_mixed,) + wide,
                (state_mine,) + mine_slot,
                (state_other,) + other_slot,
                (rows,) + lanes_of(2),
            ],
            base=base,
            grid=grid,
            scratch=[pltpu.VMEM((length, length), F32), pltpu.VMEM((length, 128), F32)],
            after=[ready],
            flops=6 * length * 128 * channels,
        )
        return done["back"][1]

    def back_gates(ready):
        done["grad_z"], token = call(
            functools.partial(grad_z_body, inner, len(all_sums)),
            [low(length, channels) + wide],
            [full(part) for part in all_sums]
            + [
                (mixed,) + wide,
                (z_input,) + wide,
                (grad_out,) + wide,
                (gain,) + lanes_of(1),
            ],
            base=base,
            grid=grid,
            after=[ready],
            token=True,
        )
        return token

    out_mine, out_other = passed(local_back, True, (back_inside, back_gates))
    partial, q_rows, r_rows, bc_partial = done["back"]
    first_rows = ((8, width), lambda g, b: (0, turn(g, b)))
    outs_in = [(out_mine,) + mine_slot, (out_other,) + other_slot]
    rim_back, grad_bc_pre = call(
        functools.partial(rim_body, own_half),
        [
            f32(3, channels + 256) + whole(3, channels + 256),
            f32(2, length, 128) + whole(2, length, 128),
        ],
        [
            full(bc),
            (step,) + rows8,
            (cumul,) + rows8,
            (done["weighted_x"],) + wide,
            (partial,) + first_rows,
            (slope,) + first_rows,
        ]
        + outs_in
        + [full(bc_partial), full(bc_slope)],
        base=base,
        grid=grid,
        scratch=[pltpu.VMEM((length, 128), F32)],
        flops=2 * length * 128 * channels,
    )
    rim_back = lax.ppermute(rim_back, "seq", [(i, i - 1) for i in range(1, count)])
    grad_dt, dt_token = call(
        functools.partial(grad_dt_body, own_half),
        [f32(heads, length) + rows8],
        [
            full(bc),
            (rate,) + rows8,
            (dt_slope,) + rows8,
            (step,) + rows8,
            (cumul,) + rows8,
            (q_rows,) + rows8,
            (r_rows,) + rows8,
            (x_low,) + wide,
            (state_mine,) + mine_slot,
            (state_other,) + other_slot,
        ]
        + outs_in,
        base=base,
        grid=grid,
        scratch=[pltpu.VMEM((width, 128), BF16), pltpu.VMEM((length, width), BF16)],
        after=[grad_bc_pre],
        token=True,
        flops=4 * length * 128 * channels,
    )
    if parts == 4:
        piece = lambda rows: f32(2, rows, 128) + whole(2, rows, 128)
        kept, sent = call(
            bc_back_body,
            [piece(length // 2), piece(length // 2)],
            [
                full(grad_bc_pre),
                (rim_back, (3, 256), lambda g, b: (0, channels // 256)),
                full(convolution_bc_taps),
            ],
            base=base,
            grid=(1,),
            scratch=[pltpu.VMEM((length + 8, 128), F32), pltpu.VMEM((length, 128), F32)],
            after=[dt_token],
        )
        taken = turn_head(sent, 2)
    grad_x, x_token = call(
        functools.partial(grad_x_body, own_half),
        [low(length, channels) + wide],
        [
            full(bc),
            (step,) + rows8,
            (cumul,) + rows8,
            (partial,) + wide,
            (slope,) + wide,
            (conv_x,) + lanes_of(4),
            (rim_back,) + lanes_of(3),
        ]
        + outs_in,
        base=base,
        grid=grid,
        scratch=[pltpu.VMEM((length + 8, 128), F32)],
        token=True,
        flops=2 * length * 128 * channels,
    )
    if parts == 4:
        kept, sent = call(
            bc_half_body,
            [piece(length // 4), piece(length // 4)],
            [full(kept), full(taken)],
            base=base,
            grid=(1,),
            scratch=[pltpu.VMEM((length // 2, 128), F32)],
            after=[x_token],
        )
        (grad_bc,) = call(
            bc_last_body,
            [low(2, length // 4, 128) + whole(2, length // 4, 128)],
            [full(kept), full(turn_head(sent, 1))],
            base=base,
            grid=(1,),
        )
    else:
        bc_halo = jnp.moveaxis(rim_back[:, channels:].reshape(3, 2, 128), 1, 0)
        bc_sum = conv_back(jnp.concatenate([grad_bc_pre, bc_halo], axis=1), convolution_bc_taps)
        share = length // parts
        first_row = lax.axis_index("head") * share
        bc_sum = lax.psum(bc_sum, "head")
        grad_bc = lax.dynamic_slice_in_dim(bc_sum, first_row, share, 1).astype(BF16)
    return (grad_x, done["grad_z"], grad_bc, grad_dt)


def solution(mesh):
    return jax.shard_map(
        shards,
        mesh=mesh,
        in_specs=(
            P("seq", "head"),
            P("seq", "head"),
            P(None, "seq", None),
            P("head", "seq"),
            P("head"),
            P("head"),
            P("head"),
            P(None, "head"),
            P(),
            P("head"),
            P("seq", "head"),
        ),
        out_specs=(
            P("seq", "head"),
            P("seq", "head"),
            P(None, ("seq", "head"), None),
            P("head", "seq"),
        ),
        check_vma=False,
    )
```

```python
import functools

import jax
import jax.numpy as jnp
from jax import lax
from jax.experimental import pallas as pl
from jax.experimental.pallas import tpu as pltpu
from jax.sharding import PartitionSpec as P

EPS = 1e-05
GROUP = 8
F32 = jnp.float32
BF16 = jnp.bfloat16
VMEM_BYTES = 16 * 2**20


def sigmoid(value):
    return 0.5 + 0.5 * jnp.tanh(0.5 * value)


def dot(a, b):
    return jnp.dot(a, b, preferred_element_type=F32)


def dot_split(a, b):
    high = a.astype(BF16)
    rest = a - high.astype(F32)
    middle = rest.astype(BF16)
    low = (rest - middle.astype(F32)).astype(BF16)
    return dot(high, b) + (dot(middle, b) + dot(low, b))


def dot_rows(a, b):
    return lax.dot_general(a, b, (((1,), (1,)), ((), ())), preferred_element_type=F32)


def dot_columns(a, b):
    return lax.dot_general(a, b, (((0,), (0,)), ((), ())), preferred_element_type=F32)


def triangle(length, upper):
    first = lax.broadcasted_iota(jnp.int32, (length, length), 0)
    second = lax.broadcasted_iota(jnp.int32, (length, length), 1)
    return first <= second if upper else first >= second


def columns_of(rows):
    return rows.T


def call(body, outs, ins, *, base=None, grid=(), scratch=(), after=(), carry=(), place=None, token=False, flops=0):
    aliases = {1 + len(ins) + len(after) + i: i for i in range(len(carry))}
    if place is not None:
        aliases[1 + place] = 0
    after = list(after) + list(carry)
    in_specs = [pl.BlockSpec(block, index) for _, block, index in ins]
    in_specs += [pl.BlockSpec(memory_space=pl.ANY) for _ in after]
    outs = list(outs)
    if token:
        outs.append(((8, 128), F32, (8, 128), lambda *_: (0, 0)))
    out_specs = [pl.BlockSpec(block, index) for _, _, block, index in outs]
    out_shape = [jax.ShapeDtypeStruct(shape, dtype) for shape, dtype, _, _ in outs]
    arrays = [array for array, _, _ in ins]
    moved = sum(a.size * a.dtype.itemsize for a in arrays + out_shape)
    read = 1 + len(arrays)

    def ordered(*refs):
        results = refs[read + len(after) :]
        if token:
            results[len(outs) - 1][...] = jnp.zeros((8, 128), F32)
            results = results[: len(outs) - 1] + results[len(outs) :]
        body(*refs[:read], *results)

    return pl.pallas_call(
        ordered,
        out_shape=out_shape,
        grid_spec=pltpu.PrefetchScalarGridSpec(
            num_scalar_prefetch=1,
            grid=grid,
            in_specs=in_specs,
            out_specs=out_specs,
            scratch_shapes=list(scratch),
        ),
        input_output_aliases=aliases,
        cost_estimate=pl.CostEstimate(flops=flops, bytes_accessed=moved, transcendentals=0),
        compiler_params=pltpu.CompilerParams(vmem_limit_bytes=VMEM_BYTES),
    )(base, *arrays, *after)


def in_hbm(array):
    return pltpu.with_memory_space_constraint(array, pltpu.HBM)


def column_of(row):
    count = row.shape[1]
    first = lax.broadcasted_iota(jnp.int32, (count, count), 0)
    second = lax.broadcasted_iota(jnp.int32, (count, count), 1)
    return jnp.sum(jnp.where(first == second, row, 0.0), axis=1, keepdims=True)


def steps_body(
    _,
    raw,
    bias,
    log_rate,
    skip,
    x_tail,
    bc_tail,
    step_out,
    cumul_out,
    rate_out,
    slope_out,
    rows_out,
    rim_out,
):
    heads, length = raw.shape
    channels = x_tail.shape[1]
    rim_out[:, 0:channels] = x_tail[...].astype(F32)[13:16, :].astype(BF16)
    for j in range(2):
        start = channels + 128 * j
        rim_out[:, start : start + 128] = bc_tail[j].astype(F32)[13:16, :].astype(BF16)
    shifted = raw[...] + column_of(bias[...])
    step = jnp.maximum(shifted, 0.0) + jnp.log1p(jnp.exp(-jnp.abs(shifted)))
    rate = jnp.broadcast_to(-jnp.exp(column_of(log_rate[...])), step.shape)
    cumul = dot_split(rate * step, triangle(length, True).astype(BF16))
    step_out[...] = step
    cumul_out[...] = cumul
    rate_out[...] = rate
    slope_out[...] = sigmoid(shifted)
    skips = column_of(skip[...])
    for head in range(heads):
        lanes = slice(head * 128, head * 128 + 128)
        rows_out[0:1, lanes] = jnp.broadcast_to(cumul[head : head + 1, length - 1 :], (1, 128))
        rows_out[1:2, lanes] = jnp.broadcast_to(skips[head : head + 1, :], (1, 128))


def pick(test, yes, no):
    return jnp.where(test, yes, no)


def first_group(place):
    return place[0] & 255


def place_bit(place, index):
    return lax.shift_right_logical(place[0], 8 + index) & 1


def weights_body(place, own, core, across, *outs):
    t0, t1 = own[0:1, :], core[...]
    e0, e1, own_chip, ex = jnp.exp(t0), jnp.exp(t1), jnp.exp(t0 + t1), jnp.exp(across[...])
    one = jnp.ones_like(e0)
    zero = jnp.zeros_like(e0)
    bits = [place_bit(place, i) for i in range(3)]
    x_first = bits[2] == 0
    for out, reverse in zip(outs, (False, True)):
        y, x, c = ((1 - bit if reverse else bit) == 1 for bit in bits)
        either = jnp.logical_or(x, y)
        scale = pick(jnp.logical_or(x_first, either), one, ex)
        rows = [pick(c, one, e1), pick(c, e0, one)]
        rows += [rows[0] * scale, rows[1] * scale]
        rows += [
            pick(x_first, pick(x, one, ex), pick(jnp.logical_and(x, y), zero, one)),
            pick(x_first, pick(x, own_chip, one), pick(y, pick(x, one, own_chip), zero)),
        ]
        a = pick(x_first, pick(x, one, zero), pick(y, pick(x, ex, one), zero))
        b = pick(x_first, pick(y, pick(x, ex, one), zero), pick(either, one, zero))
        into, send = pick(c, e1, one), pick(c, one, e0)
        rows += [into * a, into * b, pick(c, one, zero)]
        rows += [send * a, send * b, pick(c, zero, one)]
        for index, row in enumerate(rows):
            out[index : index + 1, :] = row


def combine(base, groups, weights, outs, after=()):
    arrays, columns = [], []
    for slots in outs:
        for column, terms in slots:
            if column not in columns:
                columns.append(column)
            for _, (array, slot) in terms:
                if not any(array is a and slot == s for a, s in arrays):
                    arrays.append((array, slot))
    place = lambda array, slot: [
        i for i, (a, s) in enumerate(arrays) if a is array and s == slot
    ][0]
    plan = [
        [
            (columns.index(column), [(row, place(*source)) for row, source in terms])
            for column, terms in slots
        ]
        for slots in outs
    ]

    def body(_, *refs):
        rows, values = refs[: len(columns)], refs[len(columns) : len(columns) + len(arrays)]
        results = refs[len(columns) + len(arrays) :]
        width = rows[0].shape[1]
        for result, slots in zip(results, plan):
            for slot, (column, terms) in enumerate(slots):
                for start in range(0, width, 256):
                    lanes = slice(start, start + 256)
                    total = None
                    for row, index in terms:
                        term = rows[column][row : row + 1, lanes] * values[index][
                            0, :, lanes
                        ].astype(F32)
                        total = term if total is None else total + term
                    result[slot, :, lanes] = total.astype(BF16)

    length, width = arrays[0][0].shape[1:]
    ins = [
        (
            weights,
            (weights.shape[0], width),
            lambda g, b, column=column: (0, lax.rem(first_group(b) + column, groups)),
        )
        for column in columns
    ]
    ins += [
        (array, (1, length, width), lambda g, b, slot=slot: (slot, 0, 0))
        for array, slot in arrays
    ]
    results = [
        ((len(slots), length, width), BF16, (len(slots), length, width), lambda g, b: (0, 0, 0))
        for slots in outs
    ]
    return call(body, results, ins, base=base, grid=(1,), after=after)


def scan_blocks(base, groups, weights, local, local_sent, reverse, beside):
    count = lax.axis_size("seq")
    place = lambda position: count - 1 - position if reverse else position

    def swap(block, bit_of, keep):
        route = [
            (place(i), place(i ^ bit_of(place(i) % 2)))
            for i in range(count)
            if keep(i, place(i) % 2)
        ]
        return lax.ppermute(block, "seq", route)

    def merge(*plans, after=()):
        both = [
            [
                (slot, [(row, (array, slot)) for row, array in zip(rows, sources)])
                for slot in range(2)
            ]
            for rows, sources in plans
        ]
        return combine(base, groups, weights, both, after)

    everyone = lambda i, core: True
    taken = swap(local_sent, lambda core: 1, everyone)
    chip, chip_sent = merge(((0, 1), (local, taken)), ((2, 3), (local, taken)))
    chip_a = swap(
        chip_sent, lambda core: 4 if core else 2, lambda i, core: i < 4 if core else i < 6
    )
    after_a = beside[0](chip)
    (sent,) = merge(((4, 5), (chip, chip_a)), after=[after_a])
    chip_b = swap(
        sent, lambda core: 2 if core else 4, lambda i, core: i not in (2, 3) if core else i < 4
    )
    after_b = beside[1](sent)
    mine, handed = merge(
        ((6, 7, 8), (chip_a, chip_b, taken)),
        ((9, 10, 11), (chip_a, chip_b, local)),
        after=[after_b],
    )
    return mine, swap(handed, lambda core: 1, everyone)


def gather_blocks(totals, local, reverse):
    table = lax.all_gather(totals, "seq", axis=0, tiled=True)
    blocks = lax.all_gather(local[None], "seq", axis=0, tiled=True)
    own = lax.axis_index("seq")
    order = jnp.arange(table.shape[0], dtype=jnp.int32)
    if reverse:
        inside = (order[None, :] > own) & (order[None, :] < order[:, None])
        selected = order > own
    else:
        inside = (order[None, :] > order[:, None]) & (order[None, :] < own)
        selected = order < own
    exponent = jnp.sum(jnp.where(inside[:, :, None], table[None], 0.0), axis=1)
    factor = jnp.where(selected[:, None], jnp.exp(exponent), 0.0)
    factor = factor.reshape(factor.shape[0], local.shape[0], 1, local.shape[2])
    state = jnp.sum(factor * blocks.astype(F32), axis=0).astype(BF16)
    return state, state


def prepare_body(first, base, x_in, x_halo, taps, step_in, cumul_in, *refs):
    length, width = x_in.shape
    if first:
        bc_in, bc_halo, bc_taps, x_out, slope_out, state_out = refs[:6]
        bc_out, bc_slope_out, gram_out, b_turned, ext, bc_ext = refs[6:]

        @pl.when(pl.program_id(0) == 0)
        def _():
            for j in range(2):
                bc_ext[5:8, :] = bc_halo[:, j * 128 : j * 128 + 128].astype(F32)
                bc_ext[8 : 8 + length, :] = bc_in[j].astype(F32)
                pre = bc_taps[j, 0:1, :] * bc_ext[5 : 5 + length, :]
                for k in range(1, 4):
                    pre = pre + bc_taps[j, k : k + 1, :] * bc_ext[5 + k : 5 + k + length, :]
                sigma = sigmoid(pre)
                bc_out[j] = (pre * sigma).astype(BF16)
                bc_slope_out[j] = sigma * (1.0 + pre * (1.0 - sigma))
            b_turned[...] = bc_out[0].astype(F32).T
            gram_out[...] = jnp.where(
                triangle(length, False), dot_rows(bc_out[1], bc_out[0]), 0.0
            )

    else:
        b_turned, x_out, slope_out, state_out, ext = refs

    tail_step = jnp.exp(cumul_in[:, length - 1 :] - cumul_in[...]) * step_in[...]
    for head in range(width // 128):
        lanes = slice(head * 128, head * 128 + 128)
        ext[5:8, :] = x_halo[:, lanes].astype(F32)
        ext[8 : 8 + length, :] = x_in[:, lanes].astype(F32)
        pre = taps[0:1, lanes] * ext[5 : 5 + length, :]
        for k in range(1, 4):
            pre = pre + taps[k : k + 1, lanes] * ext[5 + k : 5 + k + length, :]
        sigma = sigmoid(pre)
        x_low = (pre * sigma).astype(BF16)
        x_out[:, lanes] = x_low
        slope_out[:, lanes] = sigma * (1.0 + pre * (1.0 - sigma))
        weighted = (b_turned[...] * tail_step[head : head + 1, :]).astype(BF16)
        state_out[0, :, lanes] = dot(weighted, x_low).astype(BF16)


def inner_body(base, gram, step_in, cumul_in, x_in, rows, mixed_out):
    cumul = cumul_in[...]
    cumul_columns = columns_of(cumul)
    for head in range(x_in.shape[1] // 128):
        lanes = slice(head * 128, head * 128 + 128)
        row = cumul[head : head + 1, :]
        decay = jnp.exp(jnp.minimum(cumul_columns[:, head : head + 1] - row, 0.0))
        mixer = (gram[...] * decay * step_in[head : head + 1, :]).astype(BF16)
        x_head = x_in[:, lanes]
        mixed_out[:, lanes] = dot(mixer, x_head) + rows[1:2, lanes] * x_head.astype(F32)


def pick_state(own_half, mine, other):
    group = pl.program_id(0)
    return jnp.where(group < own_half, mine[0], other[0])


def gate_body(
    base,
    z_in,
    grad_in,
    gain,
    bc,
    step_in,
    cumul_in,
    x_in,
    gate_out,
    scaled_out,
    weighted_x,
    lifted_out,
    c_turned,
):
    @pl.when(pl.program_id(0) == 0)
    def _():
        c_turned[...] = bc[1].astype(F32).T

    weights = block_weights(step_in[...], cumul_in[...])
    lifted = jnp.exp(cumul_in[...])
    for head in range(z_in.shape[1] // 128):
        lanes = slice(head * 128, head * 128 + 128)
        z = z_in[:, lanes].astype(F32)
        gate = z * sigmoid(z)
        gate_out[:, lanes] = gate
        scaled_out[:, lanes] = grad_in[:, lanes].astype(F32) * gain[:, lanes] * gate
        weight = weights[:, head : head + 1]
        weighted_x[:, lanes] = (weight * x_in[:, lanes].astype(F32)).astype(BF16)
        lifted_out[:, lanes] = (c_turned[...] * lifted[head : head + 1, :]).astype(BF16)


def mix_body(
    base, mixed_in, c_rows, cumul_in, state, gate_in, scaled_in, sums_in, *outs
):
    mixed_out, sums_out, squares, products = outs
    group = pl.program_id(0)

    @pl.when(group == 0)
    def _():
        squares[...] = jnp.zeros_like(squares)
        products[...] = jnp.zeros_like(products)

    carried = dot(c_rows[0], state[0])
    lifted = jnp.exp(columns_of(cumul_in[...]))
    square, product = squares[...], products[...]
    for head in range(mixed_in.shape[1] // 128):
        lanes = slice(head * 128, head * 128 + 128)
        mixed = mixed_in[:, lanes] + lifted[:, head : head + 1] * carried[:, lanes]
        mixed_out[:, lanes] = mixed
        gated = mixed * gate_in[:, lanes]
        square = square + gated * gated
        product = product + mixed * scaled_in[:, lanes]
    squares[...] = square
    products[...] = product

    @pl.when(group == pl.num_programs(0) - 1)
    def _():
        sums_out[...] = sums_in[...]
        sums_out[0:1, :] += jnp.sum(squares[...].T, axis=0, keepdims=True)
        sums_out[1:2, :] += jnp.sum(products[...].T, axis=0, keepdims=True)


def norm_columns(inner, sums):
    total = sums[0][...]
    for part in sums[1:]:
        total = total + part[...]
    inv_rms = lax.rsqrt(total[0:1, :] / inner + EPS)
    mean_dot = inv_rms * total[1:2, :] / inner
    scales = jnp.concatenate(
        [inv_rms, inv_rms * inv_rms * mean_dot, jnp.zeros((6, total.shape[1]), F32)], axis=0
    )
    columns = columns_of(scales)
    return columns[:, 0:1], columns[:, 1:2]


def square_body(base, mixed_in, gate_in, squared):
    for start in range(0, mixed_in.shape[1], 128):
        lanes = slice(start, start + 128)
        gate = gate_in[:, lanes]
        squared[:, lanes] = mixed_in[:, lanes] * gate * gate


def grad_mixed_body(inner, parts, base, *refs):
    sums = refs[:parts]
    squared, scaled_in, lifted_c, grad_mixed, state_out = refs[parts:]
    alpha, beta = norm_columns(inner, sums)
    for start in range(0, squared.shape[1], 128):
        lanes = slice(start, start + 128)
        low = (alpha * scaled_in[:, lanes] - beta * squared[:, lanes]).astype(BF16)
        grad_mixed[:, lanes] = low
        state_out[0, :, lanes] = dot(lifted_c[:, lanes], low).astype(BF16)


def grad_z_body(inner, parts, base, *refs):
    sums = refs[:parts]
    mixed_in, z_in, grad_in, gain, grad_z = refs[parts:]
    alpha, beta = norm_columns(inner, sums)
    for start in range(0, z_in.shape[1], 128):
        lanes = slice(start, start + 128)
        z = z_in[:, lanes].astype(F32)
        sigma = sigmoid(z)
        mixed = mixed_in[:, lanes]
        scaled = grad_in[:, lanes].astype(F32) * gain[:, lanes]
        grad_gated = alpha * scaled - beta * (mixed * (z * sigma))
        grad_z[:, lanes] = (grad_gated * mixed * (sigma * (1.0 + z * (1.0 - sigma)))).astype(BF16)


def inner_back_body(
    own_half,
    base,
    gram,
    bc,
    step_in,
    cumul_in,
    x_in,
    grad_in,
    mine,
    other,
    rows,
    grad_x,
    q_out,
    r_out,
    bc_out,
    z_sum,
    c_sum,
):
    group = pl.program_id(0)
    length = x_in.shape[0]

    @pl.when(group == 0)
    def _():
        z_sum[...] = jnp.zeros_like(z_sum)
        c_sum[...] = jnp.zeros_like(c_sum)

    cumul = cumul_in[...]
    cumul_columns = columns_of(cumul)
    lifted = jnp.exp(cumul_columns)
    state = pick_state(own_half, mine, other)
    c_rows = bc[1].astype(F32)
    lane = lax.broadcasted_iota(jnp.int32, (length, 128), 1)
    q_columns = jnp.zeros((length, 128), F32)
    for head in range(x_in.shape[1] // 128):
        lanes = slice(head * 128, head * 128 + 128)
        step = step_in[head : head + 1, :]
        decay = jnp.exp(
            jnp.minimum(cumul_columns[:, head : head + 1] - cumul[head : head + 1, :], 0.0)
        )
        gram_decay = gram[...] * decay
        mixer = (gram_decay * step).astype(BF16)
        x_head, grad_head = x_in[:, lanes], grad_in[:, lanes]
        product = dot_rows(grad_head, x_head)
        z_sum[...] += product * decay * step
        gram_grad = product * gram_decay
        r_out[head : head + 1, :] = jnp.sum(gram_grad, axis=0, keepdims=True)
        handed = lifted[:, head : head + 1] * dot_rows(grad_head, state[:, lanes])
        c_sum[...] += handed
        q = jnp.sum(gram_grad * step + c_rows * handed, axis=1, keepdims=True)
        q_columns = jnp.where(lane == head, q, q_columns)
        grad_x[:, lanes] = dot_columns(mixer, grad_head) + rows[1:2, lanes] * grad_head.astype(F32)
    q_out[...] = q_columns.T[:GROUP, :]

    @pl.when(group == pl.num_programs(0) - 1)
    def _():
        summed = jnp.where(triangle(length, False), z_sum[...], 0.0)
        bc_out[0] = dot_split(summed.T, bc[1])
        bc_out[1] = c_sum[...] + dot_split(summed, bc[0])


def block_weights(step, cumul):
    return columns_of(jnp.exp(cumul[:, cumul.shape[1] - 1 :] - cumul) * step)


def rim_body(
    own_half,
    base,
    bc,
    step_in,
    cumul_in,
    weighted_x,
    partial,
    slope,
    out_mine,
    out_other,
    bc_partial,
    bc_slope,
    rim_out,
    bc_out,
    b_sum,
):
    group, groups = pl.program_id(0), pl.num_programs(0)
    width = weighted_x.shape[1]

    @pl.when(group == 0)
    def _():
        b_sum[...] = jnp.zeros_like(b_sum)

    out_low = pick_state(own_half, out_mine, out_other)
    b_sum[...] += dot_rows(weighted_x[...], out_low)
    weights = block_weights(step_in[...], cumul_in[...])[0:8, :]
    returned = dot(bc[0][0:16, :], out_low)[0:8, :]
    for head in range(width // 128):
        lanes = slice(head * 128, head * 128 + 128)
        weight = weights[:, head : head + 1]
        rows = (partial[:, lanes] + weight * returned[:, lanes]) * slope[:, lanes]
        place = pl.multiple_of(lax.rem(group + first_group(base), groups) * width + head * 128, 128)
        rim_out[:, pl.ds(place, 128)] = rows[0:3, :]

    @pl.when(group == groups - 1)
    def _():
        bc_out[0] = (b_sum[...] + bc_partial[0]) * bc_slope[0]
        bc_out[1] = bc_partial[1] * bc_slope[1]
        for j in range(2):
            start = rim_out.shape[1] - 256 + 128 * j
            rim_out[:, start : start + 128] = bc_out[j, 0:3, :]


def grad_dt_body(
    base,
    bc,
    rate,
    dt_slope,
    step_in,
    cumul_in,
    q_in,
    r_in,
    x_in,
    state_in,
    out_in,
    grad_dt,
    selector,
    products,
):
    length, width = x_in.shape

    @pl.when(pl.program_id(0) == 0)
    def _():
        row = lax.broadcasted_iota(jnp.int32, (width, 128), 0)
        lane = lax.broadcasted_iota(jnp.int32, (width, 128), 1)
        selector[...] = (row // 128 == lane).astype(BF16)

    cumul, step = cumul_in[...], step_in[...]
    state, out_low = state_in[0], out_in[0]
    returned = dot(bc[0], out_low)
    for start in range(0, width, 128):
        lanes = slice(start, start + 128)
        products[:, lanes] = (x_in[:, lanes].astype(F32) * returned[:, lanes]).astype(BF16)
    inner_b = dot(products[...], selector[...]).T[:GROUP, :]
    w = jnp.exp(cumul[:, length - 1 :] - cumul) * inner_b
    dots = dot(jnp.ones((16, length), BF16), state * out_low)[:GROUP, :]
    row = lax.broadcasted_iota(jnp.int32, (GROUP, width), 0)
    lane = lax.broadcasted_iota(jnp.int32, (GROUP, width), 1)
    dots = jnp.sum(jnp.where(lane // 128 == row, dots, 0.0), axis=1, keepdims=True)
    q, r = q_in[...], r_in[...]
    inside = jnp.sum(step * w, axis=1, keepdims=True)
    end = inside + jnp.exp(cumul[:, length - 1 :]) * dots
    last = lax.broadcasted_iota(jnp.int32, (GROUP, length), 1) == length - 1
    grad_cumul = q - step * (r + w) + jnp.where(last, end, 0.0)
    grad_log = dot_split(grad_cumul, triangle(length, False).astype(BF16))
    grad_dt[...] = (r + w + rate[...] * grad_log) * dt_slope[...]


def grad_x_body(
    base,
    bc,
    step_in,
    cumul_in,
    partial,
    slope,
    taps,
    halo,
    out_in,
    grad_x,
    ext,
):
    length, width = partial.shape
    weights = block_weights(step_in[...], cumul_in[...])
    returned = dot(bc[0], out_in[0])
    for head in range(width // 128):
        lanes = slice(head * 128, head * 128 + 128)
        weight = weights[:, head : head + 1]
        ext[0:length, :] = (partial[:, lanes] + weight * returned[:, lanes]) * slope[:, lanes]
        ext[length : length + 3, :] = halo[:, lanes]
        total = taps[0:1, lanes] * ext[3 : 3 + length, :]
        for k in range(1, 4):
            total = total + taps[k : k + 1, lanes] * ext[3 - k : 3 - k + length, :]
        grad_x[:, lanes] = total.astype(BF16)


def bc_back_body(place, grad_pre, halo, taps, kept, sent, ext, total):
    length, half = grad_pre.shape[1], kept.shape[1]
    for j in range(2):
        ext[0:length, :] = grad_pre[j]
        ext[length : length + 3, :] = halo[:, 128 * j : 128 * j + 128]
        summed = taps[j, 0:1, :] * ext[3 : 3 + length, :]
        for k in range(1, 4):
            summed = summed + taps[j, k : k + 1, :] * ext[3 - k : 3 - k + length, :]
        total[...] = summed
        kept[j] = total[pl.ds(pl.multiple_of(place_bit(place, 3) * half, half), half), :]
        sent[j] = total[pl.ds(pl.multiple_of((1 - place_bit(place, 3)) * half, half), half), :]


def bc_half_body(place, mine, taken, kept, sent, total):
    half = kept.shape[1]
    for j in range(2):
        total[...] = mine[j] + taken[j]
        kept[j] = total[pl.ds(pl.multiple_of(place_bit(place, 4) * half, half), half), :]
        sent[j] = total[pl.ds(pl.multiple_of((1 - place_bit(place, 4)) * half, half), half), :]


def bc_last_body(_, mine, taken, out):
    out[...] = (mine[...] + taken[...]).astype(BF16)


def conv_back(extended, weights):
    length = extended.shape[-2] - 3
    summed = weights[..., 0, :][..., None, :] * extended[..., 3 : 3 + length, :]
    for k in range(1, 4):
        summed = (
            summed
            + weights[..., k, :][..., None, :] * extended[..., 3 - k : 3 - k + length, :]
        )
    return summed


def shards(
    x_input,
    z_input,
    bc_input,
    dt_raw,
    dt_bias,
    a_log,
    d_skip,
    conv_x,
    convolution_bc_taps,
    rescale_factor,
    grad_out,
):
    length, channels = x_input.shape
    heads = dt_raw.shape[0]
    groups = heads // GROUP
    width = GROUP * 128
    count, parts = lax.axis_size("seq"), lax.axis_size("head")
    inner = channels * parts
    own = lax.axis_index("seq")
    split = count == 8 and groups == 4
    own_half = groups // 2 if split else groups
    bit = lambda value, place: lax.shift_right_logical(value, place) & 1
    along_head = lax.axis_index("head")
    base = bit(own, 0) * own_half if split else own * 0
    for place, value in enumerate(
        (bit(own, 2), bit(own, 1), bit(own, 0), bit(along_head, 1), bit(along_head, 0))
    ):
        base = base | lax.shift_left(value, 8 + place)
    base = base.astype(jnp.int32)[None]

    whole = lambda *shape: (shape, lambda g, b: (0,) * len(shape))
    turn = lambda g, b, off=0: lax.rem(g + off + first_group(b), groups)
    wide_at = lambda off: ((length, width), lambda g, b: (0, turn(g, b, off)))
    rows_at = lambda off: ((GROUP, length), lambda g, b: (turn(g, b, off), 0))
    lanes_at = lambda n, off: ((n, width), lambda g, b: (0, turn(g, b, off)))
    wide, rows8, lanes_of = wide_at(0), rows_at(0), lambda n: lanes_at(n, 0)
    slot = ((1, length, width), lambda g, b: (g, 0, 0))
    mine_slot = ((1, length, width), lambda g, b: (jnp.minimum(g, own_half - 1), 0, 0))
    other_slot = ((1, length, width), lambda g, b: (jnp.maximum(g - own_half, 0), 0, 0))
    full = lambda array: (array,) + whole(*array.shape)
    grid = (groups,)
    halves = [own_half, 0] if split else [0]
    half_grid = (own_half,)

    gain = rescale_factor[None, :]
    f32 = lambda *shape: (shape, F32)
    low = lambda *shape: (shape, BF16)

    step, cumul, rate, dt_slope, rows, rim = call(
        steps_body,
        [
            f32(heads, length) + whole(heads, length),
            f32(heads, length) + whole(heads, length),
            f32(heads, length) + whole(heads, length),
            f32(heads, length) + whole(heads, length),
            f32(2, channels) + whole(2, channels),
            low(3, channels + 256) + whole(3, channels + 256),
        ],
        [
            full(in_hbm(dt_raw)),
            full(in_hbm(dt_bias[None, :])),
            full(in_hbm(a_log[None, :])),
            full(in_hbm(d_skip[None, :])),
            (in_hbm(x_input), (16, channels), lambda g, b: (length // 16 - 1, 0)),
            (in_hbm(bc_input), (2, 16, 128), lambda g, b: (0, length // 16 - 1, 0)),
        ],
        base=base,
        grid=(1,),
    )
    rim = lax.ppermute(rim, "seq", [(i - 1, i) for i in range(1, count)])
    if split:
        swap = lambda block, bit: lax.ppermute(
            block, "seq", [(i, i ^ bit) for i in range(count)]
        )
        total = rows[0:1]
        total_core = swap(total, 1)
        chip_total = total + total_core
        total_across = swap(chip_total, 2)
        table = f32(16, channels) + whole(16, channels)
        ahead, behind = call(
            weights_body,
            [table, table],
            [full(rows), full(total_core), full(total_across)],
            base=base,
            grid=(1,),
        )

    def passed(locals_, reverse, beside):
        if split:
            local_sent, local = locals_
            weights = behind if reverse else ahead
            return scan_blocks(base, groups, weights, local, local_sent, reverse, beside)
        (local,) = locals_
        for work in beside:
            work(local)
        return gather_blocks(rows[0:1], local, reverse)

    carry, local = [], []
    for off in halves:
        first = off == halves[0]
        ins = [
            (in_hbm(x_input),) + wide_at(off),
            (rim,) + lanes_at(3, off),
            (in_hbm(conv_x),) + lanes_at(4, off),
            (step,) + rows_at(off),
            (cumul,) + rows_at(off),
        ]
        outs = [
            low(length, channels) + wide_at(off),
            f32(length, channels) + wide_at(off),
            low(own_half, length, width) + slot,
        ]
        scratch = [pltpu.VMEM((length + 8, 128), F32)]
        if first:
            ins += [
                full(in_hbm(bc_input)),
                (rim, (3, 256), lambda g, b: (0, channels // 256)),
                full(in_hbm(convolution_bc_taps)),
            ]
            outs += [
                low(2, length, 128) + whole(2, length, 128),
                f32(2, length, 128) + whole(2, length, 128),
                f32(length, length) + whole(length, length),
                f32(128, length) + whole(128, length),
            ]
            scratch += [pltpu.VMEM((length + 8, 128), F32)]
        else:
            ins += [full(b_turned)]
        result = call(
            functools.partial(prepare_body, first),
            outs,
            ins,
            base=base,
            grid=half_grid,
            scratch=scratch,
            carry=carry,
            flops=2 * length * 128 * channels,
        )
        if first:
            bc, bc_slope, gram, b_turned = result[3:]
        carry = result[:2]
        local.append(result[2])
    x_low, slope = carry
    done = {}

    def mix_inside(ready):
        done["mixed"], token = call(
            inner_body,
            [f32(length, channels) + wide],
            [
                full(gram),
                (step,) + rows8,
                (cumul,) + rows8,
                (x_low,) + wide,
                (rows,) + lanes_of(2),
            ],
            base=base,
            grid=grid,
            after=[ready],
            token=True,
            flops=2 * length * 128 * channels,
        )
        return token

    def gates(ready):
        done["gate"], done["scaled"], done["weighted_x"], done["lifted_c"], token = call(
            gate_body,
            [
                f32(length, channels) + wide,
                f32(length, channels) + wide,
                low(length, channels) + wide,
                low(length, channels) + wide,
            ],
            [
                (z_input,) + wide,
                (grad_out,) + wide,
                (gain,) + lanes_of(1),
                full(bc),
                (step,) + rows8,
                (cumul,) + rows8,
                (x_low,) + wide,
            ],
            base=base,
            grid=grid,
            scratch=[pltpu.VMEM((128, length), F32)],
            after=[ready],
            token=True,
        )
        return token

    state_mine, state_other = passed(local, False, (mix_inside, gates))
    gate, scaled = done["gate"], done["scaled"]
    c_spec = ((1, length, 128), lambda g, b: (1, 0, 0))
    mixed, sums = done["mixed"], jnp.zeros((8, length), F32)
    for off, state in zip(reversed(halves), (state_mine, state_other)):
        mixed, sums = call(
            mix_body,
            [f32(length, channels) + wide_at(off), f32(8, length) + whole(8, length)],
            [
                (mixed,) + wide_at(off),
                (bc,) + c_spec,
                (cumul,) + rows_at(off),
                (state,) + slot,
                (gate,) + wide_at(off),
                (scaled,) + wide_at(off),
                full(sums),
            ],
            base=base,
            grid=half_grid,
            scratch=[pltpu.VMEM((length, 128), F32), pltpu.VMEM((length, 128), F32)],
            place=0,
            flops=2 * length * 128 * channels,
        )
    turn_head = lambda block, bit: lax.ppermute(
        block, "head", [(i, i ^ bit) for i in range(parts)]
    )
    if parts == 4:
        sums = sums + turn_head(sums, 1)
        all_sums = [sums, turn_head(sums, 2)]
    else:
        all_sums = [lax.psum(sums, "head")]
    (squared,) = call(
        square_body,
        [f32(length, channels) + wide],
        [(mixed,) + wide, (gate,) + wide],
        base=base,
        grid=grid,
    )
    carry, local_back = [], []
    for off in halves:
        grad_mixed, state = call(
            functools.partial(grad_mixed_body, inner, len(all_sums)),
            [low(length, channels) + wide_at(off), low(own_half, length, width) + slot],
            [full(part) for part in all_sums]
            + [
                (squared,) + wide_at(off),
                (scaled,) + wide_at(off),
                (done["lifted_c"],) + wide_at(off),
            ],
            base=base,
            grid=half_grid,
            carry=carry,
            flops=2 * length * 128 * channels,
        )
        carry = [grad_mixed]
        local_back.append(state)

    def back_inside(ready):
        done["back"] = call(
            functools.partial(inner_back_body, own_half),
            [
                f32(length, channels) + wide,
                f32(heads, length) + rows8,
                f32(heads, length) + rows8,
                f32(2, length, 128) + whole(2, length, 128),
            ],
            [
                full(gram),
                full(bc),
                (step,) + rows8,
                (cumul,) + rows8,
                (x_low,) + wide,
                (grad_mixed,) + wide,
                (state_mine,) + mine_slot,
                (state_other,) + other_slot,
                (rows,) + lanes_of(2),
            ],
            base=base,
            grid=grid,
            scratch=[pltpu.VMEM((length, length), F32), pltpu.VMEM((length, 128), F32)],
            after=[ready],
            flops=6 * length * 128 * channels,
        )
        return done["back"][1]

    def back_gates(ready):
        done["grad_z"], token = call(
            functools.partial(grad_z_body, inner, len(all_sums)),
            [low(length, channels) + wide],
            [full(part) for part in all_sums]
            + [
                (mixed,) + wide,
                (z_input,) + wide,
                (grad_out,) + wide,
                (gain,) + lanes_of(1),
            ],
            base=base,
            grid=grid,
            after=[ready],
            token=True,
        )
        return token

    out_mine, out_other = passed(local_back, True, (back_inside, back_gates))
    partial, q_rows, r_rows, bc_partial = done["back"]
    first_rows = ((8, width), lambda g, b: (0, turn(g, b)))
    outs_in = [(out_mine,) + mine_slot, (out_other,) + other_slot]
    quarters = list(zip(reversed(halves), (state_mine, state_other), (out_mine, out_other)))
    carried, dt_tokens = {"dt": [], "x": []}, []

    def make_grad_dt(off, state, out, after):
        grad_dt, token = call(
            grad_dt_body,
            [f32(heads, length) + rows_at(off)],
            [
                full(bc),
                (rate,) + rows_at(off),
                (dt_slope,) + rows_at(off),
                (step,) + rows_at(off),
                (cumul,) + rows_at(off),
                (q_rows,) + rows_at(off),
                (r_rows,) + rows_at(off),
                (x_low,) + wide_at(off),
                (state,) + slot,
                (out,) + slot,
            ],
            base=base,
            grid=half_grid,
            scratch=[pltpu.VMEM((width, 128), BF16), pltpu.VMEM((length, width), BF16)],
            carry=carried["dt"],
            after=after,
            token=True,
            flops=4 * length * 128 * channels,
        )
        carried["dt"] = [grad_dt]
        return token

    def make_grad_x(off, out, after):
        grad_x, token = call(
            grad_x_body,
            [low(length, channels) + wide_at(off)],
            [
                full(bc),
                (step,) + rows_at(off),
                (cumul,) + rows_at(off),
                (partial,) + wide_at(off),
                (slope,) + wide_at(off),
                (conv_x,) + lanes_at(4, off),
                (rim_back,) + lanes_at(3, off),
                (out,) + slot,
            ],
            base=base,
            grid=half_grid,
            scratch=[pltpu.VMEM((length + 8, 128), F32)],
            carry=carried["x"],
            after=after,
            token=True,
            flops=2 * length * 128 * channels,
        )
        carried["x"] = [grad_x]
        return token

    for off, state, out in quarters[:-1]:
        dt_tokens.append(make_grad_dt(off, state, out, []))
    rim_back, grad_bc_pre = call(
        functools.partial(rim_body, own_half),
        [
            f32(3, channels + 256) + whole(3, channels + 256),
            f32(2, length, 128) + whole(2, length, 128),
        ],
        [
            full(bc),
            (step,) + rows8,
            (cumul,) + rows8,
            (done["weighted_x"],) + wide,
            (partial,) + first_rows,
            (slope,) + first_rows,
        ]
        + outs_in
        + [full(bc_partial), full(bc_slope)],
        base=base,
        grid=grid,
        after=dt_tokens,
        scratch=[pltpu.VMEM((length, 128), F32)],
        flops=2 * length * 128 * channels,
    )
    rim_back = lax.ppermute(rim_back, "seq", [(i, i - 1) for i in range(1, count)])
    off, state, out = quarters[-1]
    dt_token = make_grad_dt(off, state, out, [grad_bc_pre])
    if parts == 4:
        piece = lambda rows: f32(2, rows, 128) + whole(2, rows, 128)
        kept, sent = call(
            bc_back_body,
            [piece(length // 2), piece(length // 2)],
            [
                full(grad_bc_pre),
                (rim_back, (3, 256), lambda g, b: (0, channels // 256)),
                full(convolution_bc_taps),
            ],
            base=base,
            grid=(1,),
            scratch=[pltpu.VMEM((length + 8, 128), F32), pltpu.VMEM((length, 128), F32)],
            after=[dt_token],
        )
        taken = turn_head(sent, 2)
        x_tokens = [make_grad_x(off, out, [sent]) for off, _, out in quarters[:1]]
        kept, sent = call(
            bc_half_body,
            [piece(length // 4), piece(length // 4)],
            [full(kept), full(taken)],
            base=base,
            grid=(1,),
            scratch=[pltpu.VMEM((length // 2, 128), F32)],
            after=x_tokens,
        )
        taken = turn_head(sent, 1)
        x_tokens = [make_grad_x(off, out, [sent]) for off, _, out in quarters[1:]]
        (grad_bc,) = call(
            bc_last_body,
            [low(2, length // 4, 128) + whole(2, length // 4, 128)],
            [full(kept), full(taken)],
            base=base,
            grid=(1,),
            after=x_tokens,
        )
    else:
        for off, _, out in quarters:
            make_grad_x(off, out, [])
        bc_halo = jnp.moveaxis(rim_back[:, channels:].reshape(3, 2, 128), 1, 0)
        bc_sum = conv_back(jnp.concatenate([grad_bc_pre, bc_halo], axis=1), convolution_bc_taps)
        share = length // parts
        bc_sum = lax.psum(bc_sum, "head")
        grad_bc = lax.dynamic_slice_in_dim(bc_sum, along_head * share, share, 1).astype(BF16)
    return (carried["x"][0], done["grad_z"], grad_bc, carried["dt"][0])


def solution(mesh):
    return jax.shard_map(
        shards,
        mesh=mesh,
        in_specs=(
            P("seq", "head"),
            P("seq", "head"),
            P(None, "seq", None),
            P("head", "seq"),
            P("head"),
            P("head"),
            P("head"),
            P(None, "head"),
            P(),
            P("head"),
            P("seq", "head"),
        ),
        out_specs=(
            P("seq", "head"),
            P("seq", "head"),
            P(None, ("seq", "head"), None),
            P("head", "seq"),
        ),
        check_vma=False,
    )
```

```python
import functools

import jax
import jax.numpy as jnp
from jax import lax
from jax.experimental import pallas as pl
from jax.experimental.pallas import tpu as pltpu
from jax.sharding import PartitionSpec as P

EPS = 1e-05
GROUP = 8
F32 = jnp.float32
BF16 = jnp.bfloat16
VMEM_BYTES = 16 * 2**20


def sigmoid(value):
    return 0.5 + 0.5 * jnp.tanh(0.5 * value)


def dot(a, b):
    return jnp.dot(a, b, preferred_element_type=F32)


def dot_split(a, b):
    high = a.astype(BF16)
    rest = a - high.astype(F32)
    middle = rest.astype(BF16)
    low = (rest - middle.astype(F32)).astype(BF16)
    return dot(high, b) + (dot(middle, b) + dot(low, b))


def dot_rows(a, b):
    return lax.dot_general(a, b, (((1,), (1,)), ((), ())), preferred_element_type=F32)


def dot_columns(a, b):
    return lax.dot_general(a, b, (((0,), (0,)), ((), ())), preferred_element_type=F32)


def triangle(length, upper):
    first = lax.broadcasted_iota(jnp.int32, (length, length), 0)
    second = lax.broadcasted_iota(jnp.int32, (length, length), 1)
    return first <= second if upper else first >= second


def columns_of(rows):
    return rows.T


def call(body, outs, ins, *, base=None, grid=(), scratch=(), after=(), carry=(), place=None, token=False, flops=0):
    aliases = {1 + len(ins) + len(after) + i: i for i in range(len(carry))}
    for read, written in (place or {}).items():
        aliases[1 + read] = written
    after = list(after) + list(carry)
    in_specs = [pl.BlockSpec(block, index) for _, block, index in ins]
    in_specs += [pl.BlockSpec(memory_space=pl.ANY) for _ in after]
    outs = list(outs)
    if token:
        outs.append(((8, 128), F32, (8, 128), lambda *_: (0, 0)))
    out_specs = [pl.BlockSpec(block, index) for _, _, block, index in outs]
    out_shape = [jax.ShapeDtypeStruct(shape, dtype) for shape, dtype, _, _ in outs]
    arrays = [array for array, _, _ in ins]
    moved = sum(a.size * a.dtype.itemsize for a in arrays + out_shape)
    read = 1 + len(arrays)

    def ordered(*refs):
        results = refs[read + len(after) :]
        if token:
            results[len(outs) - 1][...] = jnp.zeros((8, 128), F32)
            results = results[: len(outs) - 1] + results[len(outs) :]
        body(*refs[:read], *results)

    return pl.pallas_call(
        ordered,
        out_shape=out_shape,
        grid_spec=pltpu.PrefetchScalarGridSpec(
            num_scalar_prefetch=1,
            grid=grid,
            in_specs=in_specs,
            out_specs=out_specs,
            scratch_shapes=list(scratch),
        ),
        input_output_aliases=aliases,
        cost_estimate=pl.CostEstimate(flops=flops, bytes_accessed=moved, transcendentals=0),
        compiler_params=pltpu.CompilerParams(vmem_limit_bytes=VMEM_BYTES),
    )(base, *arrays, *after)


def in_hbm(array):
    return pltpu.with_memory_space_constraint(array, pltpu.HBM)


def column_of(row):
    count = row.shape[1]
    first = lax.broadcasted_iota(jnp.int32, (count, count), 0)
    second = lax.broadcasted_iota(jnp.int32, (count, count), 1)
    return jnp.sum(jnp.where(first == second, row, 0.0), axis=1, keepdims=True)


def steps_body(
    _,
    raw,
    bias,
    log_rate,
    skip,
    x_tail,
    bc_tail,
    step_out,
    cumul_out,
    rate_out,
    slope_out,
    rows_out,
    rim_out,
):
    heads, length = raw.shape
    channels = x_tail.shape[1]
    rim_out[:, 0:channels] = x_tail[...].astype(F32)[13:16, :].astype(BF16)
    for j in range(2):
        start = channels + 128 * j
        rim_out[:, start : start + 128] = bc_tail[j].astype(F32)[13:16, :].astype(BF16)
    shifted = raw[...] + column_of(bias[...])
    step = jnp.maximum(shifted, 0.0) + jnp.log1p(jnp.exp(-jnp.abs(shifted)))
    rate = jnp.broadcast_to(-jnp.exp(column_of(log_rate[...])), step.shape)
    cumul = dot_split(rate * step, triangle(length, True).astype(BF16))
    step_out[...] = step
    cumul_out[...] = cumul
    rate_out[...] = rate
    slope_out[...] = sigmoid(shifted)
    skips = column_of(skip[...])
    for head in range(heads):
        lanes = slice(head * 128, head * 128 + 128)
        rows_out[0:1, lanes] = jnp.broadcast_to(cumul[head : head + 1, length - 1 :], (1, 128))
        rows_out[1:2, lanes] = jnp.broadcast_to(skips[head : head + 1, :], (1, 128))


def pick(test, yes, no):
    return jnp.where(test, yes, no)


def first_group(place):
    return place[0] & 255


def place_bit(place, index):
    return lax.shift_right_logical(place[0], 8 + index) & 1


def weights_body(place, own, core, across, *outs):
    t0, t1 = own[0:1, :], core[...]
    e0, e1, own_chip, ex = jnp.exp(t0), jnp.exp(t1), jnp.exp(t0 + t1), jnp.exp(across[...])
    one = jnp.ones_like(e0)
    zero = jnp.zeros_like(e0)
    bits = [place_bit(place, i) for i in range(3)]
    x_first = bits[2] == 0
    for out, reverse in zip(outs, (False, True)):
        y, x, c = ((1 - bit if reverse else bit) == 1 for bit in bits)
        either = jnp.logical_or(x, y)
        scale = pick(jnp.logical_or(x_first, either), one, ex)
        rows = [pick(c, one, e1), pick(c, e0, one)]
        rows += [rows[0] * scale, rows[1] * scale]
        rows += [
            pick(x_first, pick(x, one, ex), pick(jnp.logical_and(x, y), zero, one)),
            pick(x_first, pick(x, own_chip, one), pick(y, pick(x, one, own_chip), zero)),
        ]
        a = pick(x_first, pick(x, one, zero), pick(y, pick(x, ex, one), zero))
        b = pick(x_first, pick(y, pick(x, ex, one), zero), pick(either, one, zero))
        into, send = pick(c, e1, one), pick(c, one, e0)
        rows += [into * a, into * b, pick(c, one, zero)]
        rows += [send * a, send * b, pick(c, zero, one)]
        for index, row in enumerate(rows):
            out[index : index + 1, :] = row


def combine(base, groups, weights, outs, after=(), slots_of=None, at=0, carry=()):
    arrays, columns = [], []
    for slots in outs:
        for column, terms in slots:
            if column not in columns:
                columns.append(column)
            for _, (array, slot) in terms:
                if not any(array is a and slot == s for a, s in arrays):
                    arrays.append((array, slot))
    place = lambda array, slot: [
        i for i, (a, s) in enumerate(arrays) if a is array and s == slot
    ][0]
    plan = [
        [
            (columns.index(column), [(row, place(*source)) for row, source in terms])
            for column, terms in slots
        ]
        for slots in outs
    ]

    def body(_, *refs):
        rows, values = refs[: len(columns)], refs[len(columns) : len(columns) + len(arrays)]
        results = refs[len(columns) + len(arrays) :]
        width = rows[0].shape[1]
        for result, slots in zip(results, plan):
            for slot, (column, terms) in enumerate(slots):
                for start in range(0, width, 256):
                    lanes = slice(start, start + 256)
                    total = None
                    for row, index in terms:
                        term = rows[column][row : row + 1, lanes] * values[index][
                            0, :, lanes
                        ].astype(F32)
                        total = term if total is None else total + term
                    result[slot, :, lanes] = total.astype(BF16)

    length, width = arrays[0][0].shape[1:]
    ins = [
        (
            weights,
            (weights.shape[0], width),
            lambda g, b, column=column: (0, lax.rem(first_group(b) + column, groups)),
        )
        for column in columns
    ]
    ins += [
        (array, (1, length, width), lambda g, b, slot=slot: (slot, 0, 0))
        for array, slot in arrays
    ]
    results = [
        (
            (slots_of or len(slots), length, width),
            BF16,
            (len(slots), length, width),
            lambda g, b: (at, 0, 0),
        )
        for slots in outs
    ]
    return call(body, results, ins, base=base, grid=(1,), after=after, carry=carry)


def scan_blocks(base, groups, weights, local, local_sent, reverse, beside):
    count = lax.axis_size("seq")
    place = lambda position: count - 1 - position if reverse else position

    def swap(block, bit_of, keep):
        route = [
            (place(i), place(i ^ bit_of(place(i) % 2)))
            for i in range(count)
            if keep(i, place(i) % 2)
        ]
        return lax.ppermute(block, "seq", route)

    def merge(slot, *plans, **places):
        outs = [[(slot, list(zip(rows, sources)))] for rows, sources in plans]
        return combine(base, groups, weights, outs, **places)

    everyone = lambda i, core: True
    across = lambda block: swap(
        block, lambda core: 4 if core else 2, lambda i, core: i < 4 if core else i < 6
    )
    onward = lambda block: swap(
        block,
        lambda core: 2 if core else 4,
        lambda i, core: i not in (2, 3) if core else i < 4,
    )
    taken = swap(local_sent, lambda core: 1, everyone)
    chips, first_taken, sent, second_taken = [], [], [], []
    for slot in range(2):
        both = ((local, slot), (taken, slot))
        chip, chip_sent = merge(slot, ((0, 1), both), ((2, 3), both))
        chips.append(chip)
        first_taken.append(across(chip_sent))
    after = [beside[0](chips[1])]
    for slot in range(2):
        sources = ((chips[slot], 0), (first_taken[slot], 0))
        (block,) = merge(slot, ((4, 5), sources), after=after)
        sent.append(block)
        second_taken.append(onward(block))
        after = []
    after = beside[1](sent[1])
    carry = []
    for slot in range(2):
        sources = ((first_taken[slot], 0), (second_taken[slot], 0))
        mine, handed = merge(
            slot,
            ((6, 7, 8), (*sources, (taken, slot))),
            ((9, 10, 11), (*sources, (local, slot))),
            after=after[slot],
            slots_of=2,
            at=slot,
            carry=carry,
        )
        carry = [mine, handed]
    return mine, swap(handed, lambda core: 1, everyone)


def gather_blocks(totals, local, reverse):
    table = lax.all_gather(totals, "seq", axis=0, tiled=True)
    blocks = lax.all_gather(local[None], "seq", axis=0, tiled=True)
    own = lax.axis_index("seq")
    order = jnp.arange(table.shape[0], dtype=jnp.int32)
    if reverse:
        inside = (order[None, :] > own) & (order[None, :] < order[:, None])
        selected = order > own
    else:
        inside = (order[None, :] > order[:, None]) & (order[None, :] < own)
        selected = order < own
    exponent = jnp.sum(jnp.where(inside[:, :, None], table[None], 0.0), axis=1)
    factor = jnp.where(selected[:, None], jnp.exp(exponent), 0.0)
    factor = factor.reshape(factor.shape[0], local.shape[0], 1, local.shape[2])
    state = jnp.sum(factor * blocks.astype(F32), axis=0).astype(BF16)
    return state, state


def conv_body(base, x_in, taps, x_out, slope_out, ext):
    length, width = x_in.shape
    ext[0:8, :] = jnp.zeros((8, 128), F32)
    for start in range(0, width, 128):
        lanes = slice(start, start + 128)
        ext[8 : 8 + length, :] = x_in[:, lanes].astype(F32)
        pre = taps[0:1, lanes] * ext[5 : 5 + length, :]
        for k in range(1, 4):
            pre = pre + taps[k : k + 1, lanes] * ext[5 + k : 5 + k + length, :]
        sigma = sigmoid(pre)
        x_out[:, lanes] = (pre * sigma).astype(BF16)
        slope_out[:, lanes] = sigma * (1.0 + pre * (1.0 - sigma))


def state_body(first, base, x_low, x_top, x_halo, taps, step_in, cumul_in, *refs):
    length, width = x_low.shape
    if first:
        bc_in, bc_halo, bc_taps, slope_out, x_out, state_out = refs[:6]
        bc_out, bc_slope_out, gram_out, b_turned, ext, bc_ext = refs[6:]

        @pl.when(pl.program_id(0) == 0)
        def _():
            for j in range(2):
                bc_ext[5:8, :] = bc_halo[:, j * 128 : j * 128 + 128].astype(F32)
                bc_ext[8 : 8 + length, :] = bc_in[j].astype(F32)
                pre = bc_taps[j, 0:1, :] * bc_ext[5 : 5 + length, :]
                for k in range(1, 4):
                    pre = pre + bc_taps[j, k : k + 1, :] * bc_ext[5 + k : 5 + k + length, :]
                sigma = sigmoid(pre)
                bc_out[j] = (pre * sigma).astype(BF16)
                bc_slope_out[j] = sigma * (1.0 + pre * (1.0 - sigma))
            b_turned[...] = bc_out[0].astype(F32).T
            gram_out[...] = jnp.where(
                triangle(length, False), dot_rows(bc_out[1], bc_out[0]), 0.0
            )

    else:
        b_turned, slope_out, x_out, state_out, ext = refs

    top = x_top.shape[0]
    ext[5:8, :] = x_halo[...].astype(F32)
    ext[8 : 8 + top, :] = x_top[...].astype(F32)
    tail_step = jnp.exp(cumul_in[:, length - 1 :] - cumul_in[...]) * step_in[...]
    for head in range(width // 128):
        lanes = slice(head * 128, head * 128 + 128)
        pre = taps[0:1, lanes] * ext[5 : 5 + top, lanes]
        for k in range(1, 4):
            pre = pre + taps[k : k + 1, lanes] * ext[5 + k : 5 + k + top, lanes]
        sigma = sigmoid(pre)
        x_rows = (pre * sigma).astype(BF16)
        x_out[:, lanes] = x_rows
        slope_out[:, lanes] = sigma * (1.0 + pre * (1.0 - sigma))
        x_head = jnp.concatenate([x_rows, x_low[top:, lanes]], axis=0)
        weighted = (b_turned[...] * tail_step[head : head + 1, :]).astype(BF16)
        state_out[0, :, lanes] = dot(weighted, x_head).astype(BF16)


def inner_body(base, gram, step_in, cumul_in, x_in, rows, mixed_out):
    cumul = cumul_in[...]
    cumul_columns = columns_of(cumul)
    for head in range(x_in.shape[1] // 128):
        lanes = slice(head * 128, head * 128 + 128)
        row = cumul[head : head + 1, :]
        decay = jnp.exp(jnp.minimum(cumul_columns[:, head : head + 1] - row, 0.0))
        mixer = (gram[...] * decay * step_in[head : head + 1, :]).astype(BF16)
        x_head = x_in[:, lanes]
        mixed_out[:, lanes] = dot(mixer, x_head) + rows[1:2, lanes] * x_head.astype(F32)


def pick_state(own_half, mine, other):
    group = pl.program_id(0)
    return jnp.where(group < own_half, mine[0], other[0])


def gate_body(
    base,
    z_in,
    grad_in,
    gain,
    bc,
    step_in,
    cumul_in,
    x_in,
    gate_out,
    scaled_out,
    weighted_x,
    lifted_out,
    c_turned,
):
    @pl.when(pl.program_id(0) == 0)
    def _():
        c_turned[...] = bc[1].astype(F32).T

    weights = block_weights(step_in[...], cumul_in[...])
    lifted = jnp.exp(cumul_in[...])
    for head in range(z_in.shape[1] // 128):
        lanes = slice(head * 128, head * 128 + 128)
        z = z_in[:, lanes].astype(F32)
        gate = z * sigmoid(z)
        gate_out[:, lanes] = gate
        scaled_out[:, lanes] = grad_in[:, lanes].astype(F32) * gain[:, lanes] * gate
        weight = weights[:, head : head + 1]
        weighted_x[:, lanes] = (weight * x_in[:, lanes].astype(F32)).astype(BF16)
        lifted_out[:, lanes] = (c_turned[...] * lifted[head : head + 1, :]).astype(BF16)


def mix_body(
    base, mixed_in, c_rows, cumul_in, state, gate_in, scaled_in, sums_in, *outs
):
    mixed_out, sums_out, squares, products = outs
    group = pl.program_id(0)

    @pl.when(group == 0)
    def _():
        squares[...] = jnp.zeros_like(squares)
        products[...] = jnp.zeros_like(products)

    carried = dot(c_rows[0], state[0])
    lifted = jnp.exp(columns_of(cumul_in[...]))
    square, product = squares[...], products[...]
    for head in range(mixed_in.shape[1] // 128):
        lanes = slice(head * 128, head * 128 + 128)
        mixed = mixed_in[:, lanes] + lifted[:, head : head + 1] * carried[:, lanes]
        mixed_out[:, lanes] = mixed
        gated = mixed * gate_in[:, lanes]
        square = square + gated * gated
        product = product + mixed * scaled_in[:, lanes]
    squares[...] = square
    products[...] = product

    @pl.when(group == pl.num_programs(0) - 1)
    def _():
        sums_out[...] = sums_in[...]
        sums_out[0:1, :] += jnp.sum(squares[...].T, axis=0, keepdims=True)
        sums_out[1:2, :] += jnp.sum(products[...].T, axis=0, keepdims=True)


def square_body(base, mixed_in, gate_in, squared):
    for start in range(0, mixed_in.shape[1], 128):
        lanes = slice(start, start + 128)
        gate = gate_in[:, lanes]
        squared[:, lanes] = mixed_in[:, lanes] * gate * gate


def norm_scales(inner, sums, alpha, beta):
    @pl.when(pl.program_id(0) == 0)
    def _():
        total = sums[0][...]
        for part in sums[1:]:
            total = total + part[...]
        inv_rms = lax.rsqrt(total[0:1, :] / inner + EPS)
        mean_dot = inv_rms * total[1:2, :] / inner
        alpha[...] = jnp.broadcast_to(inv_rms, alpha.shape).T
        beta[...] = jnp.broadcast_to(inv_rms * inv_rms * mean_dot, beta.shape).T


def grad_mixed_body(inner, parts, base, *refs):
    sums = refs[:parts]
    squared, scaled_in, lifted_c, grad_mixed, state_out, alpha, beta = refs[parts:]
    norm_scales(inner, sums, alpha, beta)
    for start in range(0, squared.shape[1], 128):
        lanes = slice(start, start + 128)
        low = (alpha[...] * scaled_in[:, lanes] - beta[...] * squared[:, lanes]).astype(BF16)
        grad_mixed[:, lanes] = low
        state_out[0, :, lanes] = dot(lifted_c[:, lanes], low).astype(BF16)


def grad_z_body(inner, parts, base, *refs):
    sums = refs[:parts]
    mixed_in, z_in, grad_in, gain, grad_z, alpha, beta = refs[parts:]
    norm_scales(inner, sums, alpha, beta)
    for start in range(0, z_in.shape[1], 128):
        lanes = slice(start, start + 128)
        z = z_in[:, lanes].astype(F32)
        sigma = sigmoid(z)
        mixed = mixed_in[:, lanes]
        scaled = grad_in[:, lanes].astype(F32) * gain[:, lanes]
        grad_gated = alpha[...] * scaled - beta[...] * (mixed * (z * sigma))
        grad_z[:, lanes] = (grad_gated * mixed * (sigma * (1.0 + z * (1.0 - sigma)))).astype(BF16)


def inner_back_body(
    last,
    base,
    gram,
    bc,
    step_in,
    cumul_in,
    x_in,
    grad_in,
    state_in,
    rows,
    sums_in,
    grad_x,
    q_out,
    r_out,
    bc_out,
    z_sum,
    c_sum,
):
    group = pl.program_id(0)
    length = x_in.shape[0]

    @pl.when(group == 0)
    def _():
        z_sum[...] = sums_in[0]
        c_sum[...] = sums_in[1]

    cumul = cumul_in[...]
    cumul_columns = columns_of(cumul)
    lifted = jnp.exp(cumul_columns)
    state = state_in[0]
    c_rows = bc[1].astype(F32)
    lane = lax.broadcasted_iota(jnp.int32, (length, 128), 1)
    q_columns = jnp.zeros((length, 128), F32)
    for head in range(x_in.shape[1] // 128):
        lanes = slice(head * 128, head * 128 + 128)
        step = step_in[head : head + 1, :]
        decay = jnp.exp(
            jnp.minimum(cumul_columns[:, head : head + 1] - cumul[head : head + 1, :], 0.0)
        )
        gram_decay = gram[...] * decay
        mixer = (gram_decay * step).astype(BF16)
        x_head, grad_head = x_in[:, lanes], grad_in[:, lanes]
        product = dot_rows(grad_head, x_head)
        z_sum[...] += product * decay * step
        gram_grad = product * gram_decay
        r_out[head : head + 1, :] = jnp.sum(gram_grad, axis=0, keepdims=True)
        handed = lifted[:, head : head + 1] * dot_rows(grad_head, state[:, lanes])
        c_sum[...] += handed
        q = jnp.sum(gram_grad * step + c_rows * handed, axis=1, keepdims=True)
        q_columns = jnp.where(lane == head, q, q_columns)
        grad_x[:, lanes] = dot_columns(mixer, grad_head) + rows[1:2, lanes] * grad_head.astype(F32)
    q_out[...] = q_columns.T[:GROUP, :]

    @pl.when(group == pl.num_programs(0) - 1)
    def _():
        if last:
            summed = jnp.where(triangle(length, False), z_sum[...], 0.0)
            bc_out[0] = dot_split(summed.T, bc[1])
            bc_out[1] = c_sum[...] + dot_split(summed, bc[0])
        else:
            bc_out[0] = z_sum[...]
            bc_out[1] = c_sum[...]


def block_weights(step, cumul):
    return columns_of(jnp.exp(cumul[:, cumul.shape[1] - 1 :] - cumul) * step)


def rim_body(
    own_half,
    base,
    bc,
    step_in,
    cumul_in,
    weighted_x,
    partial,
    slope,
    out_mine,
    out_other,
    bc_partial,
    bc_slope,
    rim_out,
    bc_out,
    b_sum,
):
    group, groups = pl.program_id(0), pl.num_programs(0)
    width = weighted_x.shape[1]

    @pl.when(group == 0)
    def _():
        b_sum[...] = jnp.zeros_like(b_sum)

    out_low = pick_state(own_half, out_mine, out_other)
    b_sum[...] += dot_rows(weighted_x[...], out_low)
    weights = block_weights(step_in[...], cumul_in[...])[0:8, :]
    returned = dot(bc[0][0:16, :], out_low)[0:8, :]
    for head in range(width // 128):
        lanes = slice(head * 128, head * 128 + 128)
        weight = weights[:, head : head + 1]
        rows = (partial[:, lanes] + weight * returned[:, lanes]) * slope[:, lanes]
        place = pl.multiple_of(lax.rem(group + first_group(base), groups) * width + head * 128, 128)
        rim_out[:, pl.ds(place, 128)] = rows[0:3, :]

    @pl.when(group == groups - 1)
    def _():
        bc_out[0] = (b_sum[...] + bc_partial[0]) * bc_slope[0]
        bc_out[1] = bc_partial[1] * bc_slope[1]
        for j in range(2):
            start = rim_out.shape[1] - 256 + 128 * j
            rim_out[:, start : start + 128] = bc_out[j, 0:3, :]


def grad_dt_body(
    base,
    bc,
    rate,
    dt_slope,
    step_in,
    cumul_in,
    q_in,
    r_in,
    x_in,
    state_in,
    out_in,
    grad_dt,
    selector,
    products,
):
    length, width = x_in.shape

    @pl.when(pl.program_id(0) == 0)
    def _():
        row = lax.broadcasted_iota(jnp.int32, (width, 128), 0)
        lane = lax.broadcasted_iota(jnp.int32, (width, 128), 1)
        selector[...] = (row // 128 == lane).astype(BF16)

    cumul, step = cumul_in[...], step_in[...]
    state, out_low = state_in[0], out_in[0]
    returned = dot(bc[0], out_low)
    for start in range(0, width, 128):
        lanes = slice(start, start + 128)
        products[:, lanes] = (x_in[:, lanes].astype(F32) * returned[:, lanes]).astype(BF16)
    inner_b = dot(products[...], selector[...]).T[:GROUP, :]
    w = jnp.exp(cumul[:, length - 1 :] - cumul) * inner_b
    dots = dot(jnp.ones((16, length), BF16), state * out_low)[:GROUP, :]
    row = lax.broadcasted_iota(jnp.int32, (GROUP, width), 0)
    lane = lax.broadcasted_iota(jnp.int32, (GROUP, width), 1)
    dots = jnp.sum(jnp.where(lane // 128 == row, dots, 0.0), axis=1, keepdims=True)
    q, r = q_in[...], r_in[...]
    inside = jnp.sum(step * w, axis=1, keepdims=True)
    end = inside + jnp.exp(cumul[:, length - 1 :]) * dots
    last = lax.broadcasted_iota(jnp.int32, (GROUP, length), 1) == length - 1
    grad_cumul = q - step * (r + w) + jnp.where(last, end, 0.0)
    grad_log = dot_split(grad_cumul, triangle(length, False).astype(BF16))
    grad_dt[...] = (r + w + rate[...] * grad_log) * dt_slope[...]


def grad_x_body(
    base,
    bc,
    step_in,
    cumul_in,
    partial,
    slope,
    taps,
    halo,
    out_in,
    grad_x,
    ext,
):
    length, width = partial.shape
    weights = block_weights(step_in[...], cumul_in[...])
    returned = dot(bc[0], out_in[0])
    for head in range(width // 128):
        lanes = slice(head * 128, head * 128 + 128)
        weight = weights[:, head : head + 1]
        ext[0:length, :] = (partial[:, lanes] + weight * returned[:, lanes]) * slope[:, lanes]
        ext[length : length + 3, :] = halo[:, lanes]
        total = taps[0:1, lanes] * ext[3 : 3 + length, :]
        for k in range(1, 4):
            total = total + taps[k : k + 1, lanes] * ext[3 - k : 3 - k + length, :]
        grad_x[:, lanes] = total.astype(BF16)


def bc_back_body(place, grad_pre, halo, taps, kept, sent, ext, total):
    length, half = grad_pre.shape[1], kept.shape[1]
    for j in range(2):
        ext[0:length, :] = grad_pre[j]
        ext[length : length + 3, :] = halo[:, 128 * j : 128 * j + 128]
        summed = taps[j, 0:1, :] * ext[3 : 3 + length, :]
        for k in range(1, 4):
            summed = summed + taps[j, k : k + 1, :] * ext[3 - k : 3 - k + length, :]
        total[...] = summed
        kept[j] = total[pl.ds(pl.multiple_of(place_bit(place, 3) * half, half), half), :]
        sent[j] = total[pl.ds(pl.multiple_of((1 - place_bit(place, 3)) * half, half), half), :]


def bc_half_body(place, mine, taken, kept, sent, total):
    half = kept.shape[1]
    for j in range(2):
        total[...] = mine[j] + taken[j]
        kept[j] = total[pl.ds(pl.multiple_of(place_bit(place, 4) * half, half), half), :]
        sent[j] = total[pl.ds(pl.multiple_of((1 - place_bit(place, 4)) * half, half), half), :]


def bc_last_body(_, mine, taken, out):
    out[...] = (mine[...] + taken[...]).astype(BF16)


def conv_back(extended, weights):
    length = extended.shape[-2] - 3
    summed = weights[..., 0, :][..., None, :] * extended[..., 3 : 3 + length, :]
    for k in range(1, 4):
        summed = (
            summed
            + weights[..., k, :][..., None, :] * extended[..., 3 - k : 3 - k + length, :]
        )
    return summed


def shards(
    x_input,
    z_input,
    bc_input,
    dt_raw,
    dt_bias,
    a_log,
    d_skip,
    conv_x,
    convolution_bc_taps,
    rescale_factor,
    grad_out,
):
    length, channels = x_input.shape
    heads = dt_raw.shape[0]
    groups = heads // GROUP
    width = GROUP * 128
    count, parts = lax.axis_size("seq"), lax.axis_size("head")
    inner = channels * parts
    own = lax.axis_index("seq")
    split = count == 8 and groups == 4
    own_half = groups // 2 if split else groups
    bit = lambda value, place: lax.shift_right_logical(value, place) & 1
    along_head = lax.axis_index("head")
    base = bit(own, 0) * own_half if split else own * 0
    for place, value in enumerate(
        (bit(own, 2), bit(own, 1), bit(own, 0), bit(along_head, 1), bit(along_head, 0))
    ):
        base = base | lax.shift_left(value, 8 + place)
    base = base.astype(jnp.int32)[None]

    whole = lambda *shape: (shape, lambda g, b: (0,) * len(shape))
    turn = lambda g, b, off=0: lax.rem(g + off + first_group(b), groups)
    wide_at = lambda off: ((length, width), lambda g, b: (0, turn(g, b, off)))
    rows_at = lambda off: ((GROUP, length), lambda g, b: (turn(g, b, off), 0))
    lanes_at = lambda n, off: ((n, width), lambda g, b: (0, turn(g, b, off)))
    wide, rows8, lanes_of = wide_at(0), rows_at(0), lambda n: lanes_at(n, 0)
    slot = ((1, length, width), lambda g, b: (g, 0, 0))
    mine_slot = ((1, length, width), lambda g, b: (jnp.minimum(g, own_half - 1), 0, 0))
    other_slot = ((1, length, width), lambda g, b: (jnp.maximum(g - own_half, 0), 0, 0))
    full = lambda array: (array,) + whole(*array.shape)
    grid = (groups,)
    halves = [own_half, 0] if split else [0]
    half_grid = (own_half,)

    gain = rescale_factor[None, :]
    f32 = lambda *shape: (shape, F32)
    low = lambda *shape: (shape, BF16)

    step, cumul, rate, dt_slope, rows, rim = call(
        steps_body,
        [
            f32(heads, length) + whole(heads, length),
            f32(heads, length) + whole(heads, length),
            f32(heads, length) + whole(heads, length),
            f32(heads, length) + whole(heads, length),
            f32(2, channels) + whole(2, channels),
            low(3, channels + 256) + whole(3, channels + 256),
        ],
        [
            full(in_hbm(dt_raw)),
            full(in_hbm(dt_bias[None, :])),
            full(in_hbm(a_log[None, :])),
            full(in_hbm(d_skip[None, :])),
            (in_hbm(x_input), (16, channels), lambda g, b: (length // 16 - 1, 0)),
            (in_hbm(bc_input), (2, 16, 128), lambda g, b: (0, length // 16 - 1, 0)),
        ],
        base=base,
        grid=(1,),
    )
    rim_sent = rim
    rim = lax.ppermute(rim, "seq", [(i - 1, i) for i in range(1, count)])
    if split:
        swap = lambda block, bit: lax.ppermute(
            block, "seq", [(i, i ^ bit) for i in range(count)]
        )
        total = rows[0:1]
        total_core = swap(total, 1)
        chip_total = total + total_core
        total_across = swap(chip_total, 2)
        table = f32(16, channels) + whole(16, channels)
        ahead, behind = call(
            weights_body,
            [table, table],
            [full(rows), full(total_core), full(total_across)],
            base=base,
            grid=(1,),
        )

    def passed(locals_, reverse, beside):
        if split:
            local_sent, local = locals_
            weights = behind if reverse else ahead
            return scan_blocks(base, groups, weights, local, local_sent, reverse, beside)
        (local,) = locals_
        for work in beside:
            work(local)
        return gather_blocks(rows[0:1], local, reverse)

    x_low, slope = call(
        conv_body,
        [low(length, channels) + wide, f32(length, channels) + wide],
        [(in_hbm(x_input),) + wide, (in_hbm(conv_x),) + lanes_of(4)],
        base=base,
        grid=grid,
        scratch=[pltpu.VMEM((length + 8, 128), F32)],
        after=[rim_sent],
    )
    local = []
    for off in halves:
        first = off == halves[0]
        top = ((16, width), lambda g, b, off=off: (0, turn(g, b, off)))
        ins = [
            (x_low,) + wide_at(off),
            (in_hbm(x_input),) + top,
            (rim,) + lanes_at(3, off),
            (in_hbm(conv_x),) + lanes_at(4, off),
            (step,) + rows_at(off),
            (cumul,) + rows_at(off),
        ]
        outs = [
            f32(length, channels) + top,
            low(length, channels) + top,
            low(own_half, length, width) + slot,
        ]
        scratch = [pltpu.VMEM((24, width), F32)]
        if first:
            ins += [
                full(in_hbm(bc_input)),
                (rim, (3, 256), lambda g, b: (0, channels // 256)),
                full(in_hbm(convolution_bc_taps)),
            ]
            outs += [
                low(2, length, 128) + whole(2, length, 128),
                f32(2, length, 128) + whole(2, length, 128),
                f32(length, length) + whole(length, length),
                f32(128, length) + whole(128, length),
            ]
            scratch += [pltpu.VMEM((length + 8, 128), F32)]
        else:
            ins += [full(b_turned)]
        result = call(
            functools.partial(state_body, first),
            outs,
            ins,
            base=base,
            grid=half_grid,
            scratch=scratch,
            carry=[slope],
            place={0: 1},
            flops=2 * length * 128 * channels,
        )
        if first:
            bc, bc_slope, gram, b_turned = result[3:]
        slope, x_low = result[:2]
        local.append(result[2])
    done = {}

    def mix_inside(ready):
        done["mixed"], token = call(
            inner_body,
            [f32(length, channels) + wide],
            [
                full(gram),
                (step,) + rows8,
                (cumul,) + rows8,
                (x_low,) + wide,
                (rows,) + lanes_of(2),
            ],
            base=base,
            grid=grid,
            after=[ready],
            token=True,
            flops=2 * length * 128 * channels,
        )
        return token

    def gates(ready):
        done["gate"], done["scaled"], done["weighted_x"], done["lifted_c"], token = call(
            gate_body,
            [
                f32(length, channels) + wide,
                f32(length, channels) + wide,
                low(length, channels) + wide,
                low(length, channels) + wide,
            ],
            [
                (z_input,) + wide,
                (grad_out,) + wide,
                (gain,) + lanes_of(1),
                full(bc),
                (step,) + rows8,
                (cumul,) + rows8,
                (x_low,) + wide,
            ],
            base=base,
            grid=grid,
            scratch=[pltpu.VMEM((128, length), F32)],
            after=[ready],
            token=True,
        )
        return [], [token]

    state_mine, state_other = passed(local, False, (mix_inside, gates))
    gate, scaled = done["gate"], done["scaled"]
    c_spec = ((1, length, 128), lambda g, b: (1, 0, 0))
    mixed, sums = done["mixed"], jnp.zeros((8, length), F32)
    for off, state in zip(reversed(halves), (state_mine, state_other)):
        mixed, sums = call(
            mix_body,
            [f32(length, channels) + wide_at(off), f32(8, length) + whole(8, length)],
            [
                (mixed,) + wide_at(off),
                (bc,) + c_spec,
                (cumul,) + rows_at(off),
                (state,) + slot,
                (gate,) + wide_at(off),
                (scaled,) + wide_at(off),
                full(sums),
            ],
            base=base,
            grid=half_grid,
            scratch=[pltpu.VMEM((length, 128), F32), pltpu.VMEM((length, 128), F32)],
            place={0: 0},
            flops=2 * length * 128 * channels,
        )
    turn_head = lambda block, bit: lax.ppermute(
        block, "head", [(i, i ^ bit) for i in range(parts)]
    )
    if parts == 4:
        sums = sums + turn_head(sums, 1)
        all_sums = [sums, turn_head(sums, 2)]
    else:
        all_sums = [lax.psum(sums, "head")]
    (squared,) = call(
        square_body,
        [f32(length, channels) + wide],
        [(mixed,) + wide, (gate,) + wide],
        base=base,
        grid=grid,
    )
    two_scales = [pltpu.VMEM((length, 128), F32), pltpu.VMEM((length, 128), F32)]
    carry, local_back = [], []
    for off in halves:
        grad_mixed, state = call(
            functools.partial(grad_mixed_body, inner, len(all_sums)),
            [low(length, channels) + wide_at(off), low(own_half, length, width) + slot],
            [full(part) for part in all_sums]
            + [
                (squared,) + wide_at(off),
                (scaled,) + wide_at(off),
                (done["lifted_c"],) + wide_at(off),
            ],
            base=base,
            grid=half_grid,
            scratch=two_scales,
            carry=carry,
            flops=2 * length * 128 * channels,
        )
        carry = [grad_mixed]
        local_back.append(state)

    done["back"] = []
    done["sums"] = jnp.zeros((2, length, 128), F32)

    def back_inside(off, state, ready):
        *done["back"], done["sums"], token = call(
            functools.partial(inner_back_body, off == halves[0]),
            [
                f32(length, channels) + wide_at(off),
                f32(heads, length) + rows_at(off),
                f32(heads, length) + rows_at(off),
                f32(2, length, 128) + whole(2, length, 128),
            ],
            [
                full(gram),
                full(bc),
                (step,) + rows_at(off),
                (cumul,) + rows_at(off),
                (x_low,) + wide_at(off),
                (grad_mixed,) + wide_at(off),
                (state,) + slot,
                (rows,) + lanes_at(2, off),
                full(done["sums"]),
            ],
            base=base,
            grid=half_grid,
            scratch=[pltpu.VMEM((length, length), F32), pltpu.VMEM((length, 128), F32)],
            carry=done["back"],
            after=[ready],
            token=True,
            flops=6 * length * 128 * channels,
        )
        return token

    def back_gates(ready):
        done["grad_z"], token = call(
            functools.partial(grad_z_body, inner, len(all_sums)),
            [low(length, channels) + wide],
            [full(part) for part in all_sums]
            + [
                (mixed,) + wide,
                (z_input,) + wide,
                (grad_out,) + wide,
                (gain,) + lanes_of(1),
            ],
            base=base,
            grid=grid,
            scratch=two_scales,
            after=[ready],
            token=True,
        )
        return token

    def back_first(ready):
        return back_inside(0, state_mine, ready)

    def back_second(ready):
        token = back_inside(own_half, state_other, ready) if split else ready
        return [token], [back_gates(token)]

    out_mine, out_other = passed(local_back, True, (back_first, back_second))
    (partial, q_rows, r_rows), bc_partial = done["back"], done["sums"]
    first_rows = ((8, width), lambda g, b: (0, turn(g, b)))
    outs_in = [(out_mine,) + mine_slot, (out_other,) + other_slot]
    quarters = list(zip(reversed(halves), (state_mine, state_other), (out_mine, out_other)))
    carried, dt_tokens = {"dt": [], "x": []}, []

    def make_grad_dt(off, state, out, after):
        grad_dt, token = call(
            grad_dt_body,
            [f32(heads, length) + rows_at(off)],
            [
                full(bc),
                (rate,) + rows_at(off),
                (dt_slope,) + rows_at(off),
                (step,) + rows_at(off),
                (cumul,) + rows_at(off),
                (q_rows,) + rows_at(off),
                (r_rows,) + rows_at(off),
                (x_low,) + wide_at(off),
                (state,) + slot,
                (out,) + slot,
            ],
            base=base,
            grid=half_grid,
            scratch=[pltpu.VMEM((width, 128), BF16), pltpu.VMEM((length, width), BF16)],
            carry=carried["dt"],
            after=after,
            token=True,
            flops=4 * length * 128 * channels,
        )
        carried["dt"] = [grad_dt]
        return token

    def make_grad_x(off, out, after):
        grad_x, token = call(
            grad_x_body,
            [low(length, channels) + wide_at(off)],
            [
                full(bc),
                (step,) + rows_at(off),
                (cumul,) + rows_at(off),
                (partial,) + wide_at(off),
                (slope,) + wide_at(off),
                (conv_x,) + lanes_at(4, off),
                (rim_back,) + lanes_at(3, off),
                (out,) + slot,
            ],
            base=base,
            grid=half_grid,
            scratch=[pltpu.VMEM((length + 8, 128), F32)],
            carry=carried["x"],
            after=after,
            token=True,
            flops=2 * length * 128 * channels,
        )
        carried["x"] = [grad_x]
        return token

    for off, state, out in quarters[:-1]:
        dt_tokens.append(make_grad_dt(off, state, out, []))
    rim_back, grad_bc_pre = call(
        functools.partial(rim_body, own_half),
        [
            f32(3, channels + 256) + whole(3, channels + 256),
            f32(2, length, 128) + whole(2, length, 128),
        ],
        [
            full(bc),
            (step,) + rows8,
            (cumul,) + rows8,
            (done["weighted_x"],) + wide,
            (partial,) + first_rows,
            (slope,) + first_rows,
        ]
        + outs_in
        + [full(bc_partial), full(bc_slope)],
        base=base,
        grid=grid,
        after=dt_tokens,
        scratch=[pltpu.VMEM((length, 128), F32)],
        flops=2 * length * 128 * channels,
    )
    rim_back = lax.ppermute(rim_back, "seq", [(i, i - 1) for i in range(1, count)])
    off, state, out = quarters[-1]
    dt_token = make_grad_dt(off, state, out, [grad_bc_pre])
    if parts == 4:
        piece = lambda rows: f32(2, rows, 128) + whole(2, rows, 128)
        kept, sent = call(
            bc_back_body,
            [piece(length // 2), piece(length // 2)],
            [
                full(grad_bc_pre),
                (rim_back, (3, 256), lambda g, b: (0, channels // 256)),
                full(convolution_bc_taps),
            ],
            base=base,
            grid=(1,),
            scratch=[pltpu.VMEM((length + 8, 128), F32), pltpu.VMEM((length, 128), F32)],
            after=[dt_token],
        )
        taken = turn_head(sent, 2)
        x_tokens = [make_grad_x(off, out, [sent]) for off, _, out in quarters[:1]]
        kept, sent = call(
            bc_half_body,
            [piece(length // 4), piece(length // 4)],
            [full(kept), full(taken)],
            base=base,
            grid=(1,),
            scratch=[pltpu.VMEM((length // 2, 128), F32)],
            after=x_tokens,
        )
        taken = turn_head(sent, 1)
        x_tokens = [make_grad_x(off, out, [sent]) for off, _, out in quarters[1:]]
        (grad_bc,) = call(
            bc_last_body,
            [low(2, length // 4, 128) + whole(2, length // 4, 128)],
            [full(kept), full(taken)],
            base=base,
            grid=(1,),
            after=x_tokens,
        )
    else:
        for off, _, out in quarters:
            make_grad_x(off, out, [])
        bc_halo = jnp.moveaxis(rim_back[:, channels:].reshape(3, 2, 128), 1, 0)
        bc_sum = conv_back(jnp.concatenate([grad_bc_pre, bc_halo], axis=1), convolution_bc_taps)
        share = length // parts
        bc_sum = lax.psum(bc_sum, "head")
        grad_bc = lax.dynamic_slice_in_dim(bc_sum, along_head * share, share, 1).astype(BF16)
    return (carried["x"][0], done["grad_z"], grad_bc, carried["dt"][0])


def solution(mesh):
    return jax.shard_map(
        shards,
        mesh=mesh,
        in_specs=(
            P("seq", "head"),
            P("seq", "head"),
            P(None, "seq", None),
            P("head", "seq"),
            P("head"),
            P("head"),
            P("head"),
            P(None, "head"),
            P(),
            P("head"),
            P("seq", "head"),
        ),
        out_specs=(
            P("seq", "head"),
            P("seq", "head"),
            P(None, ("seq", "head"), None),
            P("head", "seq"),
        ),
        check_vma=False,
    )
```

```python
import functools

import jax
import jax.numpy as jnp
from jax import lax
from jax.experimental import pallas as pl
from jax.experimental.pallas import tpu as pltpu
from jax.sharding import PartitionSpec as P

EPS = 1e-05
GROUP = 8
F32 = jnp.float32
BF16 = jnp.bfloat16
VMEM_BYTES = 16 * 2**20


def sigmoid(value):
    return 0.5 + 0.5 * jnp.tanh(0.5 * value)


def dot(a, b):
    return jnp.dot(a, b, preferred_element_type=F32)


def dot_split(a, b):
    high = a.astype(BF16)
    rest = a - high.astype(F32)
    middle = rest.astype(BF16)
    low = (rest - middle.astype(F32)).astype(BF16)
    return dot(high, b) + (dot(middle, b) + dot(low, b))


def dot_rows(a, b):
    return lax.dot_general(a, b, (((1,), (1,)), ((), ())), preferred_element_type=F32)


def dot_columns(a, b):
    return lax.dot_general(a, b, (((0,), (0,)), ((), ())), preferred_element_type=F32)


def triangle(length, upper):
    first = lax.broadcasted_iota(jnp.int32, (length, length), 0)
    second = lax.broadcasted_iota(jnp.int32, (length, length), 1)
    return first <= second if upper else first >= second


def columns_of(rows):
    return rows.T


class Groups:
    def __init__(self, kind, block, off, groups):
        self.kind, self.block, self.off, self.groups = kind, block, off, groups

    def turn(self, group, base):
        return lax.rem(group + self.off + first_group(base), self.groups)

    def spec(self, shape):
        if self.kind == "wide":
            return pl.BlockSpec(self.block, lambda g, b: (0, self.turn(g, b)))
        if self.kind == "heads":
            return pl.BlockSpec(self.block, lambda g, b: (self.turn(g, b), 0))
        return pl.BlockSpec(self.block, lambda g, b: (g, 0, 0))

    def whole(self, shape, count):
        if self.kind == "slots":
            return pl.BlockSpec((count, *self.block[1:]), lambda g, b: (0, 0, 0))
        place = lambda b: self.turn(0, b) // count
        if count == self.groups:
            place = lambda b: 0
        if self.kind == "wide":
            block = (self.block[0], count * self.block[1])
            return pl.BlockSpec(block, lambda g, b: (0, place(b)))
        block = (count * self.block[0], self.block[1])
        return pl.BlockSpec(block, lambda g, b: (place(b), 0))

    def view(self, ref, group, count, base):
        if self.kind == "slots":
            return ref.at[pl.ds(group, 1)]
        if count == self.groups:
            group = self.turn(group, base)
        if self.kind == "wide":
            size = self.block[1]
            return ref.at[:, pl.ds(pl.multiple_of(group * size, size), size)]
        size = self.block[0]
        return ref.at[pl.ds(pl.multiple_of(group * size, size), size)]


def call(
    body,
    outs,
    ins,
    *,
    base,
    grid=1,
    loop=1,
    scratch=(),
    after=(),
    carry=(),
    place=None,
    token=False,
    flops=0,
):
    aliases = {1 + len(ins) + len(after) + i: i for i in range(len(carry))}
    for read, written in (place or {}).items():
        aliases[1 + read] = written
    after = list(after) + list(carry)
    outs = list(outs)
    if token:
        outs.append(((8, 128), F32, ((8, 128), lambda *_: (0, 0))))

    def spec(shape, block):
        if not isinstance(block, Groups):
            return pl.BlockSpec(*block)
        return block.whole(shape, loop) if grid == 1 else block.spec(shape)

    in_specs = [spec(array.shape, block) for array, block in ins]
    in_specs += [pl.BlockSpec(memory_space=pl.ANY) for _ in after]
    out_specs = [spec(shape, block) for shape, _, block in outs]
    out_shape = [jax.ShapeDtypeStruct(shape, dtype) for shape, dtype, _ in outs]
    arrays = [array for array, _ in ins]
    moved = sum(a.size * a.dtype.itemsize for a in arrays + out_shape)
    blocks = [block for _, block in ins] + [block for _, _, block in outs]

    def ordered(where, *refs):
        taken, rest = refs[: len(ins)], refs[len(ins) + len(after) :]
        results, extra = rest[: len(outs)], rest[len(outs) :]
        if token:
            results[-1][...] = jnp.zeros((8, 128), F32)

        def step(group, _):
            views = [
                block.view(ref, group, loop, where) if isinstance(block, Groups) else ref
                for ref, block in zip(taken + results, blocks)
            ]
            if token:
                views = views[:-1]
            body((group, loop), where, *views, *extra)
            return 0

        if grid > 1:
            views = taken + (results[:-1] if token else results)
            body((pl.program_id(0), grid), where, *views, *extra)
        elif loop > 1:
            lax.fori_loop(0, loop, step, 0)
        else:
            step(0, 0)

    return pl.pallas_call(
        ordered,
        out_shape=out_shape,
        grid_spec=pltpu.PrefetchScalarGridSpec(
            num_scalar_prefetch=1,
            grid=(grid,),
            in_specs=in_specs,
            out_specs=out_specs,
            scratch_shapes=list(scratch),
        ),
        input_output_aliases=aliases,
        cost_estimate=pl.CostEstimate(flops=flops, bytes_accessed=moved, transcendentals=0),
        compiler_params=pltpu.CompilerParams(vmem_limit_bytes=VMEM_BYTES),
    )(base, *arrays, *after)


def in_hbm(array):
    return pltpu.with_memory_space_constraint(array, pltpu.HBM)


def column_of(row):
    count = row.shape[1]
    first = lax.broadcasted_iota(jnp.int32, (count, count), 0)
    second = lax.broadcasted_iota(jnp.int32, (count, count), 1)
    return jnp.sum(jnp.where(first == second, row, 0.0), axis=1, keepdims=True)


def steps_body(
    at,
    base,
    raw,
    bias,
    log_rate,
    skip,
    x_tail,
    bc_tail,
    step_out,
    cumul_out,
    rate_out,
    slope_out,
    rows_out,
    rim_out,
):
    heads, length = raw.shape
    channels = x_tail.shape[1]
    rim_out[:, 0:channels] = x_tail[...].astype(F32)[13:16, :].astype(BF16)
    for j in range(2):
        start = channels + 128 * j
        rim_out[:, start : start + 128] = bc_tail[j].astype(F32)[13:16, :].astype(BF16)
    shifted = raw[...] + column_of(bias[...])
    step = jnp.maximum(shifted, 0.0) + jnp.log1p(jnp.exp(-jnp.abs(shifted)))
    rate = jnp.broadcast_to(-jnp.exp(column_of(log_rate[...])), step.shape)
    cumul = dot_split(rate * step, triangle(length, True).astype(BF16))
    step_out[...] = step
    cumul_out[...] = cumul
    rate_out[...] = rate
    slope_out[...] = sigmoid(shifted)
    skips = column_of(skip[...])
    for head in range(heads):
        lanes = slice(head * 128, head * 128 + 128)
        rows_out[0:1, lanes] = jnp.broadcast_to(cumul[head : head + 1, length - 1 :], (1, 128))
        rows_out[1:2, lanes] = jnp.broadcast_to(skips[head : head + 1, :], (1, 128))


def pick(test, yes, no):
    return jnp.where(test, yes, no)


def first_group(place):
    return place[0] & 255


def place_bit(place, index):
    return lax.shift_right_logical(place[0], 8 + index) & 1


def weights_body(at, place, own, core, across, *outs):
    t0, t1 = own[0:1, :], core[...]
    e0, e1, own_chip, ex = jnp.exp(t0), jnp.exp(t1), jnp.exp(t0 + t1), jnp.exp(across[...])
    one = jnp.ones_like(e0)
    zero = jnp.zeros_like(e0)
    bits = [place_bit(place, i) for i in range(3)]
    x_first = bits[2] == 0
    for out, reverse in zip(outs, (False, True)):
        y, x, c = ((1 - bit if reverse else bit) == 1 for bit in bits)
        either = jnp.logical_or(x, y)
        scale = pick(jnp.logical_or(x_first, either), one, ex)
        rows = [pick(c, one, e1), pick(c, e0, one)]
        rows += [rows[0] * scale, rows[1] * scale]
        rows += [
            pick(x_first, pick(x, one, ex), pick(jnp.logical_and(x, y), zero, one)),
            pick(x_first, pick(x, own_chip, one), pick(y, pick(x, one, own_chip), zero)),
        ]
        a = pick(x_first, pick(x, one, zero), pick(y, pick(x, ex, one), zero))
        b = pick(x_first, pick(y, pick(x, ex, one), zero), pick(either, one, zero))
        into, send = pick(c, e1, one), pick(c, one, e0)
        rows += [into * a, into * b, pick(c, one, zero)]
        rows += [send * a, send * b, pick(c, zero, one)]
        for index, row in enumerate(rows):
            out[index : index + 1, :] = row


def combine(base, groups, weights, outs, after=(), slots_of=None, at=0, carry=()):
    arrays, columns = [], []
    for slots in outs:
        for column, terms in slots:
            if column not in columns:
                columns.append(column)
            for _, (array, slot) in terms:
                if not any(array is a and slot == s for a, s in arrays):
                    arrays.append((array, slot))
    place = lambda array, slot: [
        i for i, (a, s) in enumerate(arrays) if a is array and s == slot
    ][0]
    plan = [
        [
            (columns.index(column), [(row, place(*source)) for row, source in terms])
            for column, terms in slots
        ]
        for slots in outs
    ]

    def body(at, base, *refs):
        rows, values = refs[: len(columns)], refs[len(columns) : len(columns) + len(arrays)]
        results = refs[len(columns) + len(arrays) :]
        width = rows[0].shape[1]
        for result, slots in zip(results, plan):
            for slot, (column, terms) in enumerate(slots):
                for start in range(0, width, 256):
                    lanes = slice(start, start + 256)
                    total = None
                    for row, index in terms:
                        term = rows[column][row : row + 1, lanes] * values[index][
                            0, :, lanes
                        ].astype(F32)
                        total = term if total is None else total + term
                    result[slot, :, lanes] = total.astype(BF16)

    length, width = arrays[0][0].shape[1:]
    block = lambda slot, count: ((count, length, width), lambda g, b: (slot, 0, 0))
    ins = [
        (
            weights,
            (
                (weights.shape[0], width),
                lambda g, b, column=column: (0, lax.rem(first_group(b) + column, groups)),
            ),
        )
        for column in columns
    ]
    ins += [(array, block(slot, 1)) for array, slot in arrays]
    results = [
        ((slots_of or len(slots), length, width), BF16, block(at, len(slots))) for slots in outs
    ]
    return call(body, results, ins, base=base, after=after, carry=carry)


def scan_blocks(base, groups, weights, local, local_sent, reverse, beside):
    count = lax.axis_size("seq")
    place = lambda position: count - 1 - position if reverse else position

    def swap(block, bit_of, keep):
        route = [
            (place(i), place(i ^ bit_of(place(i) % 2)))
            for i in range(count)
            if keep(i, place(i) % 2)
        ]
        return lax.ppermute(block, "seq", route)

    def merge(slot, *plans, **places):
        outs = [[(slot, list(zip(rows, sources)))] for rows, sources in plans]
        return combine(base, groups, weights, outs, **places)

    everyone = lambda i, core: True
    across = lambda block: swap(
        block, lambda core: 4 if core else 2, lambda i, core: i < 4 if core else i < 6
    )
    onward = lambda block: swap(
        block,
        lambda core: 2 if core else 4,
        lambda i, core: i not in (2, 3) if core else i < 4,
    )
    taken = swap(local_sent, lambda core: 1, everyone)
    chips, first_taken, sent, second_taken = [], [], [], []
    for slot in range(2):
        both = ((local, slot), (taken, slot))
        chip, chip_sent = merge(slot, ((0, 1), both), ((2, 3), both))
        chips.append(chip)
        first_taken.append(across(chip_sent))
    after = [beside[0](chips[1])]
    for slot in range(2):
        sources = ((chips[slot], 0), (first_taken[slot], 0))
        (block,) = merge(slot, ((4, 5), sources), after=after)
        sent.append(block)
        second_taken.append(onward(block))
        after = []
    after = beside[1](sent[1])
    carry = []
    for slot in range(2):
        sources = ((first_taken[slot], 0), (second_taken[slot], 0))
        mine, handed = merge(
            slot,
            ((6, 7, 8), (*sources, (taken, slot))),
            ((9, 10, 11), (*sources, (local, slot))),
            after=after[slot],
            slots_of=2,
            at=slot,
            carry=carry,
        )
        carry = [mine, handed]
    return mine, swap(handed, lambda core: 1, everyone)


def gather_blocks(totals, local, reverse):
    table = lax.all_gather(totals, "seq", axis=0, tiled=True)
    blocks = lax.all_gather(local[None], "seq", axis=0, tiled=True)
    own = lax.axis_index("seq")
    order = jnp.arange(table.shape[0], dtype=jnp.int32)
    if reverse:
        inside = (order[None, :] > own) & (order[None, :] < order[:, None])
        selected = order > own
    else:
        inside = (order[None, :] > order[:, None]) & (order[None, :] < own)
        selected = order < own
    exponent = jnp.sum(jnp.where(inside[:, :, None], table[None], 0.0), axis=1)
    factor = jnp.where(selected[:, None], jnp.exp(exponent), 0.0)
    factor = factor.reshape(factor.shape[0], local.shape[0], 1, local.shape[2])
    state = jnp.sum(factor * blocks.astype(F32), axis=0).astype(BF16)
    return state, state


def conv_body(at, base, x_in, taps, x_out, slope_out, ext):
    length, width = x_in.shape
    ext[0:8, :] = jnp.zeros((8, 128), F32)
    for start in range(0, width, 128):
        lanes = slice(start, start + 128)
        ext[8 : 8 + length, :] = x_in[:, lanes].astype(F32)
        pre = taps[0:1, lanes] * ext[5 : 5 + length, :]
        for k in range(1, 4):
            pre = pre + taps[k : k + 1, lanes] * ext[5 + k : 5 + k + length, :]
        sigma = sigmoid(pre)
        x_out[:, lanes] = (pre * sigma).astype(BF16)
        slope_out[:, lanes] = sigma * (1.0 + pre * (1.0 - sigma))


def state_body(first, at, base, x_low, x_top, x_halo, taps, step_in, cumul_in, *refs):
    length, width = x_low.shape
    if first:
        bc_in, bc_halo, bc_taps, slope_out, x_out, state_out = refs[:6]
        bc_out, bc_slope_out, gram_out, b_turned, ext, bc_ext = refs[6:]

        @pl.when(at[0] == 0)
        def _():
            for j in range(2):
                bc_ext[5:8, :] = bc_halo[:, j * 128 : j * 128 + 128].astype(F32)
                bc_ext[8 : 8 + length, :] = bc_in[j].astype(F32)
                pre = bc_taps[j, 0:1, :] * bc_ext[5 : 5 + length, :]
                for k in range(1, 4):
                    pre = pre + bc_taps[j, k : k + 1, :] * bc_ext[5 + k : 5 + k + length, :]
                sigma = sigmoid(pre)
                bc_out[j] = (pre * sigma).astype(BF16)
                bc_slope_out[j] = sigma * (1.0 + pre * (1.0 - sigma))
            b_turned[...] = bc_out[0].astype(F32).T
            gram_out[...] = jnp.where(
                triangle(length, False), dot_rows(bc_out[1], bc_out[0]), 0.0
            )

    else:
        b_turned, slope_out, x_out, state_out, ext = refs

    top = x_top.shape[0]
    ext[5:8, :] = x_halo[...].astype(F32)
    ext[8 : 8 + top, :] = x_top[...].astype(F32)
    tail_step = jnp.exp(cumul_in[:, length - 1 :] - cumul_in[...]) * step_in[...]
    for head in range(width // 128):
        lanes = slice(head * 128, head * 128 + 128)
        pre = taps[0:1, lanes] * ext[5 : 5 + top, lanes]
        for k in range(1, 4):
            pre = pre + taps[k : k + 1, lanes] * ext[5 + k : 5 + k + top, lanes]
        sigma = sigmoid(pre)
        x_rows = (pre * sigma).astype(BF16)
        x_out[:, lanes] = x_rows
        slope_out[:, lanes] = sigma * (1.0 + pre * (1.0 - sigma))
        x_head = jnp.concatenate([x_rows, x_low[top:, lanes]], axis=0)
        weighted = (b_turned[...] * tail_step[head : head + 1, :]).astype(BF16)
        state_out[0, :, lanes] = dot(weighted, x_head).astype(BF16)


def inner_body(at, base, gram, step_in, cumul_in, x_in, rows, mixed_out):
    cumul = cumul_in[...]
    cumul_columns = columns_of(cumul)
    for head in range(x_in.shape[1] // 128):
        lanes = slice(head * 128, head * 128 + 128)
        row = cumul[head : head + 1, :]
        decay = jnp.exp(jnp.minimum(cumul_columns[:, head : head + 1] - row, 0.0))
        mixer = (gram[...] * decay * step_in[head : head + 1, :]).astype(BF16)
        x_head = x_in[:, lanes]
        mixed_out[:, lanes] = dot(mixer, x_head) + rows[1:2, lanes] * x_head.astype(F32)


def pick_state(at, own_half, mine, other):
    group, _ = at
    first = mine[jnp.minimum(group, own_half - 1)]
    return jnp.where(group < own_half, first, other[jnp.maximum(group - own_half, 0)])


def gate_body(
    at,
    base,
    z_in,
    grad_in,
    gain,
    bc,
    step_in,
    cumul_in,
    x_in,
    gate_out,
    scaled_out,
    weighted_x,
    lifted_out,
    c_turned,
):
    @pl.when(at[0] == 0)
    def _():
        c_turned[...] = bc[1].astype(F32).T

    weights = block_weights(step_in[...], cumul_in[...])
    lifted = jnp.exp(cumul_in[...])
    for head in range(z_in.shape[1] // 128):
        lanes = slice(head * 128, head * 128 + 128)
        z = z_in[:, lanes].astype(F32)
        gate = z * sigmoid(z)
        gate_out[:, lanes] = gate
        scaled_out[:, lanes] = grad_in[:, lanes].astype(F32) * gain[:, lanes] * gate
        weight = weights[:, head : head + 1]
        weighted_x[:, lanes] = (weight * x_in[:, lanes].astype(F32)).astype(BF16)
        lifted_out[:, lanes] = (c_turned[...] * lifted[head : head + 1, :]).astype(BF16)


def mix_body(
    at, base, mixed_in, c_rows, cumul_in, state, gate_in, scaled_in, sums_in, *outs
):
    mixed_out, sums_out, squares, products = outs
    group, groups = at

    @pl.when(group == 0)
    def _():
        squares[...] = jnp.zeros_like(squares)
        products[...] = jnp.zeros_like(products)

    carried = dot(c_rows[0], state[0])
    lifted = jnp.exp(columns_of(cumul_in[...]))
    square, product = squares[...], products[...]
    for head in range(mixed_in.shape[1] // 128):
        lanes = slice(head * 128, head * 128 + 128)
        mixed = mixed_in[:, lanes] + lifted[:, head : head + 1] * carried[:, lanes]
        mixed_out[:, lanes] = mixed
        gated = mixed * gate_in[:, lanes]
        square = square + gated * gated
        product = product + mixed * scaled_in[:, lanes]
    squares[...] = square
    products[...] = product

    @pl.when(group == groups - 1)
    def _():
        sums_out[...] = sums_in[...]
        sums_out[0:1, :] += jnp.sum(squares[...].T, axis=0, keepdims=True)
        sums_out[1:2, :] += jnp.sum(products[...].T, axis=0, keepdims=True)


def square_body(at, base, mixed_in, gate_in, squared):
    for start in range(0, mixed_in.shape[1], 128):
        lanes = slice(start, start + 128)
        gate = gate_in[:, lanes]
        squared[:, lanes] = mixed_in[:, lanes] * gate * gate


def norm_scales(at, inner, sums, alpha, beta):
    @pl.when(at[0] == 0)
    def _():
        total = sums[0][...]
        for part in sums[1:]:
            total = total + part[...]
        inv_rms = lax.rsqrt(total[0:1, :] / inner + EPS)
        mean_dot = inv_rms * total[1:2, :] / inner
        alpha[...] = jnp.broadcast_to(inv_rms, alpha.shape).T
        beta[...] = jnp.broadcast_to(inv_rms * inv_rms * mean_dot, beta.shape).T


def grad_mixed_body(inner, parts, at, base, *refs):
    sums = refs[:parts]
    squared, scaled_in, lifted_c, grad_mixed, state_out, alpha, beta = refs[parts:]
    norm_scales(at, inner, sums, alpha, beta)
    for start in range(0, squared.shape[1], 128):
        lanes = slice(start, start + 128)
        low = (alpha[...] * scaled_in[:, lanes] - beta[...] * squared[:, lanes]).astype(BF16)
        grad_mixed[:, lanes] = low
        state_out[0, :, lanes] = dot(lifted_c[:, lanes], low).astype(BF16)


def grad_z_body(inner, parts, at, base, *refs):
    sums = refs[:parts]
    mixed_in, z_in, grad_in, gain, grad_z, alpha, beta = refs[parts:]
    norm_scales(at, inner, sums, alpha, beta)
    for start in range(0, z_in.shape[1], 128):
        lanes = slice(start, start + 128)
        z = z_in[:, lanes].astype(F32)
        sigma = sigmoid(z)
        mixed = mixed_in[:, lanes]
        scaled = grad_in[:, lanes].astype(F32) * gain[:, lanes]
        grad_gated = alpha[...] * scaled - beta[...] * (mixed * (z * sigma))
        grad_z[:, lanes] = (grad_gated * mixed * (sigma * (1.0 + z * (1.0 - sigma)))).astype(BF16)


def inner_back_body(
    last,
    at,
    base,
    gram,
    bc,
    step_in,
    cumul_in,
    x_in,
    grad_in,
    state_in,
    rows,
    sums_in,
    grad_x,
    q_out,
    r_out,
    bc_out,
    z_sum,
    c_sum,
):
    group, groups = at
    length = x_in.shape[0]

    @pl.when(group == 0)
    def _():
        z_sum[...] = sums_in[0]
        c_sum[...] = sums_in[1]

    cumul = cumul_in[...]
    cumul_columns = columns_of(cumul)
    lifted = jnp.exp(cumul_columns)
    state = state_in[0]
    c_rows = bc[1].astype(F32)
    lane = lax.broadcasted_iota(jnp.int32, (length, 128), 1)
    q_columns = jnp.zeros((length, 128), F32)
    for head in range(x_in.shape[1] // 128):
        lanes = slice(head * 128, head * 128 + 128)
        step = step_in[head : head + 1, :]
        decay = jnp.exp(
            jnp.minimum(cumul_columns[:, head : head + 1] - cumul[head : head + 1, :], 0.0)
        )
        gram_decay = gram[...] * decay
        mixer = (gram_decay * step).astype(BF16)
        x_head, grad_head = x_in[:, lanes], grad_in[:, lanes]
        product = dot_rows(grad_head, x_head)
        z_sum[...] += product * decay * step
        gram_grad = product * gram_decay
        r_out[head : head + 1, :] = jnp.sum(gram_grad, axis=0, keepdims=True)
        handed = lifted[:, head : head + 1] * dot_rows(grad_head, state[:, lanes])
        c_sum[...] += handed
        q = jnp.sum(gram_grad * step + c_rows * handed, axis=1, keepdims=True)
        q_columns = jnp.where(lane == head, q, q_columns)
        grad_x[:, lanes] = dot_columns(mixer, grad_head) + rows[1:2, lanes] * grad_head.astype(F32)
    q_out[...] = q_columns.T[:GROUP, :]

    @pl.when(group == groups - 1)
    def _():
        if last:
            summed = jnp.where(triangle(length, False), z_sum[...], 0.0)
            bc_out[0] = dot_split(summed.T, bc[1])
            bc_out[1] = c_sum[...] + dot_split(summed, bc[0])
        else:
            bc_out[0] = z_sum[...]
            bc_out[1] = c_sum[...]


def block_weights(step, cumul):
    return columns_of(jnp.exp(cumul[:, cumul.shape[1] - 1 :] - cumul) * step)


def rim_body(
    own_half,
    at,
    base,
    bc,
    step_in,
    cumul_in,
    weighted_x,
    partial,
    slope,
    out_mine,
    out_other,
    bc_partial,
    bc_slope,
    rim_out,
    bc_out,
    b_sum,
):
    group, groups = at
    width = weighted_x.shape[1]

    @pl.when(group == 0)
    def _():
        b_sum[...] = jnp.zeros_like(b_sum)

    out_low = pick_state(at, own_half, out_mine, out_other)
    b_sum[...] += dot_rows(weighted_x[...], out_low)
    weights = block_weights(step_in[...], cumul_in[...])[0:8, :]
    returned = dot(bc[0][0:16, :], out_low)[0:8, :]
    for head in range(width // 128):
        lanes = slice(head * 128, head * 128 + 128)
        weight = weights[:, head : head + 1]
        rows = (partial[:, lanes] + weight * returned[:, lanes]) * slope[:, lanes]
        place = pl.multiple_of(lax.rem(group + first_group(base), groups) * width + head * 128, 128)
        rim_out[:, pl.ds(place, 128)] = rows[0:3, :]

    @pl.when(group == groups - 1)
    def _():
        bc_out[0] = (b_sum[...] + bc_partial[0]) * bc_slope[0]
        bc_out[1] = bc_partial[1] * bc_slope[1]
        for j in range(2):
            start = rim_out.shape[1] - 256 + 128 * j
            rim_out[:, start : start + 128] = bc_out[j, 0:3, :]


def grad_dt_body(
    at,
    base,
    bc,
    rate,
    dt_slope,
    step_in,
    cumul_in,
    q_in,
    r_in,
    x_in,
    state_in,
    out_in,
    grad_dt,
    selector,
    products,
):
    length, width = x_in.shape

    @pl.when(at[0] == 0)
    def _():
        row = lax.broadcasted_iota(jnp.int32, (width, 128), 0)
        lane = lax.broadcasted_iota(jnp.int32, (width, 128), 1)
        selector[...] = (row // 128 == lane).astype(BF16)

    cumul, step = cumul_in[...], step_in[...]
    state, out_low = state_in[0], out_in[0]
    returned = dot(bc[0], out_low)
    for start in range(0, width, 128):
        lanes = slice(start, start + 128)
        products[:, lanes] = (x_in[:, lanes].astype(F32) * returned[:, lanes]).astype(BF16)
    inner_b = dot(products[...], selector[...]).T[:GROUP, :]
    w = jnp.exp(cumul[:, length - 1 :] - cumul) * inner_b
    dots = dot(jnp.ones((16, length), BF16), state * out_low)[:GROUP, :]
    row = lax.broadcasted_iota(jnp.int32, (GROUP, width), 0)
    lane = lax.broadcasted_iota(jnp.int32, (GROUP, width), 1)
    dots = jnp.sum(jnp.where(lane // 128 == row, dots, 0.0), axis=1, keepdims=True)
    q, r = q_in[...], r_in[...]
    inside = jnp.sum(step * w, axis=1, keepdims=True)
    end = inside + jnp.exp(cumul[:, length - 1 :]) * dots
    last = lax.broadcasted_iota(jnp.int32, (GROUP, length), 1) == length - 1
    grad_cumul = q - step * (r + w) + jnp.where(last, end, 0.0)
    grad_log = dot_split(grad_cumul, triangle(length, False).astype(BF16))
    grad_dt[...] = (r + w + rate[...] * grad_log) * dt_slope[...]


def grad_x_body(
    at,
    base,
    bc,
    step_in,
    cumul_in,
    partial,
    slope,
    taps,
    halo,
    out_in,
    grad_x,
    ext,
):
    length, width = partial.shape
    weights = block_weights(step_in[...], cumul_in[...])
    returned = dot(bc[0], out_in[0])
    for head in range(width // 128):
        lanes = slice(head * 128, head * 128 + 128)
        weight = weights[:, head : head + 1]
        ext[0:length, :] = (partial[:, lanes] + weight * returned[:, lanes]) * slope[:, lanes]
        ext[length : length + 3, :] = halo[:, lanes]
        total = taps[0:1, lanes] * ext[3 : 3 + length, :]
        for k in range(1, 4):
            total = total + taps[k : k + 1, lanes] * ext[3 - k : 3 - k + length, :]
        grad_x[:, lanes] = total.astype(BF16)


def bc_back_body(at, place, grad_pre, halo, taps, kept, sent, ext, total):
    length, half = grad_pre.shape[1], kept.shape[1]
    for j in range(2):
        ext[0:length, :] = grad_pre[j]
        ext[length : length + 3, :] = halo[:, 128 * j : 128 * j + 128]
        summed = taps[j, 0:1, :] * ext[3 : 3 + length, :]
        for k in range(1, 4):
            summed = summed + taps[j, k : k + 1, :] * ext[3 - k : 3 - k + length, :]
        total[...] = summed
        kept[j] = total[pl.ds(pl.multiple_of(place_bit(place, 3) * half, half), half), :]
        sent[j] = total[pl.ds(pl.multiple_of((1 - place_bit(place, 3)) * half, half), half), :]


def bc_half_body(at, place, mine, taken, kept, sent, total):
    half = kept.shape[1]
    for j in range(2):
        total[...] = mine[j] + taken[j]
        kept[j] = total[pl.ds(pl.multiple_of(place_bit(place, 4) * half, half), half), :]
        sent[j] = total[pl.ds(pl.multiple_of((1 - place_bit(place, 4)) * half, half), half), :]


def bc_last_body(at, _, mine, taken, out):
    out[...] = (mine[...] + taken[...]).astype(BF16)


def conv_back(extended, weights):
    length = extended.shape[-2] - 3
    summed = weights[..., 0, :][..., None, :] * extended[..., 3 : 3 + length, :]
    for k in range(1, 4):
        summed = (
            summed
            + weights[..., k, :][..., None, :] * extended[..., 3 - k : 3 - k + length, :]
        )
    return summed


def shards(
    x_input,
    z_input,
    bc_input,
    dt_raw,
    dt_bias,
    a_log,
    d_skip,
    conv_x,
    convolution_bc_taps,
    rescale_factor,
    grad_out,
):
    length, channels = x_input.shape
    heads = dt_raw.shape[0]
    groups = heads // GROUP
    width = GROUP * 128
    count, parts = lax.axis_size("seq"), lax.axis_size("head")
    inner = channels * parts
    own = lax.axis_index("seq")
    split = count == 8 and groups == 4
    own_half = groups // 2 if split else groups
    bit = lambda value, place: lax.shift_right_logical(value, place) & 1
    along_head = lax.axis_index("head")
    base = bit(own, 0) * own_half if split else own * 0
    for place, value in enumerate(
        (bit(own, 2), bit(own, 1), bit(own, 0), bit(along_head, 1), bit(along_head, 0))
    ):
        base = base | lax.shift_left(value, 8 + place)
    base = base.astype(jnp.int32)[None]

    whole = lambda *shape: ((shape, lambda g, b: (0,) * len(shape)),)
    wide_at = lambda off: (Groups("wide", (length, width), off, groups),)
    rows_at = lambda off: (Groups("heads", (GROUP, length), off, groups),)
    lanes_at = lambda n, off: (Groups("wide", (n, width), off, groups),)
    wide, rows8, lanes_of = wide_at(0), rows_at(0), lambda n: lanes_at(n, 0)
    slot = (Groups("slots", (1, length, width), 0, groups),)
    full = lambda array: (array,) + whole(*array.shape)
    halves = [own_half, 0] if split else [0]

    gain = rescale_factor[None, :]
    f32 = lambda *shape: (shape, F32)
    low = lambda *shape: (shape, BF16)

    step, cumul, rate, dt_slope, rows, rim = call(
        steps_body,
        [
            f32(heads, length) + whole(heads, length),
            f32(heads, length) + whole(heads, length),
            f32(heads, length) + whole(heads, length),
            f32(heads, length) + whole(heads, length),
            f32(2, channels) + whole(2, channels),
            low(3, channels + 256) + whole(3, channels + 256),
        ],
        [
            full(in_hbm(dt_raw)),
            full(in_hbm(dt_bias[None, :])),
            full(in_hbm(a_log[None, :])),
            full(in_hbm(d_skip[None, :])),
            (in_hbm(x_input), ((16, channels), lambda g, b: (length // 16 - 1, 0))),
            (in_hbm(bc_input), ((2, 16, 128), lambda g, b: (0, length // 16 - 1, 0))),
        ],
        base=base,
    )
    rim_sent = rim
    rim = lax.ppermute(rim, "seq", [(i - 1, i) for i in range(1, count)])
    if split:
        swap = lambda block, bit: lax.ppermute(
            block, "seq", [(i, i ^ bit) for i in range(count)]
        )
        total = rows[0:1]
        total_core = swap(total, 1)
        chip_total = total + total_core
        total_across = swap(chip_total, 2)
        table = f32(16, channels) + whole(16, channels)
        ahead, behind = call(
            weights_body,
            [table, table],
            [full(rows), full(total_core), full(total_across)],
            base=base,
            )

    def passed(locals_, reverse, beside):
        if split:
            local_sent, local = locals_
            weights = behind if reverse else ahead
            return scan_blocks(base, groups, weights, local, local_sent, reverse, beside)
        (local,) = locals_
        for work in beside:
            work(local)
        return gather_blocks(rows[0:1], local, reverse)

    x_low, slope = call(
        conv_body,
        [low(length, channels) + wide, f32(length, channels) + wide],
        [(in_hbm(x_input),) + wide, (in_hbm(conv_x),) + lanes_of(4)],
        base=base,
        grid=groups,
        scratch=[pltpu.VMEM((length + 8, 128), F32)],
        after=[rim_sent],
    )
    local = []
    for off in halves:
        first = off == halves[0]
        top = lanes_at(16, off)
        ins = [
            (x_low,) + wide_at(off),
            (in_hbm(x_input),) + top,
            (rim,) + lanes_at(3, off),
            (in_hbm(conv_x),) + lanes_at(4, off),
            (step,) + rows_at(off),
            (cumul,) + rows_at(off),
        ]
        outs = [
            f32(length, channels) + top,
            low(length, channels) + top,
            low(own_half, length, width) + slot,
        ]
        scratch = [pltpu.VMEM((24, width), F32)]
        if first:
            ins += [
                full(in_hbm(bc_input)),
                (rim, ((3, 256), lambda g, b: (0, channels // 256))),
                full(in_hbm(convolution_bc_taps)),
            ]
            outs += [
                low(2, length, 128) + whole(2, length, 128),
                f32(2, length, 128) + whole(2, length, 128),
                f32(length, length) + whole(length, length),
                f32(128, length) + whole(128, length),
            ]
            scratch += [pltpu.VMEM((length + 8, 128), F32)]
        else:
            ins += [full(b_turned)]
        result = call(
            functools.partial(state_body, first),
            outs,
            ins,
            base=base,
            loop=own_half,
            scratch=scratch,
            carry=[slope],
            place={0: 1},
            flops=2 * length * 128 * channels,
        )
        if first:
            bc, bc_slope, gram, b_turned = result[3:]
        slope, x_low = result[:2]
        local.append(result[2])
    done = {}

    def mix_inside(ready):
        done["mixed"], token = call(
            inner_body,
            [f32(length, channels) + wide],
            [
                full(gram),
                (step,) + rows8,
                (cumul,) + rows8,
                (x_low,) + wide,
                (rows,) + lanes_of(2),
            ],
            base=base,
            loop=groups,
            after=[ready],
            token=True,
            flops=2 * length * 128 * channels,
        )
        return token

    def gates(ready):
        done["gate"], done["scaled"], done["weighted_x"], done["lifted_c"], token = call(
            gate_body,
            [
                f32(length, channels) + wide,
                f32(length, channels) + wide,
                low(length, channels) + wide,
                low(length, channels) + wide,
            ],
            [
                (z_input,) + wide,
                (grad_out,) + wide,
                (gain,) + lanes_of(1),
                full(bc),
                (step,) + rows8,
                (cumul,) + rows8,
                (x_low,) + wide,
            ],
            base=base,
            loop=groups,
            scratch=[pltpu.VMEM((128, length), F32)],
            after=[ready],
            token=True,
        )
        return [], [token]

    state_mine, state_other = passed(local, False, (mix_inside, gates))
    gate, scaled = done["gate"], done["scaled"]
    c_spec = (((1, length, 128), lambda g, b: (1, 0, 0)),)
    mixed, sums = done["mixed"], jnp.zeros((8, length), F32)
    for off, state in zip(reversed(halves), (state_mine, state_other)):
        mixed, sums = call(
            mix_body,
            [f32(length, channels) + wide_at(off), f32(8, length) + whole(8, length)],
            [
                (mixed,) + wide_at(off),
                (bc,) + c_spec,
                (cumul,) + rows_at(off),
                (state,) + slot,
                (gate,) + wide_at(off),
                (scaled,) + wide_at(off),
                full(sums),
            ],
            base=base,
            loop=own_half,
            scratch=[pltpu.VMEM((length, 128), F32), pltpu.VMEM((length, 128), F32)],
            place={0: 0},
            flops=2 * length * 128 * channels,
        )
    turn_head = lambda block, bit: lax.ppermute(
        block, "head", [(i, i ^ bit) for i in range(parts)]
    )
    if parts == 4:
        sums = sums + turn_head(sums, 1)
        all_sums = [sums, turn_head(sums, 2)]
    else:
        all_sums = [lax.psum(sums, "head")]
    (squared,) = call(
        square_body,
        [f32(length, channels) + wide],
        [(mixed,) + wide, (gate,) + wide],
        base=base,
        loop=groups,
    )
    two_scales = [pltpu.VMEM((length, 128), F32), pltpu.VMEM((length, 128), F32)]
    carry, local_back = [], []
    for off in halves:
        grad_mixed, state = call(
            functools.partial(grad_mixed_body, inner, len(all_sums)),
            [low(length, channels) + wide_at(off), low(own_half, length, width) + slot],
            [full(part) for part in all_sums]
            + [
                (squared,) + wide_at(off),
                (scaled,) + wide_at(off),
                (done["lifted_c"],) + wide_at(off),
            ],
            base=base,
            loop=own_half,
            scratch=two_scales,
            carry=carry,
            flops=2 * length * 128 * channels,
        )
        carry = [grad_mixed]
        local_back.append(state)

    done["back"] = []
    done["sums"] = jnp.zeros((2, length, 128), F32)

    def back_inside(off, state, ready):
        *done["back"], done["sums"], token = call(
            functools.partial(inner_back_body, off == halves[0]),
            [
                f32(length, channels) + wide_at(off),
                f32(heads, length) + rows_at(off),
                f32(heads, length) + rows_at(off),
                f32(2, length, 128) + whole(2, length, 128),
            ],
            [
                full(gram),
                full(bc),
                (step,) + rows_at(off),
                (cumul,) + rows_at(off),
                (x_low,) + wide_at(off),
                (grad_mixed,) + wide_at(off),
                (state,) + slot,
                (rows,) + lanes_at(2, off),
                full(done["sums"]),
            ],
            base=base,
            loop=own_half,
            scratch=[pltpu.VMEM((length, length), F32), pltpu.VMEM((length, 128), F32)],
            carry=done["back"],
            after=[ready],
            token=True,
            flops=6 * length * 128 * channels,
        )
        return token

    def back_gates(ready):
        done["grad_z"], token = call(
            functools.partial(grad_z_body, inner, len(all_sums)),
            [low(length, channels) + wide],
            [full(part) for part in all_sums]
            + [
                (mixed,) + wide,
                (z_input,) + wide,
                (grad_out,) + wide,
                (gain,) + lanes_of(1),
            ],
            base=base,
            loop=groups,
            scratch=two_scales,
            after=[ready],
            token=True,
        )
        return token

    def back_first(ready):
        return back_inside(0, state_mine, ready)

    def back_second(ready):
        token = back_inside(own_half, state_other, ready) if split else ready
        return [token], [back_gates(token)]

    out_mine, out_other = passed(local_back, True, (back_first, back_second))
    (partial, q_rows, r_rows), bc_partial = done["back"], done["sums"]
    first_rows = lanes_of(8)
    quarters = list(zip(reversed(halves), (state_mine, state_other), (out_mine, out_other)))
    carried, dt_tokens = {"dt": [], "x": []}, []

    def make_grad_dt(off, state, out, after):
        grad_dt, token = call(
            grad_dt_body,
            [f32(heads, length) + rows_at(off)],
            [
                full(bc),
                (rate,) + rows_at(off),
                (dt_slope,) + rows_at(off),
                (step,) + rows_at(off),
                (cumul,) + rows_at(off),
                (q_rows,) + rows_at(off),
                (r_rows,) + rows_at(off),
                (x_low,) + wide_at(off),
                (state,) + slot,
                (out,) + slot,
            ],
            base=base,
            loop=own_half,
            scratch=[pltpu.VMEM((width, 128), BF16), pltpu.VMEM((length, width), BF16)],
            carry=carried["dt"],
            after=after,
            token=True,
            flops=4 * length * 128 * channels,
        )
        carried["dt"] = [grad_dt]
        return token

    def make_grad_x(off, out, after):
        grad_x, token = call(
            grad_x_body,
            [low(length, channels) + wide_at(off)],
            [
                full(bc),
                (step,) + rows_at(off),
                (cumul,) + rows_at(off),
                (partial,) + wide_at(off),
                (slope,) + wide_at(off),
                (conv_x,) + lanes_at(4, off),
                (rim_back,) + lanes_at(3, off),
                (out,) + slot,
            ],
            base=base,
            loop=own_half,
            scratch=[pltpu.VMEM((length + 8, 128), F32)],
            carry=carried["x"],
            after=after,
            token=True,
            flops=2 * length * 128 * channels,
        )
        carried["x"] = [grad_x]
        return token

    for off, state, out in quarters[:-1]:
        dt_tokens.append(make_grad_dt(off, state, out, []))
    rim_back, grad_bc_pre = call(
        functools.partial(rim_body, own_half),
        [
            f32(3, channels + 256) + whole(3, channels + 256),
            f32(2, length, 128) + whole(2, length, 128),
        ],
        [
            full(bc),
            (step,) + rows8,
            (cumul,) + rows8,
            (done["weighted_x"],) + wide,
            (partial,) + first_rows,
            (slope,) + first_rows,
        ]
        + [full(out_mine), full(out_other), full(bc_partial), full(bc_slope)],
        base=base,
        loop=groups,
        after=dt_tokens,
        scratch=[pltpu.VMEM((length, 128), F32)],
        flops=2 * length * 128 * channels,
    )
    rim_back = lax.ppermute(rim_back, "seq", [(i, i - 1) for i in range(1, count)])
    off, state, out = quarters[-1]
    dt_token = make_grad_dt(off, state, out, [grad_bc_pre])
    if parts == 4:
        piece = lambda rows: f32(2, rows, 128) + whole(2, rows, 128)
        kept, sent = call(
            bc_back_body,
            [piece(length // 2), piece(length // 2)],
            [
                full(grad_bc_pre),
                (rim_back, ((3, 256), lambda g, b: (0, channels // 256))),
                full(convolution_bc_taps),
            ],
            base=base,
                scratch=[pltpu.VMEM((length + 8, 128), F32), pltpu.VMEM((length, 128), F32)],
            after=[dt_token],
        )
        taken = turn_head(sent, 2)
        x_tokens = [make_grad_x(off, out, [sent]) for off, _, out in quarters[:1]]
        kept, sent = call(
            bc_half_body,
            [piece(length // 4), piece(length // 4)],
            [full(kept), full(taken)],
            base=base,
                scratch=[pltpu.VMEM((length // 2, 128), F32)],
            after=x_tokens,
        )
        taken = turn_head(sent, 1)
        x_tokens = [make_grad_x(off, out, [sent]) for off, _, out in quarters[1:]]
        (grad_bc,) = call(
            bc_last_body,
            [low(2, length // 4, 128) + whole(2, length // 4, 128)],
            [full(kept), full(taken)],
            base=base,
                after=x_tokens,
        )
    else:
        for off, _, out in quarters:
            make_grad_x(off, out, [])
        bc_halo = jnp.moveaxis(rim_back[:, channels:].reshape(3, 2, 128), 1, 0)
        bc_sum = conv_back(jnp.concatenate([grad_bc_pre, bc_halo], axis=1), convolution_bc_taps)
        share = length // parts
        bc_sum = lax.psum(bc_sum, "head")
        grad_bc = lax.dynamic_slice_in_dim(bc_sum, along_head * share, share, 1).astype(BF16)
    return (carried["x"][0], done["grad_z"], grad_bc, carried["dt"][0])


def solution(mesh):
    return jax.shard_map(
        shards,
        mesh=mesh,
        in_specs=(
            P("seq", "head"),
            P("seq", "head"),
            P(None, "seq", None),
            P("head", "seq"),
            P("head"),
            P("head"),
            P("head"),
            P(None, "head"),
            P(),
            P("head"),
            P("seq", "head"),
        ),
        out_specs=(
            P("seq", "head"),
            P("seq", "head"),
            P(None, ("seq", "head"), None),
            P("head", "seq"),
        ),
        check_vma=False,
    )
```

```python
import functools

import jax
import jax.numpy as jnp
from jax import lax
from jax.experimental import pallas as pl
from jax.experimental.pallas import tpu as pltpu
from jax.sharding import PartitionSpec as P

EPS = 1e-05
GROUP = 8
F32 = jnp.float32
BF16 = jnp.bfloat16
VMEM_BYTES = 16 * 2**20


def sigmoid(value):
    return 0.5 + 0.5 * jnp.tanh(0.5 * value)


def dot(a, b):
    return jnp.dot(a, b, preferred_element_type=F32)


def dot_split(a, b):
    high = a.astype(BF16)
    rest = a - high.astype(F32)
    middle = rest.astype(BF16)
    low = (rest - middle.astype(F32)).astype(BF16)
    return dot(high, b) + (dot(middle, b) + dot(low, b))


def dot_rows(a, b):
    return lax.dot_general(a, b, (((1,), (1,)), ((), ())), preferred_element_type=F32)


def dot_columns(a, b):
    return lax.dot_general(a, b, (((0,), (0,)), ((), ())), preferred_element_type=F32)


def triangle(length, upper):
    first = lax.broadcasted_iota(jnp.int32, (length, length), 0)
    second = lax.broadcasted_iota(jnp.int32, (length, length), 1)
    return first <= second if upper else first >= second


def columns_of(rows):
    return rows.T


class Groups:
    def __init__(self, kind, block, off, groups):
        self.kind, self.block, self.off, self.groups = kind, block, off, groups
        self.by_rows = kind.endswith("heads")

    def turn(self, group, base):
        return lax.rem(group + self.off + first_group(base), self.groups)

    def place(self, index):
        return (index, 0) if self.by_rows else (0, index)

    def spec(self):
        if self.kind == "slots":
            return pl.BlockSpec(self.block, lambda g, b: (g, 0, 0))
        if self.kind.startswith("half"):
            return pl.BlockSpec(self.block, lambda g, b: self.place(g))
        return pl.BlockSpec(self.block, lambda g, b: self.place(self.turn(g, b)))

    def whole(self, shape, count):
        if self.kind.startswith("window"):
            block = list(self.block)
            block[0 if self.by_rows else 1] *= count
            return pl.BlockSpec(
                tuple(block), lambda g, b: self.place(self.turn(0, b) // count)
            )
        if self.kind == "top":
            shape = (self.block[0], count * self.block[1])
        return pl.BlockSpec(shape, lambda g, b: (0,) * len(shape))

    def view(self, ref, group, base):
        if self.kind == "slots":
            return ref.at[pl.ds(group, 1)]
        if self.kind in ("wide", "heads"):
            group = self.turn(group, base)
        size = self.block[0 if self.by_rows else 1]
        span = pl.ds(pl.multiple_of(jnp.int32(group) * size, size), size)
        return ref.at[span] if self.by_rows else ref.at[:, span]


def call(
    body,
    outs,
    ins,
    *,
    base,
    grid=1,
    loop=1,
    scratch=(),
    after=(),
    carry=(),
    place=None,
    token=False,
    flops=0,
):
    aliases = {1 + len(ins) + len(after) + i: i for i in range(len(carry))}
    for read, written in (place or {}).items():
        aliases[1 + read] = written
    after = list(after) + list(carry)
    outs = list(outs)
    if token:
        outs.append(((8, 128), F32, ((8, 128), lambda *_: (0, 0))))

    def spec(shape, block):
        if not isinstance(block, Groups):
            return pl.BlockSpec(*block)
        return block.whole(shape, loop) if grid == 1 else block.spec()

    in_specs = [spec(array.shape, block) for array, block in ins]
    in_specs += [pl.BlockSpec(memory_space=pl.ANY) for _ in after]
    out_specs = [spec(shape, block) for shape, _, block in outs]
    out_shape = [jax.ShapeDtypeStruct(shape, dtype) for shape, dtype, _ in outs]
    arrays = [array for array, _ in ins]
    moved = sum(a.size * a.dtype.itemsize for a in arrays + out_shape)
    blocks = [block for _, block in ins] + [block for _, _, block in outs]

    def ordered(where, *refs):
        taken, rest = refs[: len(ins)], refs[len(ins) + len(after) :]
        results, extra = rest[: len(outs)], rest[len(outs) :]
        if token:
            results[-1][...] = jnp.zeros((8, 128), F32)

        def step(group, _):
            views = [
                block.view(ref, group, where) if isinstance(block, Groups) else ref
                for ref, block in zip(taken + results, blocks)
            ]
            if token:
                views = views[:-1]
            body((group, loop), where, *views, *extra)
            return 0

        if grid > 1:
            views = taken + (results[:-1] if token else results)
            body((pl.program_id(0), grid), where, *views, *extra)
        elif loop > 1:
            lax.fori_loop(0, loop, step, 0)
        else:
            step(0, 0)

    return pl.pallas_call(
        ordered,
        out_shape=out_shape,
        grid_spec=pltpu.PrefetchScalarGridSpec(
            num_scalar_prefetch=1,
            grid=(grid,),
            in_specs=in_specs,
            out_specs=out_specs,
            scratch_shapes=list(scratch),
        ),
        input_output_aliases=aliases,
        cost_estimate=pl.CostEstimate(flops=flops, bytes_accessed=moved, transcendentals=0),
        compiler_params=pltpu.CompilerParams(vmem_limit_bytes=VMEM_BYTES),
    )(base, *arrays, *after)


def in_hbm(array):
    return pltpu.with_memory_space_constraint(array, pltpu.HBM)


def column_of(row):
    count = row.shape[1]
    first = lax.broadcasted_iota(jnp.int32, (count, count), 0)
    second = lax.broadcasted_iota(jnp.int32, (count, count), 1)
    return jnp.sum(jnp.where(first == second, row, 0.0), axis=1, keepdims=True)


def steps_body(
    at,
    base,
    raw,
    bias,
    log_rate,
    skip,
    x_tail,
    bc_tail,
    step_out,
    cumul_out,
    rate_out,
    slope_out,
    rows_out,
    rim_out,
):
    heads, length = raw.shape
    channels = x_tail.shape[1]
    rim_out[:, 0:channels] = x_tail[...].astype(F32)[13:16, :].astype(BF16)
    for j in range(2):
        start = channels + 128 * j
        rim_out[:, start : start + 128] = bc_tail[j].astype(F32)[13:16, :].astype(BF16)
    shifted = raw[...] + column_of(bias[...])
    step = jnp.maximum(shifted, 0.0) + jnp.log1p(jnp.exp(-jnp.abs(shifted)))
    rate = jnp.broadcast_to(-jnp.exp(column_of(log_rate[...])), step.shape)
    cumul = dot_split(rate * step, triangle(length, True).astype(BF16))
    step_out[...] = step
    cumul_out[...] = cumul
    rate_out[...] = rate
    slope_out[...] = sigmoid(shifted)
    skips = column_of(skip[...])
    for head in range(heads):
        lanes = slice(head * 128, head * 128 + 128)
        rows_out[0:1, lanes] = jnp.broadcast_to(cumul[head : head + 1, length - 1 :], (1, 128))
        rows_out[1:2, lanes] = jnp.broadcast_to(skips[head : head + 1, :], (1, 128))


def pick(test, yes, no):
    return jnp.where(test, yes, no)


def first_group(place):
    return place[0] & 255


def place_bit(place, index):
    return lax.shift_right_logical(place[0], 8 + index) & 1


def weights_body(at, place, own, core, across, *outs):
    t0, t1 = own[0:1, :], core[...]
    e0, e1, own_chip, ex = jnp.exp(t0), jnp.exp(t1), jnp.exp(t0 + t1), jnp.exp(across[...])
    one = jnp.ones_like(e0)
    zero = jnp.zeros_like(e0)
    bits = [place_bit(place, i) for i in range(3)]
    x_first = bits[2] == 0
    for out, reverse in zip(outs, (False, True)):
        y, x, c = ((1 - bit if reverse else bit) == 1 for bit in bits)
        either = jnp.logical_or(x, y)
        scale = pick(jnp.logical_or(x_first, either), one, ex)
        rows = [pick(c, one, e1), pick(c, e0, one)]
        rows += [rows[0] * scale, rows[1] * scale]
        rows += [
            pick(x_first, pick(x, one, ex), pick(jnp.logical_and(x, y), zero, one)),
            pick(x_first, pick(x, own_chip, one), pick(y, pick(x, one, own_chip), zero)),
        ]
        a = pick(x_first, pick(x, one, zero), pick(y, pick(x, ex, one), zero))
        b = pick(x_first, pick(y, pick(x, ex, one), zero), pick(either, one, zero))
        into, send = pick(c, e1, one), pick(c, one, e0)
        rows += [into * a, into * b, pick(c, one, zero)]
        rows += [send * a, send * b, pick(c, zero, one)]
        for index, row in enumerate(rows):
            out[index : index + 1, :] = row


def combine(base, groups, weights, outs, after=(), slots_of=None, at=0, carry=()):
    arrays, columns = [], []
    for slots in outs:
        for column, terms in slots:
            if column not in columns:
                columns.append(column)
            for _, (array, slot) in terms:
                if not any(array is a and slot == s for a, s in arrays):
                    arrays.append((array, slot))
    place = lambda array, slot: [
        i for i, (a, s) in enumerate(arrays) if a is array and s == slot
    ][0]
    plan = [
        [
            (columns.index(column), [(row, place(*source)) for row, source in terms])
            for column, terms in slots
        ]
        for slots in outs
    ]

    def body(at, base, *refs):
        rows, values = refs[: len(columns)], refs[len(columns) : len(columns) + len(arrays)]
        results = refs[len(columns) + len(arrays) :]
        width = rows[0].shape[1]
        for result, slots in zip(results, plan):
            for slot, (column, terms) in enumerate(slots):
                for start in range(0, width, 256):
                    lanes = slice(start, start + 256)
                    total = None
                    for row, index in terms:
                        term = rows[column][row : row + 1, lanes] * values[index][
                            0, :, lanes
                        ].astype(F32)
                        total = term if total is None else total + term
                    result[slot, :, lanes] = total.astype(BF16)

    length, width = arrays[0][0].shape[1:]
    block = lambda slot, count: ((count, length, width), lambda g, b: (slot, 0, 0))
    ins = [
        (
            weights,
            (
                (weights.shape[0], width),
                lambda g, b, column=column: (0, lax.rem(first_group(b) + column, groups)),
            ),
        )
        for column in columns
    ]
    ins += [(array, block(slot, 1)) for array, slot in arrays]
    results = [
        ((slots_of or len(slots), length, width), BF16, block(at, len(slots))) for slots in outs
    ]
    return call(body, results, ins, base=base, after=after, carry=carry)


def scan_blocks(base, groups, weights, local, local_sent, reverse, beside):
    count = lax.axis_size("seq")
    place = lambda position: count - 1 - position if reverse else position

    def swap(block, bit_of, keep):
        route = [
            (place(i), place(i ^ bit_of(place(i) % 2)))
            for i in range(count)
            if keep(i, place(i) % 2)
        ]
        return lax.ppermute(block, "seq", route)

    def merge(slot, *plans, **places):
        outs = [[(slot, list(zip(rows, sources)))] for rows, sources in plans]
        return combine(base, groups, weights, outs, **places)

    everyone = lambda i, core: True
    across = lambda block: swap(
        block, lambda core: 4 if core else 2, lambda i, core: i < 4 if core else i < 6
    )
    onward = lambda block: swap(
        block,
        lambda core: 2 if core else 4,
        lambda i, core: i not in (2, 3) if core else i < 4,
    )
    taken = swap(local_sent, lambda core: 1, everyone)
    chips, first_taken, sent, second_taken = [], [], [], []
    for slot in range(2):
        both = ((local, slot), (taken, slot))
        chip, chip_sent = merge(slot, ((0, 1), both), ((2, 3), both))
        chips.append(chip)
        first_taken.append(across(chip_sent))
    after = [beside[0](chips[1])]
    for slot in range(2):
        sources = ((chips[slot], 0), (first_taken[slot], 0))
        (block,) = merge(slot, ((4, 5), sources), after=after)
        sent.append(block)
        second_taken.append(onward(block))
        after = []
    after = beside[1](sent[1])
    carry = []
    for slot in range(2):
        sources = ((first_taken[slot], 0), (second_taken[slot], 0))
        mine, handed = merge(
            slot,
            ((6, 7, 8), (*sources, (taken, slot))),
            ((9, 10, 11), (*sources, (local, slot))),
            after=after[slot],
            slots_of=2,
            at=slot,
            carry=carry,
        )
        carry = [mine, handed]
    return mine, swap(handed, lambda core: 1, everyone)


def gather_blocks(totals, local, reverse):
    table = lax.all_gather(totals, "seq", axis=0, tiled=True)
    blocks = lax.all_gather(local[None], "seq", axis=0, tiled=True)
    own = lax.axis_index("seq")
    order = jnp.arange(table.shape[0], dtype=jnp.int32)
    if reverse:
        inside = (order[None, :] > own) & (order[None, :] < order[:, None])
        selected = order > own
    else:
        inside = (order[None, :] > order[:, None]) & (order[None, :] < own)
        selected = order < own
    exponent = jnp.sum(jnp.where(inside[:, :, None], table[None], 0.0), axis=1)
    factor = jnp.where(selected[:, None], jnp.exp(exponent), 0.0)
    factor = factor.reshape(factor.shape[0], local.shape[0], 1, local.shape[2])
    state = jnp.sum(factor * blocks.astype(F32), axis=0).astype(BF16)
    return state, state


def conv_body(at, base, x_in, taps, x_out, slope_out, ext):
    length, width = x_in.shape
    ext[0:8, :] = jnp.zeros((8, 128), F32)
    for start in range(0, width, 128):
        lanes = slice(start, start + 128)
        ext[8 : 8 + length, :] = x_in[:, lanes].astype(F32)
        pre = taps[0:1, lanes] * ext[5 : 5 + length, :]
        for k in range(1, 4):
            pre = pre + taps[k : k + 1, lanes] * ext[5 + k : 5 + k + length, :]
        sigma = sigmoid(pre)
        x_out[:, lanes] = (pre * sigma).astype(BF16)
        slope_out[:, lanes] = sigma * (1.0 + pre * (1.0 - sigma))


def state_body(first, at, base, x_low, x_top, x_halo, taps, step_in, cumul_in, *refs):
    length, width = x_low.shape
    if first:
        bc_in, bc_halo, bc_taps, slope_out, x_out, state_out = refs[:6]
        bc_out, bc_slope_out, gram_out, b_turned, ext, bc_ext = refs[6:]

        @pl.when(at[0] == 0)
        def _():
            for j in range(2):
                bc_ext[5:8, :] = bc_halo[:, j * 128 : j * 128 + 128].astype(F32)
                bc_ext[8 : 8 + length, :] = bc_in[j].astype(F32)
                pre = bc_taps[j, 0:1, :] * bc_ext[5 : 5 + length, :]
                for k in range(1, 4):
                    pre = pre + bc_taps[j, k : k + 1, :] * bc_ext[5 + k : 5 + k + length, :]
                sigma = sigmoid(pre)
                bc_out[j] = (pre * sigma).astype(BF16)
                bc_slope_out[j] = sigma * (1.0 + pre * (1.0 - sigma))
            b_turned[...] = bc_out[0].astype(F32).T
            gram_out[...] = jnp.where(
                triangle(length, False), dot_rows(bc_out[1], bc_out[0]), 0.0
            )

    else:
        b_turned, slope_out, x_out, state_out, ext = refs

    top = x_top.shape[0]
    ext[5:8, :] = x_halo[...].astype(F32)
    ext[8 : 8 + top, :] = x_top[...].astype(F32)
    tail_step = jnp.exp(cumul_in[:, length - 1 :] - cumul_in[...]) * step_in[...]
    for head in range(width // 128):
        lanes = slice(head * 128, head * 128 + 128)
        pre = taps[0:1, lanes] * ext[5 : 5 + top, lanes]
        for k in range(1, 4):
            pre = pre + taps[k : k + 1, lanes] * ext[5 + k : 5 + k + top, lanes]
        sigma = sigmoid(pre)
        x_rows = (pre * sigma).astype(BF16)
        x_out[:, lanes] = x_rows
        slope_out[:, lanes] = sigma * (1.0 + pre * (1.0 - sigma))
        x_head = jnp.concatenate([x_rows, x_low[top:, lanes]], axis=0)
        weighted = (b_turned[...] * tail_step[head : head + 1, :]).astype(BF16)
        state_out[0, :, lanes] = dot(weighted, x_head).astype(BF16)


def inner_body(at, base, gram, step_in, cumul_in, x_in, rows, mixed_out):
    cumul = cumul_in[...]
    cumul_columns = columns_of(cumul)
    for head in range(x_in.shape[1] // 128):
        lanes = slice(head * 128, head * 128 + 128)
        row = cumul[head : head + 1, :]
        decay = jnp.exp(jnp.minimum(cumul_columns[:, head : head + 1] - row, 0.0))
        mixer = (gram[...] * decay * step_in[head : head + 1, :]).astype(BF16)
        x_head = x_in[:, lanes]
        mixed_out[:, lanes] = dot(mixer, x_head) + rows[1:2, lanes] * x_head.astype(F32)


def gate_body(at, base, z_in, grad_in, gain, gate_out, scaled_out):
    for start in range(0, z_in.shape[1], 128):
        lanes = slice(start, start + 128)
        z = z_in[:, lanes].astype(F32)
        gate = z * sigmoid(z)
        gate_out[:, lanes] = gate
        scaled_out[:, lanes] = grad_in[:, lanes].astype(F32) * gain[:, lanes] * gate


def lift_body(at, base, bc, step_in, cumul_in, x_in, weighted_x, lifted_out, c_turned):
    @pl.when(at[0] == 0)
    def _():
        c_turned[...] = bc[1].astype(F32).T

    weights = block_weights(step_in[...], cumul_in[...])
    lifted = jnp.exp(cumul_in[...])
    for head in range(x_in.shape[1] // 128):
        lanes = slice(head * 128, head * 128 + 128)
        weight = weights[:, head : head + 1]
        weighted_x[:, lanes] = (weight * x_in[:, lanes].astype(F32)).astype(BF16)
        lifted_out[:, lanes] = (c_turned[...] * lifted[head : head + 1, :]).astype(BF16)


def mix_body(
    at, base, mixed_in, c_rows, cumul_in, state, gate_in, scaled_in, sums_in, *outs
):
    mixed_out, sums_out, squares, products = outs
    group, groups = at

    @pl.when(group == 0)
    def _():
        squares[...] = jnp.zeros_like(squares)
        products[...] = jnp.zeros_like(products)

    carried = dot(c_rows[0], state[0])
    lifted = jnp.exp(columns_of(cumul_in[...]))
    square, product = squares[...], products[...]
    for head in range(mixed_in.shape[1] // 128):
        lanes = slice(head * 128, head * 128 + 128)
        mixed = mixed_in[:, lanes] + lifted[:, head : head + 1] * carried[:, lanes]
        mixed_out[:, lanes] = mixed
        gated = mixed * gate_in[:, lanes]
        square = square + gated * gated
        product = product + mixed * scaled_in[:, lanes]
    squares[...] = square
    products[...] = product

    @pl.when(group == groups - 1)
    def _():
        sums_out[...] = sums_in[...]
        sums_out[0:1, :] += jnp.sum(squares[...].T, axis=0, keepdims=True)
        sums_out[1:2, :] += jnp.sum(products[...].T, axis=0, keepdims=True)


def square_body(at, base, mixed_in, gate_in, squared):
    for start in range(0, mixed_in.shape[1], 128):
        lanes = slice(start, start + 128)
        gate = gate_in[:, lanes]
        squared[:, lanes] = mixed_in[:, lanes] * gate * gate


def norm_scales(at, inner, sums, alpha, beta):
    @pl.when(at[0] == 0)
    def _():
        total = sums[0][...]
        for part in sums[1:]:
            total = total + part[...]
        inv_rms = lax.rsqrt(total[0:1, :] / inner + EPS)
        mean_dot = inv_rms * total[1:2, :] / inner
        alpha[...] = jnp.broadcast_to(inv_rms, alpha.shape).T
        beta[...] = jnp.broadcast_to(inv_rms * inv_rms * mean_dot, beta.shape).T


def grad_mixed_body(inner, parts, at, base, *refs):
    sums = refs[:parts]
    squared, scaled_in, lifted_c, grad_mixed, state_out, alpha, beta = refs[parts:]
    norm_scales(at, inner, sums, alpha, beta)
    for start in range(0, squared.shape[1], 128):
        lanes = slice(start, start + 128)
        low = (alpha[...] * scaled_in[:, lanes] - beta[...] * squared[:, lanes]).astype(BF16)
        grad_mixed[:, lanes] = low
        state_out[0, :, lanes] = dot(lifted_c[:, lanes], low).astype(BF16)


def grad_z_body(inner, parts, at, base, *refs):
    sums = refs[:parts]
    mixed_in, z_in, grad_in, gain, grad_z, alpha, beta = refs[parts:]
    norm_scales(at, inner, sums, alpha, beta)
    for start in range(0, z_in.shape[1], 128):
        lanes = slice(start, start + 128)
        z = z_in[:, lanes].astype(F32)
        sigma = sigmoid(z)
        mixed = mixed_in[:, lanes]
        scaled = grad_in[:, lanes].astype(F32) * gain[:, lanes]
        grad_gated = alpha[...] * scaled - beta[...] * (mixed * (z * sigma))
        grad_z[:, lanes] = (grad_gated * mixed * (sigma * (1.0 + z * (1.0 - sigma)))).astype(BF16)


def inner_back_body(
    last,
    at,
    base,
    gram,
    bc,
    step_in,
    cumul_in,
    x_in,
    grad_in,
    state_in,
    rows,
    sums_in,
    grad_x,
    q_out,
    r_out,
    bc_out,
    z_sum,
    c_sum,
):
    group, groups = at
    length = x_in.shape[0]

    @pl.when(group == 0)
    def _():
        z_sum[...] = sums_in[0]
        c_sum[...] = sums_in[1]

    cumul = cumul_in[...]
    cumul_columns = columns_of(cumul)
    lifted = jnp.exp(cumul_columns)
    state = state_in[0]
    c_rows = bc[1].astype(F32)
    lane = lax.broadcasted_iota(jnp.int32, (length, 128), 1)
    q_columns = jnp.zeros((length, 128), F32)
    for head in range(x_in.shape[1] // 128):
        lanes = slice(head * 128, head * 128 + 128)
        step = step_in[head : head + 1, :]
        decay = jnp.exp(
            jnp.minimum(cumul_columns[:, head : head + 1] - cumul[head : head + 1, :], 0.0)
        )
        gram_decay = gram[...] * decay
        mixer = (gram_decay * step).astype(BF16)
        x_head, grad_head = x_in[:, lanes], grad_in[:, lanes]
        product = dot_rows(grad_head, x_head)
        z_sum[...] += product * decay * step
        gram_grad = product * gram_decay
        r_out[head : head + 1, :] = jnp.sum(gram_grad, axis=0, keepdims=True)
        handed = lifted[:, head : head + 1] * dot_rows(grad_head, state[:, lanes])
        c_sum[...] += handed
        q = jnp.sum(gram_grad * step + c_rows * handed, axis=1, keepdims=True)
        q_columns = jnp.where(lane == head, q, q_columns)
        grad_x[:, lanes] = dot_columns(mixer, grad_head) + rows[1:2, lanes] * grad_head.astype(F32)
    q_out[...] = q_columns.T[:GROUP, :]

    @pl.when(group == groups - 1)
    def _():
        if last:
            summed = jnp.where(triangle(length, False), z_sum[...], 0.0)
            bc_out[0] = dot_split(summed.T, bc[1])
            bc_out[1] = c_sum[...] + dot_split(summed, bc[0])
        else:
            bc_out[0] = z_sum[...]
            bc_out[1] = c_sum[...]


def block_weights(step, cumul):
    return columns_of(jnp.exp(cumul[:, cumul.shape[1] - 1 :] - cumul) * step)


def rim_body(last, at, base, bc, step_in, cumul_in, weighted_x, partial, slope, out_in, *refs):
    group, groups = at
    width = weighted_x.shape[1]
    if last:
        rows_before, b_before, bc_partial, bc_slope, rim_out, bc_out, b_sum = refs
    else:
        rim_out, b_sum = refs

    @pl.when(group == 0)
    def _():
        b_sum[...] = b_before[...] if last else jnp.zeros_like(b_sum)

    out_low = out_in[0]
    b_sum[...] += dot_rows(weighted_x[...], out_low)
    weights = block_weights(step_in[...], cumul_in[...])[0:8, :]
    returned = dot(bc[0][0:16, :], out_low)[0:8, :]
    start = group
    if last:
        count = rim_out.shape[1] // width
        start = lax.rem(group + count - groups + first_group(base), count)
    for head in range(width // 128):
        lanes = slice(head * 128, head * 128 + 128)
        weight = weights[:, head : head + 1]
        rows = (partial[0:8, lanes] + weight * returned[:, lanes]) * slope[0:8, lanes]
        place = pl.multiple_of(jnp.int32(start) * width + head * 128, 128)
        rim_out[:, pl.ds(place, 128)] = rows[0:3, :]

    if last:

        @pl.when(group == groups - 1)
        def _():
            before = rows_before.shape[1]
            if before < rim_out.shape[1] - 256:
                place = pl.multiple_of(first_group(base) * width, 128)
                rim_out[:, pl.ds(place, before)] = rows_before[...]
            bc_out[0] = (b_sum[...] + bc_partial[0]) * bc_slope[0]
            bc_out[1] = bc_partial[1] * bc_slope[1]
            for j in range(2):
                lanes = rim_out.shape[1] - 256 + 128 * j
                rim_out[:, lanes : lanes + 128] = bc_out[j, 0:3, :]


def grad_dt_body(
    at,
    base,
    bc,
    rate,
    dt_slope,
    step_in,
    cumul_in,
    q_in,
    r_in,
    x_in,
    state_in,
    out_in,
    grad_dt,
    selector,
    products,
):
    length, width = x_in.shape

    @pl.when(at[0] == 0)
    def _():
        row = lax.broadcasted_iota(jnp.int32, (width, 128), 0)
        lane = lax.broadcasted_iota(jnp.int32, (width, 128), 1)
        selector[...] = (row // 128 == lane).astype(BF16)

    cumul, step = cumul_in[...], step_in[...]
    state, out_low = state_in[0], out_in[0]
    returned = dot(bc[0], out_low)
    for start in range(0, width, 128):
        lanes = slice(start, start + 128)
        products[:, lanes] = (x_in[:, lanes].astype(F32) * returned[:, lanes]).astype(BF16)
    inner_b = dot(products[...], selector[...]).T[:GROUP, :]
    w = jnp.exp(cumul[:, length - 1 :] - cumul) * inner_b
    dots = dot(jnp.ones((16, length), BF16), state * out_low)[:GROUP, :]
    row = lax.broadcasted_iota(jnp.int32, (GROUP, width), 0)
    lane = lax.broadcasted_iota(jnp.int32, (GROUP, width), 1)
    dots = jnp.sum(jnp.where(lane // 128 == row, dots, 0.0), axis=1, keepdims=True)
    q, r = q_in[...], r_in[...]
    inside = jnp.sum(step * w, axis=1, keepdims=True)
    end = inside + jnp.exp(cumul[:, length - 1 :]) * dots
    last = lax.broadcasted_iota(jnp.int32, (GROUP, length), 1) == length - 1
    grad_cumul = q - step * (r + w) + jnp.where(last, end, 0.0)
    grad_log = dot_split(grad_cumul, triangle(length, False).astype(BF16))
    grad_dt[...] = (r + w + rate[...] * grad_log) * dt_slope[...]


def grad_x_body(
    at,
    base,
    bc,
    step_in,
    cumul_in,
    partial,
    slope,
    taps,
    halo,
    out_in,
    grad_x,
    ext,
):
    length, width = partial.shape
    weights = block_weights(step_in[...], cumul_in[...])
    returned = dot(bc[0], out_in[0])
    for head in range(width // 128):
        lanes = slice(head * 128, head * 128 + 128)
        weight = weights[:, head : head + 1]
        ext[0:length, :] = (partial[:, lanes] + weight * returned[:, lanes]) * slope[:, lanes]
        ext[length : length + 3, :] = halo[:, lanes]
        total = taps[0:1, lanes] * ext[3 : 3 + length, :]
        for k in range(1, 4):
            total = total + taps[k : k + 1, lanes] * ext[3 - k : 3 - k + length, :]
        grad_x[:, lanes] = total.astype(BF16)


def bc_back_body(at, place, grad_pre, halo, taps, kept, sent, ext, total):
    length, half = grad_pre.shape[1], kept.shape[1]
    for j in range(2):
        ext[0:length, :] = grad_pre[j]
        ext[length : length + 3, :] = halo[:, 128 * j : 128 * j + 128]
        summed = taps[j, 0:1, :] * ext[3 : 3 + length, :]
        for k in range(1, 4):
            summed = summed + taps[j, k : k + 1, :] * ext[3 - k : 3 - k + length, :]
        total[...] = summed
        kept[j] = total[pl.ds(pl.multiple_of(place_bit(place, 3) * half, half), half), :]
        sent[j] = total[pl.ds(pl.multiple_of((1 - place_bit(place, 3)) * half, half), half), :]


def bc_half_body(at, place, mine, taken, kept, sent, total):
    half = kept.shape[1]
    for j in range(2):
        total[...] = mine[j] + taken[j]
        kept[j] = total[pl.ds(pl.multiple_of(place_bit(place, 4) * half, half), half), :]
        sent[j] = total[pl.ds(pl.multiple_of((1 - place_bit(place, 4)) * half, half), half), :]


def bc_last_body(at, _, mine, taken, out):
    out[...] = (mine[...] + taken[...]).astype(BF16)


def conv_back(extended, weights):
    length = extended.shape[-2] - 3
    summed = weights[..., 0, :][..., None, :] * extended[..., 3 : 3 + length, :]
    for k in range(1, 4):
        summed = (
            summed
            + weights[..., k, :][..., None, :] * extended[..., 3 - k : 3 - k + length, :]
        )
    return summed


def shards(
    x_input,
    z_input,
    bc_input,
    dt_raw,
    dt_bias,
    a_log,
    d_skip,
    conv_x,
    convolution_bc_taps,
    rescale_factor,
    grad_out,
):
    length, channels = x_input.shape
    heads = dt_raw.shape[0]
    groups = heads // GROUP
    width = GROUP * 128
    count, parts = lax.axis_size("seq"), lax.axis_size("head")
    inner = channels * parts
    own = lax.axis_index("seq")
    split = count == 8 and groups == 4
    own_half = groups // 2 if split else groups
    bit = lambda value, place: lax.shift_right_logical(value, place) & 1
    along_head = lax.axis_index("head")
    base = bit(own, 0) * own_half if split else own * 0
    for place, value in enumerate(
        (bit(own, 2), bit(own, 1), bit(own, 0), bit(along_head, 1), bit(along_head, 0))
    ):
        base = base | lax.shift_left(value, 8 + place)
    base = base.astype(jnp.int32)[None]

    whole = lambda *shape: ((shape, lambda g, b: (0,) * len(shape)),)
    wide_at = lambda off: (Groups("wide", (length, width), off, groups),)
    rows_at = lambda off: (Groups("heads", (GROUP, length), off, groups),)
    lanes_at = lambda n, off: (Groups("wide", (n, width), off, groups),)
    slot = (Groups("slots", (1, length, width), 0, groups),)
    full = lambda array: (array,) + whole(*array.shape)
    half_width = own_half * width
    half_heads = own_half * GROUP
    half = lambda n: (Groups("half", (n, width), 0, groups),)
    half_rows = (Groups("half heads", (GROUP, length), 0, groups),)
    window_at = lambda n, off: (Groups("window", (n, width), off, groups),)
    window_rows_at = lambda off: (Groups("window heads", (GROUP, length), off, groups),)
    halves = [own_half, 0] if split else [0]
    rest = halves[0]

    gain = rescale_factor[None, :]
    f32 = lambda *shape: (shape, F32)
    low = lambda *shape: (shape, BF16)

    step, cumul, rate, dt_slope, rows, rim = call(
        steps_body,
        [
            f32(heads, length) + whole(heads, length),
            f32(heads, length) + whole(heads, length),
            f32(heads, length) + whole(heads, length),
            f32(heads, length) + whole(heads, length),
            f32(2, channels) + whole(2, channels),
            low(3, channels + 256) + whole(3, channels + 256),
        ],
        [
            full(in_hbm(dt_raw)),
            full(in_hbm(dt_bias[None, :])),
            full(in_hbm(a_log[None, :])),
            full(in_hbm(d_skip[None, :])),
            (in_hbm(x_input), ((16, channels), lambda g, b: (length // 16 - 1, 0))),
            (in_hbm(bc_input), ((2, 16, 128), lambda g, b: (0, length // 16 - 1, 0))),
        ],
        base=base,
    )
    rim_sent = rim
    rim = lax.ppermute(rim, "seq", [(i - 1, i) for i in range(1, count)])
    if split:
        swap = lambda block, bit: lax.ppermute(
            block, "seq", [(i, i ^ bit) for i in range(count)]
        )
        total = rows[0:1]
        total_core = swap(total, 1)
        chip_total = total + total_core
        total_across = swap(chip_total, 2)
        table = f32(16, channels) + whole(16, channels)
        ahead, behind = call(
            weights_body,
            [table, table],
            [full(rows), full(total_core), full(total_across)],
            base=base,
            )

    def passed(locals_, reverse, beside):
        if split:
            local_sent, local = locals_[rest], locals_[0]
            weights = behind if reverse else ahead
            return scan_blocks(base, groups, weights, local, local_sent, reverse, beside)
        local = locals_[0]
        for work in beside:
            work(local)
        return gather_blocks(rows[0:1], local, reverse)

    x_low, slope, local = {}, {}, {}
    ready = rim_sent
    for off in halves:
        x_low[off], slope[off] = call(
            conv_body,
            [low(length, half_width) + half(length), f32(length, half_width) + half(length)],
            [(in_hbm(x_input),) + wide_at(off), (in_hbm(conv_x),) + lanes_at(4, off)],
            base=base,
            grid=own_half,
            scratch=[pltpu.VMEM((length + 8, 128), F32)],
            after=[ready],
        )
        first = off == rest
        top = (Groups("top", (16, width), 0, groups),)
        ins = [
            (x_low[off],) + half(length),
            (in_hbm(x_input),) + window_at(16, off),
            (rim,) + lanes_at(3, off),
            (in_hbm(conv_x),) + window_at(4, off),
            (step,) + rows_at(off),
            (cumul,) + rows_at(off),
        ]
        outs = [
            f32(length, half_width) + top,
            low(length, half_width) + top,
            low(own_half, length, width) + slot,
        ]
        scratch = [pltpu.VMEM((24, width), F32)]
        if first:
            ins += [
                full(in_hbm(bc_input)),
                (rim, ((3, 256), lambda g, b: (0, channels // 256))),
                full(in_hbm(convolution_bc_taps)),
            ]
            outs += [
                low(2, length, 128) + whole(2, length, 128),
                f32(2, length, 128) + whole(2, length, 128),
                f32(length, length) + whole(length, length),
                f32(128, length) + whole(128, length),
            ]
            scratch += [pltpu.VMEM((length + 8, 128), F32)]
        else:
            ins += [full(b_turned)]
        result = call(
            functools.partial(state_body, first),
            outs,
            ins,
            base=base,
            loop=own_half,
            scratch=scratch,
            carry=[slope[off]],
            place={0: 1},
            flops=2 * length * 128 * half_width,
        )
        if first:
            bc, bc_slope, gram, b_turned = result[3:]
        slope[off], x_low[off], local[off] = result[:3]
        ready = local[off]

    inside, gate, scaled = {}, {}, {}

    def mix_inside(off, ready):
        inside[off], token = call(
            inner_body,
            [f32(length, half_width) + half(length)],
            [
                full(gram),
                (step,) + rows_at(off),
                (cumul,) + rows_at(off),
                (x_low[off],) + half(length),
                (rows,) + lanes_at(2, off),
            ],
            base=base,
            loop=own_half,
            after=[ready],
            token=True,
            flops=2 * length * 128 * half_width,
        )
        return token

    def gates(off, ready):
        gate[off], scaled[off], token = call(
            gate_body,
            [f32(length, half_width) + half(length), f32(length, half_width) + half(length)],
            [
                (z_input,) + wide_at(off),
                (grad_out,) + wide_at(off),
                (gain,) + lanes_at(1, off),
            ],
            base=base,
            loop=own_half,
            after=[ready],
            token=True,
        )
        return token

    def mix_second(ready):
        tokens = [mix_inside(rest, ready)] if split else []
        tokens += [gates(off, ready) for off in reversed(halves)]
        return [], tokens

    states = passed(local, False, (functools.partial(mix_inside, 0), mix_second))
    states = dict(zip((0, rest), states))
    mixed, sums = {}, jnp.zeros((8, length), F32)
    two_scales = [pltpu.VMEM((length, 128), F32), pltpu.VMEM((length, 128), F32)]
    for off in reversed(halves):
        mixed[off], sums = call(
            mix_body,
            [f32(length, half_width) + half(length), f32(8, length) + whole(8, length)],
            [
                (inside[off],) + half(length),
                (bc, ((1, length, 128), lambda g, b: (1, 0, 0))),
                (cumul,) + rows_at(off),
                (states[off],) + slot,
                (gate[off],) + half(length),
                (scaled[off],) + half(length),
                full(sums),
            ],
            base=base,
            loop=own_half,
            scratch=two_scales,
            flops=2 * length * 128 * half_width,
        )
    turn_head = lambda block, bit: lax.ppermute(
        block, "head", [(i, i ^ bit) for i in range(parts)]
    )
    weighted_x, lifted_c, squared = {}, {}, {}
    for off in halves:
        weighted_x[off], lifted_c[off] = call(
            lift_body,
            [low(length, half_width) + half(length), low(length, half_width) + half(length)],
            [
                full(bc),
                (step,) + rows_at(off),
                (cumul,) + rows_at(off),
                (x_low[off],) + half(length),
            ],
            base=base,
            loop=own_half,
            scratch=[pltpu.VMEM((128, length), F32)],
            after=[sums],
        )
        (squared[off],) = call(
            square_body,
            [f32(length, half_width) + half(length)],
            [(mixed[off],) + half(length), (gate[off],) + half(length)],
            base=base,
            loop=own_half,
        )
    if parts == 4:
        sums = sums + turn_head(sums, 1)
        all_sums = [sums, turn_head(sums, 2)]
    else:
        all_sums = [lax.psum(sums, "head")]
    grad_mixed, local_back = {}, {}
    for off in halves:
        grad_mixed[off], local_back[off] = call(
            functools.partial(grad_mixed_body, inner, len(all_sums)),
            [low(length, half_width) + half(length), low(own_half, length, width) + slot],
            [full(part) for part in all_sums]
            + [
                (squared[off],) + half(length),
                (scaled[off],) + half(length),
                (lifted_c[off],) + half(length),
            ],
            base=base,
            loop=own_half,
            scratch=two_scales,
            flops=2 * length * 128 * half_width,
        )

    partial, q_rows, r_rows = {}, {}, {}
    carried = {"sums": jnp.zeros((2, length, 128), F32), "z": [], "dt": [], "x": []}

    def back_inside(off, ready):
        partial[off], q_rows[off], r_rows[off], carried["sums"], token = call(
            functools.partial(inner_back_body, off == rest),
            [
                f32(length, half_width) + half(length),
                f32(half_heads, length) + half_rows,
                f32(half_heads, length) + half_rows,
                f32(2, length, 128) + whole(2, length, 128),
            ],
            [
                full(gram),
                full(bc),
                (step,) + rows_at(off),
                (cumul,) + rows_at(off),
                (x_low[off],) + half(length),
                (grad_mixed[off],) + half(length),
                (states[off],) + slot,
                (rows,) + lanes_at(2, off),
                full(carried["sums"]),
            ],
            base=base,
            loop=own_half,
            scratch=[pltpu.VMEM((length, length), F32), pltpu.VMEM((length, 128), F32)],
            after=[ready],
            token=True,
            flops=6 * length * 128 * half_width,
        )
        return token

    def back_gates(off, ready):
        grad_z, token = call(
            functools.partial(grad_z_body, inner, len(all_sums)),
            [low(length, channels) + window_at(length, off)],
            [full(part) for part in all_sums]
            + [
                (mixed[off],) + half(length),
                (z_input,) + wide_at(off),
                (grad_out,) + wide_at(off),
                (gain,) + lanes_at(1, off),
            ],
            base=base,
            loop=own_half,
            scratch=two_scales,
            carry=carried["z"],
            after=[ready],
            token=True,
        )
        carried["z"] = [grad_z]
        carried["z_token"] = token
        return token

    def back_second(ready):
        token = back_inside(rest, ready) if split else ready
        return [token], [back_gates(0, token)]

    backs = passed(local_back, True, (functools.partial(back_inside, 0), back_second))
    backs = dict(zip((0, rest), backs))
    z_tokens = [back_gates(rest, carried["z_token"])] if split else []

    def make_grad_dt(off, after):
        grad_dt, token = call(
            grad_dt_body,
            [f32(heads, length) + window_rows_at(off)],
            [
                full(bc),
                (rate,) + rows_at(off),
                (dt_slope,) + rows_at(off),
                (step,) + rows_at(off),
                (cumul,) + rows_at(off),
                (q_rows[off],) + half_rows,
                (r_rows[off],) + half_rows,
                (x_low[off],) + half(length),
                (states[off],) + slot,
                (backs[off],) + slot,
            ],
            base=base,
            loop=own_half,
            scratch=[pltpu.VMEM((width, 128), BF16), pltpu.VMEM((length, width), BF16)],
            carry=carried["dt"],
            after=after,
            token=True,
            flops=4 * length * 128 * half_width,
        )
        carried["dt"] = [grad_dt]
        return token

    def make_grad_x(off, after):
        grad_x, token = call(
            grad_x_body,
            [low(length, channels) + window_at(length, off)],
            [
                full(bc),
                (step,) + rows_at(off),
                (cumul,) + rows_at(off),
                (partial[off],) + half(length),
                (slope[off],) + half(length),
                (conv_x,) + lanes_at(4, off),
                (rim_back,) + lanes_at(3, off),
                (backs[off],) + slot,
            ],
            base=base,
            loop=own_half,
            scratch=[pltpu.VMEM((length + 8, 128), F32)],
            carry=carried["x"],
            after=after,
            token=True,
            flops=2 * length * 128 * half_width,
        )
        carried["x"] = [grad_x]
        return token

    def make_rim(off, before, after):
        last = off == rest
        if last:
            outs = [
                f32(3, channels + 256) + whole(3, channels + 256),
                f32(2, length, 128) + whole(2, length, 128),
            ]
        else:
            outs = [f32(3, half_width) + whole(3, half_width), f32(length, 128) + whole(length, 128)]
        return call(
            functools.partial(rim_body, last),
            outs,
            [
                full(bc),
                (step,) + rows_at(off),
                (cumul,) + rows_at(off),
                (weighted_x[off],) + half(length),
                (partial[off],) + half(length),
                (slope[off],) + half(length),
                (backs[off],) + slot,
            ]
            + [full(array) for array in before],
            base=base,
            loop=own_half,
            scratch=[pltpu.VMEM((length, 128), F32)] if last else [],
            after=after,
            flops=2 * length * 128 * half_width,
        )

    if split:
        before = make_rim(0, [], [])
        z_tokens.append(make_grad_dt(0, [before[1]]))
    else:
        before = [jnp.zeros((3, channels), F32), jnp.zeros((length, 128), F32)]
    rim_back, grad_bc_pre = make_rim(rest, [*before, carried["sums"], bc_slope], z_tokens)
    rim_back = lax.ppermute(rim_back, "seq", [(i, i - 1) for i in range(1, count)])
    dt_token = make_grad_dt(rest, [grad_bc_pre])
    if parts == 4:
        piece = lambda rows: f32(2, rows, 128) + whole(2, rows, 128)
        kept, sent = call(
            bc_back_body,
            [piece(length // 2), piece(length // 2)],
            [
                full(grad_bc_pre),
                (rim_back, ((3, 256), lambda g, b: (0, channels // 256))),
                full(convolution_bc_taps),
            ],
            base=base,
            scratch=[pltpu.VMEM((length + 8, 128), F32), pltpu.VMEM((length, 128), F32)],
            after=[dt_token],
        )
        taken = turn_head(sent, 2)
        x_tokens = [make_grad_x(0, [sent])]
        kept, sent = call(
            bc_half_body,
            [piece(length // 4), piece(length // 4)],
            [full(kept), full(taken)],
            base=base,
            scratch=[pltpu.VMEM((length // 2, 128), F32)],
            after=x_tokens,
        )
        taken = turn_head(sent, 1)
        x_tokens = [make_grad_x(rest, [sent])] if split else []
        (grad_bc,) = call(
            bc_last_body,
            [low(2, length // 4, 128) + whole(2, length // 4, 128)],
            [full(kept), full(taken)],
            base=base,
            after=x_tokens,
        )
    else:
        for off in halves:
            make_grad_x(off, [])
        bc_halo = jnp.moveaxis(rim_back[:, channels:].reshape(3, 2, 128), 1, 0)
        bc_sum = conv_back(jnp.concatenate([grad_bc_pre, bc_halo], axis=1), convolution_bc_taps)
        share = length // parts
        bc_sum = lax.psum(bc_sum, "head")
        grad_bc = lax.dynamic_slice_in_dim(bc_sum, along_head * share, share, 1).astype(BF16)
    return (carried["x"][0], carried["z"][0], grad_bc, carried["dt"][0])


def solution(mesh):
    return jax.shard_map(
        shards,
        mesh=mesh,
        in_specs=(
            P("seq", "head"),
            P("seq", "head"),
            P(None, "seq", None),
            P("head", "seq"),
            P("head"),
            P("head"),
            P("head"),
            P(None, "head"),
            P(),
            P("head"),
            P("seq", "head"),
        ),
        out_specs=(
            P("seq", "head"),
            P("seq", "head"),
            P(None, ("seq", "head"), None),
            P("head", "seq"),
        ),
        check_vma=False,
    )
```

```python
import functools

import jax
import jax.numpy as jnp
from jax import lax
from jax.experimental import pallas as pl
from jax.experimental.pallas import tpu as pltpu
from jax.sharding import PartitionSpec as P

EPS = 1e-05
GROUP = 8
F32 = jnp.float32
BF16 = jnp.bfloat16
VMEM_BYTES = 16 * 2**20


def sigmoid(value):
    return 0.5 + 0.5 * jnp.tanh(0.5 * value)


def dot(a, b):
    return jnp.dot(a, b, preferred_element_type=F32)


def dot_split(a, b):
    high = a.astype(BF16)
    rest = a - high.astype(F32)
    middle = rest.astype(BF16)
    low = (rest - middle.astype(F32)).astype(BF16)
    return dot(high, b) + (dot(middle, b) + dot(low, b))


def dot_rows(a, b):
    return lax.dot_general(a, b, (((1,), (1,)), ((), ())), preferred_element_type=F32)


def dot_columns(a, b):
    return lax.dot_general(a, b, (((0,), (0,)), ((), ())), preferred_element_type=F32)


def triangle(length, upper):
    first = lax.broadcasted_iota(jnp.int32, (length, length), 0)
    second = lax.broadcasted_iota(jnp.int32, (length, length), 1)
    return first <= second if upper else first >= second


def columns_of(rows):
    return rows.T


class Groups:
    def __init__(self, kind, block, off, groups, size=1):
        self.kind, self.block, self.off, self.groups = kind, block, off, groups
        self.size = size
        self.by_rows = kind.endswith("heads")

    def turn(self, group, base):
        first = self.off + first_group(base)
        return lax.rem(group * self.size + first, self.groups) // self.size

    def place(self, index):
        return (index, 0) if self.by_rows else (0, index)

    def spec(self):
        if self.kind == "slots":
            return pl.BlockSpec(self.block, lambda g, b: (g, 0, 0))
        if self.kind.startswith("half"):
            return pl.BlockSpec(self.block, lambda g, b: self.place(g))
        return pl.BlockSpec(self.block, lambda g, b: self.place(self.turn(g, b)))

    def whole(self, shape, count):
        if self.kind.startswith("window"):
            block = list(self.block)
            block[0 if self.by_rows else 1] *= count
            return pl.BlockSpec(
                tuple(block), lambda g, b: self.place(self.turn(0, b) // count)
            )
        if self.kind == "top":
            shape = (self.block[0], count * self.block[1])
        return pl.BlockSpec(shape, lambda g, b: (0,) * len(shape))

    def view(self, ref, group, base):
        if self.kind == "slots":
            return ref.at[pl.ds(group, 1)]
        if self.kind in ("wide", "heads"):
            group = self.turn(group, base)
        size = self.block[0 if self.by_rows else 1]
        span = pl.ds(pl.multiple_of(jnp.int32(group) * size, size), size)
        return ref.at[span] if self.by_rows else ref.at[:, span]


def call(
    body,
    outs,
    ins,
    *,
    base,
    grid=1,
    loop=1,
    scratch=(),
    after=(),
    carry=(),
    place=None,
    token=False,
    flops=0,
):
    aliases = {1 + len(ins) + len(after) + i: i for i in range(len(carry))}
    for read, written in (place or {}).items():
        aliases[1 + read] = written
    after = list(after) + list(carry)
    outs = list(outs)
    if token:
        outs.append(((8, 128), F32, ((8, 128), lambda *_: (0, 0))))

    def spec(shape, block):
        if not isinstance(block, Groups):
            return pl.BlockSpec(*block)
        return block.whole(shape, loop) if grid == 1 else block.spec()

    in_specs = [spec(array.shape, block) for array, block in ins]
    in_specs += [pl.BlockSpec(memory_space=pl.ANY) for _ in after]
    out_specs = [spec(shape, block) for shape, _, block in outs]
    out_shape = [jax.ShapeDtypeStruct(shape, dtype) for shape, dtype, _ in outs]
    arrays = [array for array, _ in ins]
    moved = sum(a.size * a.dtype.itemsize for a in arrays + out_shape)
    blocks = [block for _, block in ins] + [block for _, _, block in outs]

    def ordered(where, *refs):
        taken, rest = refs[: len(ins)], refs[len(ins) + len(after) :]
        results, extra = rest[: len(outs)], rest[len(outs) :]
        if token:
            results[-1][...] = jnp.zeros((8, 128), F32)

        def step(group, _):
            views = [
                block.view(ref, group, where) if isinstance(block, Groups) else ref
                for ref, block in zip(taken + results, blocks)
            ]
            if token:
                views = views[:-1]
            body((group, loop), where, *views, *extra)
            return 0

        if grid > 1:
            views = taken + (results[:-1] if token else results)
            body((pl.program_id(0), grid), where, *views, *extra)
        elif loop > 1:
            lax.fori_loop(0, loop, step, 0)
        else:
            step(0, 0)

    return pl.pallas_call(
        ordered,
        out_shape=out_shape,
        grid_spec=pltpu.PrefetchScalarGridSpec(
            num_scalar_prefetch=1,
            grid=(grid,),
            in_specs=in_specs,
            out_specs=out_specs,
            scratch_shapes=list(scratch),
        ),
        input_output_aliases=aliases,
        cost_estimate=pl.CostEstimate(flops=flops, bytes_accessed=moved, transcendentals=0),
        compiler_params=pltpu.CompilerParams(vmem_limit_bytes=VMEM_BYTES),
    )(base, *arrays, *after)


def in_hbm(array):
    return pltpu.with_memory_space_constraint(array, pltpu.HBM)


def column_of(row):
    count = row.shape[1]
    first = lax.broadcasted_iota(jnp.int32, (count, count), 0)
    second = lax.broadcasted_iota(jnp.int32, (count, count), 1)
    return jnp.sum(jnp.where(first == second, row, 0.0), axis=1, keepdims=True)


def steps_body(
    at,
    base,
    raw,
    bias,
    log_rate,
    skip,
    x_tail,
    bc_in,
    bc_taps,
    step_out,
    cumul_out,
    rate_out,
    slope_out,
    rows_out,
    rim_out,
    bc_in_out,
    bc_taps_out,
):
    bc_in_out[...] = bc_in[...]
    bc_taps_out[...] = bc_taps[...]
    heads, length = raw.shape
    channels = x_tail.shape[1]
    rim_out[:, 0:channels] = x_tail[...].astype(F32)[13:16, :].astype(BF16)
    for j in range(2):
        start = channels + 128 * j
        rim_out[:, start : start + 128] = bc_in[j, length - 16 :].astype(F32)[13:16, :].astype(BF16)
    shifted = raw[...] + column_of(bias[...])
    step = jnp.maximum(shifted, 0.0) + jnp.log1p(jnp.exp(-jnp.abs(shifted)))
    rate = jnp.broadcast_to(-jnp.exp(column_of(log_rate[...])), step.shape)
    cumul = dot_split(rate * step, triangle(length, True).astype(BF16))
    step_out[...] = step
    cumul_out[...] = cumul
    rate_out[...] = rate
    slope_out[...] = sigmoid(shifted)
    skips = column_of(skip[...])
    for head in range(heads):
        lanes = slice(head * 128, head * 128 + 128)
        rows_out[0:1, lanes] = jnp.broadcast_to(cumul[head : head + 1, length - 1 :], (1, 128))
        rows_out[1:2, lanes] = jnp.broadcast_to(skips[head : head + 1, :], (1, 128))


def pick(test, yes, no):
    return jnp.where(test, yes, no)


def first_group(place):
    return place[0] & 255


def place_bit(place, index):
    return lax.shift_right_logical(place[0], 8 + index) & 1


def weights_body(at, place, own, core, across, *outs):
    t0, t1 = own[0:1, :], core[...]
    e0, e1, own_chip, ex = jnp.exp(t0), jnp.exp(t1), jnp.exp(t0 + t1), jnp.exp(across[...])
    one = jnp.ones_like(e0)
    zero = jnp.zeros_like(e0)
    bits = [place_bit(place, i) for i in range(3)]
    x_first = bits[2] == 0
    for out, reverse in zip(outs, (False, True)):
        y, x, c = ((1 - bit if reverse else bit) == 1 for bit in bits)
        either = jnp.logical_or(x, y)
        scale = pick(jnp.logical_or(x_first, either), one, ex)
        rows = [pick(c, one, e1), pick(c, e0, one)]
        rows += [rows[0] * scale, rows[1] * scale]
        rows += [
            pick(x_first, pick(x, one, ex), pick(jnp.logical_and(x, y), zero, one)),
            pick(x_first, pick(x, own_chip, one), pick(y, pick(x, one, own_chip), zero)),
        ]
        a = pick(x_first, pick(x, one, zero), pick(y, pick(x, ex, one), zero))
        b = pick(x_first, pick(y, pick(x, ex, one), zero), pick(either, one, zero))
        into, send = pick(c, e1, one), pick(c, one, e0)
        rows += [into * a, into * b, pick(c, one, zero)]
        rows += [send * a, send * b, pick(c, zero, one)]
        for index, row in enumerate(rows):
            out[index : index + 1, :] = row


def combine(base, groups, weights, outs, after=(), slots_of=None, at=0, carry=()):
    arrays, columns = [], []
    for slots in outs:
        for column, terms in slots:
            if column not in columns:
                columns.append(column)
            for _, (array, slot) in terms:
                if not any(array is a and slot == s for a, s in arrays):
                    arrays.append((array, slot))
    place = lambda array, slot: [
        i for i, (a, s) in enumerate(arrays) if a is array and s == slot
    ][0]
    plan = [
        [
            (columns.index(column), [(row, place(*source)) for row, source in terms])
            for column, terms in slots
        ]
        for slots in outs
    ]

    def body(at, base, *refs):
        rows, values = refs[: len(columns)], refs[len(columns) : len(columns) + len(arrays)]
        results = refs[len(columns) + len(arrays) :]
        width = rows[0].shape[1]
        for result, slots in zip(results, plan):
            for slot, (column, terms) in enumerate(slots):
                for start in range(0, width, 256):
                    lanes = slice(start, start + 256)
                    total = None
                    for row, index in terms:
                        term = rows[column][row : row + 1, lanes] * values[index][
                            0, :, lanes
                        ].astype(F32)
                        total = term if total is None else total + term
                    result[slot, :, lanes] = total.astype(BF16)

    length, width = arrays[0][0].shape[1:]
    block = lambda slot, count: ((count, length, width), lambda g, b: (slot, 0, 0))
    ins = [
        (
            weights,
            (
                (weights.shape[0], width),
                lambda g, b, column=column: (0, lax.rem(first_group(b) + column, groups)),
            ),
        )
        for column in columns
    ]
    ins += [(array, block(slot, 1)) for array, slot in arrays]
    results = [
        ((slots_of or len(slots), length, width), BF16, block(at, len(slots))) for slots in outs
    ]
    return call(body, results, ins, base=base, after=after, carry=carry)


def scan_blocks(base, groups, weights, local, local_sent, reverse, beside):
    count = lax.axis_size("seq")
    place = lambda position: count - 1 - position if reverse else position

    def swap(block, bit_of, keep):
        route = [
            (place(i), place(i ^ bit_of(place(i) % 2)))
            for i in range(count)
            if keep(i, place(i) % 2)
        ]
        return lax.ppermute(block, "seq", route)

    def merge(slot, *plans, **places):
        outs = [[(slot, list(zip(rows, sources)))] for rows, sources in plans]
        return combine(base, groups, weights, outs, **places)

    everyone = lambda i, core: True
    across = lambda block: swap(
        block, lambda core: 4 if core else 2, lambda i, core: i < 4 if core else i < 6
    )
    onward = lambda block: swap(
        block,
        lambda core: 2 if core else 4,
        lambda i, core: i not in (2, 3) if core else i < 4,
    )
    taken = swap(local_sent, lambda core: 1, everyone)
    chips, first_taken, sent, second_taken = [], [], [], []
    after = []
    for slot in range(2):
        both = ((local, slot), (taken, slot))
        chip, chip_sent = merge(slot, ((0, 1), both), ((2, 3), both), after=after)
        chips.append(chip)
        first_taken.append(across(chip_sent))
        if slot == 0:
            after = [beside[0](chip)]
    for slot in range(2):
        sources = ((chips[slot], 0), (first_taken[slot], 0))
        (block,) = merge(slot, ((4, 5), sources))
        sent.append(block)
        second_taken.append(onward(block))
    after = beside[1](sent[1])
    carry = []
    for slot in range(2):
        sources = ((first_taken[slot], 0), (second_taken[slot], 0))
        mine, handed = merge(
            slot,
            ((6, 7, 8), (*sources, (taken, slot))),
            ((9, 10, 11), (*sources, (local, slot))),
            after=after[slot],
            slots_of=2,
            at=slot,
            carry=carry,
        )
        carry = [mine, handed]
    return mine, swap(handed, lambda core: 1, everyone)


def gather_blocks(totals, local, reverse):
    table = lax.all_gather(totals, "seq", axis=0, tiled=True)
    blocks = lax.all_gather(local[None], "seq", axis=0, tiled=True)
    own = lax.axis_index("seq")
    order = jnp.arange(table.shape[0], dtype=jnp.int32)
    if reverse:
        inside = (order[None, :] > own) & (order[None, :] < order[:, None])
        selected = order > own
    else:
        inside = (order[None, :] > order[:, None]) & (order[None, :] < own)
        selected = order < own
    exponent = jnp.sum(jnp.where(inside[:, :, None], table[None], 0.0), axis=1)
    factor = jnp.where(selected[:, None], jnp.exp(exponent), 0.0)
    factor = factor.reshape(factor.shape[0], local.shape[0], 1, local.shape[2])
    state = jnp.sum(factor * blocks.astype(F32), axis=0).astype(BF16)
    return state, state


def conv_body(at, base, x_in, taps, x_out, slope_out, top_out, taps_out, ext):
    length, width = x_in.shape
    top_out[...] = x_in[0:16, :]
    taps_out[...] = taps[...]
    ext[0:8, :] = jnp.zeros((8, 128), F32)
    for start in range(0, width, 128):
        lanes = slice(start, start + 128)
        ext[8 : 8 + length, :] = x_in[:, lanes].astype(F32)
        pre = taps[0:1, lanes] * ext[5 : 5 + length, :]
        for k in range(1, 4):
            pre = pre + taps[k : k + 1, lanes] * ext[5 + k : 5 + k + length, :]
        sigma = sigmoid(pre)
        x_out[:, lanes] = (pre * sigma).astype(BF16)
        slope_out[:, lanes] = sigma * (1.0 + pre * (1.0 - sigma))


def state_body(first, at, base, x_low, x_top, x_halo, taps, step_in, cumul_in, *refs):
    length, width = x_low.shape
    if first:
        bc_in, bc_halo, bc_taps, slope_out, x_out, state_out = refs[:6]
        bc_out, bc_slope_out, gram_out, b_turned, ext, bc_ext = refs[6:]

        @pl.when(at[0] == 0)
        def _():
            for j in range(2):
                bc_ext[5:8, :] = bc_halo[:, j * 128 : j * 128 + 128].astype(F32)
                bc_ext[8 : 8 + length, :] = bc_in[j].astype(F32)
                pre = bc_taps[j, 0:1, :] * bc_ext[5 : 5 + length, :]
                for k in range(1, 4):
                    pre = pre + bc_taps[j, k : k + 1, :] * bc_ext[5 + k : 5 + k + length, :]
                sigma = sigmoid(pre)
                bc_out[j] = (pre * sigma).astype(BF16)
                bc_slope_out[j] = sigma * (1.0 + pre * (1.0 - sigma))
            b_turned[...] = bc_out[0].astype(F32).T
            gram_out[...] = jnp.where(
                triangle(length, False), dot_rows(bc_out[1], bc_out[0]), 0.0
            )

    else:
        b_turned, slope_out, x_out, state_out, ext = refs

    top = x_top.shape[0]
    ext[5:8, :] = x_halo[...].astype(F32)
    ext[8 : 8 + top, :] = x_top[...].astype(F32)
    tail_step = jnp.exp(cumul_in[:, length - 1 :] - cumul_in[...]) * step_in[...]
    for head in range(width // 128):
        lanes = slice(head * 128, head * 128 + 128)
        pre = taps[0:1, lanes] * ext[5 : 5 + top, lanes]
        for k in range(1, 4):
            pre = pre + taps[k : k + 1, lanes] * ext[5 + k : 5 + k + top, lanes]
        sigma = sigmoid(pre)
        x_rows = (pre * sigma).astype(BF16)
        x_out[:, lanes] = x_rows
        slope_out[:, lanes] = sigma * (1.0 + pre * (1.0 - sigma))
        x_head = jnp.concatenate([x_rows, x_low[top:, lanes]], axis=0)
        weighted = (b_turned[...] * tail_step[head : head + 1, :]).astype(BF16)
        state_out[0, :, lanes] = dot(weighted, x_head).astype(BF16)


def inner_body(at, base, gram, step_in, cumul_in, x_in, rows, mixed_out):
    cumul = cumul_in[...]
    cumul_columns = columns_of(cumul)
    for head in range(x_in.shape[1] // 128):
        lanes = slice(head * 128, head * 128 + 128)
        row = cumul[head : head + 1, :]
        decay = jnp.exp(jnp.minimum(cumul_columns[:, head : head + 1] - row, 0.0))
        mixer = (gram[...] * decay * step_in[head : head + 1, :]).astype(BF16)
        x_head = x_in[:, lanes]
        mixed_out[:, lanes] = dot(mixer, x_head) + rows[1:2, lanes] * x_head.astype(F32)


def gate_body(
    at, base, z_in, grad_in, gain, gate_out, gate_slope_out, scaled_out, scaled_gate_out
):
    for start in range(0, z_in.shape[1], 128):
        lanes = slice(start, start + 128)
        z = z_in[:, lanes].astype(F32)
        sigma = sigmoid(z)
        gate = z * sigma
        scaled = grad_in[:, lanes].astype(F32) * gain[:, lanes]
        gate_out[:, lanes] = gate
        gate_slope_out[:, lanes] = sigma * (1.0 + z * (1.0 - sigma))
        scaled_out[:, lanes] = scaled
        scaled_gate_out[:, lanes] = scaled * gate


def lift_body(at, base, bc, step_in, cumul_in, x_in, weighted_x, lifted_out, c_turned):
    @pl.when(at[0] == 0)
    def _():
        c_turned[...] = bc[1].astype(F32).T

    weights = block_weights(step_in[...], cumul_in[...])
    lifted = jnp.exp(cumul_in[...])
    for head in range(x_in.shape[1] // 128):
        lanes = slice(head * 128, head * 128 + 128)
        weight = weights[:, head : head + 1]
        weighted_x[:, lanes] = (weight * x_in[:, lanes].astype(F32)).astype(BF16)
        lifted_out[:, lanes] = (c_turned[...] * lifted[head : head + 1, :]).astype(BF16)


def mix_body(
    at, base, mixed_in, c_rows, cumul_in, state, gate_in, scaled_in, sums_in, *outs
):
    mixed_out, sums_out, squares, products = outs
    group, groups = at

    @pl.when(group == 0)
    def _():
        squares[...] = jnp.zeros_like(squares)
        products[...] = jnp.zeros_like(products)

    carried = dot(c_rows[0], state[0])
    lifted = jnp.exp(columns_of(cumul_in[...]))
    square, product = squares[...], products[...]
    for head in range(mixed_in.shape[1] // 128):
        lanes = slice(head * 128, head * 128 + 128)
        mixed = mixed_in[:, lanes] + lifted[:, head : head + 1] * carried[:, lanes]
        mixed_out[:, lanes] = mixed
        gated = mixed * gate_in[:, lanes]
        square = square + gated * gated
        product = product + mixed * scaled_in[:, lanes]
    squares[...] = square
    products[...] = product

    @pl.when(group == groups - 1)
    def _():
        sums_out[...] = sums_in[...]
        sums_out[0:1, :] += jnp.sum(squares[...].T, axis=0, keepdims=True)
        sums_out[1:2, :] += jnp.sum(products[...].T, axis=0, keepdims=True)


def square_body(at, base, mixed_in, gate_in, squared):
    for start in range(0, mixed_in.shape[1], 128):
        lanes = slice(start, start + 128)
        gate = gate_in[:, lanes]
        squared[:, lanes] = mixed_in[:, lanes] * gate * gate


def norm_scales(at, inner, sums, alpha, beta):
    @pl.when(at[0] == 0)
    def _():
        total = sums[0][...]
        for part in sums[1:]:
            total = total + part[...]
        inv_rms = lax.rsqrt(total[0:1, :] / inner + EPS)
        mean_dot = inv_rms * total[1:2, :] / inner
        alpha[...] = jnp.broadcast_to(inv_rms, alpha.shape).T
        beta[...] = jnp.broadcast_to(inv_rms * inv_rms * mean_dot, beta.shape).T


def grad_mixed_body(inner, parts, at, base, *refs):
    sums = refs[:parts]
    squared, scaled_in, lifted_c, grad_mixed, state_out, alpha, beta = refs[parts:]
    norm_scales(at, inner, sums, alpha, beta)
    for start in range(0, squared.shape[1], 128):
        lanes = slice(start, start + 128)
        low = (alpha[...] * scaled_in[:, lanes] - beta[...] * squared[:, lanes]).astype(BF16)
        grad_mixed[:, lanes] = low
        state_out[0, :, lanes] = dot(lifted_c[:, lanes], low).astype(BF16)


def grad_z_body(inner, parts, at, base, *refs):
    sums = refs[:parts]
    mixed_in, gate_in, gate_slope_in, scaled_in, grad_z, alpha, beta = refs[parts:]
    norm_scales(at, inner, sums, alpha, beta)
    for start in range(0, mixed_in.shape[1], 128):
        lanes = slice(start, start + 128)
        mixed = mixed_in[:, lanes]
        grad_gated = alpha[...] * scaled_in[:, lanes] - beta[...] * (mixed * gate_in[:, lanes])
        grad_z[:, lanes] = (grad_gated * (mixed * gate_slope_in[:, lanes])).astype(BF16)


def inner_back_body(
    last,
    at,
    base,
    gram,
    bc,
    step_in,
    cumul_in,
    x_in,
    grad_in,
    state_in,
    rows,
    sums_in,
    grad_x,
    q_out,
    r_out,
    bc_out,
    z_sum,
    c_sum,
):
    group, groups = at
    length = x_in.shape[0]

    @pl.when(group == 0)
    def _():
        z_sum[...] = sums_in[0]
        c_sum[...] = sums_in[1]

    cumul = cumul_in[...]
    cumul_columns = columns_of(cumul)
    lifted = jnp.exp(cumul_columns)
    state = state_in[0]
    c_rows = bc[1].astype(F32)
    lane = lax.broadcasted_iota(jnp.int32, (length, 128), 1)
    q_columns = jnp.zeros((length, 128), F32)
    for head in range(x_in.shape[1] // 128):
        lanes = slice(head * 128, head * 128 + 128)
        step = step_in[head : head + 1, :]
        decay = jnp.exp(
            jnp.minimum(cumul_columns[:, head : head + 1] - cumul[head : head + 1, :], 0.0)
        )
        gram_decay = gram[...] * decay
        mixer = (gram_decay * step).astype(BF16)
        x_head, grad_head = x_in[:, lanes], grad_in[:, lanes]
        product = dot_rows(grad_head, x_head)
        z_sum[...] += product * decay * step
        gram_grad = product * gram_decay
        r_out[head : head + 1, :] = jnp.sum(gram_grad, axis=0, keepdims=True)
        handed = lifted[:, head : head + 1] * dot_rows(grad_head, state[:, lanes])
        c_sum[...] += handed
        q = jnp.sum(gram_grad * step + c_rows * handed, axis=1, keepdims=True)
        q_columns = jnp.where(lane == head, q, q_columns)
        grad_x[:, lanes] = dot_columns(mixer, grad_head) + rows[1:2, lanes] * grad_head.astype(F32)
    q_out[...] = q_columns.T[:GROUP, :]

    @pl.when(group == groups - 1)
    def _():
        if last:
            summed = jnp.where(triangle(length, False), z_sum[...], 0.0)
            bc_out[0] = dot_split(summed.T, bc[1])
            bc_out[1] = c_sum[...] + dot_split(summed, bc[0])
        else:
            bc_out[0] = z_sum[...]
            bc_out[1] = c_sum[...]


def block_weights(step, cumul):
    return columns_of(jnp.exp(cumul[:, cumul.shape[1] - 1 :] - cumul) * step)


def rim_body(last, at, base, bc, step_in, cumul_in, weighted_x, partial, slope, out_in, *refs):
    group, groups = at
    width = weighted_x.shape[1]
    if last:
        rows_before, b_before, bc_partial, bc_slope, rim_out, bc_out, b_sum = refs
    else:
        rim_out, b_sum = refs

    @pl.when(group == 0)
    def _():
        b_sum[...] = b_before[...] if last else jnp.zeros_like(b_sum)

    out_low = out_in[0]
    b_sum[...] += dot_rows(weighted_x[...], out_low)
    weights = block_weights(step_in[...], cumul_in[...])[0:8, :]
    returned = dot(bc[0][0:16, :], out_low)[0:8, :]
    start = group
    if last:
        count = rim_out.shape[1] // width
        start = lax.rem(group + count - groups + first_group(base), count)
    for head in range(width // 128):
        lanes = slice(head * 128, head * 128 + 128)
        weight = weights[:, head : head + 1]
        rows = (partial[0:8, lanes] + weight * returned[:, lanes]) * slope[0:8, lanes]
        place = pl.multiple_of(jnp.int32(start) * width + head * 128, 128)
        rim_out[:, pl.ds(place, 128)] = rows[0:3, :]

    if last:

        @pl.when(group == groups - 1)
        def _():
            before = rows_before.shape[1]
            if before < rim_out.shape[1] - 256:
                place = pl.multiple_of(first_group(base) * width, 128)
                rim_out[:, pl.ds(place, before)] = rows_before[...]
            bc_out[0] = (b_sum[...] + bc_partial[0]) * bc_slope[0]
            bc_out[1] = bc_partial[1] * bc_slope[1]
            for j in range(2):
                lanes = rim_out.shape[1] - 256 + 128 * j
                rim_out[:, lanes : lanes + 128] = bc_out[j, 0:3, :]


def grad_dt_body(
    at,
    base,
    bc,
    rate,
    dt_slope,
    step_in,
    cumul_in,
    q_in,
    r_in,
    x_in,
    state_in,
    out_in,
    grad_dt,
    selector,
    products,
):
    heads, length = q_in.shape
    width = state_in.shape[2]
    row = lax.broadcasted_iota(jnp.int32, selector.shape, 0)
    lane = lax.broadcasted_iota(jnp.int32, selector.shape, 1)
    selector[...] = (lax.shift_right_logical(row, 7) == lane).astype(BF16)
    row = lax.broadcasted_iota(jnp.int32, (16, width), 0)
    lane = lax.shift_right_logical(lax.broadcasted_iota(jnp.int32, (16, width), 1), 7)
    dots = jnp.zeros((16, 1), F32)
    for group in range(state_in.shape[0]):
        out_low = out_in[group]
        returned = dot(bc[0], out_low)
        for start in range(0, width, 128):
            lanes = slice(start, start + 128)
            place = slice(group * width + start, group * width + start + 128)
            products[:, place] = (x_in[:, place].astype(F32) * returned[:, lanes]).astype(BF16)
        summed = dot(jnp.ones((16, length), BF16), state_in[group] * out_low)
        own = row - GROUP * group == lane
        dots = dots + jnp.sum(jnp.where(own, summed, 0.0), axis=1, keepdims=True)
    inner_b = dot(products[...], selector[...]).T[:heads, :]
    cumul, step = cumul_in[...], step_in[...]
    w = jnp.exp(cumul[:, length - 1 :] - cumul) * inner_b
    q, r = q_in[...], r_in[...]
    inside = jnp.sum(step * w, axis=1, keepdims=True)
    end = inside + jnp.exp(cumul[:, length - 1 :]) * dots[:heads]
    last = lax.broadcasted_iota(jnp.int32, (heads, length), 1) == length - 1
    grad_cumul = q - step * (r + w) + jnp.where(last, end, 0.0)
    grad_log = dot_split(grad_cumul, triangle(length, False).astype(BF16))
    grad_dt[...] = (r + w + rate[...] * grad_log) * dt_slope[...]


def grad_x_body(
    at,
    base,
    bc,
    step_in,
    cumul_in,
    partial,
    slope,
    taps,
    halo,
    out_in,
    grad_x,
    ext,
):
    length, width = partial.shape
    weights = block_weights(step_in[...], cumul_in[...])
    returned = dot(bc[0], out_in[0])
    for head in range(width // 128):
        lanes = slice(head * 128, head * 128 + 128)
        weight = weights[:, head : head + 1]
        ext[0:length, :] = (partial[:, lanes] + weight * returned[:, lanes]) * slope[:, lanes]
        ext[length : length + 3, :] = halo[:, lanes]
        total = taps[0:1, lanes] * ext[3 : 3 + length, :]
        for k in range(1, 4):
            total = total + taps[k : k + 1, lanes] * ext[3 - k : 3 - k + length, :]
        grad_x[:, lanes] = total.astype(BF16)


def bc_back_body(at, place, grad_pre, halo, taps, kept, sent, ext, total):
    length, half = grad_pre.shape[1], kept.shape[1]
    for j in range(2):
        ext[0:length, :] = grad_pre[j]
        ext[length : length + 3, :] = halo[:, 128 * j : 128 * j + 128]
        summed = taps[j, 0:1, :] * ext[3 : 3 + length, :]
        for k in range(1, 4):
            summed = summed + taps[j, k : k + 1, :] * ext[3 - k : 3 - k + length, :]
        total[...] = summed
        kept[j] = total[pl.ds(pl.multiple_of(place_bit(place, 3) * half, half), half), :]
        sent[j] = total[pl.ds(pl.multiple_of((1 - place_bit(place, 3)) * half, half), half), :]


def bc_half_body(at, place, mine, taken, kept, sent, total):
    half = kept.shape[1]
    for j in range(2):
        total[...] = mine[j] + taken[j]
        kept[j] = total[pl.ds(pl.multiple_of(place_bit(place, 4) * half, half), half), :]
        sent[j] = total[pl.ds(pl.multiple_of((1 - place_bit(place, 4)) * half, half), half), :]


def bc_last_body(at, _, mine, taken, out):
    out[...] = (mine[...] + taken[...]).astype(BF16)


def conv_back(extended, weights):
    length = extended.shape[-2] - 3
    summed = weights[..., 0, :][..., None, :] * extended[..., 3 : 3 + length, :]
    for k in range(1, 4):
        summed = (
            summed
            + weights[..., k, :][..., None, :] * extended[..., 3 - k : 3 - k + length, :]
        )
    return summed


def shards(
    x_input,
    z_input,
    bc_input,
    dt_raw,
    dt_bias,
    a_log,
    d_skip,
    conv_x,
    convolution_bc_taps,
    rescale_factor,
    grad_out,
):
    length, channels = x_input.shape
    heads = dt_raw.shape[0]
    groups = heads // GROUP
    width = GROUP * 128
    count, parts = lax.axis_size("seq"), lax.axis_size("head")
    inner = channels * parts
    own = lax.axis_index("seq")
    split = count == 8 and groups == 4
    own_half = groups // 2 if split else groups
    bit = lambda value, place: lax.shift_right_logical(value, place) & 1
    along_head = lax.axis_index("head")
    base = bit(own, 0) * own_half if split else own * 0
    for place, value in enumerate(
        (bit(own, 2), bit(own, 1), bit(own, 0), bit(along_head, 1), bit(along_head, 0))
    ):
        base = base | lax.shift_left(value, 8 + place)
    base = base.astype(jnp.int32)[None]

    whole = lambda *shape: ((shape, lambda g, b: (0,) * len(shape)),)
    wide_at = lambda off: (Groups("wide", (length, width), off, groups),)
    rows_at = lambda off: (Groups("heads", (GROUP, length), off, groups),)
    lanes_at = lambda n, off: (Groups("wide", (n, width), off, groups),)
    slot = (Groups("slots", (1, length, width), 0, groups),)
    full = lambda array: (array,) + whole(*array.shape)
    half_width = own_half * width
    half_heads = own_half * GROUP
    half = lambda n: (Groups("half", (n, width), 0, groups),)
    half_rows = (Groups("half heads", (GROUP, length), 0, groups),)
    window_at = lambda n, off: (Groups("window", (n, width), off, groups),)
    halves = [own_half, 0] if split else [0]
    rest = halves[0]

    gain = rescale_factor[None, :]
    f32 = lambda *shape: (shape, F32)
    low = lambda *shape: (shape, BF16)

    step, cumul, rate, dt_slope, rows, rim, bc_rows, bc_taps = call(
        steps_body,
        [
            f32(heads, length) + whole(heads, length),
            f32(heads, length) + whole(heads, length),
            f32(heads, length) + whole(heads, length),
            f32(heads, length) + whole(heads, length),
            f32(2, channels) + whole(2, channels),
            low(3, channels + 256) + whole(3, channels + 256),
            low(2, length, 128) + whole(2, length, 128),
            f32(2, 4, 128) + whole(2, 4, 128),
        ],
        [
            full(in_hbm(dt_raw)),
            full(in_hbm(dt_bias[None, :])),
            full(in_hbm(a_log[None, :])),
            full(in_hbm(d_skip[None, :])),
            (in_hbm(x_input), ((16, channels), lambda g, b: (length // 16 - 1, 0))),
            full(in_hbm(bc_input)),
            full(in_hbm(convolution_bc_taps)),
        ],
        base=base,
    )
    rim_sent = rim
    rim = lax.ppermute(rim, "seq", [(i - 1, i) for i in range(1, count)])
    if split:
        swap = lambda block, bit: lax.ppermute(
            block, "seq", [(i, i ^ bit) for i in range(count)]
        )
        total = rows[0:1]
        total_core = swap(total, 1)
        chip_total = total + total_core
        total_across = swap(chip_total, 2)
        table = f32(16, channels) + whole(16, channels)
        ahead, behind = call(
            weights_body,
            [table, table],
            [full(rows), full(total_core), full(total_across)],
            base=base,
            )

    def passed(locals_, reverse, beside):
        if split:
            local_sent, local = locals_[rest], locals_[0]
            weights = behind if reverse else ahead
            return scan_blocks(base, groups, weights, local, local_sent, reverse, beside)
        local = locals_[0]
        for work in beside:
            work(local)
        return gather_blocks(rows[0:1], local, reverse)

    x_low, slope, local = {}, {}, {}
    ready = rim_sent
    for off in halves:
        x_low[off], slope[off], x_top, taps = call(
            conv_body,
            [
                low(length, half_width) + half(length),
                f32(length, half_width) + half(length),
                low(16, half_width) + half(16),
                f32(4, half_width) + half(4),
            ],
            [(in_hbm(x_input),) + wide_at(off), (in_hbm(conv_x),) + lanes_at(4, off)],
            base=base,
            grid=own_half,
            scratch=[pltpu.VMEM((length + 8, 128), F32)],
            after=[ready],
        )
        first = off == rest
        top = (Groups("top", (16, width), 0, groups),)
        ins = [
            (x_low[off],) + half(length),
            (x_top,) + half(16),
            (rim,) + lanes_at(3, off),
            (taps,) + half(4),
            (step,) + rows_at(off),
            (cumul,) + rows_at(off),
        ]
        outs = [
            f32(length, half_width) + top,
            low(length, half_width) + top,
            low(own_half, length, width) + slot,
        ]
        scratch = [pltpu.VMEM((24, width), F32)]
        if first:
            ins += [
                full(bc_rows),
                (rim, ((3, 256), lambda g, b: (0, channels // 256))),
                full(bc_taps),
            ]
            outs += [
                low(2, length, 128) + whole(2, length, 128),
                f32(2, length, 128) + whole(2, length, 128),
                f32(length, length) + whole(length, length),
                f32(128, length) + whole(128, length),
            ]
            scratch += [pltpu.VMEM((length + 8, 128), F32)]
        else:
            ins += [full(b_turned)]
        result = call(
            functools.partial(state_body, first),
            outs,
            ins,
            base=base,
            loop=own_half,
            scratch=scratch,
            carry=[slope[off]],
            place={0: 1},
            flops=2 * length * 128 * half_width,
        )
        if first:
            bc, bc_slope, gram, b_turned = result[3:]
        slope[off], x_low[off], local[off] = result[:3]
        ready = local[off]

    inside, gate, gate_slope, scaled, scaled_gate = {}, {}, {}, {}, {}

    def mix_inside(off, ready):
        inside[off], token = call(
            inner_body,
            [f32(length, half_width) + half(length)],
            [
                full(gram),
                (step,) + rows_at(off),
                (cumul,) + rows_at(off),
                (x_low[off],) + half(length),
                (rows,) + lanes_at(2, off),
            ],
            base=base,
            loop=own_half,
            after=[ready],
            token=True,
            flops=2 * length * 128 * half_width,
        )
        return token

    def gates(off, ready):
        gate[off], gate_slope[off], scaled[off], scaled_gate[off], token = call(
            gate_body,
            [f32(length, half_width) + half(length)] * 4,
            [
                (z_input,) + wide_at(off),
                (grad_out,) + wide_at(off),
                (gain,) + lanes_at(1, off),
            ],
            base=base,
            loop=own_half,
            after=[ready],
            token=True,
        )
        return token

    def mix_second(ready):
        tokens = [mix_inside(rest, ready)] if split else []
        tokens += [gates(off, ready) for off in reversed(halves)]
        return [], tokens

    states = passed(local, False, (functools.partial(mix_inside, 0), mix_second))
    states = dict(zip((0, rest), states))
    mixed, sums = {}, jnp.zeros((8, length), F32)
    two_scales = [pltpu.VMEM((length, 128), F32), pltpu.VMEM((length, 128), F32)]
    for off in reversed(halves):
        mixed[off], sums = call(
            mix_body,
            [f32(length, half_width) + half(length), f32(8, length) + whole(8, length)],
            [
                (inside[off],) + half(length),
                (bc, ((1, length, 128), lambda g, b: (1, 0, 0))),
                (cumul,) + rows_at(off),
                (states[off],) + slot,
                (gate[off],) + half(length),
                (scaled_gate[off],) + half(length),
                full(sums),
            ],
            base=base,
            loop=own_half,
            scratch=two_scales,
            flops=2 * length * 128 * half_width,
        )
    turn_head = lambda block, bit: lax.ppermute(
        block, "head", [(i, i ^ bit) for i in range(parts)]
    )
    weighted_x, lifted_c, squared = {}, {}, {}
    for off in halves:
        weighted_x[off], lifted_c[off] = call(
            lift_body,
            [low(length, half_width) + half(length), low(length, half_width) + half(length)],
            [
                full(bc),
                (step,) + rows_at(off),
                (cumul,) + rows_at(off),
                (x_low[off],) + half(length),
            ],
            base=base,
            loop=own_half,
            scratch=[pltpu.VMEM((128, length), F32)],
            after=[sums],
        )
        (squared[off],) = call(
            square_body,
            [f32(length, half_width) + half(length)],
            [(mixed[off],) + half(length), (gate[off],) + half(length)],
            base=base,
            loop=own_half,
        )
    if parts == 4:
        sums = sums + turn_head(sums, 1)
        all_sums = [sums, turn_head(sums, 2)]
    else:
        all_sums = [lax.psum(sums, "head")]
    grad_mixed, local_back = {}, {}
    for off in halves:
        grad_mixed[off], local_back[off] = call(
            functools.partial(grad_mixed_body, inner, len(all_sums)),
            [low(length, half_width) + half(length), low(own_half, length, width) + slot],
            [full(part) for part in all_sums]
            + [
                (squared[off],) + half(length),
                (scaled_gate[off],) + half(length),
                (lifted_c[off],) + half(length),
            ],
            base=base,
            loop=own_half,
            scratch=two_scales,
            flops=2 * length * 128 * half_width,
        )

    partial, q_rows, r_rows = {}, {}, {}
    carried = {"sums": jnp.zeros((2, length, 128), F32), "z": [], "dt": [], "x": []}

    def back_inside(off, ready):
        partial[off], q_rows[off], r_rows[off], carried["sums"], token = call(
            functools.partial(inner_back_body, off == rest),
            [
                f32(length, half_width) + half(length),
                f32(half_heads, length) + half_rows,
                f32(half_heads, length) + half_rows,
                f32(2, length, 128) + whole(2, length, 128),
            ],
            [
                full(gram),
                full(bc),
                (step,) + rows_at(off),
                (cumul,) + rows_at(off),
                (x_low[off],) + half(length),
                (grad_mixed[off],) + half(length),
                (states[off],) + slot,
                (rows,) + lanes_at(2, off),
                full(carried["sums"]),
            ],
            base=base,
            loop=own_half,
            scratch=[pltpu.VMEM((length, length), F32), pltpu.VMEM((length, 128), F32)],
            after=[ready],
            token=True,
            flops=6 * length * 128 * half_width,
        )
        return token

    def back_gates(off, ready):
        grad_z, token = call(
            functools.partial(grad_z_body, inner, len(all_sums)),
            [low(length, channels) + window_at(length, off)],
            [full(part) for part in all_sums]
            + [
                (mixed[off],) + half(length),
                (gate[off],) + half(length),
                (gate_slope[off],) + half(length),
                (scaled[off],) + half(length),
            ],
            base=base,
            loop=own_half,
            scratch=two_scales,
            carry=carried["z"],
            after=[ready],
            token=True,
        )
        carried["z"] = [grad_z]
        carried["z_token"] = token
        return token

    def back_second(ready):
        token = back_inside(rest, ready) if split else ready
        return [token], [back_gates(0, token)]

    backs = passed(local_back, True, (functools.partial(back_inside, 0), back_second))
    backs = dict(zip((0, rest), backs))
    z_tokens = [back_gates(rest, carried["z_token"])] if split else []

    def make_grad_dt(off, after):
        table = (Groups("heads", (half_heads, length), off, groups, own_half),)
        window = (Groups("window heads", (half_heads, length), off, groups, own_half),)
        grad_dt, token = call(
            grad_dt_body,
            [f32(heads, length) + window],
            [
                full(bc),
                (rate,) + table,
                (dt_slope,) + table,
                (step,) + table,
                (cumul,) + table,
                full(q_rows[off]),
                full(r_rows[off]),
                full(x_low[off]),
                full(states[off]),
                full(backs[off]),
            ],
            base=base,
            scratch=[pltpu.VMEM((half_width, 128), BF16), pltpu.VMEM((length, half_width), BF16)],
            carry=carried["dt"],
            after=after,
            token=True,
            flops=4 * length * 128 * half_width,
        )
        carried["dt"] = [grad_dt]
        return token

    def make_grad_x(off, after):
        grad_x, token = call(
            grad_x_body,
            [low(length, channels) + window_at(length, off)],
            [
                full(bc),
                (step,) + rows_at(off),
                (cumul,) + rows_at(off),
                (partial[off],) + half(length),
                (slope[off],) + half(length),
                (conv_x,) + lanes_at(4, off),
                (rim_back,) + lanes_at(3, off),
                (backs[off],) + slot,
            ],
            base=base,
            loop=own_half,
            scratch=[pltpu.VMEM((length + 8, 128), F32)],
            carry=carried["x"],
            after=after,
            token=True,
            flops=2 * length * 128 * half_width,
        )
        carried["x"] = [grad_x]
        return token

    def make_rim(off, before, after):
        last = off == rest
        if last:
            outs = [
                f32(3, channels + 256) + whole(3, channels + 256),
                f32(2, length, 128) + whole(2, length, 128),
            ]
        else:
            outs = [f32(3, half_width) + whole(3, half_width), f32(length, 128) + whole(length, 128)]
        return call(
            functools.partial(rim_body, last),
            outs,
            [
                full(bc),
                (step,) + rows_at(off),
                (cumul,) + rows_at(off),
                (weighted_x[off],) + half(length),
                (partial[off],) + half(length),
                (slope[off],) + half(length),
                (backs[off],) + slot,
            ]
            + [full(array) for array in before],
            base=base,
            loop=own_half,
            scratch=[pltpu.VMEM((length, 128), F32)] if last else [],
            after=after,
            flops=2 * length * 128 * half_width,
        )

    if split:
        before = make_rim(0, [], [])
        z_tokens.append(make_grad_dt(0, [before[1]]))
    else:
        before = [jnp.zeros((3, channels), F32), jnp.zeros((length, 128), F32)]
    rim_back, grad_bc_pre = make_rim(rest, [*before, carried["sums"], bc_slope], z_tokens)
    rim_back = lax.ppermute(rim_back, "seq", [(i, i - 1) for i in range(1, count)])
    dt_token = make_grad_dt(rest, [grad_bc_pre])
    if parts == 4:
        piece = lambda rows: f32(2, rows, 128) + whole(2, rows, 128)
        kept, sent = call(
            bc_back_body,
            [piece(length // 2), piece(length // 2)],
            [
                full(grad_bc_pre),
                (rim_back, ((3, 256), lambda g, b: (0, channels // 256))),
                full(bc_taps),
            ],
            base=base,
            scratch=[pltpu.VMEM((length + 8, 128), F32), pltpu.VMEM((length, 128), F32)],
            after=[dt_token],
        )
        taken = turn_head(sent, 2)
        x_tokens = [make_grad_x(0, [sent])]
        kept, sent = call(
            bc_half_body,
            [piece(length // 4), piece(length // 4)],
            [full(kept), full(taken)],
            base=base,
            scratch=[pltpu.VMEM((length // 2, 128), F32)],
            after=x_tokens,
        )
        taken = turn_head(sent, 1)
        x_tokens = [make_grad_x(rest, [sent])] if split else []
        (grad_bc,) = call(
            bc_last_body,
            [low(2, length // 4, 128) + whole(2, length // 4, 128)],
            [full(kept), full(taken)],
            base=base,
            after=x_tokens,
        )
    else:
        for off in halves:
            make_grad_x(off, [])
        bc_halo = jnp.moveaxis(rim_back[:, channels:].reshape(3, 2, 128), 1, 0)
        bc_sum = conv_back(jnp.concatenate([grad_bc_pre, bc_halo], axis=1), convolution_bc_taps)
        share = length // parts
        bc_sum = lax.psum(bc_sum, "head")
        grad_bc = lax.dynamic_slice_in_dim(bc_sum, along_head * share, share, 1).astype(BF16)
    return (carried["x"][0], carried["z"][0], grad_bc, carried["dt"][0])


def solution(mesh):
    return jax.shard_map(
        shards,
        mesh=mesh,
        in_specs=(
            P("seq", "head"),
            P("seq", "head"),
            P(None, "seq", None),
            P("head", "seq"),
            P("head"),
            P("head"),
            P("head"),
            P(None, "head"),
            P(),
            P("head"),
            P("seq", "head"),
        ),
        out_specs=(
            P("seq", "head"),
            P("seq", "head"),
            P(None, ("seq", "head"), None),
            P("head", "seq"),
        ),
        check_vma=False,
    )
```

```python
import functools

import jax
import jax.numpy as jnp
from jax import lax
from jax.experimental import pallas as pl
from jax.experimental.pallas import tpu as pltpu
from jax.sharding import PartitionSpec as P

EPS = 1e-05
GROUP = 8
F32 = jnp.float32
BF16 = jnp.bfloat16
VMEM_BYTES = 16 * 2**20


def sigmoid(value):
    return 0.5 + 0.5 * jnp.tanh(0.5 * value)


def dot(a, b):
    return jnp.dot(a, b, preferred_element_type=F32)


def dot_split(a, b):
    high = a.astype(BF16)
    rest = a - high.astype(F32)
    middle = rest.astype(BF16)
    low = (rest - middle.astype(F32)).astype(BF16)
    return dot(high, b) + (dot(middle, b) + dot(low, b))


def dot_rows(a, b):
    return lax.dot_general(a, b, (((1,), (1,)), ((), ())), preferred_element_type=F32)


def dot_columns(a, b):
    return lax.dot_general(a, b, (((0,), (0,)), ((), ())), preferred_element_type=F32)


def triangle(length, upper):
    first = lax.broadcasted_iota(jnp.int32, (length, length), 0)
    second = lax.broadcasted_iota(jnp.int32, (length, length), 1)
    return first <= second if upper else first >= second


def columns_of(rows):
    return rows.T


class Groups:
    def __init__(self, kind, block, off, groups, size=1):
        self.kind, self.block, self.off, self.groups = kind, block, off, groups
        self.size = size
        self.by_rows = kind.endswith("heads")

    def turn(self, group, base):
        first = self.off + first_group(base)
        return lax.rem(group * self.size + first, self.groups) // self.size

    def place(self, index):
        return (index, 0) if self.by_rows else (0, index)

    def spec(self):
        if self.kind == "slots":
            return pl.BlockSpec(self.block, lambda g, b: (g, 0, 0))
        if self.kind.startswith("half"):
            return pl.BlockSpec(self.block, lambda g, b: self.place(g))
        return pl.BlockSpec(self.block, lambda g, b: self.place(self.turn(g, b)))

    def whole(self, shape, count):
        if self.kind.startswith("window"):
            block = list(self.block)
            block[0 if self.by_rows else 1] *= count
            return pl.BlockSpec(
                tuple(block), lambda g, b: self.place(self.turn(0, b) // count)
            )
        if self.kind == "top":
            shape = (self.block[0], count * self.block[1])
        return pl.BlockSpec(shape, lambda g, b: (0,) * len(shape))

    def view(self, ref, group, base):
        if self.kind == "slots":
            return ref.at[pl.ds(group, 1)]
        if self.kind in ("wide", "heads"):
            group = self.turn(group, base)
        size = self.block[0 if self.by_rows else 1]
        span = pl.ds(pl.multiple_of(jnp.int32(group) * size, size), size)
        return ref.at[span] if self.by_rows else ref.at[:, span]


def call(
    body,
    outs,
    ins,
    *,
    base,
    grid=1,
    loop=1,
    scratch=(),
    after=(),
    carry=(),
    place=None,
    token=False,
    flops=0,
):
    aliases = {1 + len(ins) + len(after) + i: i for i in range(len(carry))}
    for read, written in (place or {}).items():
        aliases[1 + read] = written
    after = list(after) + list(carry)
    outs = list(outs)
    if token:
        outs.append(((8, 128), F32, ((8, 128), lambda *_: (0, 0))))

    def spec(shape, block):
        if not isinstance(block, Groups):
            return pl.BlockSpec(*block)
        return block.whole(shape, loop) if grid == 1 else block.spec()

    in_specs = [spec(array.shape, block) for array, block in ins]
    in_specs += [pl.BlockSpec(memory_space=pl.ANY) for _ in after]
    out_specs = [spec(shape, block) for shape, _, block in outs]
    out_shape = [jax.ShapeDtypeStruct(shape, dtype) for shape, dtype, _ in outs]
    arrays = [array for array, _ in ins]
    moved = sum(a.size * a.dtype.itemsize for a in arrays + out_shape)
    blocks = [block for _, block in ins] + [block for _, _, block in outs]

    def ordered(where, *refs):
        taken, rest = refs[: len(ins)], refs[len(ins) + len(after) :]
        results, extra = rest[: len(outs)], rest[len(outs) :]
        if token:
            results[-1][...] = jnp.zeros((8, 128), F32)

        def step(group, _):
            views = [
                block.view(ref, group, where) if isinstance(block, Groups) else ref
                for ref, block in zip(taken + results, blocks)
            ]
            if token:
                views = views[:-1]
            body((group, loop), where, *views, *extra)
            return 0

        if grid > 1:
            views = taken + (results[:-1] if token else results)
            body((pl.program_id(0), grid), where, *views, *extra)
        elif loop > 1:
            lax.fori_loop(0, loop, step, 0)
        else:
            step(0, 0)

    return pl.pallas_call(
        ordered,
        out_shape=out_shape,
        grid_spec=pltpu.PrefetchScalarGridSpec(
            num_scalar_prefetch=1,
            grid=(grid,),
            in_specs=in_specs,
            out_specs=out_specs,
            scratch_shapes=list(scratch),
        ),
        input_output_aliases=aliases,
        cost_estimate=pl.CostEstimate(flops=flops, bytes_accessed=moved, transcendentals=0),
        compiler_params=pltpu.CompilerParams(vmem_limit_bytes=VMEM_BYTES),
    )(base, *arrays, *after)


def in_hbm(array):
    return pltpu.with_memory_space_constraint(array, pltpu.HBM)


def column_of(row):
    count = row.shape[1]
    first = lax.broadcasted_iota(jnp.int32, (count, count), 0)
    second = lax.broadcasted_iota(jnp.int32, (count, count), 1)
    return jnp.sum(jnp.where(first == second, row, 0.0), axis=1, keepdims=True)


def steps_body(
    at,
    base,
    raw,
    bias,
    log_rate,
    skip,
    x_tail,
    bc_in,
    bc_taps,
    step_out,
    cumul_out,
    rate_out,
    slope_out,
    rows_out,
    rim_out,
    bc_in_out,
    bc_taps_out,
):
    bc_in_out[...] = bc_in[...]
    bc_taps_out[...] = bc_taps[...]
    heads, length = raw.shape
    channels = x_tail.shape[1]
    rim_out[:, 0:channels] = x_tail[...].astype(F32)[13:16, :].astype(BF16)
    for j in range(2):
        start = channels + 128 * j
        rim_out[:, start : start + 128] = bc_in[j, length - 16 :].astype(F32)[13:16, :].astype(BF16)
    shifted = raw[...] + column_of(bias[...])
    step = jnp.maximum(shifted, 0.0) + jnp.log1p(jnp.exp(-jnp.abs(shifted)))
    rate = jnp.broadcast_to(-jnp.exp(column_of(log_rate[...])), step.shape)
    cumul = dot_split(rate * step, triangle(length, True).astype(BF16))
    step_out[...] = step
    cumul_out[...] = cumul
    rate_out[...] = rate
    slope_out[...] = sigmoid(shifted)
    skips = column_of(skip[...])
    for head in range(heads):
        lanes = slice(head * 128, head * 128 + 128)
        rows_out[0:1, lanes] = jnp.broadcast_to(cumul[head : head + 1, length - 1 :], (1, 128))
        rows_out[1:2, lanes] = jnp.broadcast_to(skips[head : head + 1, :], (1, 128))


def pick(test, yes, no):
    return jnp.where(test, yes, no)


def first_group(place):
    return place[0] & 255


def place_bit(place, index):
    return lax.shift_right_logical(place[0], 8 + index) & 1


def weights_body(at, place, own, core, across, *outs):
    t0, t1 = own[0:1, :], core[...]
    e0, e1, own_chip, ex = jnp.exp(t0), jnp.exp(t1), jnp.exp(t0 + t1), jnp.exp(across[...])
    one = jnp.ones_like(e0)
    zero = jnp.zeros_like(e0)
    bits = [place_bit(place, i) for i in range(3)]
    x_first = bits[2] == 0
    for out, reverse in zip(outs, (False, True)):
        y, x, c = ((1 - bit if reverse else bit) == 1 for bit in bits)
        either = jnp.logical_or(x, y)
        scale = pick(jnp.logical_or(x_first, either), one, ex)
        rows = [pick(c, one, e1), pick(c, e0, one)]
        rows += [rows[0] * scale, rows[1] * scale]
        rows += [
            pick(x_first, pick(x, one, ex), pick(jnp.logical_and(x, y), zero, one)),
            pick(x_first, pick(x, own_chip, one), pick(y, pick(x, one, own_chip), zero)),
        ]
        a = pick(x_first, pick(x, one, zero), pick(y, pick(x, ex, one), zero))
        b = pick(x_first, pick(y, pick(x, ex, one), zero), pick(either, one, zero))
        into, send = pick(c, e1, one), pick(c, one, e0)
        rows += [into * a, into * b, pick(c, one, zero)]
        rows += [send * a, send * b, pick(c, zero, one)]
        for index, row in enumerate(rows):
            out[index : index + 1, :] = row


def combine(base, groups, weights, outs, after=(), slots_of=None, at=0, carry=()):
    arrays, columns = [], []
    for slots in outs:
        for column, terms in slots:
            if column not in columns:
                columns.append(column)
            for _, (array, slot) in terms:
                if not any(array is a and slot == s for a, s in arrays):
                    arrays.append((array, slot))
    place = lambda array, slot: [
        i for i, (a, s) in enumerate(arrays) if a is array and s == slot
    ][0]
    plan = [
        [
            (columns.index(column), [(row, place(*source)) for row, source in terms])
            for column, terms in slots
        ]
        for slots in outs
    ]

    def body(at, base, *refs):
        rows, values = refs[: len(columns)], refs[len(columns) : len(columns) + len(arrays)]
        results = refs[len(columns) + len(arrays) :]
        width = rows[0].shape[1]
        for result, slots in zip(results, plan):
            for slot, (column, terms) in enumerate(slots):
                for start in range(0, width, 256):
                    lanes = slice(start, start + 256)
                    total = None
                    for row, index in terms:
                        term = rows[column][row : row + 1, lanes] * values[index][
                            0, :, lanes
                        ].astype(F32)
                        total = term if total is None else total + term
                    result[slot, :, lanes] = total.astype(BF16)

    length, width = arrays[0][0].shape[1:]
    block = lambda slot, count: ((count, length, width), lambda g, b: (slot, 0, 0))
    ins = [
        (
            weights,
            (
                (weights.shape[0], width),
                lambda g, b, column=column: (0, lax.rem(first_group(b) + column, groups)),
            ),
        )
        for column in columns
    ]
    ins += [(array, block(slot, 1)) for array, slot in arrays]
    results = [
        ((slots_of or len(slots), length, width), BF16, block(at, len(slots))) for slots in outs
    ]
    return call(body, results, ins, base=base, after=after, carry=carry)


def scan_blocks(base, groups, weights, local, local_sent, reverse, beside):
    count = lax.axis_size("seq")

    def swap(block, bits):
        route = [(i, i ^ bits[i % 2]) for i in range(count)]
        return lax.ppermute(block, "seq", route)

    def merge(slot, *plans, **places):
        outs = [[(slot, list(zip(rows, sources)))] for rows, sources in plans]
        return combine(base, groups, weights, outs, **places)

    taken = swap(local_sent, (1, 1))
    chips, first_taken, sent, second_taken = [], [], [], []
    after = []
    for slot in range(2):
        both = ((local, slot), (taken, slot))
        chip, chip_sent = merge(slot, ((0, 1), both), ((2, 3), both), after=after)
        chips.append(chip)
        first_taken.append(swap(chip_sent, (2, 4)))
        if slot == 0 and not reverse:
            after = [beside[0](chip)]
    if reverse:
        beside[0](chips[1])
    for slot in range(2):
        sources = ((chips[slot], 0), (first_taken[slot], 0))
        (block,) = merge(slot, ((4, 5), sources))
        sent.append(block)
        second_taken.append(swap(block, (4, 2)))
    after = beside[1](sent[1])
    carry = []
    for slot in range(2):
        sources = ((first_taken[slot], 0), (second_taken[slot], 0))
        mine, handed = merge(
            slot,
            ((6, 7, 8), (*sources, (taken, slot))),
            ((9, 10, 11), (*sources, (local, slot))),
            after=after[slot],
            slots_of=2,
            at=slot,
            carry=carry,
        )
        carry = [mine, handed]
    return mine, swap(handed, (1, 1))


def gather_blocks(totals, local, reverse):
    table = lax.all_gather(totals, "seq", axis=0, tiled=True)
    blocks = lax.all_gather(local[None], "seq", axis=0, tiled=True)
    own = lax.axis_index("seq")
    order = jnp.arange(table.shape[0], dtype=jnp.int32)
    if reverse:
        inside = (order[None, :] > own) & (order[None, :] < order[:, None])
        selected = order > own
    else:
        inside = (order[None, :] > order[:, None]) & (order[None, :] < own)
        selected = order < own
    exponent = jnp.sum(jnp.where(inside[:, :, None], table[None], 0.0), axis=1)
    factor = jnp.where(selected[:, None], jnp.exp(exponent), 0.0)
    factor = factor.reshape(factor.shape[0], local.shape[0], 1, local.shape[2])
    state = jnp.sum(factor * blocks.astype(F32), axis=0).astype(BF16)
    return state, state


def conv_body(at, base, x_in, taps, x_out, slope_out, top_out, taps_out, ext):
    length, width = x_in.shape
    top_out[...] = x_in[0:16, :]
    taps_out[...] = taps[...]
    ext[0:8, :] = jnp.zeros((8, 128), F32)
    for start in range(0, width, 128):
        lanes = slice(start, start + 128)
        ext[8 : 8 + length, :] = x_in[:, lanes].astype(F32)
        pre = taps[0:1, lanes] * ext[5 : 5 + length, :]
        for k in range(1, 4):
            pre = pre + taps[k : k + 1, lanes] * ext[5 + k : 5 + k + length, :]
        sigma = sigmoid(pre)
        x_out[:, lanes] = (pre * sigma).astype(BF16)
        slope_out[:, lanes] = sigma * (1.0 + pre * (1.0 - sigma))


def state_body(first, at, base, x_low, x_top, x_halo, taps, step_in, cumul_in, *refs):
    length, width = x_low.shape
    if first:
        bc_in, bc_halo, bc_taps, slope_out, x_out, state_out = refs[:6]
        bc_out, bc_slope_out, gram_out, b_turned, ext, bc_ext = refs[6:]

        @pl.when(at[0] == 0)
        def _():
            for j in range(2):
                halo = bc_halo[:, j * 128 : j * 128 + 128].astype(F32)
                bc_ext[5:8, :] = jnp.where(place_bit(base, 5) == 1, 0.0, halo)
                bc_ext[8 : 8 + length, :] = bc_in[j].astype(F32)
                pre = bc_taps[j, 0:1, :] * bc_ext[5 : 5 + length, :]
                for k in range(1, 4):
                    pre = pre + bc_taps[j, k : k + 1, :] * bc_ext[5 + k : 5 + k + length, :]
                sigma = sigmoid(pre)
                bc_out[j] = (pre * sigma).astype(BF16)
                bc_slope_out[j] = sigma * (1.0 + pre * (1.0 - sigma))
            b_turned[...] = bc_out[0].astype(F32).T
            gram_out[...] = jnp.where(
                triangle(length, False), dot_rows(bc_out[1], bc_out[0]), 0.0
            )

    else:
        b_turned, slope_out, x_out, state_out, ext = refs

    top = x_top.shape[0]
    ext[5:8, :] = jnp.where(place_bit(base, 5) == 1, 0.0, x_halo[...].astype(F32))
    ext[8 : 8 + top, :] = x_top[...].astype(F32)
    tail_step = jnp.exp(cumul_in[:, length - 1 :] - cumul_in[...]) * step_in[...]
    for head in range(width // 128):
        lanes = slice(head * 128, head * 128 + 128)
        pre = taps[0:1, lanes] * ext[5 : 5 + top, lanes]
        for k in range(1, 4):
            pre = pre + taps[k : k + 1, lanes] * ext[5 + k : 5 + k + top, lanes]
        sigma = sigmoid(pre)
        x_rows = (pre * sigma).astype(BF16)
        x_out[:, lanes] = x_rows
        slope_out[:, lanes] = sigma * (1.0 + pre * (1.0 - sigma))
        x_head = jnp.concatenate([x_rows, x_low[top:, lanes]], axis=0)
        weighted = (b_turned[...] * tail_step[head : head + 1, :]).astype(BF16)
        state_out[0, :, lanes] = dot(weighted, x_head).astype(BF16)


def inner_body(at, base, gram, step_in, cumul_in, x_in, rows, mixed_out):
    cumul = cumul_in[...]
    cumul_columns = columns_of(cumul)
    for head in range(x_in.shape[1] // 128):
        lanes = slice(head * 128, head * 128 + 128)
        row = cumul[head : head + 1, :]
        decay = jnp.exp(jnp.minimum(cumul_columns[:, head : head + 1] - row, 0.0))
        mixer = (gram[...] * decay * step_in[head : head + 1, :]).astype(BF16)
        x_head = x_in[:, lanes]
        mixed_out[:, lanes] = dot(mixer, x_head) + rows[1:2, lanes] * x_head.astype(F32)


def gate_body(
    at, base, z_in, grad_in, gain, gate_out, gate_slope_out, scaled_out, scaled_gate_out
):
    for start in range(0, z_in.shape[1], 128):
        lanes = slice(start, start + 128)
        z = z_in[:, lanes].astype(F32)
        sigma = sigmoid(z)
        gate = z * sigma
        scaled = grad_in[:, lanes].astype(F32) * gain[:, lanes]
        gate_out[:, lanes] = gate
        gate_slope_out[:, lanes] = sigma * (1.0 + z * (1.0 - sigma))
        scaled_out[:, lanes] = scaled
        scaled_gate_out[:, lanes] = scaled * gate


def lift_body(at, base, bc, step_in, cumul_in, x_in, weighted_x, lifted_out, c_turned):
    @pl.when(at[0] == 0)
    def _():
        c_turned[...] = bc[1].astype(F32).T

    weights = block_weights(step_in[...], cumul_in[...])
    lifted = jnp.exp(cumul_in[...])
    for head in range(x_in.shape[1] // 128):
        lanes = slice(head * 128, head * 128 + 128)
        weight = weights[:, head : head + 1]
        weighted_x[:, lanes] = (weight * x_in[:, lanes].astype(F32)).astype(BF16)
        lifted_out[:, lanes] = (c_turned[...] * lifted[head : head + 1, :]).astype(BF16)


def mix_body(
    at, base, mixed_in, c_rows, cumul_in, state, gate_in, scaled_in, sums_in, *outs
):
    mixed_out, sums_out, squares, products = outs
    group, groups = at

    @pl.when(group == 0)
    def _():
        squares[...] = jnp.zeros_like(squares)
        products[...] = jnp.zeros_like(products)

    carried = dot(c_rows[0], state[0])
    lifted = jnp.exp(columns_of(cumul_in[...]))
    square, product = squares[...], products[...]
    for head in range(mixed_in.shape[1] // 128):
        lanes = slice(head * 128, head * 128 + 128)
        mixed = mixed_in[:, lanes] + lifted[:, head : head + 1] * carried[:, lanes]
        mixed_out[:, lanes] = mixed
        gated = mixed * gate_in[:, lanes]
        square = square + gated * gated
        product = product + mixed * scaled_in[:, lanes]
    squares[...] = square
    products[...] = product

    @pl.when(group == groups - 1)
    def _():
        sums_out[...] = sums_in[...]
        sums_out[0:1, :] += jnp.sum(squares[...].T, axis=0, keepdims=True)
        sums_out[1:2, :] += jnp.sum(products[...].T, axis=0, keepdims=True)


def square_body(at, base, mixed_in, gate_in, squared):
    for start in range(0, mixed_in.shape[1], 128):
        lanes = slice(start, start + 128)
        gate = gate_in[:, lanes]
        squared[:, lanes] = mixed_in[:, lanes] * gate * gate


def norm_scales(at, inner, sums, alpha, beta):
    @pl.when(at[0] == 0)
    def _():
        total = sums[0][...]
        for part in sums[1:]:
            total = total + part[...]
        inv_rms = lax.rsqrt(total[0:1, :] / inner + EPS)
        mean_dot = inv_rms * total[1:2, :] / inner
        alpha[...] = jnp.broadcast_to(inv_rms, alpha.shape).T
        beta[...] = jnp.broadcast_to(inv_rms * inv_rms * mean_dot, beta.shape).T


def grad_mixed_body(inner, parts, at, base, *refs):
    sums = refs[:parts]
    squared, scaled_in, lifted_c, grad_mixed, state_out, alpha, beta = refs[parts:]
    norm_scales(at, inner, sums, alpha, beta)
    for start in range(0, squared.shape[1], 128):
        lanes = slice(start, start + 128)
        low = (alpha[...] * scaled_in[:, lanes] - beta[...] * squared[:, lanes]).astype(BF16)
        grad_mixed[:, lanes] = low
        state_out[0, :, lanes] = dot(lifted_c[:, lanes], low).astype(BF16)


def grad_z_body(inner, parts, at, base, *refs):
    sums = refs[:parts]
    mixed_in, gate_in, gate_slope_in, scaled_in, grad_z, alpha, beta = refs[parts:]
    norm_scales(at, inner, sums, alpha, beta)
    for start in range(0, mixed_in.shape[1], 128):
        lanes = slice(start, start + 128)
        mixed = mixed_in[:, lanes]
        grad_gated = alpha[...] * scaled_in[:, lanes] - beta[...] * (mixed * gate_in[:, lanes])
        grad_z[:, lanes] = (grad_gated * (mixed * gate_slope_in[:, lanes])).astype(BF16)


def inner_back_body(
    last,
    at,
    base,
    gram,
    bc,
    step_in,
    cumul_in,
    x_in,
    grad_in,
    state_in,
    rows,
    sums_in,
    grad_x,
    q_out,
    r_out,
    bc_out,
    z_sum,
    c_sum,
):
    group, groups = at
    length = x_in.shape[0]

    @pl.when(group == 0)
    def _():
        z_sum[...] = sums_in[0]
        c_sum[...] = sums_in[1]

    cumul = cumul_in[...]
    cumul_columns = columns_of(cumul)
    lifted = jnp.exp(cumul_columns)
    state = state_in[0]
    c_rows = bc[1].astype(F32)
    lane = lax.broadcasted_iota(jnp.int32, (length, 128), 1)
    q_columns = jnp.zeros((length, 128), F32)
    for head in range(x_in.shape[1] // 128):
        lanes = slice(head * 128, head * 128 + 128)
        step = step_in[head : head + 1, :]
        decay = jnp.exp(
            jnp.minimum(cumul_columns[:, head : head + 1] - cumul[head : head + 1, :], 0.0)
        )
        gram_decay = gram[...] * decay
        mixer = (gram_decay * step).astype(BF16)
        x_head, grad_head = x_in[:, lanes], grad_in[:, lanes]
        product = dot_rows(grad_head, x_head)
        z_sum[...] += product * decay * step
        gram_grad = product * gram_decay
        r_out[head : head + 1, :] = jnp.sum(gram_grad, axis=0, keepdims=True)
        handed = lifted[:, head : head + 1] * dot_rows(grad_head, state[:, lanes])
        c_sum[...] += handed
        q = jnp.sum(gram_grad * step + c_rows * handed, axis=1, keepdims=True)
        q_columns = jnp.where(lane == head, q, q_columns)
        grad_x[:, lanes] = dot_columns(mixer, grad_head) + rows[1:2, lanes] * grad_head.astype(F32)
    q_out[...] = q_columns.T[:GROUP, :]

    @pl.when(group == groups - 1)
    def _():
        if last:
            summed = jnp.where(triangle(length, False), z_sum[...], 0.0)
            bc_out[0] = dot_split(summed.T, bc[1])
            bc_out[1] = c_sum[...] + dot_split(summed, bc[0])
        else:
            bc_out[0] = z_sum[...]
            bc_out[1] = c_sum[...]


def block_weights(step, cumul):
    return columns_of(jnp.exp(cumul[:, cumul.shape[1] - 1 :] - cumul) * step)


def rim_body(last, at, base, bc, step_in, cumul_in, weighted_x, partial, slope, out_in, *refs):
    group, groups = at
    width = weighted_x.shape[1]
    if last:
        rows_before, b_before, bc_partial, bc_slope, rim_out, bc_out, b_sum = refs
    else:
        rim_out, b_sum = refs

    @pl.when(group == 0)
    def _():
        b_sum[...] = b_before[...] if last else jnp.zeros_like(b_sum)

    out_low = out_in[0]
    b_sum[...] += dot_rows(weighted_x[...], out_low)
    weights = block_weights(step_in[...], cumul_in[...])[0:8, :]
    returned = dot(bc[0][0:16, :], out_low)[0:8, :]
    start = group
    if last:
        count = rim_out.shape[1] // width
        start = lax.rem(group + count - groups + first_group(base), count)
    for head in range(width // 128):
        lanes = slice(head * 128, head * 128 + 128)
        weight = weights[:, head : head + 1]
        rows = (partial[0:8, lanes] + weight * returned[:, lanes]) * slope[0:8, lanes]
        place = pl.multiple_of(jnp.int32(start) * width + head * 128, 128)
        rim_out[:, pl.ds(place, 128)] = rows[0:3, :]

    if last:

        @pl.when(group == groups - 1)
        def _():
            before = rows_before.shape[1]
            if before < rim_out.shape[1] - 256:
                place = pl.multiple_of(first_group(base) * width, 128)
                rim_out[:, pl.ds(place, before)] = rows_before[...]
            bc_out[0] = (b_sum[...] + bc_partial[0]) * bc_slope[0]
            bc_out[1] = bc_partial[1] * bc_slope[1]
            for j in range(2):
                lanes = rim_out.shape[1] - 256 + 128 * j
                rim_out[:, lanes : lanes + 128] = bc_out[j, 0:3, :]


def grad_dt_body(
    at,
    base,
    bc,
    rate,
    dt_slope,
    step_in,
    cumul_in,
    q_in,
    r_in,
    x_in,
    state_in,
    out_in,
    grad_dt,
    selector,
    products,
):
    heads, length = q_in.shape
    width = state_in.shape[2]
    row = lax.broadcasted_iota(jnp.int32, selector.shape, 0)
    lane = lax.broadcasted_iota(jnp.int32, selector.shape, 1)
    selector[...] = (lax.shift_right_logical(row, 7) == lane).astype(BF16)
    row = lax.broadcasted_iota(jnp.int32, (16, width), 0)
    lane = lax.shift_right_logical(lax.broadcasted_iota(jnp.int32, (16, width), 1), 7)
    dots = jnp.zeros((16, 1), F32)
    for group in range(state_in.shape[0]):
        out_low = out_in[group]
        returned = dot(bc[0], out_low)
        for start in range(0, width, 128):
            lanes = slice(start, start + 128)
            place = slice(group * width + start, group * width + start + 128)
            products[:, place] = (x_in[:, place].astype(F32) * returned[:, lanes]).astype(BF16)
        summed = dot(jnp.ones((16, length), BF16), state_in[group] * out_low)
        own = row - GROUP * group == lane
        dots = dots + jnp.sum(jnp.where(own, summed, 0.0), axis=1, keepdims=True)
    inner_b = dot(products[...], selector[...]).T[:heads, :]
    cumul, step = cumul_in[...], step_in[...]
    w = jnp.exp(cumul[:, length - 1 :] - cumul) * inner_b
    q, r = q_in[...], r_in[...]
    inside = jnp.sum(step * w, axis=1, keepdims=True)
    end = inside + jnp.exp(cumul[:, length - 1 :]) * dots[:heads]
    last = lax.broadcasted_iota(jnp.int32, (heads, length), 1) == length - 1
    grad_cumul = q - step * (r + w) + jnp.where(last, end, 0.0)
    grad_log = dot_split(grad_cumul, triangle(length, False).astype(BF16))
    grad_dt[...] = (r + w + rate[...] * grad_log) * dt_slope[...]


def grad_x_body(
    at,
    base,
    bc,
    step_in,
    cumul_in,
    partial,
    slope,
    taps,
    halo,
    out_in,
    grad_x,
    ext,
):
    length, width = partial.shape
    weights = block_weights(step_in[...], cumul_in[...])
    returned = dot(bc[0], out_in[0])
    for head in range(width // 128):
        lanes = slice(head * 128, head * 128 + 128)
        weight = weights[:, head : head + 1]
        ext[0:length, :] = (partial[:, lanes] + weight * returned[:, lanes]) * slope[:, lanes]
        ext[length : length + 3, :] = jnp.where(place_bit(base, 6) == 1, 0.0, halo[:, lanes])
        total = taps[0:1, lanes] * ext[3 : 3 + length, :]
        for k in range(1, 4):
            total = total + taps[k : k + 1, lanes] * ext[3 - k : 3 - k + length, :]
        grad_x[:, lanes] = total.astype(BF16)


def bc_back_body(at, place, grad_pre, halo, taps, kept, sent, ext, total):
    length, half = grad_pre.shape[1], kept.shape[1]
    for j in range(2):
        ext[0:length, :] = grad_pre[j]
        rim = halo[:, 128 * j : 128 * j + 128]
        ext[length : length + 3, :] = jnp.where(place_bit(place, 6) == 1, 0.0, rim)
        summed = taps[j, 0:1, :] * ext[3 : 3 + length, :]
        for k in range(1, 4):
            summed = summed + taps[j, k : k + 1, :] * ext[3 - k : 3 - k + length, :]
        total[...] = summed
        kept[j] = total[pl.ds(pl.multiple_of(place_bit(place, 3) * half, half), half), :]
        sent[j] = total[pl.ds(pl.multiple_of((1 - place_bit(place, 3)) * half, half), half), :]


def bc_half_body(at, place, mine, taken, kept, sent, total):
    half = kept.shape[1]
    for j in range(2):
        total[...] = mine[j] + taken[j]
        kept[j] = total[pl.ds(pl.multiple_of(place_bit(place, 4) * half, half), half), :]
        sent[j] = total[pl.ds(pl.multiple_of((1 - place_bit(place, 4)) * half, half), half), :]


def bc_last_body(at, _, mine, taken, out):
    out[...] = (mine[...] + taken[...]).astype(BF16)


def conv_back(extended, weights):
    length = extended.shape[-2] - 3
    summed = weights[..., 0, :][..., None, :] * extended[..., 3 : 3 + length, :]
    for k in range(1, 4):
        summed = (
            summed
            + weights[..., k, :][..., None, :] * extended[..., 3 - k : 3 - k + length, :]
        )
    return summed


def shards(
    x_input,
    z_input,
    bc_input,
    dt_raw,
    dt_bias,
    a_log,
    d_skip,
    conv_x,
    convolution_bc_taps,
    rescale_factor,
    grad_out,
):
    length, channels = x_input.shape
    heads = dt_raw.shape[0]
    groups = heads // GROUP
    width = GROUP * 128
    count, parts = lax.axis_size("seq"), lax.axis_size("head")
    inner = channels * parts
    own = lax.axis_index("seq")
    split = count == 8 and groups == 4
    own_half = groups // 2 if split else groups
    bit = lambda value, place: lax.shift_right_logical(value, place) & 1
    along_head = lax.axis_index("head")
    base = bit(own, 0) * own_half if split else own * 0
    ends = (own == 0).astype(jnp.int32), (own == count - 1).astype(jnp.int32)
    for place, value in enumerate(
        (bit(own, 2), bit(own, 1), bit(own, 0), bit(along_head, 1), bit(along_head, 0), *ends)
    ):
        base = base | lax.shift_left(value, 8 + place)
    base = base.astype(jnp.int32)[None]

    whole = lambda *shape: ((shape, lambda g, b: (0,) * len(shape)),)
    wide_at = lambda off: (Groups("wide", (length, width), off, groups),)
    rows_at = lambda off: (Groups("heads", (GROUP, length), off, groups),)
    lanes_at = lambda n, off: (Groups("wide", (n, width), off, groups),)
    slot = (Groups("slots", (1, length, width), 0, groups),)
    full = lambda array: (array,) + whole(*array.shape)
    half_width = own_half * width
    half_heads = own_half * GROUP
    half = lambda n: (Groups("half", (n, width), 0, groups),)
    half_rows = (Groups("half heads", (GROUP, length), 0, groups),)
    window_at = lambda n, off: (Groups("window", (n, width), off, groups),)
    halves = [own_half, 0] if split else [0]
    rest = halves[0]

    gain = rescale_factor[None, :]
    f32 = lambda *shape: (shape, F32)
    low = lambda *shape: (shape, BF16)

    step, cumul, rate, dt_slope, rows, rim, bc_rows, bc_taps = call(
        steps_body,
        [
            f32(heads, length) + whole(heads, length),
            f32(heads, length) + whole(heads, length),
            f32(heads, length) + whole(heads, length),
            f32(heads, length) + whole(heads, length),
            f32(2, channels) + whole(2, channels),
            low(3, channels + 256) + whole(3, channels + 256),
            low(2, length, 128) + whole(2, length, 128),
            f32(2, 4, 128) + whole(2, 4, 128),
        ],
        [
            full(in_hbm(dt_raw)),
            full(in_hbm(dt_bias[None, :])),
            full(in_hbm(a_log[None, :])),
            full(in_hbm(d_skip[None, :])),
            (in_hbm(x_input), ((16, channels), lambda g, b: (length // 16 - 1, 0))),
            full(in_hbm(bc_input)),
            full(in_hbm(convolution_bc_taps)),
        ],
        base=base,
    )
    rim_sent = rim
    rim = lax.ppermute(rim, "seq", [(i, (i + 1) % count) for i in range(count)])
    if split:
        swap = lambda block, bit: lax.ppermute(
            block, "seq", [(i, i ^ bit) for i in range(count)]
        )
        total = rows[0:1]
        total_core = swap(total, 1)
        chip_total = total + total_core
        total_across = swap(chip_total, 2)
        table = f32(16, channels) + whole(16, channels)
        ahead, behind = call(
            weights_body,
            [table, table],
            [full(rows), full(total_core), full(total_across)],
            base=base,
            )

    def passed(locals_, reverse, beside):
        if split:
            local_sent, local = locals_[rest], locals_[0]
            weights = behind if reverse else ahead
            return scan_blocks(base, groups, weights, local, local_sent, reverse, beside)
        local = locals_[0]
        for work in beside:
            work(local)
        return gather_blocks(rows[0:1], local, reverse)

    x_low, slope, local = {}, {}, {}
    ready = rim_sent
    for off in halves:
        x_low[off], slope[off], x_top, taps = call(
            conv_body,
            [
                low(length, half_width) + half(length),
                f32(length, half_width) + half(length),
                low(16, half_width) + half(16),
                f32(4, half_width) + half(4),
            ],
            [(in_hbm(x_input),) + wide_at(off), (in_hbm(conv_x),) + lanes_at(4, off)],
            base=base,
            grid=own_half,
            scratch=[pltpu.VMEM((length + 8, 128), F32)],
            after=[ready],
        )
        first = off == rest
        top = (Groups("top", (16, width), 0, groups),)
        ins = [
            (x_low[off],) + half(length),
            (x_top,) + half(16),
            (rim,) + lanes_at(3, off),
            (taps,) + half(4),
            (step,) + rows_at(off),
            (cumul,) + rows_at(off),
        ]
        outs = [
            f32(length, half_width) + top,
            low(length, half_width) + top,
            low(own_half, length, width) + slot,
        ]
        scratch = [pltpu.VMEM((24, width), F32)]
        if first:
            ins += [
                full(bc_rows),
                (rim, ((3, 256), lambda g, b: (0, channels // 256))),
                full(bc_taps),
            ]
            outs += [
                low(2, length, 128) + whole(2, length, 128),
                f32(2, length, 128) + whole(2, length, 128),
                f32(length, length) + whole(length, length),
                f32(128, length) + whole(128, length),
            ]
            scratch += [pltpu.VMEM((length + 8, 128), F32)]
        else:
            ins += [full(b_turned)]
        result = call(
            functools.partial(state_body, first),
            outs,
            ins,
            base=base,
            loop=own_half,
            scratch=scratch,
            carry=[slope[off]],
            place={0: 1},
            flops=2 * length * 128 * half_width,
        )
        if first:
            bc, bc_slope, gram, b_turned = result[3:]
        slope[off], x_low[off], local[off] = result[:3]
        ready = local[off]

    inside, gate, gate_slope, scaled, scaled_gate = {}, {}, {}, {}, {}

    def mix_inside(off, ready):
        inside[off], token = call(
            inner_body,
            [f32(length, half_width) + half(length)],
            [
                full(gram),
                (step,) + rows_at(off),
                (cumul,) + rows_at(off),
                (x_low[off],) + half(length),
                (rows,) + lanes_at(2, off),
            ],
            base=base,
            loop=own_half,
            after=[ready],
            token=True,
            flops=2 * length * 128 * half_width,
        )
        return token

    def gates(off, ready):
        gate[off], gate_slope[off], scaled[off], scaled_gate[off], token = call(
            gate_body,
            [f32(length, half_width) + half(length)] * 4,
            [
                (z_input,) + wide_at(off),
                (grad_out,) + wide_at(off),
                (gain,) + lanes_at(1, off),
            ],
            base=base,
            loop=own_half,
            after=[ready],
            token=True,
        )
        return token

    def mix_second(ready):
        tokens = [mix_inside(rest, ready)] if split else []
        tokens += [gates(off, ready) for off in reversed(halves)]
        return [], tokens

    states = passed(local, False, (functools.partial(mix_inside, 0), mix_second))
    states = dict(zip((0, rest), states))
    mixed, sums = {}, jnp.zeros((8, length), F32)
    two_scales = [pltpu.VMEM((length, 128), F32), pltpu.VMEM((length, 128), F32)]
    for off in reversed(halves):
        mixed[off], sums = call(
            mix_body,
            [f32(length, half_width) + half(length), f32(8, length) + whole(8, length)],
            [
                (inside[off],) + half(length),
                (bc, ((1, length, 128), lambda g, b: (1, 0, 0))),
                (cumul,) + rows_at(off),
                (states[off],) + slot,
                (gate[off],) + half(length),
                (scaled_gate[off],) + half(length),
                full(sums),
            ],
            base=base,
            loop=own_half,
            scratch=two_scales,
            flops=2 * length * 128 * half_width,
        )
    turn_head = lambda block, bit: lax.ppermute(
        block, "head", [(i, i ^ bit) for i in range(parts)]
    )
    weighted_x, lifted_c, squared = {}, {}, {}
    for off in halves:
        weighted_x[off], lifted_c[off] = call(
            lift_body,
            [low(length, half_width) + half(length), low(length, half_width) + half(length)],
            [
                full(bc),
                (step,) + rows_at(off),
                (cumul,) + rows_at(off),
                (x_low[off],) + half(length),
            ],
            base=base,
            loop=own_half,
            scratch=[pltpu.VMEM((128, length), F32)],
            after=[sums],
        )
        (squared[off],) = call(
            square_body,
            [f32(length, half_width) + half(length)],
            [(mixed[off],) + half(length), (gate[off],) + half(length)],
            base=base,
            loop=own_half,
        )
    if parts == 4:
        sums = sums + turn_head(sums, 1)
        all_sums = [sums, turn_head(sums, 2)]
    else:
        all_sums = [lax.psum(sums, "head")]
    grad_mixed, local_back = {}, {}
    for off in halves:
        grad_mixed[off], local_back[off] = call(
            functools.partial(grad_mixed_body, inner, len(all_sums)),
            [low(length, half_width) + half(length), low(own_half, length, width) + slot],
            [full(part) for part in all_sums]
            + [
                (squared[off],) + half(length),
                (scaled_gate[off],) + half(length),
                (lifted_c[off],) + half(length),
            ],
            base=base,
            loop=own_half,
            scratch=two_scales,
            flops=2 * length * 128 * half_width,
        )

    partial, q_rows, r_rows = {}, {}, {}
    carried = {"sums": jnp.zeros((2, length, 128), F32), "z": [], "dt": [], "x": []}

    def back_inside(off, ready):
        partial[off], q_rows[off], r_rows[off], carried["sums"], token = call(
            functools.partial(inner_back_body, off == rest),
            [
                f32(length, half_width) + half(length),
                f32(half_heads, length) + half_rows,
                f32(half_heads, length) + half_rows,
                f32(2, length, 128) + whole(2, length, 128),
            ],
            [
                full(gram),
                full(bc),
                (step,) + rows_at(off),
                (cumul,) + rows_at(off),
                (x_low[off],) + half(length),
                (grad_mixed[off],) + half(length),
                (states[off],) + slot,
                (rows,) + lanes_at(2, off),
                full(carried["sums"]),
            ],
            base=base,
            loop=own_half,
            scratch=[pltpu.VMEM((length, length), F32), pltpu.VMEM((length, 128), F32)],
            after=[ready],
            token=True,
            flops=6 * length * 128 * half_width,
        )
        return token

    def back_gates(off, ready):
        grad_z, token = call(
            functools.partial(grad_z_body, inner, len(all_sums)),
            [low(length, channels) + window_at(length, off)],
            [full(part) for part in all_sums]
            + [
                (mixed[off],) + half(length),
                (gate[off],) + half(length),
                (gate_slope[off],) + half(length),
                (scaled[off],) + half(length),
            ],
            base=base,
            loop=own_half,
            scratch=two_scales,
            carry=carried["z"],
            after=[ready],
            token=True,
        )
        carried["z"] = [grad_z]
        carried["z_token"] = token
        return token

    def back_second(ready):
        token = back_inside(rest, ready) if split else ready
        return [token], [back_gates(0, token)]

    backs = passed(local_back, True, (functools.partial(back_inside, 0), back_second))
    backs = dict(zip((0, rest), backs))
    z_tokens = [back_gates(rest, carried["z_token"])] if split else []

    def make_grad_dt(off, after):
        table = (Groups("heads", (half_heads, length), off, groups, own_half),)
        window = (Groups("window heads", (half_heads, length), off, groups, own_half),)
        grad_dt, token = call(
            grad_dt_body,
            [f32(heads, length) + window],
            [
                full(bc),
                (rate,) + table,
                (dt_slope,) + table,
                (step,) + table,
                (cumul,) + table,
                full(q_rows[off]),
                full(r_rows[off]),
                full(x_low[off]),
                full(states[off]),
                full(backs[off]),
            ],
            base=base,
            scratch=[pltpu.VMEM((half_width, 128), BF16), pltpu.VMEM((length, half_width), BF16)],
            carry=carried["dt"],
            after=after,
            token=True,
            flops=4 * length * 128 * half_width,
        )
        carried["dt"] = [grad_dt]
        return token

    def make_grad_x(off, after):
        grad_x, token = call(
            grad_x_body,
            [low(length, channels) + window_at(length, off)],
            [
                full(bc),
                (step,) + rows_at(off),
                (cumul,) + rows_at(off),
                (partial[off],) + half(length),
                (slope[off],) + half(length),
                (conv_x,) + lanes_at(4, off),
                (rim_back,) + lanes_at(3, off),
                (backs[off],) + slot,
            ],
            base=base,
            loop=own_half,
            scratch=[pltpu.VMEM((length + 8, 128), F32)],
            carry=carried["x"],
            after=after,
            token=True,
            flops=2 * length * 128 * half_width,
        )
        carried["x"] = [grad_x]
        return token

    def make_rim(off, before, after):
        last = off == rest
        if last:
            outs = [
                f32(3, channels + 256) + whole(3, channels + 256),
                f32(2, length, 128) + whole(2, length, 128),
            ]
        else:
            outs = [f32(3, half_width) + whole(3, half_width), f32(length, 128) + whole(length, 128)]
        return call(
            functools.partial(rim_body, last),
            outs,
            [
                full(bc),
                (step,) + rows_at(off),
                (cumul,) + rows_at(off),
                (weighted_x[off],) + half(length),
                (partial[off],) + half(length),
                (slope[off],) + half(length),
                (backs[off],) + slot,
            ]
            + [full(array) for array in before],
            base=base,
            loop=own_half,
            scratch=[pltpu.VMEM((length, 128), F32)] if last else [],
            after=after,
            flops=2 * length * 128 * half_width,
        )

    if split:
        before = make_rim(0, [], [])
        z_tokens.append(make_grad_dt(0, [before[1]]))
    else:
        before = [jnp.zeros((3, channels), F32), jnp.zeros((length, 128), F32)]
    rim_back, grad_bc_pre = make_rim(rest, [*before, carried["sums"], bc_slope], z_tokens)
    rim_back = lax.ppermute(rim_back, "seq", [(i, (i - 1) % count) for i in range(count)])
    dt_token = make_grad_dt(rest, [grad_bc_pre])
    if parts == 4:
        piece = lambda rows: f32(2, rows, 128) + whole(2, rows, 128)
        kept, sent = call(
            bc_back_body,
            [piece(length // 2), piece(length // 2)],
            [
                full(grad_bc_pre),
                (rim_back, ((3, 256), lambda g, b: (0, channels // 256))),
                full(bc_taps),
            ],
            base=base,
            scratch=[pltpu.VMEM((length + 8, 128), F32), pltpu.VMEM((length, 128), F32)],
            after=[dt_token],
        )
        taken = turn_head(sent, 2)
        x_tokens = [make_grad_x(0, [sent])]
        kept, sent = call(
            bc_half_body,
            [piece(length // 4), piece(length // 4)],
            [full(kept), full(taken)],
            base=base,
            scratch=[pltpu.VMEM((length // 2, 128), F32)],
            after=x_tokens,
        )
        taken = turn_head(sent, 1)
        x_tokens = [make_grad_x(rest, [sent])] if split else []
        (grad_bc,) = call(
            bc_last_body,
            [low(2, length // 4, 128) + whole(2, length // 4, 128)],
            [full(kept), full(taken)],
            base=base,
            after=x_tokens,
        )
    else:
        for off in halves:
            make_grad_x(off, [])
        bc_halo = jnp.moveaxis(rim_back[:, channels:].reshape(3, 2, 128), 1, 0)
        bc_halo = jnp.where(own == count - 1, 0.0, bc_halo)
        bc_sum = conv_back(jnp.concatenate([grad_bc_pre, bc_halo], axis=1), convolution_bc_taps)
        share = length // parts
        bc_sum = lax.psum(bc_sum, "head")
        grad_bc = lax.dynamic_slice_in_dim(bc_sum, along_head * share, share, 1).astype(BF16)
    return (carried["x"][0], carried["z"][0], grad_bc, carried["dt"][0])


def solution(mesh):
    return jax.shard_map(
        shards,
        mesh=mesh,
        in_specs=(
            P("seq", "head"),
            P("seq", "head"),
            P(None, "seq", None),
            P("head", "seq"),
            P("head"),
            P("head"),
            P("head"),
            P(None, "head"),
            P(),
            P("head"),
            P("seq", "head"),
        ),
        out_specs=(
            P("seq", "head"),
            P("seq", "head"),
            P(None, ("seq", "head"), None),
            P("head", "seq"),
        ),
        check_vma=False,
    )
```

```python
import functools

import jax
import jax.numpy as jnp
from jax import lax
from jax.experimental import pallas as pl
from jax.experimental.pallas import tpu as pltpu
from jax.sharding import PartitionSpec as P

EPS = 1e-05
GROUP = 8
F32 = jnp.float32
BF16 = jnp.bfloat16
VMEM_BYTES = 16 * 2**20


def sigmoid(value):
    return 0.5 + 0.5 * jnp.tanh(0.5 * value)


def dot(a, b):
    return jnp.dot(a, b, preferred_element_type=F32)


def dot_split(a, b):
    high = a.astype(BF16)
    rest = a - high.astype(F32)
    middle = rest.astype(BF16)
    low = (rest - middle.astype(F32)).astype(BF16)
    return dot(high, b) + (dot(middle, b) + dot(low, b))


def dot_rows(a, b):
    return lax.dot_general(a, b, (((1,), (1,)), ((), ())), preferred_element_type=F32)


def dot_columns(a, b):
    return lax.dot_general(a, b, (((0,), (0,)), ((), ())), preferred_element_type=F32)


def triangle(length, upper):
    first = lax.broadcasted_iota(jnp.int32, (length, length), 0)
    second = lax.broadcasted_iota(jnp.int32, (length, length), 1)
    return first <= second if upper else first >= second


def columns_of(rows):
    return rows.T


class Groups:
    def __init__(self, kind, block, off, groups, size=1):
        self.kind, self.block, self.off, self.groups = kind, block, off, groups
        self.size = size
        self.by_rows = kind.endswith("heads")

    def turn(self, group, base):
        first = self.off + first_group(base)
        return lax.rem(group * self.size + first, self.groups) // self.size

    def place(self, index):
        return (index, 0) if self.by_rows else (0, index)

    def spec(self):
        if self.kind == "slots":
            return pl.BlockSpec(self.block, lambda g, b: (g, 0, 0))
        if self.kind.startswith("half"):
            return pl.BlockSpec(self.block, lambda g, b: self.place(g))
        return pl.BlockSpec(self.block, lambda g, b: self.place(self.turn(g, b)))

    def whole(self, shape, count):
        if self.kind.startswith("window"):
            block = list(self.block)
            block[0 if self.by_rows else 1] *= count
            return pl.BlockSpec(
                tuple(block), lambda g, b: self.place(self.turn(0, b) // count)
            )
        if self.kind == "top":
            shape = (self.block[0], count * self.block[1])
        return pl.BlockSpec(shape, lambda g, b: (0,) * len(shape))

    def view(self, ref, group, base):
        if self.kind == "slots":
            return ref.at[pl.ds(group, 1)]
        if self.kind in ("wide", "heads"):
            group = self.turn(group, base)
        size = self.block[0 if self.by_rows else 1]
        span = pl.ds(pl.multiple_of(jnp.int32(group) * size, size), size)
        return ref.at[span] if self.by_rows else ref.at[:, span]


def call(
    body,
    outs,
    ins,
    *,
    base,
    grid=1,
    loop=1,
    scratch=(),
    after=(),
    carry=(),
    place=None,
    token=False,
    flops=0,
):
    aliases = {1 + len(ins) + len(after) + i: i for i in range(len(carry))}
    for read, written in (place or {}).items():
        aliases[1 + read] = written
    after = list(after) + list(carry)
    outs = list(outs)
    if token:
        outs.append(((8, 128), F32, ((8, 128), lambda *_: (0, 0))))

    def spec(shape, block):
        if not isinstance(block, Groups):
            return pl.BlockSpec(*block)
        return block.whole(shape, loop) if grid == 1 else block.spec()

    in_specs = [spec(array.shape, block) for array, block in ins]
    in_specs += [pl.BlockSpec(memory_space=pl.ANY) for _ in after]
    out_specs = [spec(shape, block) for shape, _, block in outs]
    out_shape = [jax.ShapeDtypeStruct(shape, dtype) for shape, dtype, _ in outs]
    arrays = [array for array, _ in ins]
    moved = sum(a.size * a.dtype.itemsize for a in arrays + out_shape)
    blocks = [block for _, block in ins] + [block for _, _, block in outs]

    def ordered(where, *refs):
        taken, rest = refs[: len(ins)], refs[len(ins) + len(after) :]
        results, extra = rest[: len(outs)], rest[len(outs) :]
        if token:
            results[-1][...] = jnp.zeros((8, 128), F32)

        def step(group, _):
            views = [
                block.view(ref, group, where) if isinstance(block, Groups) else ref
                for ref, block in zip(taken + results, blocks)
            ]
            if token:
                views = views[:-1]
            body((group, loop), where, *views, *extra)
            return 0

        if grid > 1:
            views = taken + (results[:-1] if token else results)
            body((pl.program_id(0), grid), where, *views, *extra)
        elif loop > 1:
            lax.fori_loop(0, loop, step, 0)
        else:
            step(0, 0)

    return pl.pallas_call(
        ordered,
        out_shape=out_shape,
        grid_spec=pltpu.PrefetchScalarGridSpec(
            num_scalar_prefetch=1,
            grid=(grid,),
            in_specs=in_specs,
            out_specs=out_specs,
            scratch_shapes=list(scratch),
        ),
        input_output_aliases=aliases,
        cost_estimate=pl.CostEstimate(flops=flops, bytes_accessed=moved, transcendentals=0),
        compiler_params=pltpu.CompilerParams(vmem_limit_bytes=VMEM_BYTES),
    )(base, *arrays, *after)


def in_hbm(array):
    return pltpu.with_memory_space_constraint(array, pltpu.HBM)


def column_of(row):
    count = row.shape[1]
    first = lax.broadcasted_iota(jnp.int32, (count, count), 0)
    second = lax.broadcasted_iota(jnp.int32, (count, count), 1)
    return jnp.sum(jnp.where(first == second, row, 0.0), axis=1, keepdims=True)


def steps_body(
    at,
    base,
    raw,
    bias,
    log_rate,
    skip,
    x_tail,
    bc_in,
    bc_taps,
    step_out,
    cumul_out,
    rate_out,
    slope_out,
    rows_out,
    rim_out,
    bc_in_out,
    bc_taps_out,
):
    bc_in_out[...] = bc_in[...]
    bc_taps_out[...] = bc_taps[...]
    heads, length = raw.shape
    channels = x_tail.shape[1]
    rim_out[:, 0:channels] = x_tail[...].astype(F32)[13:16, :].astype(BF16)
    for j in range(2):
        start = channels + 128 * j
        rim_out[:, start : start + 128] = bc_in[j, length - 16 :].astype(F32)[13:16, :].astype(BF16)
    shifted = raw[...] + column_of(bias[...])
    step = jnp.maximum(shifted, 0.0) + jnp.log1p(jnp.exp(-jnp.abs(shifted)))
    rate = jnp.broadcast_to(-jnp.exp(column_of(log_rate[...])), step.shape)
    cumul = dot_split(rate * step, triangle(length, True).astype(BF16))
    step_out[...] = step
    cumul_out[...] = cumul
    rate_out[...] = rate
    slope_out[...] = sigmoid(shifted)
    skips = column_of(skip[...])
    for head in range(heads):
        lanes = slice(head * 128, head * 128 + 128)
        rows_out[0:1, lanes] = jnp.broadcast_to(cumul[head : head + 1, length - 1 :], (1, 128))
        rows_out[1:2, lanes] = jnp.broadcast_to(skips[head : head + 1, :], (1, 128))


def pick(test, yes, no):
    return jnp.where(test, yes, no)


def first_group(place):
    return place[0] & 255


def place_bit(place, index):
    return lax.shift_right_logical(place[0], 8 + index) & 1


def weights_body(at, place, own, core, across, *outs):
    t0, t1 = own[0:1, :], core[...]
    e0, e1, own_chip, ex = jnp.exp(t0), jnp.exp(t1), jnp.exp(t0 + t1), jnp.exp(across[...])
    one = jnp.ones_like(e0)
    zero = jnp.zeros_like(e0)
    bits = [place_bit(place, i) for i in range(3)]
    x_first = bits[2] == 0
    for out, reverse in zip(outs, (False, True)):
        y, x, c = ((1 - bit if reverse else bit) == 1 for bit in bits)
        either = jnp.logical_or(x, y)
        scale = pick(jnp.logical_or(x_first, either), one, ex)
        rows = [pick(c, one, e1), pick(c, e0, one)]
        rows += [rows[0] * scale, rows[1] * scale]
        rows += [
            pick(x_first, pick(x, one, ex), pick(jnp.logical_and(x, y), zero, one)),
            pick(x_first, pick(x, own_chip, one), pick(y, pick(x, one, own_chip), zero)),
        ]
        a = pick(x_first, pick(x, one, zero), pick(y, pick(x, ex, one), zero))
        b = pick(x_first, pick(y, pick(x, ex, one), zero), pick(either, one, zero))
        into, send = pick(c, e1, one), pick(c, one, e0)
        rows += [into * a, into * b, pick(c, one, zero)]
        rows += [send * a, send * b, pick(c, zero, one)]
        for index, row in enumerate(rows):
            out[index : index + 1, :] = row


def combine(base, groups, weights, outs, after=(), slots_of=None, at=0, carry=()):
    arrays, columns = [], []
    for slots in outs:
        for column, terms in slots:
            if column not in columns:
                columns.append(column)
            for _, (array, slot) in terms:
                if not any(array is a and slot == s for a, s in arrays):
                    arrays.append((array, slot))
    place = lambda array, slot: [
        i for i, (a, s) in enumerate(arrays) if a is array and s == slot
    ][0]
    plan = [
        [
            (columns.index(column), [(row, place(*source)) for row, source in terms])
            for column, terms in slots
        ]
        for slots in outs
    ]

    def body(at, base, *refs):
        rows, values = refs[: len(columns)], refs[len(columns) : len(columns) + len(arrays)]
        results = refs[len(columns) + len(arrays) :]
        width = rows[0].shape[1]
        for result, slots in zip(results, plan):
            for slot, (column, terms) in enumerate(slots):
                for start in range(0, width, 256):
                    lanes = slice(start, start + 256)
                    total = None
                    for row, index in terms:
                        term = rows[column][row : row + 1, lanes] * values[index][
                            0, :, lanes
                        ].astype(F32)
                        total = term if total is None else total + term
                    result[slot, :, lanes] = total.astype(BF16)

    length, width = arrays[0][0].shape[1:]
    block = lambda slot, count: ((count, length, width), lambda g, b: (slot, 0, 0))
    ins = [
        (
            weights,
            (
                (weights.shape[0], width),
                lambda g, b, column=column: (0, lax.rem(first_group(b) + column, groups)),
            ),
        )
        for column in columns
    ]
    ins += [(array, block(slot, 1)) for array, slot in arrays]
    results = [
        ((slots_of or len(slots), length, width), BF16, block(at, len(slots))) for slots in outs
    ]
    return call(body, results, ins, base=base, after=after, carry=carry)


def scan_blocks(base, groups, weights, local, local_sent, reverse, beside):
    count = lax.axis_size("seq")

    def swap(block, bits):
        route = [(i, i ^ bits[i % 2]) for i in range(count)]
        return lax.ppermute(block, "seq", route)

    def merge(slot, *plans, **places):
        outs = [[(slot, list(zip(rows, sources)))] for rows, sources in plans]
        return combine(base, groups, weights, outs, **places)

    taken = swap(local_sent, (1, 1))
    chips, first_taken, sent, second_taken = [], [], [], []
    for slot in range(2):
        both = ((local, slot), (taken, slot))
        chip, chip_sent = merge(slot, ((0, 1), both), ((2, 3), both))
        chips.append(chip)
        first_taken.append(swap(chip_sent, (2, 4)))
    after = [beside[0](chips[1])]
    for slot in range(2):
        sources = ((chips[slot], 0), (first_taken[slot], 0))
        (block,) = merge(slot, ((4, 5), sources), after=after)
        sent.append(block)
        second_taken.append(swap(block, (4, 2)))
        after = []
    after = beside[1](sent[1])
    carry = []
    for slot in range(2):
        sources = ((first_taken[slot], 0), (second_taken[slot], 0))
        mine, handed = merge(
            slot,
            ((6, 7, 8), (*sources, (taken, slot))),
            ((9, 10, 11), (*sources, (local, slot))),
            after=after[slot],
            slots_of=2,
            at=slot,
            carry=carry,
        )
        carry = [mine, handed]
    return mine, swap(handed, (1, 1))


def gather_blocks(totals, local, reverse):
    table = lax.all_gather(totals, "seq", axis=0, tiled=True)
    blocks = lax.all_gather(local[None], "seq", axis=0, tiled=True)
    own = lax.axis_index("seq")
    order = jnp.arange(table.shape[0], dtype=jnp.int32)
    if reverse:
        inside = (order[None, :] > own) & (order[None, :] < order[:, None])
        selected = order > own
    else:
        inside = (order[None, :] > order[:, None]) & (order[None, :] < own)
        selected = order < own
    exponent = jnp.sum(jnp.where(inside[:, :, None], table[None], 0.0), axis=1)
    factor = jnp.where(selected[:, None], jnp.exp(exponent), 0.0)
    factor = factor.reshape(factor.shape[0], local.shape[0], 1, local.shape[2])
    state = jnp.sum(factor * blocks.astype(F32), axis=0).astype(BF16)
    return state, state


def conv_body(at, base, x_in, taps, x_out, slope_out, top_out, taps_out, ext):
    length, width = x_in.shape
    top_out[...] = x_in[0:16, :]
    taps_out[...] = taps[...]
    ext[0:8, :] = jnp.zeros((8, 128), F32)
    for start in range(0, width, 128):
        lanes = slice(start, start + 128)
        ext[8 : 8 + length, :] = x_in[:, lanes].astype(F32)
        pre = taps[0:1, lanes] * ext[5 : 5 + length, :]
        for k in range(1, 4):
            pre = pre + taps[k : k + 1, lanes] * ext[5 + k : 5 + k + length, :]
        sigma = sigmoid(pre)
        x_out[:, lanes] = (pre * sigma).astype(BF16)
        slope_out[:, lanes] = sigma * (1.0 + pre * (1.0 - sigma))


def state_body(first, at, base, x_low, x_top, x_halo, taps, step_in, cumul_in, *refs):
    length, width = x_low.shape
    if first:
        bc_in, bc_halo, bc_taps, slope_out, x_out, state_out = refs[:6]
        bc_out, bc_slope_out, gram_out, b_turned, ext, bc_ext = refs[6:]

        @pl.when(at[0] == 0)
        def _():
            for j in range(2):
                halo = bc_halo[:, j * 128 : j * 128 + 128].astype(F32)
                bc_ext[5:8, :] = jnp.where(place_bit(base, 5) == 1, 0.0, halo)
                bc_ext[8 : 8 + length, :] = bc_in[j].astype(F32)
                pre = bc_taps[j, 0:1, :] * bc_ext[5 : 5 + length, :]
                for k in range(1, 4):
                    pre = pre + bc_taps[j, k : k + 1, :] * bc_ext[5 + k : 5 + k + length, :]
                sigma = sigmoid(pre)
                bc_out[j] = (pre * sigma).astype(BF16)
                bc_slope_out[j] = sigma * (1.0 + pre * (1.0 - sigma))
            b_turned[...] = bc_out[0].astype(F32).T
            gram_out[...] = jnp.where(
                triangle(length, False), dot_rows(bc_out[1], bc_out[0]), 0.0
            )

    else:
        b_turned, slope_out, x_out, state_out, ext = refs

    top = x_top.shape[0]
    ext[5:8, :] = jnp.where(place_bit(base, 5) == 1, 0.0, x_halo[...].astype(F32))
    ext[8 : 8 + top, :] = x_top[...].astype(F32)
    tail_step = jnp.exp(cumul_in[:, length - 1 :] - cumul_in[...]) * step_in[...]
    for head in range(width // 128):
        lanes = slice(head * 128, head * 128 + 128)
        pre = taps[0:1, lanes] * ext[5 : 5 + top, lanes]
        for k in range(1, 4):
            pre = pre + taps[k : k + 1, lanes] * ext[5 + k : 5 + k + top, lanes]
        sigma = sigmoid(pre)
        x_rows = (pre * sigma).astype(BF16)
        x_out[:, lanes] = x_rows
        slope_out[:, lanes] = sigma * (1.0 + pre * (1.0 - sigma))
        x_head = jnp.concatenate([x_rows, x_low[top:, lanes]], axis=0)
        weighted = (b_turned[...] * tail_step[head : head + 1, :]).astype(BF16)
        state_out[0, :, lanes] = dot(weighted, x_head).astype(BF16)


def inner_body(at, base, gram, step_in, cumul_in, x_in, rows, mixed_out):
    cumul = cumul_in[...]
    cumul_columns = columns_of(cumul)
    for head in range(x_in.shape[1] // 128):
        lanes = slice(head * 128, head * 128 + 128)
        row = cumul[head : head + 1, :]
        decay = jnp.exp(jnp.minimum(cumul_columns[:, head : head + 1] - row, 0.0))
        mixer = (gram[...] * decay * step_in[head : head + 1, :]).astype(BF16)
        x_head = x_in[:, lanes]
        mixed_out[:, lanes] = dot(mixer, x_head) + rows[1:2, lanes] * x_head.astype(F32)


def gate_body(
    at, base, z_in, grad_in, gain, gate_out, gate_slope_out, scaled_out, scaled_gate_out
):
    for start in range(0, z_in.shape[1], 128):
        lanes = slice(start, start + 128)
        z = z_in[:, lanes].astype(F32)
        sigma = sigmoid(z)
        gate = z * sigma
        scaled = grad_in[:, lanes].astype(F32) * gain[:, lanes]
        gate_out[:, lanes] = gate
        gate_slope_out[:, lanes] = sigma * (1.0 + z * (1.0 - sigma))
        scaled_out[:, lanes] = scaled
        scaled_gate_out[:, lanes] = scaled * gate


def lift_body(at, base, bc, step_in, cumul_in, x_in, weighted_x, lifted_out, c_turned):
    @pl.when(at[0] == 0)
    def _():
        c_turned[...] = bc[1].astype(F32).T

    weights = block_weights(step_in[...], cumul_in[...])
    lifted = jnp.exp(cumul_in[...])
    for head in range(x_in.shape[1] // 128):
        lanes = slice(head * 128, head * 128 + 128)
        weight = weights[:, head : head + 1]
        weighted_x[:, lanes] = (weight * x_in[:, lanes].astype(F32)).astype(BF16)
        lifted_out[:, lanes] = (c_turned[...] * lifted[head : head + 1, :]).astype(BF16)


def mix_body(
    at, base, mixed_in, c_rows, cumul_in, state, gate_in, scaled_in, sums_in, *outs
):
    mixed_out, sums_out, squares, products = outs
    group, groups = at

    @pl.when(group == 0)
    def _():
        squares[...] = jnp.zeros_like(squares)
        products[...] = jnp.zeros_like(products)

    carried = dot(c_rows[0], state[0])
    lifted = jnp.exp(columns_of(cumul_in[...]))
    square, product = squares[...], products[...]
    for head in range(mixed_in.shape[1] // 128):
        lanes = slice(head * 128, head * 128 + 128)
        mixed = mixed_in[:, lanes] + lifted[:, head : head + 1] * carried[:, lanes]
        mixed_out[:, lanes] = mixed
        gated = mixed * gate_in[:, lanes]
        square = square + gated * gated
        product = product + mixed * scaled_in[:, lanes]
    squares[...] = square
    products[...] = product

    @pl.when(group == groups - 1)
    def _():
        sums_out[...] = sums_in[...]
        sums_out[0:1, :] += jnp.sum(squares[...].T, axis=0, keepdims=True)
        sums_out[1:2, :] += jnp.sum(products[...].T, axis=0, keepdims=True)


def square_body(at, base, mixed_in, gate_in, squared):
    for start in range(0, mixed_in.shape[1], 128):
        lanes = slice(start, start + 128)
        gate = gate_in[:, lanes]
        squared[:, lanes] = mixed_in[:, lanes] * gate * gate


def norm_scales(at, inner, sums, alpha, beta):
    @pl.when(at[0] == 0)
    def _():
        total = sums[0][...]
        for part in sums[1:]:
            total = total + part[...]
        inv_rms = lax.rsqrt(total[0:1, :] / inner + EPS)
        mean_dot = inv_rms * total[1:2, :] / inner
        alpha[...] = jnp.broadcast_to(inv_rms, alpha.shape).T
        beta[...] = jnp.broadcast_to(inv_rms * inv_rms * mean_dot, beta.shape).T


def grad_mixed_body(inner, parts, at, base, *refs):
    sums = refs[:parts]
    squared, scaled_in, lifted_c, grad_mixed, state_out, alpha, beta = refs[parts:]
    norm_scales(at, inner, sums, alpha, beta)
    for start in range(0, squared.shape[1], 128):
        lanes = slice(start, start + 128)
        low = (alpha[...] * scaled_in[:, lanes] - beta[...] * squared[:, lanes]).astype(BF16)
        grad_mixed[:, lanes] = low
        state_out[0, :, lanes] = dot(lifted_c[:, lanes], low).astype(BF16)


def grad_z_body(inner, parts, at, base, *refs):
    sums = refs[:parts]
    mixed_in, gate_in, gate_slope_in, scaled_in, grad_z, alpha, beta = refs[parts:]
    norm_scales(at, inner, sums, alpha, beta)
    for start in range(0, mixed_in.shape[1], 128):
        lanes = slice(start, start + 128)
        mixed = mixed_in[:, lanes]
        grad_gated = alpha[...] * scaled_in[:, lanes] - beta[...] * (mixed * gate_in[:, lanes])
        grad_z[:, lanes] = (grad_gated * (mixed * gate_slope_in[:, lanes])).astype(BF16)


def inner_back_body(
    last,
    at,
    base,
    gram,
    bc,
    step_in,
    cumul_in,
    x_in,
    grad_in,
    state_in,
    rows,
    sums_in,
    grad_x,
    q_out,
    r_out,
    bc_out,
    z_sum,
    c_sum,
):
    group, groups = at
    length = x_in.shape[0]

    @pl.when(group == 0)
    def _():
        z_sum[...] = sums_in[0]
        c_sum[...] = sums_in[1]

    cumul = cumul_in[...]
    cumul_columns = columns_of(cumul)
    lifted = jnp.exp(cumul_columns)
    state = state_in[0]
    c_rows = bc[1].astype(F32)
    lane = lax.broadcasted_iota(jnp.int32, (length, 128), 1)
    q_columns = jnp.zeros((length, 128), F32)
    for head in range(x_in.shape[1] // 128):
        lanes = slice(head * 128, head * 128 + 128)
        step = step_in[head : head + 1, :]
        decay = jnp.exp(
            jnp.minimum(cumul_columns[:, head : head + 1] - cumul[head : head + 1, :], 0.0)
        )
        gram_decay = gram[...] * decay
        mixer = (gram_decay * step).astype(BF16)
        x_head, grad_head = x_in[:, lanes], grad_in[:, lanes]
        product = dot_rows(grad_head, x_head)
        z_sum[...] += product * decay * step
        gram_grad = product * gram_decay
        r_out[head : head + 1, :] = jnp.sum(gram_grad, axis=0, keepdims=True)
        handed = lifted[:, head : head + 1] * dot_rows(grad_head, state[:, lanes])
        c_sum[...] += handed
        q = jnp.sum(gram_grad * step + c_rows * handed, axis=1, keepdims=True)
        q_columns = jnp.where(lane == head, q, q_columns)
        grad_x[:, lanes] = dot_columns(mixer, grad_head) + rows[1:2, lanes] * grad_head.astype(F32)
    q_out[...] = q_columns.T[:GROUP, :]

    @pl.when(group == groups - 1)
    def _():
        if last:
            summed = jnp.where(triangle(length, False), z_sum[...], 0.0)
            bc_out[0] = dot_split(summed.T, bc[1])
            bc_out[1] = c_sum[...] + dot_split(summed, bc[0])
        else:
            bc_out[0] = z_sum[...]
            bc_out[1] = c_sum[...]


def block_weights(step, cumul):
    return columns_of(jnp.exp(cumul[:, cumul.shape[1] - 1 :] - cumul) * step)


def rim_body(last, at, base, bc, step_in, cumul_in, weighted_x, partial, slope, out_in, *refs):
    group, groups = at
    width = weighted_x.shape[1]
    if last:
        rows_before, b_before, bc_partial, bc_slope, rim_out, bc_out, b_sum = refs
    else:
        rim_out, b_sum = refs

    @pl.when(group == 0)
    def _():
        b_sum[...] = b_before[...] if last else jnp.zeros_like(b_sum)

    out_low = out_in[0]
    b_sum[...] += dot_rows(weighted_x[...], out_low)
    weights = block_weights(step_in[...], cumul_in[...])[0:8, :]
    returned = dot(bc[0][0:16, :], out_low)[0:8, :]
    start = group
    if last:
        count = rim_out.shape[1] // width
        start = lax.rem(group + count - groups + first_group(base), count)
    for head in range(width // 128):
        lanes = slice(head * 128, head * 128 + 128)
        weight = weights[:, head : head + 1]
        rows = (partial[0:8, lanes] + weight * returned[:, lanes]) * slope[0:8, lanes]
        place = pl.multiple_of(jnp.int32(start) * width + head * 128, 128)
        rim_out[:, pl.ds(place, 128)] = rows[0:3, :]

    if last:

        @pl.when(group == groups - 1)
        def _():
            before = rows_before.shape[1]
            if before < rim_out.shape[1] - 256:
                place = pl.multiple_of(first_group(base) * width, 128)
                rim_out[:, pl.ds(place, before)] = rows_before[...]
            bc_out[0] = (b_sum[...] + bc_partial[0]) * bc_slope[0]
            bc_out[1] = bc_partial[1] * bc_slope[1]
            for j in range(2):
                lanes = rim_out.shape[1] - 256 + 128 * j
                rim_out[:, lanes : lanes + 128] = bc_out[j, 0:3, :]


def grad_dt_body(
    at,
    base,
    bc,
    rate,
    dt_slope,
    step_in,
    cumul_in,
    q_in,
    r_in,
    x_in,
    state_in,
    out_in,
    grad_dt,
    selector,
    products,
):
    heads, length = q_in.shape
    width = state_in.shape[2]
    row = lax.broadcasted_iota(jnp.int32, selector.shape, 0)
    lane = lax.broadcasted_iota(jnp.int32, selector.shape, 1)
    selector[...] = (lax.shift_right_logical(row, 7) == lane).astype(BF16)
    row = lax.broadcasted_iota(jnp.int32, (16, width), 0)
    lane = lax.shift_right_logical(lax.broadcasted_iota(jnp.int32, (16, width), 1), 7)
    dots = jnp.zeros((16, 1), F32)
    for group in range(state_in.shape[0]):
        out_low = out_in[group]
        returned = dot(bc[0], out_low)
        for start in range(0, width, 128):
            lanes = slice(start, start + 128)
            place = slice(group * width + start, group * width + start + 128)
            products[:, place] = (x_in[:, place].astype(F32) * returned[:, lanes]).astype(BF16)
        summed = dot(jnp.ones((16, length), BF16), state_in[group] * out_low)
        own = row - GROUP * group == lane
        dots = dots + jnp.sum(jnp.where(own, summed, 0.0), axis=1, keepdims=True)
    inner_b = dot(products[...], selector[...]).T[:heads, :]
    cumul, step = cumul_in[...], step_in[...]
    w = jnp.exp(cumul[:, length - 1 :] - cumul) * inner_b
    q, r = q_in[...], r_in[...]
    inside = jnp.sum(step * w, axis=1, keepdims=True)
    end = inside + jnp.exp(cumul[:, length - 1 :]) * dots[:heads]
    last = lax.broadcasted_iota(jnp.int32, (heads, length), 1) == length - 1
    grad_cumul = q - step * (r + w) + jnp.where(last, end, 0.0)
    grad_log = dot_split(grad_cumul, triangle(length, False).astype(BF16))
    grad_dt[...] = (r + w + rate[...] * grad_log) * dt_slope[...]


def grad_x_body(
    at,
    base,
    bc,
    step_in,
    cumul_in,
    partial,
    slope,
    taps,
    halo,
    out_in,
    grad_x,
    ext,
):
    length, width = partial.shape
    weights = block_weights(step_in[...], cumul_in[...])
    returned = dot(bc[0], out_in[0])
    for head in range(width // 128):
        lanes = slice(head * 128, head * 128 + 128)
        weight = weights[:, head : head + 1]
        ext[0:length, :] = (partial[:, lanes] + weight * returned[:, lanes]) * slope[:, lanes]
        ext[length : length + 3, :] = jnp.where(place_bit(base, 6) == 1, 0.0, halo[:, lanes])
        total = taps[0:1, lanes] * ext[3 : 3 + length, :]
        for k in range(1, 4):
            total = total + taps[k : k + 1, lanes] * ext[3 - k : 3 - k + length, :]
        grad_x[:, lanes] = total.astype(BF16)


def bc_back_body(at, place, grad_pre, halo, taps, kept, sent, ext, total):
    length, half = grad_pre.shape[1], kept.shape[1]
    for j in range(2):
        ext[0:length, :] = grad_pre[j]
        rim = halo[:, 128 * j : 128 * j + 128]
        ext[length : length + 3, :] = jnp.where(place_bit(place, 6) == 1, 0.0, rim)
        summed = taps[j, 0:1, :] * ext[3 : 3 + length, :]
        for k in range(1, 4):
            summed = summed + taps[j, k : k + 1, :] * ext[3 - k : 3 - k + length, :]
        total[...] = summed
        kept[j] = total[pl.ds(pl.multiple_of(place_bit(place, 3) * half, half), half), :]
        sent[j] = total[pl.ds(pl.multiple_of((1 - place_bit(place, 3)) * half, half), half), :]


def bc_half_body(at, place, mine, taken, kept, sent, total):
    half = kept.shape[1]
    for j in range(2):
        total[...] = mine[j] + taken[j]
        kept[j] = total[pl.ds(pl.multiple_of(place_bit(place, 4) * half, half), half), :]
        sent[j] = total[pl.ds(pl.multiple_of((1 - place_bit(place, 4)) * half, half), half), :]


def bc_last_body(at, _, mine, taken, out):
    out[...] = (mine[...] + taken[...]).astype(BF16)


def conv_back(extended, weights):
    length = extended.shape[-2] - 3
    summed = weights[..., 0, :][..., None, :] * extended[..., 3 : 3 + length, :]
    for k in range(1, 4):
        summed = (
            summed
            + weights[..., k, :][..., None, :] * extended[..., 3 - k : 3 - k + length, :]
        )
    return summed


def shards(
    x_input,
    z_input,
    bc_input,
    dt_raw,
    dt_bias,
    a_log,
    d_skip,
    conv_x,
    convolution_bc_taps,
    rescale_factor,
    grad_out,
):
    length, channels = x_input.shape
    heads = dt_raw.shape[0]
    groups = heads // GROUP
    width = GROUP * 128
    count, parts = lax.axis_size("seq"), lax.axis_size("head")
    inner = channels * parts
    own = lax.axis_index("seq")
    split = count == 8 and groups == 4
    own_half = groups // 2 if split else groups
    bit = lambda value, place: lax.shift_right_logical(value, place) & 1
    along_head = lax.axis_index("head")
    base = bit(own, 0) * own_half if split else own * 0
    ends = (own == 0).astype(jnp.int32), (own == count - 1).astype(jnp.int32)
    for place, value in enumerate(
        (bit(own, 2), bit(own, 1), bit(own, 0), bit(along_head, 1), bit(along_head, 0), *ends)
    ):
        base = base | lax.shift_left(value, 8 + place)
    base = base.astype(jnp.int32)[None]

    whole = lambda *shape: ((shape, lambda g, b: (0,) * len(shape)),)
    wide_at = lambda off: (Groups("wide", (length, width), off, groups),)
    rows_at = lambda off: (Groups("heads", (GROUP, length), off, groups),)
    lanes_at = lambda n, off: (Groups("wide", (n, width), off, groups),)
    slot = (Groups("slots", (1, length, width), 0, groups),)
    full = lambda array: (array,) + whole(*array.shape)
    half_width = own_half * width
    half_heads = own_half * GROUP
    half = lambda n: (Groups("half", (n, width), 0, groups),)
    half_rows = (Groups("half heads", (GROUP, length), 0, groups),)
    window_at = lambda n, off: (Groups("window", (n, width), off, groups),)
    halves = [own_half, 0] if split else [0]
    rest = halves[0]

    gain = rescale_factor[None, :]
    f32 = lambda *shape: (shape, F32)
    low = lambda *shape: (shape, BF16)

    step, cumul, rate, dt_slope, rows, rim, bc_rows, bc_taps = call(
        steps_body,
        [
            f32(heads, length) + whole(heads, length),
            f32(heads, length) + whole(heads, length),
            f32(heads, length) + whole(heads, length),
            f32(heads, length) + whole(heads, length),
            f32(2, channels) + whole(2, channels),
            low(3, channels + 256) + whole(3, channels + 256),
            low(2, length, 128) + whole(2, length, 128),
            f32(2, 4, 128) + whole(2, 4, 128),
        ],
        [
            full(in_hbm(dt_raw)),
            full(in_hbm(dt_bias[None, :])),
            full(in_hbm(a_log[None, :])),
            full(in_hbm(d_skip[None, :])),
            (in_hbm(x_input), ((16, channels), lambda g, b: (length // 16 - 1, 0))),
            full(in_hbm(bc_input)),
            full(in_hbm(convolution_bc_taps)),
        ],
        base=base,
    )
    rim_sent = rim
    rim = lax.ppermute(rim, "seq", [(i, (i + 1) % count) for i in range(count)])
    if split:
        swap = lambda block, bit: lax.ppermute(
            block, "seq", [(i, i ^ bit) for i in range(count)]
        )
        total = rows[0:1]
        total_core = swap(total, 1)
        chip_total = total + total_core
        total_across = swap(chip_total, 2)
        table = f32(16, channels) + whole(16, channels)
        ahead, behind = call(
            weights_body,
            [table, table],
            [full(rows), full(total_core), full(total_across)],
            base=base,
            )

    def passed(locals_, reverse, beside):
        if split:
            local_sent, local = locals_[rest], locals_[0]
            weights = behind if reverse else ahead
            return scan_blocks(base, groups, weights, local, local_sent, reverse, beside)
        local = locals_[0]
        for work in beside:
            work(local)
        return gather_blocks(rows[0:1], local, reverse)

    x_low, slope, local = {}, {}, {}
    ready = rim_sent
    for off in halves:
        x_low[off], slope[off], x_top, taps = call(
            conv_body,
            [
                low(length, half_width) + half(length),
                f32(length, half_width) + half(length),
                low(16, half_width) + half(16),
                f32(4, half_width) + half(4),
            ],
            [(in_hbm(x_input),) + wide_at(off), (in_hbm(conv_x),) + lanes_at(4, off)],
            base=base,
            grid=own_half,
            scratch=[pltpu.VMEM((length + 8, 128), F32)],
            after=[ready],
        )
        first = off == rest
        top = (Groups("top", (16, width), 0, groups),)
        ins = [
            (x_low[off],) + half(length),
            (x_top,) + half(16),
            (rim,) + lanes_at(3, off),
            (taps,) + half(4),
            (step,) + rows_at(off),
            (cumul,) + rows_at(off),
        ]
        outs = [
            f32(length, half_width) + top,
            low(length, half_width) + top,
            low(own_half, length, width) + slot,
        ]
        scratch = [pltpu.VMEM((24, width), F32)]
        if first:
            ins += [
                full(bc_rows),
                (rim, ((3, 256), lambda g, b: (0, channels // 256))),
                full(bc_taps),
            ]
            outs += [
                low(2, length, 128) + whole(2, length, 128),
                f32(2, length, 128) + whole(2, length, 128),
                f32(length, length) + whole(length, length),
                f32(128, length) + whole(128, length),
            ]
            scratch += [pltpu.VMEM((length + 8, 128), F32)]
        else:
            ins += [full(b_turned)]
        result = call(
            functools.partial(state_body, first),
            outs,
            ins,
            base=base,
            loop=own_half,
            scratch=scratch,
            carry=[slope[off]],
            place={0: 1},
            flops=2 * length * 128 * half_width,
        )
        if first:
            bc, bc_slope, gram, b_turned = result[3:]
        slope[off], x_low[off], local[off] = result[:3]
        ready = local[off]

    inside, gate, gate_slope, scaled, scaled_gate = {}, {}, {}, {}, {}

    def mix_inside(off, ready):
        inside[off], token = call(
            inner_body,
            [f32(length, half_width) + half(length)],
            [
                full(gram),
                (step,) + rows_at(off),
                (cumul,) + rows_at(off),
                (x_low[off],) + half(length),
                (rows,) + lanes_at(2, off),
            ],
            base=base,
            loop=own_half,
            after=[ready],
            token=True,
            flops=2 * length * 128 * half_width,
        )
        return token

    def gates(off, ready):
        gate[off], gate_slope[off], scaled[off], scaled_gate[off], token = call(
            gate_body,
            [f32(length, half_width) + half(length)] * 4,
            [
                (z_input,) + wide_at(off),
                (grad_out,) + wide_at(off),
                (gain,) + lanes_at(1, off),
            ],
            base=base,
            loop=own_half,
            after=[ready],
            token=True,
        )
        return token

    def mix_second(ready):
        tokens = [mix_inside(rest, ready)] if split else []
        tokens += [gates(off, ready) for off in reversed(halves)]
        return [], tokens

    states = passed(local, False, (functools.partial(mix_inside, 0), mix_second))
    states = dict(zip((0, rest), states))
    mixed, sums = {}, jnp.zeros((8, length), F32)
    two_scales = [pltpu.VMEM((length, 128), F32), pltpu.VMEM((length, 128), F32)]
    for off in reversed(halves):
        mixed[off], sums = call(
            mix_body,
            [f32(length, half_width) + half(length), f32(8, length) + whole(8, length)],
            [
                (inside[off],) + half(length),
                (bc, ((1, length, 128), lambda g, b: (1, 0, 0))),
                (cumul,) + rows_at(off),
                (states[off],) + slot,
                (gate[off],) + half(length),
                (scaled_gate[off],) + half(length),
                full(sums),
            ],
            base=base,
            loop=own_half,
            scratch=two_scales,
            flops=2 * length * 128 * half_width,
        )
    turn_head = lambda block, bit: lax.ppermute(
        block, "head", [(i, i ^ bit) for i in range(parts)]
    )
    weighted_x, lifted_c, squared = {}, {}, {}
    for off in halves:
        weighted_x[off], lifted_c[off] = call(
            lift_body,
            [low(length, half_width) + half(length), low(length, half_width) + half(length)],
            [
                full(bc),
                (step,) + rows_at(off),
                (cumul,) + rows_at(off),
                (x_low[off],) + half(length),
            ],
            base=base,
            loop=own_half,
            scratch=[pltpu.VMEM((128, length), F32)],
            after=[sums],
        )
        (squared[off],) = call(
            square_body,
            [f32(length, half_width) + half(length)],
            [(mixed[off],) + half(length), (gate[off],) + half(length)],
            base=base,
            loop=own_half,
        )
    if parts == 4:
        sums = sums + turn_head(sums, 1)
        all_sums = [sums, turn_head(sums, 2)]
    else:
        all_sums = [lax.psum(sums, "head")]
    grad_mixed, local_back = {}, {}
    for off in halves:
        grad_mixed[off], local_back[off] = call(
            functools.partial(grad_mixed_body, inner, len(all_sums)),
            [low(length, half_width) + half(length), low(own_half, length, width) + slot],
            [full(part) for part in all_sums]
            + [
                (squared[off],) + half(length),
                (scaled_gate[off],) + half(length),
                (lifted_c[off],) + half(length),
            ],
            base=base,
            loop=own_half,
            scratch=two_scales,
            flops=2 * length * 128 * half_width,
        )

    partial, q_rows, r_rows = {}, {}, {}
    carried = {"sums": jnp.zeros((2, length, 128), F32), "z": [], "dt": [], "x": []}

    def back_inside(off, ready):
        partial[off], q_rows[off], r_rows[off], carried["sums"], token = call(
            functools.partial(inner_back_body, off == rest),
            [
                f32(length, half_width) + half(length),
                f32(half_heads, length) + half_rows,
                f32(half_heads, length) + half_rows,
                f32(2, length, 128) + whole(2, length, 128),
            ],
            [
                full(gram),
                full(bc),
                (step,) + rows_at(off),
                (cumul,) + rows_at(off),
                (x_low[off],) + half(length),
                (grad_mixed[off],) + half(length),
                (states[off],) + slot,
                (rows,) + lanes_at(2, off),
                full(carried["sums"]),
            ],
            base=base,
            loop=own_half,
            scratch=[pltpu.VMEM((length, length), F32), pltpu.VMEM((length, 128), F32)],
            after=[ready],
            token=True,
            flops=6 * length * 128 * half_width,
        )
        return token

    def back_gates(off, ready):
        grad_z, token = call(
            functools.partial(grad_z_body, inner, len(all_sums)),
            [low(length, channels) + window_at(length, off)],
            [full(part) for part in all_sums]
            + [
                (mixed[off],) + half(length),
                (gate[off],) + half(length),
                (gate_slope[off],) + half(length),
                (scaled[off],) + half(length),
            ],
            base=base,
            loop=own_half,
            scratch=two_scales,
            carry=carried["z"],
            after=[ready],
            token=True,
        )
        carried["z"] = [grad_z]
        carried["z_token"] = token
        return token

    def back_second(ready):
        token = back_inside(rest, ready) if split else ready
        return [token], [back_gates(0, token)]

    backs = passed(local_back, True, (functools.partial(back_inside, 0), back_second))
    backs = dict(zip((0, rest), backs))
    tokens = []

    def make_grad_dt(off, after):
        table = (Groups("heads", (half_heads, length), off, groups, own_half),)
        window = (Groups("window heads", (half_heads, length), off, groups, own_half),)
        grad_dt, token = call(
            grad_dt_body,
            [f32(heads, length) + window],
            [
                full(bc),
                (rate,) + table,
                (dt_slope,) + table,
                (step,) + table,
                (cumul,) + table,
                full(q_rows[off]),
                full(r_rows[off]),
                full(x_low[off]),
                full(states[off]),
                full(backs[off]),
            ],
            base=base,
            scratch=[pltpu.VMEM((half_width, 128), BF16), pltpu.VMEM((length, half_width), BF16)],
            carry=carried["dt"],
            after=after,
            token=True,
            flops=4 * length * 128 * half_width,
        )
        carried["dt"] = [grad_dt]
        return token

    def make_grad_x(off, after):
        grad_x, token = call(
            grad_x_body,
            [low(length, channels) + window_at(length, off)],
            [
                full(bc),
                (step,) + rows_at(off),
                (cumul,) + rows_at(off),
                (partial[off],) + half(length),
                (slope[off],) + half(length),
                (conv_x,) + lanes_at(4, off),
                (rim_back,) + lanes_at(3, off),
                (backs[off],) + slot,
            ],
            base=base,
            loop=own_half,
            scratch=[pltpu.VMEM((length + 8, 128), F32)],
            carry=carried["x"],
            after=after,
            token=True,
            flops=2 * length * 128 * half_width,
        )
        carried["x"] = [grad_x]
        return token

    def make_rim(off, before, after):
        last = off == rest
        if last:
            outs = [
                f32(3, channels + 256) + whole(3, channels + 256),
                f32(2, length, 128) + whole(2, length, 128),
            ]
        else:
            outs = [f32(3, half_width) + whole(3, half_width), f32(length, 128) + whole(length, 128)]
        return call(
            functools.partial(rim_body, last),
            outs,
            [
                full(bc),
                (step,) + rows_at(off),
                (cumul,) + rows_at(off),
                (weighted_x[off],) + half(length),
                (partial[off],) + half(length),
                (slope[off],) + half(length),
                (backs[off],) + slot,
            ]
            + [full(array) for array in before],
            base=base,
            loop=own_half,
            scratch=[pltpu.VMEM((length, 128), F32)] if last else [],
            after=after,
            flops=2 * length * 128 * half_width,
        )

    if split:
        before = make_rim(0, [], [])
        tokens.append(make_grad_dt(0, [before[1]]))
    else:
        before = [jnp.zeros((3, channels), F32), jnp.zeros((length, 128), F32)]
    rim_back, grad_bc_pre = make_rim(rest, [*before, carried["sums"], bc_slope], tokens)
    rim_back = lax.ppermute(rim_back, "seq", [(i, (i - 1) % count) for i in range(count)])
    dt_token = make_grad_dt(rest, [grad_bc_pre])
    if parts == 4:
        piece = lambda rows: f32(2, rows, 128) + whole(2, rows, 128)
        kept, sent = call(
            bc_back_body,
            [piece(length // 2), piece(length // 2)],
            [
                full(grad_bc_pre),
                (rim_back, ((3, 256), lambda g, b: (0, channels // 256))),
                full(bc_taps),
            ],
            base=base,
            scratch=[pltpu.VMEM((length + 8, 128), F32), pltpu.VMEM((length, 128), F32)],
            after=[dt_token],
        )
        taken = turn_head(sent, 2)
        x_tokens = [make_grad_x(0, [sent])]
        if split:
            x_tokens = [back_gates(rest, x_tokens[0])]
        kept, sent = call(
            bc_half_body,
            [piece(length // 4), piece(length // 4)],
            [full(kept), full(taken)],
            base=base,
            scratch=[pltpu.VMEM((length // 2, 128), F32)],
            after=x_tokens,
        )
        taken = turn_head(sent, 1)
        x_tokens = [make_grad_x(rest, [sent])] if split else []
        (grad_bc,) = call(
            bc_last_body,
            [low(2, length // 4, 128) + whole(2, length // 4, 128)],
            [full(kept), full(taken)],
            base=base,
            after=x_tokens,
        )
    else:
        for off in halves:
            make_grad_x(off, [])
        bc_halo = jnp.moveaxis(rim_back[:, channels:].reshape(3, 2, 128), 1, 0)
        bc_halo = jnp.where(own == count - 1, 0.0, bc_halo)
        bc_sum = conv_back(jnp.concatenate([grad_bc_pre, bc_halo], axis=1), convolution_bc_taps)
        share = length // parts
        bc_sum = lax.psum(bc_sum, "head")
        grad_bc = lax.dynamic_slice_in_dim(bc_sum, along_head * share, share, 1).astype(BF16)
    return (carried["x"][0], carried["z"][0], grad_bc, carried["dt"][0])


def solution(mesh):
    return jax.shard_map(
        shards,
        mesh=mesh,
        in_specs=(
            P("seq", "head"),
            P("seq", "head"),
            P(None, "seq", None),
            P("head", "seq"),
            P("head"),
            P("head"),
            P("head"),
            P(None, "head"),
            P(),
            P("head"),
            P("seq", "head"),
        ),
        out_specs=(
            P("seq", "head"),
            P("seq", "head"),
            P(None, ("seq", "head"), None),
            P("head", "seq"),
        ),
        check_vma=False,
    )
```

```python
import functools

import jax
import jax.numpy as jnp
from jax import lax
from jax.experimental import pallas as pl
from jax.experimental.pallas import tpu as pltpu
from jax.sharding import PartitionSpec as P

EPS = 1e-05
GROUP = 8
F32 = jnp.float32
BF16 = jnp.bfloat16
VMEM_BYTES = 16 * 2**20


def sigmoid(value):
    return 0.5 + 0.5 * jnp.tanh(0.5 * value)


def dot(a, b):
    return jnp.dot(a, b, preferred_element_type=F32)


def dot_split(a, b):
    high = a.astype(BF16)
    rest = a - high.astype(F32)
    middle = rest.astype(BF16)
    low = (rest - middle.astype(F32)).astype(BF16)
    return dot(high, b) + (dot(middle, b) + dot(low, b))


def dot_rows(a, b):
    return lax.dot_general(a, b, (((1,), (1,)), ((), ())), preferred_element_type=F32)


def dot_columns(a, b):
    return lax.dot_general(a, b, (((0,), (0,)), ((), ())), preferred_element_type=F32)


def triangle(length, upper):
    first = lax.broadcasted_iota(jnp.int32, (length, length), 0)
    second = lax.broadcasted_iota(jnp.int32, (length, length), 1)
    return first <= second if upper else first >= second


def columns_of(rows):
    return rows.T


class Groups:
    def __init__(self, kind, block, off, groups, size=1):
        self.kind, self.block, self.off, self.groups = kind, block, off, groups
        self.size = size
        self.by_rows = kind.endswith("heads")

    def turn(self, group, base):
        first = self.off + first_group(base)
        return lax.rem(group * self.size + first, self.groups) // self.size

    def place(self, index):
        return (index, 0) if self.by_rows else (0, index)

    def spec(self):
        if self.kind == "slots":
            return pl.BlockSpec(self.block, lambda g, b: (g, 0, 0))
        if self.kind.startswith("half"):
            return pl.BlockSpec(self.block, lambda g, b: self.place(g))
        return pl.BlockSpec(self.block, lambda g, b: self.place(self.turn(g, b)))

    def whole(self, shape, count):
        if self.kind.startswith("window"):
            block = list(self.block)
            block[0 if self.by_rows else 1] *= count
            return pl.BlockSpec(
                tuple(block), lambda g, b: self.place(self.turn(0, b) // count)
            )
        if self.kind == "top":
            shape = (self.block[0], count * self.block[1])
        return pl.BlockSpec(shape, lambda g, b: (0,) * len(shape))

    def view(self, ref, group, base):
        if self.kind == "slots":
            return ref.at[pl.ds(group, 1)]
        if self.kind in ("wide", "heads"):
            group = self.turn(group, base)
        size = self.block[0 if self.by_rows else 1]
        span = pl.ds(pl.multiple_of(jnp.int32(group) * size, size), size)
        return ref.at[span] if self.by_rows else ref.at[:, span]


def call(
    body,
    outs,
    ins,
    *,
    base,
    grid=1,
    loop=1,
    scratch=(),
    after=(),
    carry=(),
    place=None,
    token=False,
    flops=0,
):
    aliases = {1 + len(ins) + len(after) + i: i for i in range(len(carry))}
    for read, written in (place or {}).items():
        aliases[1 + read] = written
    after = list(after) + list(carry)
    outs = list(outs)
    if token:
        outs.append(((8, 128), F32, ((8, 128), lambda *_: (0, 0))))

    def spec(shape, block):
        if not isinstance(block, Groups):
            return pl.BlockSpec(*block)
        return block.whole(shape, loop) if grid == 1 else block.spec()

    in_specs = [spec(array.shape, block) for array, block in ins]
    in_specs += [pl.BlockSpec(memory_space=pl.ANY) for _ in after]
    out_specs = [spec(shape, block) for shape, _, block in outs]
    out_shape = [jax.ShapeDtypeStruct(shape, dtype) for shape, dtype, _ in outs]
    arrays = [array for array, _ in ins]
    moved = sum(a.size * a.dtype.itemsize for a in arrays + out_shape)
    blocks = [block for _, block in ins] + [block for _, _, block in outs]

    def ordered(where, *refs):
        taken, rest = refs[: len(ins)], refs[len(ins) + len(after) :]
        results, extra = rest[: len(outs)], rest[len(outs) :]
        if token:
            results[-1][...] = jnp.zeros((8, 128), F32)

        def step(group, _):
            views = [
                block.view(ref, group, where) if isinstance(block, Groups) else ref
                for ref, block in zip(taken + results, blocks)
            ]
            if token:
                views = views[:-1]
            body((group, loop), where, *views, *extra)
            return 0

        if grid > 1:
            views = taken + (results[:-1] if token else results)
            body((pl.program_id(0), grid), where, *views, *extra)
        elif loop > 1:
            lax.fori_loop(0, loop, step, 0)
        else:
            step(0, 0)

    return pl.pallas_call(
        ordered,
        out_shape=out_shape,
        grid_spec=pltpu.PrefetchScalarGridSpec(
            num_scalar_prefetch=1,
            grid=(grid,),
            in_specs=in_specs,
            out_specs=out_specs,
            scratch_shapes=list(scratch),
        ),
        input_output_aliases=aliases,
        cost_estimate=pl.CostEstimate(flops=flops, bytes_accessed=moved, transcendentals=0),
        compiler_params=pltpu.CompilerParams(vmem_limit_bytes=VMEM_BYTES),
    )(base, *arrays, *after)


def in_hbm(array):
    return pltpu.with_memory_space_constraint(array, pltpu.HBM)


def column_of(row):
    count = row.shape[1]
    first = lax.broadcasted_iota(jnp.int32, (count, count), 0)
    second = lax.broadcasted_iota(jnp.int32, (count, count), 1)
    return jnp.sum(jnp.where(first == second, row, 0.0), axis=1, keepdims=True)


def steps_body(
    at,
    base,
    raw,
    bias,
    log_rate,
    skip,
    x_tail,
    bc_in,
    bc_taps,
    step_out,
    cumul_out,
    rate_out,
    slope_out,
    rows_out,
    rim_out,
    bc_in_out,
    bc_taps_out,
):
    bc_in_out[...] = bc_in[...]
    bc_taps_out[...] = bc_taps[...]
    heads, length = raw.shape
    channels = x_tail.shape[1]
    rim_out[:, 0:channels] = x_tail[...].astype(F32)[13:16, :].astype(BF16)
    for j in range(2):
        start = channels + 128 * j
        rim_out[:, start : start + 128] = bc_in[j, length - 16 :].astype(F32)[13:16, :].astype(BF16)
    shifted = raw[...] + column_of(bias[...])
    step = jnp.maximum(shifted, 0.0) + jnp.log1p(jnp.exp(-jnp.abs(shifted)))
    rate = jnp.broadcast_to(-jnp.exp(column_of(log_rate[...])), step.shape)
    cumul = dot_split(rate * step, triangle(length, True).astype(BF16))
    step_out[...] = step
    cumul_out[...] = cumul
    rate_out[...] = rate
    slope_out[...] = sigmoid(shifted)
    skips = column_of(skip[...])
    for head in range(heads):
        lanes = slice(head * 128, head * 128 + 128)
        rows_out[0:1, lanes] = jnp.broadcast_to(cumul[head : head + 1, length - 1 :], (1, 128))
        rows_out[1:2, lanes] = jnp.broadcast_to(skips[head : head + 1, :], (1, 128))


def pick(test, yes, no):
    return jnp.where(test, yes, no)


def first_group(place):
    return place[0] & 255


def place_bit(place, index):
    return lax.shift_right_logical(place[0], 8 + index) & 1


def weights_body(at, place, own, core, across, *outs):
    t0, t1 = own[0:1, :], core[...]
    e0, e1, own_chip, ex = jnp.exp(t0), jnp.exp(t1), jnp.exp(t0 + t1), jnp.exp(across[...])
    one = jnp.ones_like(e0)
    zero = jnp.zeros_like(e0)
    bits = [place_bit(place, i) for i in range(3)]
    x_first = bits[2] == 0
    for out, reverse in zip(outs, (False, True)):
        y, x, c = ((1 - bit if reverse else bit) == 1 for bit in bits)
        either = jnp.logical_or(x, y)
        scale = pick(jnp.logical_or(x_first, either), one, ex)
        rows = [pick(c, one, e1), pick(c, e0, one)]
        rows += [rows[0] * scale, rows[1] * scale]
        rows += [
            pick(x_first, pick(x, one, ex), pick(jnp.logical_and(x, y), zero, one)),
            pick(x_first, pick(x, own_chip, one), pick(y, pick(x, one, own_chip), zero)),
        ]
        a = pick(x_first, pick(x, one, zero), pick(y, pick(x, ex, one), zero))
        b = pick(x_first, pick(y, pick(x, ex, one), zero), pick(either, one, zero))
        into, send = pick(c, e1, one), pick(c, one, e0)
        rows += [into * a, into * b, pick(c, one, zero)]
        rows += [send * a, send * b, pick(c, zero, one)]
        for index, row in enumerate(rows):
            out[index : index + 1, :] = row


def combine(base, groups, weights, outs, after=(), slots_of=None, at=0, carry=()):
    arrays, columns = [], []
    for slots in outs:
        for column, terms in slots:
            if column not in columns:
                columns.append(column)
            for _, (array, slot) in terms:
                if not any(array is a and slot == s for a, s in arrays):
                    arrays.append((array, slot))
    place = lambda array, slot: [
        i for i, (a, s) in enumerate(arrays) if a is array and s == slot
    ][0]
    plan = [
        [
            (columns.index(column), [(row, place(*source)) for row, source in terms])
            for column, terms in slots
        ]
        for slots in outs
    ]

    def body(at, base, *refs):
        rows, values = refs[: len(columns)], refs[len(columns) : len(columns) + len(arrays)]
        results = refs[len(columns) + len(arrays) :]
        width = rows[0].shape[1]
        for result, slots in zip(results, plan):
            for slot, (column, terms) in enumerate(slots):
                for start in range(0, width, 256):
                    lanes = slice(start, start + 256)
                    total = None
                    for row, index in terms:
                        term = rows[column][row : row + 1, lanes] * values[index][
                            0, :, lanes
                        ].astype(F32)
                        total = term if total is None else total + term
                    result[slot, :, lanes] = total.astype(BF16)

    length, width = arrays[0][0].shape[1:]
    block = lambda slot, count: ((count, length, width), lambda g, b: (slot, 0, 0))
    ins = [
        (
            weights,
            (
                (weights.shape[0], width),
                lambda g, b, column=column: (0, lax.rem(first_group(b) + column, groups)),
            ),
        )
        for column in columns
    ]
    ins += [(array, block(slot, 1)) for array, slot in arrays]
    results = [
        ((slots_of or len(slots), length, width), BF16, block(at, len(slots))) for slots in outs
    ]
    return call(body, results, ins, base=base, after=after, carry=carry)


def scan_blocks(base, groups, weights, local, local_sent, reverse, beside):
    count = lax.axis_size("seq")

    def swap(block, bits):
        route = [(i, i ^ bits[i % 2]) for i in range(count)]
        return lax.ppermute(block, "seq", route)

    def merge(slot, *plans, **places):
        outs = [[(slot, list(zip(rows, sources)))] for rows, sources in plans]
        return combine(base, groups, weights, outs, **places)

    taken = swap(local_sent, (1, 1))
    chips, first_taken, sent, second_taken = [], [], [], []
    for slot in range(2):
        both = ((local, slot), (taken, slot))
        chip, chip_sent = merge(slot, ((0, 1), both), ((2, 3), both))
        chips.append(chip)
        first_taken.append(swap(chip_sent, (2, 4)))
    after = [beside[0](chips[1])]
    for slot in range(2):
        sources = ((chips[slot], 0), (first_taken[slot], 0))
        (block,) = merge(slot, ((4, 5), sources), after=after)
        sent.append(block)
        second_taken.append(swap(block, (4, 2)))
        after = []
    after = beside[1](sent[1])
    carry = []
    for slot in range(2):
        sources = ((first_taken[slot], 0), (second_taken[slot], 0))
        mine, handed = merge(
            slot,
            ((6, 7, 8), (*sources, (taken, slot))),
            ((9, 10, 11), (*sources, (local, slot))),
            after=after[slot],
            slots_of=2,
            at=slot,
            carry=carry,
        )
        carry = [mine, handed]
    return mine, swap(handed, (1, 1))


def gather_blocks(totals, local, reverse):
    table = lax.all_gather(totals, "seq", axis=0, tiled=True)
    blocks = lax.all_gather(local[None], "seq", axis=0, tiled=True)
    own = lax.axis_index("seq")
    order = jnp.arange(table.shape[0], dtype=jnp.int32)
    if reverse:
        inside = (order[None, :] > own) & (order[None, :] < order[:, None])
        selected = order > own
    else:
        inside = (order[None, :] > order[:, None]) & (order[None, :] < own)
        selected = order < own
    exponent = jnp.sum(jnp.where(inside[:, :, None], table[None], 0.0), axis=1)
    factor = jnp.where(selected[:, None], jnp.exp(exponent), 0.0)
    factor = factor.reshape(factor.shape[0], local.shape[0], 1, local.shape[2])
    state = jnp.sum(factor * blocks.astype(F32), axis=0).astype(BF16)
    return state, state


def conv_body(at, base, x_in, taps, x_out, slope_out, top_out, taps_out, ext):
    length, width = x_in.shape
    top_out[...] = x_in[0:16, :]
    taps_out[...] = taps[...]
    ext[0:8, :] = jnp.zeros((8, 128), F32)
    for start in range(0, width, 128):
        lanes = slice(start, start + 128)
        ext[8 : 8 + length, :] = x_in[:, lanes].astype(F32)
        pre = taps[0:1, lanes] * ext[5 : 5 + length, :]
        for k in range(1, 4):
            pre = pre + taps[k : k + 1, lanes] * ext[5 + k : 5 + k + length, :]
        sigma = sigmoid(pre)
        x_out[:, lanes] = (pre * sigma).astype(BF16)
        slope_out[:, lanes] = sigma * (1.0 + pre * (1.0 - sigma))


def state_body(first, at, base, x_low, x_top, x_halo, taps, step_in, cumul_in, *refs):
    length, width = x_low.shape
    if first:
        bc_in, bc_halo, bc_taps, slope_out, x_out, state_out = refs[:6]
        bc_out, bc_slope_out, gram_out, b_turned, ext, bc_ext = refs[6:]

        @pl.when(at[0] == 0)
        def _():
            for j in range(2):
                halo = bc_halo[:, j * 128 : j * 128 + 128].astype(F32)
                bc_ext[5:8, :] = jnp.where(place_bit(base, 5) == 1, 0.0, halo)
                bc_ext[8 : 8 + length, :] = bc_in[j].astype(F32)
                pre = bc_taps[j, 0:1, :] * bc_ext[5 : 5 + length, :]
                for k in range(1, 4):
                    pre = pre + bc_taps[j, k : k + 1, :] * bc_ext[5 + k : 5 + k + length, :]
                sigma = sigmoid(pre)
                bc_out[j] = (pre * sigma).astype(BF16)
                bc_slope_out[j] = sigma * (1.0 + pre * (1.0 - sigma))
            b_turned[...] = bc_out[0].astype(F32).T
            gram_out[...] = jnp.where(
                triangle(length, False), dot_rows(bc_out[1], bc_out[0]), 0.0
            )

    else:
        b_turned, slope_out, x_out, state_out, ext = refs

    top = x_top.shape[0]
    ext[5:8, :] = jnp.where(place_bit(base, 5) == 1, 0.0, x_halo[...].astype(F32))
    ext[8 : 8 + top, :] = x_top[...].astype(F32)
    tail_step = jnp.exp(cumul_in[:, length - 1 :] - cumul_in[...]) * step_in[...]
    for head in range(width // 128):
        lanes = slice(head * 128, head * 128 + 128)
        pre = taps[0:1, lanes] * ext[5 : 5 + top, lanes]
        for k in range(1, 4):
            pre = pre + taps[k : k + 1, lanes] * ext[5 + k : 5 + k + top, lanes]
        sigma = sigmoid(pre)
        x_rows = (pre * sigma).astype(BF16)
        x_out[:, lanes] = x_rows
        slope_out[:, lanes] = sigma * (1.0 + pre * (1.0 - sigma))
        x_head = jnp.concatenate([x_rows, x_low[top:, lanes]], axis=0)
        weighted = (b_turned[...] * tail_step[head : head + 1, :]).astype(BF16)
        state_out[0, :, lanes] = dot(weighted, x_head).astype(BF16)


def inner_body(at, base, gram, step_in, cumul_in, x_in, rows, mixed_out):
    cumul = cumul_in[...]
    cumul_columns = columns_of(cumul)
    for head in range(x_in.shape[1] // 128):
        lanes = slice(head * 128, head * 128 + 128)
        row = cumul[head : head + 1, :]
        decay = jnp.exp(jnp.minimum(cumul_columns[:, head : head + 1] - row, 0.0))
        mixer = (gram[...] * decay * step_in[head : head + 1, :]).astype(BF16)
        x_head = x_in[:, lanes]
        mixed_out[:, lanes] = dot(mixer, x_head) + rows[1:2, lanes] * x_head.astype(F32)


def gate_body(
    at, base, z_in, grad_in, gain, gate_out, gate_slope_out, scaled_out, scaled_gate_out
):
    for start in range(0, z_in.shape[1], 128):
        lanes = slice(start, start + 128)
        z = z_in[:, lanes].astype(F32)
        sigma = sigmoid(z)
        gate = z * sigma
        scaled = grad_in[:, lanes].astype(F32) * gain[:, lanes]
        gate_out[:, lanes] = gate
        gate_slope_out[:, lanes] = sigma * (1.0 + z * (1.0 - sigma))
        scaled_out[:, lanes] = scaled
        scaled_gate_out[:, lanes] = scaled * gate


def lift_body(at, base, bc, step_in, cumul_in, x_in, weighted_x, lifted_out, c_turned):
    @pl.when(at[0] == 0)
    def _():
        c_turned[...] = bc[1].astype(F32).T

    weights = block_weights(step_in[...], cumul_in[...])
    lifted = jnp.exp(cumul_in[...])
    for head in range(x_in.shape[1] // 128):
        lanes = slice(head * 128, head * 128 + 128)
        weight = weights[:, head : head + 1]
        weighted_x[:, lanes] = (weight * x_in[:, lanes].astype(F32)).astype(BF16)
        lifted_out[:, lanes] = (c_turned[...] * lifted[head : head + 1, :]).astype(BF16)


def mix_body(
    at, base, mixed_in, c_rows, cumul_in, state, gate_in, scaled_in, sums_in, *outs
):
    mixed_out, sums_out, squares, products = outs
    group, groups = at

    @pl.when(group == 0)
    def _():
        squares[...] = jnp.zeros_like(squares)
        products[...] = jnp.zeros_like(products)

    carried = dot(c_rows[0], state[0])
    lifted = jnp.exp(columns_of(cumul_in[...]))
    square, product = squares[...], products[...]
    for head in range(mixed_in.shape[1] // 128):
        lanes = slice(head * 128, head * 128 + 128)
        mixed = mixed_in[:, lanes] + lifted[:, head : head + 1] * carried[:, lanes]
        mixed_out[:, lanes] = mixed
        gated = mixed * gate_in[:, lanes]
        square = square + gated * gated
        product = product + mixed * scaled_in[:, lanes]
    squares[...] = square
    products[...] = product

    @pl.when(group == groups - 1)
    def _():
        sums_out[...] = sums_in[...]
        sums_out[0:1, :] += jnp.sum(squares[...].T, axis=0, keepdims=True)
        sums_out[1:2, :] += jnp.sum(products[...].T, axis=0, keepdims=True)


def square_body(at, base, mixed_in, gate_in, squared):
    for start in range(0, mixed_in.shape[1], 128):
        lanes = slice(start, start + 128)
        gate = gate_in[:, lanes]
        squared[:, lanes] = mixed_in[:, lanes] * gate * gate


def norm_scales(at, inner, sums, alpha, beta):
    @pl.when(at[0] == 0)
    def _():
        total = jnp.sum(sums[0][...], axis=0)
        inv_rms = lax.rsqrt(total[0:1, :] / inner + EPS)
        mean_dot = inv_rms * total[1:2, :] / inner
        alpha[...] = jnp.broadcast_to(inv_rms, alpha.shape).T
        beta[...] = jnp.broadcast_to(inv_rms * inv_rms * mean_dot, beta.shape).T


def grad_mixed_body(inner, parts, at, base, *refs):
    sums = refs[:parts]
    squared, scaled_in, lifted_c, grad_mixed, state_out, alpha, beta = refs[parts:]
    norm_scales(at, inner, sums, alpha, beta)
    for start in range(0, squared.shape[1], 128):
        lanes = slice(start, start + 128)
        low = (alpha[...] * scaled_in[:, lanes] - beta[...] * squared[:, lanes]).astype(BF16)
        grad_mixed[:, lanes] = low
        state_out[0, :, lanes] = dot(lifted_c[:, lanes], low).astype(BF16)


def grad_z_body(inner, parts, at, base, *refs):
    sums = refs[:parts]
    mixed_in, gate_in, gate_slope_in, scaled_in, grad_z, alpha, beta = refs[parts:]
    norm_scales(at, inner, sums, alpha, beta)
    for start in range(0, mixed_in.shape[1], 128):
        lanes = slice(start, start + 128)
        mixed = mixed_in[:, lanes]
        grad_gated = alpha[...] * scaled_in[:, lanes] - beta[...] * (mixed * gate_in[:, lanes])
        grad_z[:, lanes] = (grad_gated * (mixed * gate_slope_in[:, lanes])).astype(BF16)


def inner_back_body(
    last,
    at,
    base,
    gram,
    bc,
    step_in,
    cumul_in,
    x_in,
    grad_in,
    state_in,
    rows,
    sums_in,
    grad_x,
    q_out,
    r_out,
    bc_out,
    z_sum,
    c_sum,
):
    group, groups = at
    length = x_in.shape[0]

    @pl.when(group == 0)
    def _():
        z_sum[...] = sums_in[0]
        c_sum[...] = sums_in[1]

    cumul = cumul_in[...]
    cumul_columns = columns_of(cumul)
    lifted = jnp.exp(cumul_columns)
    state = state_in[0]
    c_rows = bc[1].astype(F32)
    lane = lax.broadcasted_iota(jnp.int32, (length, 128), 1)
    q_columns = jnp.zeros((length, 128), F32)
    for head in range(x_in.shape[1] // 128):
        lanes = slice(head * 128, head * 128 + 128)
        step = step_in[head : head + 1, :]
        decay = jnp.exp(
            jnp.minimum(cumul_columns[:, head : head + 1] - cumul[head : head + 1, :], 0.0)
        )
        gram_decay = gram[...] * decay
        mixer = (gram_decay * step).astype(BF16)
        x_head, grad_head = x_in[:, lanes], grad_in[:, lanes]
        product = dot_rows(grad_head, x_head)
        z_sum[...] += product * decay * step
        gram_grad = product * gram_decay
        r_out[head : head + 1, :] = jnp.sum(gram_grad, axis=0, keepdims=True)
        handed = lifted[:, head : head + 1] * dot_rows(grad_head, state[:, lanes])
        c_sum[...] += handed
        q = jnp.sum(gram_grad * step + c_rows * handed, axis=1, keepdims=True)
        q_columns = jnp.where(lane == head, q, q_columns)
        grad_x[:, lanes] = dot_columns(mixer, grad_head) + rows[1:2, lanes] * grad_head.astype(F32)
    q_out[...] = q_columns.T[:GROUP, :]

    @pl.when(group == groups - 1)
    def _():
        if last:
            summed = jnp.where(triangle(length, False), z_sum[...], 0.0)
            bc_out[0] = dot_split(summed.T, bc[1])
            bc_out[1] = c_sum[...] + dot_split(summed, bc[0])
        else:
            bc_out[0] = z_sum[...]
            bc_out[1] = c_sum[...]


def block_weights(step, cumul):
    return columns_of(jnp.exp(cumul[:, cumul.shape[1] - 1 :] - cumul) * step)


def rim_body(last, at, base, bc, step_in, cumul_in, weighted_x, partial, slope, out_in, *refs):
    group, groups = at
    width = weighted_x.shape[1]
    if last:
        rows_before, b_before, bc_partial, bc_slope, rim_out, bc_out, b_sum = refs
    else:
        rim_out, b_sum = refs

    @pl.when(group == 0)
    def _():
        b_sum[...] = b_before[...] if last else jnp.zeros_like(b_sum)

    out_low = out_in[0]
    b_sum[...] += dot_rows(weighted_x[...], out_low)
    weights = block_weights(step_in[...], cumul_in[...])[0:8, :]
    returned = dot(bc[0][0:16, :], out_low)[0:8, :]
    start = group
    if last:
        count = rim_out.shape[1] // width
        start = lax.rem(group + count - groups + first_group(base), count)
    for head in range(width // 128):
        lanes = slice(head * 128, head * 128 + 128)
        weight = weights[:, head : head + 1]
        rows = (partial[0:8, lanes] + weight * returned[:, lanes]) * slope[0:8, lanes]
        place = pl.multiple_of(jnp.int32(start) * width + head * 128, 128)
        rim_out[:, pl.ds(place, 128)] = rows[0:3, :]

    if last:

        @pl.when(group == groups - 1)
        def _():
            before = rows_before.shape[1]
            if before < rim_out.shape[1] - 256:
                place = pl.multiple_of(first_group(base) * width, 128)
                rim_out[:, pl.ds(place, before)] = rows_before[...]
            bc_out[0] = (b_sum[...] + bc_partial[0]) * bc_slope[0]
            bc_out[1] = bc_partial[1] * bc_slope[1]
            for j in range(2):
                lanes = rim_out.shape[1] - 256 + 128 * j
                rim_out[:, lanes : lanes + 128] = bc_out[j, 0:3, :]


def grad_dt_body(
    at,
    base,
    bc,
    rate,
    dt_slope,
    step_in,
    cumul_in,
    q_in,
    r_in,
    x_in,
    state_in,
    out_in,
    grad_dt,
    selector,
    products,
):
    heads, length = q_in.shape
    width = state_in.shape[2]
    row = lax.broadcasted_iota(jnp.int32, selector.shape, 0)
    lane = lax.broadcasted_iota(jnp.int32, selector.shape, 1)
    selector[...] = (lax.shift_right_logical(row, 7) == lane).astype(BF16)
    row = lax.broadcasted_iota(jnp.int32, (16, width), 0)
    lane = lax.shift_right_logical(lax.broadcasted_iota(jnp.int32, (16, width), 1), 7)
    dots = jnp.zeros((16, 1), F32)
    for group in range(state_in.shape[0]):
        out_low = out_in[group]
        returned = dot(bc[0], out_low)
        for start in range(0, width, 128):
            lanes = slice(start, start + 128)
            place = slice(group * width + start, group * width + start + 128)
            products[:, place] = (x_in[:, place].astype(F32) * returned[:, lanes]).astype(BF16)
        summed = dot(jnp.ones((16, length), BF16), state_in[group] * out_low)
        own = row - GROUP * group == lane
        dots = dots + jnp.sum(jnp.where(own, summed, 0.0), axis=1, keepdims=True)
    inner_b = dot(products[...], selector[...]).T[:heads, :]
    cumul, step = cumul_in[...], step_in[...]
    w = jnp.exp(cumul[:, length - 1 :] - cumul) * inner_b
    q, r = q_in[...], r_in[...]
    inside = jnp.sum(step * w, axis=1, keepdims=True)
    end = inside + jnp.exp(cumul[:, length - 1 :]) * dots[:heads]
    last = lax.broadcasted_iota(jnp.int32, (heads, length), 1) == length - 1
    grad_cumul = q - step * (r + w) + jnp.where(last, end, 0.0)
    grad_log = dot_split(grad_cumul, triangle(length, False).astype(BF16))
    grad_dt[...] = (r + w + rate[...] * grad_log) * dt_slope[...]


def grad_x_body(
    at,
    base,
    bc,
    step_in,
    cumul_in,
    partial,
    slope,
    taps,
    halo,
    out_in,
    grad_x,
    ext,
):
    length, width = partial.shape
    weights = block_weights(step_in[...], cumul_in[...])
    returned = dot(bc[0], out_in[0])
    for head in range(width // 128):
        lanes = slice(head * 128, head * 128 + 128)
        weight = weights[:, head : head + 1]
        ext[0:length, :] = (partial[:, lanes] + weight * returned[:, lanes]) * slope[:, lanes]
        ext[length : length + 3, :] = jnp.where(place_bit(base, 6) == 1, 0.0, halo[:, lanes])
        total = taps[0:1, lanes] * ext[3 : 3 + length, :]
        for k in range(1, 4):
            total = total + taps[k : k + 1, lanes] * ext[3 - k : 3 - k + length, :]
        grad_x[:, lanes] = total.astype(BF16)


def bc_back_body(at, place, grad_pre, halo, taps, out, ext, total):
    length, share = grad_pre.shape[1], out.shape[2]
    for j in range(2):
        ext[0:length, :] = grad_pre[j]
        rim = halo[:, 128 * j : 128 * j + 128]
        ext[length : length + 3, :] = jnp.where(place_bit(place, 6) == 1, 0.0, rim)
        summed = taps[j, 0:1, :] * ext[3 : 3 + length, :]
        for k in range(1, 4):
            summed = summed + taps[j, k : k + 1, :] * ext[3 - k : 3 - k + length, :]
        total[...] = summed
        for part in range(out.shape[0]):
            out[part, j] = total[part * share : part * share + share, :]


def bc_last_body(at, _, taken, out):
    out[...] = jnp.sum(taken[...], axis=0).astype(BF16)


def conv_back(extended, weights):
    length = extended.shape[-2] - 3
    summed = weights[..., 0, :][..., None, :] * extended[..., 3 : 3 + length, :]
    for k in range(1, 4):
        summed = (
            summed
            + weights[..., k, :][..., None, :] * extended[..., 3 - k : 3 - k + length, :]
        )
    return summed


def shards(
    x_input,
    z_input,
    bc_input,
    dt_raw,
    dt_bias,
    a_log,
    d_skip,
    conv_x,
    convolution_bc_taps,
    rescale_factor,
    grad_out,
):
    length, channels = x_input.shape
    heads = dt_raw.shape[0]
    groups = heads // GROUP
    width = GROUP * 128
    count, parts = lax.axis_size("seq"), lax.axis_size("head")
    inner = channels * parts
    own = lax.axis_index("seq")
    split = count == 8 and groups == 4
    own_half = groups // 2 if split else groups
    bit = lambda value, place: lax.shift_right_logical(value, place) & 1
    along_head = lax.axis_index("head")
    base = bit(own, 0) * own_half if split else own * 0
    ends = (own == 0).astype(jnp.int32), (own == count - 1).astype(jnp.int32)
    for place, value in enumerate(
        (bit(own, 2), bit(own, 1), bit(own, 0), bit(along_head, 1), bit(along_head, 0), *ends)
    ):
        base = base | lax.shift_left(value, 8 + place)
    base = base.astype(jnp.int32)[None]

    whole = lambda *shape: ((shape, lambda g, b: (0,) * len(shape)),)
    wide_at = lambda off: (Groups("wide", (length, width), off, groups),)
    rows_at = lambda off: (Groups("heads", (GROUP, length), off, groups),)
    lanes_at = lambda n, off: (Groups("wide", (n, width), off, groups),)
    slot = (Groups("slots", (1, length, width), 0, groups),)
    full = lambda array: (array,) + whole(*array.shape)
    half_width = own_half * width
    half_heads = own_half * GROUP
    half = lambda n: (Groups("half", (n, width), 0, groups),)
    half_rows = (Groups("half heads", (GROUP, length), 0, groups),)
    window_at = lambda n, off: (Groups("window", (n, width), off, groups),)
    halves = [own_half, 0] if split else [0]
    rest = halves[0]

    gain = rescale_factor[None, :]
    f32 = lambda *shape: (shape, F32)
    low = lambda *shape: (shape, BF16)

    step, cumul, rate, dt_slope, rows, rim, bc_rows, bc_taps = call(
        steps_body,
        [
            f32(heads, length) + whole(heads, length),
            f32(heads, length) + whole(heads, length),
            f32(heads, length) + whole(heads, length),
            f32(heads, length) + whole(heads, length),
            f32(2, channels) + whole(2, channels),
            low(3, channels + 256) + whole(3, channels + 256),
            low(2, length, 128) + whole(2, length, 128),
            f32(2, 4, 128) + whole(2, 4, 128),
        ],
        [
            full(in_hbm(dt_raw)),
            full(in_hbm(dt_bias[None, :])),
            full(in_hbm(a_log[None, :])),
            full(in_hbm(d_skip[None, :])),
            (in_hbm(x_input), ((16, channels), lambda g, b: (length // 16 - 1, 0))),
            full(in_hbm(bc_input)),
            full(in_hbm(convolution_bc_taps)),
        ],
        base=base,
    )
    rim_sent = rim
    rim = lax.ppermute(rim, "seq", [(i, (i + 1) % count) for i in range(count)])
    if split:
        swap = lambda block, bit: lax.ppermute(
            block, "seq", [(i, i ^ bit) for i in range(count)]
        )
        total = rows[0:1]
        total_core = swap(total, 1)
        chip_total = total + total_core
        total_across = swap(chip_total, 2)
        table = f32(16, channels) + whole(16, channels)
        ahead, behind = call(
            weights_body,
            [table, table],
            [full(rows), full(total_core), full(total_across)],
            base=base,
            )

    def passed(locals_, reverse, beside):
        if split:
            local_sent, local = locals_[rest], locals_[0]
            weights = behind if reverse else ahead
            return scan_blocks(base, groups, weights, local, local_sent, reverse, beside)
        local = locals_[0]
        for work in beside:
            work(local)
        return gather_blocks(rows[0:1], local, reverse)

    x_low, slope, local = {}, {}, {}
    ready = rim_sent
    for off in halves:
        x_low[off], slope[off], x_top, taps = call(
            conv_body,
            [
                low(length, half_width) + half(length),
                f32(length, half_width) + half(length),
                low(16, half_width) + half(16),
                f32(4, half_width) + half(4),
            ],
            [(in_hbm(x_input),) + wide_at(off), (in_hbm(conv_x),) + lanes_at(4, off)],
            base=base,
            grid=own_half,
            scratch=[pltpu.VMEM((length + 8, 128), F32)],
            after=[ready],
        )
        first = off == rest
        top = (Groups("top", (16, width), 0, groups),)
        ins = [
            (x_low[off],) + half(length),
            (x_top,) + half(16),
            (rim,) + lanes_at(3, off),
            (taps,) + half(4),
            (step,) + rows_at(off),
            (cumul,) + rows_at(off),
        ]
        outs = [
            f32(length, half_width) + top,
            low(length, half_width) + top,
            low(own_half, length, width) + slot,
        ]
        scratch = [pltpu.VMEM((24, width), F32)]
        if first:
            ins += [
                full(bc_rows),
                (rim, ((3, 256), lambda g, b: (0, channels // 256))),
                full(bc_taps),
            ]
            outs += [
                low(2, length, 128) + whole(2, length, 128),
                f32(2, length, 128) + whole(2, length, 128),
                f32(length, length) + whole(length, length),
                f32(128, length) + whole(128, length),
            ]
            scratch += [pltpu.VMEM((length + 8, 128), F32)]
        else:
            ins += [full(b_turned)]
        result = call(
            functools.partial(state_body, first),
            outs,
            ins,
            base=base,
            loop=own_half,
            scratch=scratch,
            carry=[slope[off]],
            place={0: 1},
            flops=2 * length * 128 * half_width,
        )
        if first:
            bc, bc_slope, gram, b_turned = result[3:]
        slope[off], x_low[off], local[off] = result[:3]
        ready = local[off]

    inside, gate, gate_slope, scaled, scaled_gate = {}, {}, {}, {}, {}

    def mix_inside(off, ready):
        inside[off], token = call(
            inner_body,
            [f32(length, half_width) + half(length)],
            [
                full(gram),
                (step,) + rows_at(off),
                (cumul,) + rows_at(off),
                (x_low[off],) + half(length),
                (rows,) + lanes_at(2, off),
            ],
            base=base,
            loop=own_half,
            after=[ready],
            token=True,
            flops=2 * length * 128 * half_width,
        )
        return token

    def gates(off, ready):
        gate[off], gate_slope[off], scaled[off], scaled_gate[off], token = call(
            gate_body,
            [f32(length, half_width) + half(length)] * 4,
            [
                (z_input,) + wide_at(off),
                (grad_out,) + wide_at(off),
                (gain,) + lanes_at(1, off),
            ],
            base=base,
            loop=own_half,
            after=[ready],
            token=True,
        )
        return token

    def mix_second(ready):
        tokens = [mix_inside(rest, ready)] if split else []
        tokens += [gates(off, ready) for off in reversed(halves)]
        return [], tokens

    states = passed(local, False, (functools.partial(mix_inside, 0), mix_second))
    states = dict(zip((0, rest), states))
    mixed, sums = {}, jnp.zeros((8, length), F32)
    two_scales = [pltpu.VMEM((length, 128), F32), pltpu.VMEM((length, 128), F32)]
    for off in reversed(halves):
        mixed[off], sums = call(
            mix_body,
            [f32(length, half_width) + half(length), f32(8, length) + whole(8, length)],
            [
                (inside[off],) + half(length),
                (bc, ((1, length, 128), lambda g, b: (1, 0, 0))),
                (cumul,) + rows_at(off),
                (states[off],) + slot,
                (gate[off],) + half(length),
                (scaled_gate[off],) + half(length),
                full(sums),
            ],
            base=base,
            loop=own_half,
            scratch=two_scales,
            flops=2 * length * 128 * half_width,
        )
    weighted_x, lifted_c, squared = {}, {}, {}
    for off in halves:
        weighted_x[off], lifted_c[off] = call(
            lift_body,
            [low(length, half_width) + half(length), low(length, half_width) + half(length)],
            [
                full(bc),
                (step,) + rows_at(off),
                (cumul,) + rows_at(off),
                (x_low[off],) + half(length),
            ],
            base=base,
            loop=own_half,
            scratch=[pltpu.VMEM((128, length), F32)],
            after=[sums],
        )
        (squared[off],) = call(
            square_body,
            [f32(length, half_width) + half(length)],
            [(mixed[off],) + half(length), (gate[off],) + half(length)],
            base=base,
            loop=own_half,
        )
    if parts == 4:
        sums = jnp.broadcast_to(sums[None], (parts, *sums.shape))
        all_sums = [lax.all_to_all(sums, "head", 0, 0, tiled=True)]
    else:
        all_sums = [lax.psum(sums, "head")[None]]
    grad_mixed, local_back = {}, {}
    for off in halves:
        grad_mixed[off], local_back[off] = call(
            functools.partial(grad_mixed_body, inner, len(all_sums)),
            [low(length, half_width) + half(length), low(own_half, length, width) + slot],
            [full(part) for part in all_sums]
            + [
                (squared[off],) + half(length),
                (scaled_gate[off],) + half(length),
                (lifted_c[off],) + half(length),
            ],
            base=base,
            loop=own_half,
            scratch=two_scales,
            flops=2 * length * 128 * half_width,
        )

    partial, q_rows, r_rows = {}, {}, {}
    carried = {"sums": jnp.zeros((2, length, 128), F32), "z": [], "dt": [], "x": []}

    def back_inside(off, ready):
        partial[off], q_rows[off], r_rows[off], carried["sums"], token = call(
            functools.partial(inner_back_body, off == rest),
            [
                f32(length, half_width) + half(length),
                f32(half_heads, length) + half_rows,
                f32(half_heads, length) + half_rows,
                f32(2, length, 128) + whole(2, length, 128),
            ],
            [
                full(gram),
                full(bc),
                (step,) + rows_at(off),
                (cumul,) + rows_at(off),
                (x_low[off],) + half(length),
                (grad_mixed[off],) + half(length),
                (states[off],) + slot,
                (rows,) + lanes_at(2, off),
                full(carried["sums"]),
            ],
            base=base,
            loop=own_half,
            scratch=[pltpu.VMEM((length, length), F32), pltpu.VMEM((length, 128), F32)],
            after=[ready],
            token=True,
            flops=6 * length * 128 * half_width,
        )
        return token

    def back_gates(off, ready):
        grad_z, token = call(
            functools.partial(grad_z_body, inner, len(all_sums)),
            [low(length, channels) + window_at(length, off)],
            [full(part) for part in all_sums]
            + [
                (mixed[off],) + half(length),
                (gate[off],) + half(length),
                (gate_slope[off],) + half(length),
                (scaled[off],) + half(length),
            ],
            base=base,
            loop=own_half,
            scratch=two_scales,
            carry=carried["z"],
            after=[ready],
            token=True,
        )
        carried["z"] = [grad_z]
        carried["z_token"] = token
        return token

    def back_second(ready):
        token = back_inside(rest, ready) if split else ready
        return [token], [back_gates(0, token)]

    backs = passed(local_back, True, (functools.partial(back_inside, 0), back_second))
    backs = dict(zip((0, rest), backs))
    tokens = []

    def make_grad_dt(off, after):
        table = (Groups("heads", (half_heads, length), off, groups, own_half),)
        window = (Groups("window heads", (half_heads, length), off, groups, own_half),)
        grad_dt, token = call(
            grad_dt_body,
            [f32(heads, length) + window],
            [
                full(bc),
                (rate,) + table,
                (dt_slope,) + table,
                (step,) + table,
                (cumul,) + table,
                full(q_rows[off]),
                full(r_rows[off]),
                full(x_low[off]),
                full(states[off]),
                full(backs[off]),
            ],
            base=base,
            scratch=[pltpu.VMEM((half_width, 128), BF16), pltpu.VMEM((length, half_width), BF16)],
            carry=carried["dt"],
            after=after,
            token=True,
            flops=4 * length * 128 * half_width,
        )
        carried["dt"] = [grad_dt]
        return token

    def make_grad_x(off, after):
        grad_x, token = call(
            grad_x_body,
            [low(length, channels) + window_at(length, off)],
            [
                full(bc),
                (step,) + rows_at(off),
                (cumul,) + rows_at(off),
                (partial[off],) + half(length),
                (slope[off],) + half(length),
                (conv_x,) + lanes_at(4, off),
                (rim_back,) + lanes_at(3, off),
                (backs[off],) + slot,
            ],
            base=base,
            loop=own_half,
            scratch=[pltpu.VMEM((length + 8, 128), F32)],
            carry=carried["x"],
            after=after,
            token=True,
            flops=2 * length * 128 * half_width,
        )
        carried["x"] = [grad_x]
        return token

    def make_rim(off, before, after):
        last = off == rest
        if last:
            outs = [
                f32(3, channels + 256) + whole(3, channels + 256),
                f32(2, length, 128) + whole(2, length, 128),
            ]
        else:
            outs = [f32(3, half_width) + whole(3, half_width), f32(length, 128) + whole(length, 128)]
        return call(
            functools.partial(rim_body, last),
            outs,
            [
                full(bc),
                (step,) + rows_at(off),
                (cumul,) + rows_at(off),
                (weighted_x[off],) + half(length),
                (partial[off],) + half(length),
                (slope[off],) + half(length),
                (backs[off],) + slot,
            ]
            + [full(array) for array in before],
            base=base,
            loop=own_half,
            scratch=[pltpu.VMEM((length, 128), F32)] if last else [],
            after=after,
            flops=2 * length * 128 * half_width,
        )

    if split:
        before = make_rim(0, [], [])
        tokens.append(make_grad_dt(0, [before[1]]))
    else:
        before = [jnp.zeros((3, channels), F32), jnp.zeros((length, 128), F32)]
    rim_back, grad_bc_pre = make_rim(rest, [*before, carried["sums"], bc_slope], tokens)
    rim_back = lax.ppermute(rim_back, "seq", [(i, (i - 1) % count) for i in range(count)])
    dt_token = make_grad_dt(rest, [grad_bc_pre])
    if parts == 4:
        share = (parts, 2, length // parts, 128)
        (pieces,) = call(
            bc_back_body,
            [f32(*share) + whole(*share)],
            [
                full(grad_bc_pre),
                (rim_back, ((3, 256), lambda g, b: (0, channels // 256))),
                full(bc_taps),
            ],
            base=base,
            scratch=[pltpu.VMEM((length + 8, 128), F32), pltpu.VMEM((length, 128), F32)],
            after=[dt_token],
        )
        taken = lax.all_to_all(pieces, "head", 0, 0, tiled=True)
        x_tokens = [make_grad_x(0, [pieces])]
        if split:
            x_tokens = [back_gates(rest, x_tokens[0])]
            x_tokens = [make_grad_x(rest, x_tokens)]
        (grad_bc,) = call(
            bc_last_body,
            [low(*share[1:]) + whole(*share[1:])],
            [full(taken)],
            base=base,
            after=x_tokens,
        )
    else:
        for off in halves:
            make_grad_x(off, [])
        bc_halo = jnp.moveaxis(rim_back[:, channels:].reshape(3, 2, 128), 1, 0)
        bc_halo = jnp.where(own == count - 1, 0.0, bc_halo)
        bc_sum = conv_back(jnp.concatenate([grad_bc_pre, bc_halo], axis=1), convolution_bc_taps)
        share = length // parts
        bc_sum = lax.psum(bc_sum, "head")
        grad_bc = lax.dynamic_slice_in_dim(bc_sum, along_head * share, share, 1).astype(BF16)
    return (carried["x"][0], carried["z"][0], grad_bc, carried["dt"][0])


def solution(mesh):
    return jax.shard_map(
        shards,
        mesh=mesh,
        in_specs=(
            P("seq", "head"),
            P("seq", "head"),
            P(None, "seq", None),
            P("head", "seq"),
            P("head"),
            P("head"),
            P("head"),
            P(None, "head"),
            P(),
            P("head"),
            P("seq", "head"),
        ),
        out_specs=(
            P("seq", "head"),
            P("seq", "head"),
            P(None, ("seq", "head"), None),
            P("head", "seq"),
        ),
        check_vma=False,
    )
```

```python
import functools

import jax
import jax.numpy as jnp
from jax import lax
from jax.experimental import pallas as pl
from jax.experimental.pallas import tpu as pltpu
from jax.sharding import PartitionSpec as P

EPS = 1e-05
GROUP = 8
F32 = jnp.float32
BF16 = jnp.bfloat16
VMEM_BYTES = 16 * 2**20


def sigmoid(value):
    return 0.5 + 0.5 * jnp.tanh(0.5 * value)


def dot(a, b):
    return jnp.dot(a, b, preferred_element_type=F32)


def dot_split(a, b):
    high = a.astype(BF16)
    rest = a - high.astype(F32)
    middle = rest.astype(BF16)
    low = (rest - middle.astype(F32)).astype(BF16)
    return dot(high, b) + (dot(middle, b) + dot(low, b))


def dot_rows(a, b):
    return lax.dot_general(a, b, (((1,), (1,)), ((), ())), preferred_element_type=F32)


def dot_columns(a, b):
    return lax.dot_general(a, b, (((0,), (0,)), ((), ())), preferred_element_type=F32)


def triangle(length, upper):
    first = lax.broadcasted_iota(jnp.int32, (length, length), 0)
    second = lax.broadcasted_iota(jnp.int32, (length, length), 1)
    return first <= second if upper else first >= second


def columns_of(rows):
    return rows.T


class Groups:
    def __init__(self, kind, block, off, groups, size=1):
        self.kind, self.block, self.off, self.groups = kind, block, off, groups
        self.size = size
        self.by_rows = kind.endswith("heads")

    def turn(self, group, base):
        first = self.off + first_group(base)
        return lax.rem(group * self.size + first, self.groups) // self.size

    def place(self, index):
        return (index, 0) if self.by_rows else (0, index)

    def spec(self):
        if self.kind == "slots":
            return pl.BlockSpec(self.block, lambda g, b: (g, 0, 0))
        if self.kind.startswith("half"):
            return pl.BlockSpec(self.block, lambda g, b: self.place(g))
        return pl.BlockSpec(self.block, lambda g, b: self.place(self.turn(g, b)))

    def whole(self, shape, count):
        if self.kind.startswith("window"):
            block = list(self.block)
            block[0 if self.by_rows else 1] *= count
            return pl.BlockSpec(
                tuple(block), lambda g, b: self.place(self.turn(0, b) // count)
            )
        if self.kind == "top":
            shape = (self.block[0], count * self.block[1])
        return pl.BlockSpec(shape, lambda g, b: (0,) * len(shape))

    def view(self, ref, group, base):
        if self.kind == "slots":
            return ref.at[pl.ds(group, 1)]
        if self.kind in ("wide", "heads"):
            group = self.turn(group, base)
        size = self.block[0 if self.by_rows else 1]
        span = pl.ds(pl.multiple_of(jnp.int32(group) * size, size), size)
        return ref.at[span] if self.by_rows else ref.at[:, span]


def call(
    body,
    outs,
    ins,
    *,
    base,
    grid=1,
    loop=1,
    scratch=(),
    after=(),
    carry=(),
    place=None,
    token=False,
    flops=0,
):
    aliases = {1 + len(ins) + len(after) + i: i for i in range(len(carry))}
    for read, written in (place or {}).items():
        aliases[1 + read] = written
    after = list(after) + list(carry)
    outs = list(outs)
    if token:
        outs.append(((8, 128), F32, ((8, 128), lambda *_: (0, 0))))

    def spec(shape, block):
        if block is None:
            return pl.BlockSpec(memory_space=pl.ANY)
        if not isinstance(block, Groups):
            return pl.BlockSpec(*block)
        return block.whole(shape, loop) if grid == 1 else block.spec()

    in_specs = [spec(array.shape, block) for array, block in ins]
    in_specs += [pl.BlockSpec(memory_space=pl.ANY) for _ in after]
    out_specs = [spec(shape, block) for shape, _, block in outs]
    out_shape = [jax.ShapeDtypeStruct(shape, dtype) for shape, dtype, _ in outs]
    arrays = [array for array, _ in ins]
    moved = sum(a.size * a.dtype.itemsize for a in arrays + out_shape)
    blocks = [block for _, block in ins] + [block for _, _, block in outs]

    def ordered(where, *refs):
        taken, rest = refs[: len(ins)], refs[len(ins) + len(after) :]
        results, extra = rest[: len(outs)], rest[len(outs) :]
        if token:
            results[-1][...] = jnp.zeros((8, 128), F32)

        def step(group, _):
            views = [
                block.view(ref, group, where) if isinstance(block, Groups) else ref
                for ref, block in zip(taken + results, blocks)
            ]
            if token:
                views = views[:-1]
            body((group, loop), where, *views, *extra)
            return 0

        if grid > 1:
            views = taken + (results[:-1] if token else results)
            body((pl.program_id(0), grid), where, *views, *extra)
        elif loop > 1:
            lax.fori_loop(0, loop, step, 0)
        else:
            step(0, 0)

    return pl.pallas_call(
        ordered,
        out_shape=out_shape,
        grid_spec=pltpu.PrefetchScalarGridSpec(
            num_scalar_prefetch=1,
            grid=(grid,),
            in_specs=in_specs,
            out_specs=out_specs,
            scratch_shapes=list(scratch),
        ),
        input_output_aliases=aliases,
        cost_estimate=pl.CostEstimate(flops=flops, bytes_accessed=moved, transcendentals=0),
        compiler_params=pltpu.CompilerParams(vmem_limit_bytes=VMEM_BYTES),
    )(base, *arrays, *after)


def in_hbm(array):
    return pltpu.with_memory_space_constraint(array, pltpu.HBM)


def column_of(row):
    count = row.shape[1]
    first = lax.broadcasted_iota(jnp.int32, (count, count), 0)
    second = lax.broadcasted_iota(jnp.int32, (count, count), 1)
    return jnp.sum(jnp.where(first == second, row, 0.0), axis=1, keepdims=True)


def steps_body(
    at,
    base,
    raw,
    bias,
    log_rate,
    skip,
    x_tail,
    bc_in,
    bc_taps,
    step_out,
    cumul_out,
    rate_out,
    slope_out,
    rows_out,
    rim_out,
    bc_in_out,
    bc_taps_out,
):
    bc_in_out[...] = bc_in[...]
    bc_taps_out[...] = bc_taps[...]
    heads, length = raw.shape
    channels = x_tail.shape[1]
    rim_out[:, 0:channels] = x_tail[...].astype(F32)[13:16, :].astype(BF16)
    for j in range(2):
        start = channels + 128 * j
        rim_out[:, start : start + 128] = bc_in[j, length - 16 :].astype(F32)[13:16, :].astype(BF16)
    shifted = raw[...] + column_of(bias[...])
    step = jnp.maximum(shifted, 0.0) + jnp.log1p(jnp.exp(-jnp.abs(shifted)))
    rate = jnp.broadcast_to(-jnp.exp(column_of(log_rate[...])), step.shape)
    cumul = dot_split(rate * step, triangle(length, True).astype(BF16))
    step_out[...] = step
    cumul_out[...] = cumul
    rate_out[...] = rate
    slope_out[...] = sigmoid(shifted)
    skips = column_of(skip[...])
    for head in range(heads):
        lanes = slice(head * 128, head * 128 + 128)
        rows_out[0:1, lanes] = jnp.broadcast_to(cumul[head : head + 1, length - 1 :], (1, 128))
        rows_out[1:2, lanes] = jnp.broadcast_to(skips[head : head + 1, :], (1, 128))


def pick(test, yes, no):
    return jnp.where(test, yes, no)


def first_group(place):
    return place[0] & 255


def place_bit(place, index):
    return lax.shift_right_logical(place[0], 8 + index) & 1


def weights_body(at, place, own, core, across, *outs):
    t0, t1 = own[0:1, :], core[...]
    e0, e1, own_chip, ex = jnp.exp(t0), jnp.exp(t1), jnp.exp(t0 + t1), jnp.exp(across[...])
    one = jnp.ones_like(e0)
    zero = jnp.zeros_like(e0)
    bits = [place_bit(place, i) for i in range(3)]
    x_first = bits[2] == 0
    for out, reverse in zip(outs, (False, True)):
        y, x, c = ((1 - bit if reverse else bit) == 1 for bit in bits)
        either = jnp.logical_or(x, y)
        scale = pick(jnp.logical_or(x_first, either), one, ex)
        rows = [pick(c, one, e1), pick(c, e0, one)]
        rows += [rows[0] * scale, rows[1] * scale]
        rows += [
            pick(x_first, pick(x, one, ex), pick(jnp.logical_and(x, y), zero, one)),
            pick(x_first, pick(x, own_chip, one), pick(y, pick(x, one, own_chip), zero)),
        ]
        a = pick(x_first, pick(x, one, zero), pick(y, pick(x, ex, one), zero))
        b = pick(x_first, pick(y, pick(x, ex, one), zero), pick(either, one, zero))
        into, send = pick(c, e1, one), pick(c, one, e0)
        rows += [into * a, into * b, pick(c, one, zero)]
        rows += [send * a, send * b, pick(c, zero, one)]
        for index, row in enumerate(rows):
            out[index : index + 1, :] = row


def combine(base, groups, weights, outs, after=(), slots_of=None, at=0, carry=()):
    arrays, columns = [], []
    for slots in outs:
        for column, terms in slots:
            if column not in columns:
                columns.append(column)
            for _, (array, slot) in terms:
                if not any(array is a and slot == s for a, s in arrays):
                    arrays.append((array, slot))
    place = lambda array, slot: [
        i for i, (a, s) in enumerate(arrays) if a is array and s == slot
    ][0]
    plan = [
        [
            (columns.index(column), [(row, place(*source)) for row, source in terms])
            for column, terms in slots
        ]
        for slots in outs
    ]

    def body(at, base, *refs):
        rows, values = refs[: len(columns)], refs[len(columns) : len(columns) + len(arrays)]
        results = refs[len(columns) + len(arrays) :]
        width = rows[0].shape[1]
        for result, slots in zip(results, plan):
            for slot, (column, terms) in enumerate(slots):
                for start in range(0, width, 256):
                    lanes = slice(start, start + 256)
                    total = None
                    for row, index in terms:
                        term = rows[column][row : row + 1, lanes] * values[index][
                            0, :, lanes
                        ].astype(F32)
                        total = term if total is None else total + term
                    result[slot, :, lanes] = total.astype(BF16)

    length, width = arrays[0][0].shape[1:]
    block = lambda slot, count: ((count, length, width), lambda g, b: (slot, 0, 0))
    ins = [
        (
            weights,
            (
                (weights.shape[0], width),
                lambda g, b, column=column: (0, lax.rem(first_group(b) + column, groups)),
            ),
        )
        for column in columns
    ]
    ins += [(array, block(slot, 1)) for array, slot in arrays]
    results = [
        ((slots_of or len(slots), length, width), BF16, block(at, len(slots))) for slots in outs
    ]
    return call(body, results, ins, base=base, after=after, carry=carry)


def scan_blocks(base, groups, weights, local, local_sent, reverse, beside):
    count = lax.axis_size("seq")

    def swap(block, bits):
        route = [(i, i ^ bits[i % 2]) for i in range(count)]
        return lax.ppermute(block, "seq", route)

    def merge(slot, *plans, **places):
        outs = [[(slot, list(zip(rows, sources)))] for rows, sources in plans]
        return combine(base, groups, weights, outs, **places)

    taken = swap(local_sent, (1, 1))
    chips, first_taken, sent, second_taken = [], [], [], []
    for slot in range(2):
        both = ((local, slot), (taken, slot))
        chip, chip_sent = merge(slot, ((0, 1), both), ((2, 3), both))
        chips.append(chip)
        first_taken.append(swap(chip_sent, (2, 4)))
    after = [beside[0](chips[1])]
    for slot in range(2):
        sources = ((chips[slot], 0), (first_taken[slot], 0))
        (block,) = merge(slot, ((4, 5), sources), after=after)
        sent.append(block)
        second_taken.append(swap(block, (4, 2)))
        if slot == 0:
            after = [beside[1](block)]
    after = beside[2](sent[1])
    carry = []
    for slot in range(2):
        sources = ((first_taken[slot], 0), (second_taken[slot], 0))
        mine, handed = merge(
            slot,
            ((6, 7, 8), (*sources, (taken, slot))),
            ((9, 10, 11), (*sources, (local, slot))),
            after=after[slot],
            slots_of=2,
            at=slot,
            carry=carry,
        )
        carry = [mine, handed]
    return mine, swap(handed, (1, 1))


def gather_blocks(totals, local, reverse):
    table = lax.all_gather(totals, "seq", axis=0, tiled=True)
    blocks = lax.all_gather(local[None], "seq", axis=0, tiled=True)
    own = lax.axis_index("seq")
    order = jnp.arange(table.shape[0], dtype=jnp.int32)
    if reverse:
        inside = (order[None, :] > own) & (order[None, :] < order[:, None])
        selected = order > own
    else:
        inside = (order[None, :] > order[:, None]) & (order[None, :] < own)
        selected = order < own
    exponent = jnp.sum(jnp.where(inside[:, :, None], table[None], 0.0), axis=1)
    factor = jnp.where(selected[:, None], jnp.exp(exponent), 0.0)
    factor = factor.reshape(factor.shape[0], local.shape[0], 1, local.shape[2])
    state = jnp.sum(factor * blocks.astype(F32), axis=0).astype(BF16)
    return state, state


def conv_body(fetch, at, base, x_in, taps, *refs):
    length, width = x_in.shape
    group, groups = at
    if fetch:
        x_all, taps_all, x_out, slope_out, top_out, taps_out, x_mine, taps_mine, ext, sems = refs
        lanes = pl.ds(pl.multiple_of(first_group(base) * width, 128), x_mine.shape[1])
        copies = [
            pltpu.make_async_copy(x_all.at[:, lanes], x_mine, sems.at[0]),
            pltpu.make_async_copy(taps_all.at[:, lanes], taps_mine, sems.at[1]),
        ]

        @pl.when(group == 0)
        def _():
            for copy in copies:
                copy.start()

    else:
        x_out, slope_out, top_out, taps_out, ext = refs
    top_out[...] = x_in[0:16, :]
    taps_out[...] = taps[...]
    ext[0:8, :] = jnp.zeros((8, 128), F32)
    for start in range(0, width, 128):
        lanes = slice(start, start + 128)
        ext[8 : 8 + length, :] = x_in[:, lanes].astype(F32)
        pre = taps[0:1, lanes] * ext[5 : 5 + length, :]
        for k in range(1, 4):
            pre = pre + taps[k : k + 1, lanes] * ext[5 + k : 5 + k + length, :]
        sigma = sigmoid(pre)
        x_out[:, lanes] = (pre * sigma).astype(BF16)
        slope_out[:, lanes] = sigma * (1.0 + pre * (1.0 - sigma))
    if fetch:

        @pl.when(group == groups - 1)
        def _():
            for copy in copies:
                copy.wait()


def state_body(first, at, base, x_low, x_top, x_halo, taps, step_in, cumul_in, *refs):
    length, width = x_low.shape
    if first:
        bc_in, bc_halo, bc_taps, slope_out, x_out, state_out = refs[:6]
        bc_out, bc_slope_out, gram_out, b_turned, ext, bc_ext = refs[6:]

        @pl.when(at[0] == 0)
        def _():
            for j in range(2):
                halo = bc_halo[:, j * 128 : j * 128 + 128].astype(F32)
                bc_ext[5:8, :] = jnp.where(place_bit(base, 5) == 1, 0.0, halo)
                bc_ext[8 : 8 + length, :] = bc_in[j].astype(F32)
                pre = bc_taps[j, 0:1, :] * bc_ext[5 : 5 + length, :]
                for k in range(1, 4):
                    pre = pre + bc_taps[j, k : k + 1, :] * bc_ext[5 + k : 5 + k + length, :]
                sigma = sigmoid(pre)
                bc_out[j] = (pre * sigma).astype(BF16)
                bc_slope_out[j] = sigma * (1.0 + pre * (1.0 - sigma))
            b_turned[...] = bc_out[0].astype(F32).T
            gram_out[...] = jnp.where(
                triangle(length, False), dot_rows(bc_out[1], bc_out[0]), 0.0
            )

    else:
        b_turned, slope_out, x_out, state_out, ext = refs

    top = x_top.shape[0]
    ext[5:8, :] = jnp.where(place_bit(base, 5) == 1, 0.0, x_halo[...].astype(F32))
    ext[8 : 8 + top, :] = x_top[...].astype(F32)
    tail_step = jnp.exp(cumul_in[:, length - 1 :] - cumul_in[...]) * step_in[...]
    for head in range(width // 128):
        lanes = slice(head * 128, head * 128 + 128)
        pre = taps[0:1, lanes] * ext[5 : 5 + top, lanes]
        for k in range(1, 4):
            pre = pre + taps[k : k + 1, lanes] * ext[5 + k : 5 + k + top, lanes]
        sigma = sigmoid(pre)
        x_rows = (pre * sigma).astype(BF16)
        x_out[:, lanes] = x_rows
        slope_out[:, lanes] = sigma * (1.0 + pre * (1.0 - sigma))
        x_head = jnp.concatenate([x_rows, x_low[top:, lanes]], axis=0)
        weighted = (b_turned[...] * tail_step[head : head + 1, :]).astype(BF16)
        state_out[0, :, lanes] = dot(weighted, x_head).astype(BF16)


def inner_body(at, base, gram, step_in, cumul_in, x_in, rows, mixed_out):
    cumul = cumul_in[...]
    cumul_columns = columns_of(cumul)
    for head in range(x_in.shape[1] // 128):
        lanes = slice(head * 128, head * 128 + 128)
        row = cumul[head : head + 1, :]
        decay = jnp.exp(jnp.minimum(cumul_columns[:, head : head + 1] - row, 0.0))
        mixer = (gram[...] * decay * step_in[head : head + 1, :]).astype(BF16)
        x_head = x_in[:, lanes]
        mixed_out[:, lanes] = dot(mixer, x_head) + rows[1:2, lanes] * x_head.astype(F32)


def gate_body(
    at, base, z_in, grad_in, gain, gate_out, gate_slope_out, scaled_out, scaled_gate_out
):
    for start in range(0, z_in.shape[1], 128):
        lanes = slice(start, start + 128)
        z = z_in[:, lanes].astype(F32)
        sigma = sigmoid(z)
        gate = z * sigma
        scaled = grad_in[:, lanes].astype(F32) * gain[:, lanes]
        gate_out[:, lanes] = gate
        gate_slope_out[:, lanes] = sigma * (1.0 + z * (1.0 - sigma))
        scaled_out[:, lanes] = scaled
        scaled_gate_out[:, lanes] = scaled * gate


def lift_body(at, base, bc, step_in, cumul_in, x_in, weighted_x, lifted_out, c_turned):
    @pl.when(at[0] == 0)
    def _():
        c_turned[...] = bc[1].astype(F32).T

    weights = block_weights(step_in[...], cumul_in[...])
    lifted = jnp.exp(cumul_in[...])
    for head in range(x_in.shape[1] // 128):
        lanes = slice(head * 128, head * 128 + 128)
        weight = weights[:, head : head + 1]
        weighted_x[:, lanes] = (weight * x_in[:, lanes].astype(F32)).astype(BF16)
        lifted_out[:, lanes] = (c_turned[...] * lifted[head : head + 1, :]).astype(BF16)


def mix_body(
    at, base, mixed_in, c_rows, cumul_in, state, gate_in, scaled_in, sums_in, *outs
):
    mixed_out, sums_out, squares, products = outs
    group, groups = at

    @pl.when(group == 0)
    def _():
        squares[...] = jnp.zeros_like(squares)
        products[...] = jnp.zeros_like(products)

    carried = dot(c_rows[0], state[0])
    lifted = jnp.exp(columns_of(cumul_in[...]))
    square, product = squares[...], products[...]
    for head in range(mixed_in.shape[1] // 128):
        lanes = slice(head * 128, head * 128 + 128)
        mixed = mixed_in[:, lanes] + lifted[:, head : head + 1] * carried[:, lanes]
        mixed_out[:, lanes] = mixed
        gated = mixed * gate_in[:, lanes]
        square = square + gated * gated
        product = product + mixed * scaled_in[:, lanes]
    squares[...] = square
    products[...] = product

    @pl.when(group == groups - 1)
    def _():
        sums_out[...] = sums_in[...]
        sums_out[0:1, :] += jnp.sum(squares[...].T, axis=0, keepdims=True)
        sums_out[1:2, :] += jnp.sum(products[...].T, axis=0, keepdims=True)


def square_body(at, base, mixed_in, gate_in, squared):
    for start in range(0, mixed_in.shape[1], 128):
        lanes = slice(start, start + 128)
        gate = gate_in[:, lanes]
        squared[:, lanes] = mixed_in[:, lanes] * gate * gate


def norm_scales(at, inner, sums, alpha, beta):
    @pl.when(at[0] == 0)
    def _():
        total = sums[0][...]
        for part in sums[1:]:
            total = total + part[...]
        inv_rms = lax.rsqrt(total[0:1, :] / inner + EPS)
        mean_dot = inv_rms * total[1:2, :] / inner
        alpha[...] = jnp.broadcast_to(inv_rms, alpha.shape).T
        beta[...] = jnp.broadcast_to(inv_rms * inv_rms * mean_dot, beta.shape).T


def grad_mixed_body(inner, parts, at, base, *refs):
    sums = refs[:parts]
    squared, scaled_in, lifted_c, grad_mixed, state_out, alpha, beta = refs[parts:]
    norm_scales(at, inner, sums, alpha, beta)
    for start in range(0, squared.shape[1], 128):
        lanes = slice(start, start + 128)
        low = (alpha[...] * scaled_in[:, lanes] - beta[...] * squared[:, lanes]).astype(BF16)
        grad_mixed[:, lanes] = low
        state_out[0, :, lanes] = dot(lifted_c[:, lanes], low).astype(BF16)


def grad_z_body(inner, parts, at, base, *refs):
    sums = refs[:parts]
    mixed_in, gate_in, gate_slope_in, scaled_in, grad_z, alpha, beta = refs[parts:]
    norm_scales(at, inner, sums, alpha, beta)
    for start in range(0, mixed_in.shape[1], 128):
        lanes = slice(start, start + 128)
        mixed = mixed_in[:, lanes]
        grad_gated = alpha[...] * scaled_in[:, lanes] - beta[...] * (mixed * gate_in[:, lanes])
        grad_z[:, lanes] = (grad_gated * (mixed * gate_slope_in[:, lanes])).astype(BF16)


def inner_back_body(
    last,
    at,
    base,
    gram,
    bc,
    step_in,
    cumul_in,
    x_in,
    grad_in,
    state_in,
    rows,
    sums_in,
    grad_x,
    q_out,
    r_out,
    bc_out,
    z_sum,
    c_sum,
):
    group, groups = at
    length = x_in.shape[0]

    @pl.when(group == 0)
    def _():
        z_sum[...] = sums_in[0]
        c_sum[...] = sums_in[1]

    cumul = cumul_in[...]
    cumul_columns = columns_of(cumul)
    lifted = jnp.exp(cumul_columns)
    state = state_in[0]
    c_rows = bc[1].astype(F32)
    lane = lax.broadcasted_iota(jnp.int32, (length, 128), 1)
    q_columns = jnp.zeros((length, 128), F32)
    for head in range(x_in.shape[1] // 128):
        lanes = slice(head * 128, head * 128 + 128)
        step = step_in[head : head + 1, :]
        decay = jnp.exp(
            jnp.minimum(cumul_columns[:, head : head + 1] - cumul[head : head + 1, :], 0.0)
        )
        gram_decay = gram[...] * decay
        mixer = (gram_decay * step).astype(BF16)
        x_head, grad_head = x_in[:, lanes], grad_in[:, lanes]
        product = dot_rows(grad_head, x_head)
        z_sum[...] += product * decay * step
        gram_grad = product * gram_decay
        r_out[head : head + 1, :] = jnp.sum(gram_grad, axis=0, keepdims=True)
        handed = lifted[:, head : head + 1] * dot_rows(grad_head, state[:, lanes])
        c_sum[...] += handed
        q = jnp.sum(gram_grad * step + c_rows * handed, axis=1, keepdims=True)
        q_columns = jnp.where(lane == head, q, q_columns)
        grad_x[:, lanes] = dot_columns(mixer, grad_head) + rows[1:2, lanes] * grad_head.astype(F32)
    q_out[...] = q_columns.T[:GROUP, :]

    @pl.when(group == groups - 1)
    def _():
        if last:
            summed = jnp.where(triangle(length, False), z_sum[...], 0.0)
            bc_out[0] = dot_split(summed.T, bc[1])
            bc_out[1] = c_sum[...] + dot_split(summed, bc[0])
        else:
            bc_out[0] = z_sum[...]
            bc_out[1] = c_sum[...]


def block_weights(step, cumul):
    return columns_of(jnp.exp(cumul[:, cumul.shape[1] - 1 :] - cumul) * step)


def rim_body(last, at, base, bc, step_in, cumul_in, weighted_x, partial, slope, out_in, *refs):
    group, groups = at
    width = weighted_x.shape[1]
    if last:
        rows_before, b_before, bc_partial, bc_slope, rim_out, bc_out, b_sum = refs
    else:
        rim_out, b_sum = refs

    @pl.when(group == 0)
    def _():
        b_sum[...] = b_before[...] if last else jnp.zeros_like(b_sum)

    out_low = out_in[0]
    b_sum[...] += dot_rows(weighted_x[...], out_low)
    weights = block_weights(step_in[...], cumul_in[...])[0:8, :]
    returned = dot(bc[0][0:16, :], out_low)[0:8, :]
    start = group
    if last:
        count = rim_out.shape[1] // width
        start = lax.rem(group + count - groups + first_group(base), count)
    for head in range(width // 128):
        lanes = slice(head * 128, head * 128 + 128)
        weight = weights[:, head : head + 1]
        rows = (partial[0:8, lanes] + weight * returned[:, lanes]) * slope[0:8, lanes]
        place = pl.multiple_of(jnp.int32(start) * width + head * 128, 128)
        rim_out[:, pl.ds(place, 128)] = rows[0:3, :]

    if last:

        @pl.when(group == groups - 1)
        def _():
            before = rows_before.shape[1]
            if before < rim_out.shape[1] - 256:
                place = pl.multiple_of(first_group(base) * width, 128)
                rim_out[:, pl.ds(place, before)] = rows_before[...]
            bc_out[0] = (b_sum[...] + bc_partial[0]) * bc_slope[0]
            bc_out[1] = bc_partial[1] * bc_slope[1]
            for j in range(2):
                lanes = rim_out.shape[1] - 256 + 128 * j
                rim_out[:, lanes : lanes + 128] = bc_out[j, 0:3, :]


def grad_dt_body(
    at,
    base,
    bc,
    rate,
    dt_slope,
    step_in,
    cumul_in,
    q_in,
    r_in,
    x_in,
    state_in,
    out_in,
    grad_dt,
    selector,
    products,
):
    heads, length = q_in.shape
    width = state_in.shape[2]
    row = lax.broadcasted_iota(jnp.int32, selector.shape, 0)
    lane = lax.broadcasted_iota(jnp.int32, selector.shape, 1)
    selector[...] = (lax.shift_right_logical(row, 7) == lane).astype(BF16)
    row = lax.broadcasted_iota(jnp.int32, (16, width), 0)
    lane = lax.shift_right_logical(lax.broadcasted_iota(jnp.int32, (16, width), 1), 7)
    dots = jnp.zeros((16, 1), F32)
    for group in range(state_in.shape[0]):
        out_low = out_in[group]
        returned = dot(bc[0], out_low)
        for start in range(0, width, 128):
            lanes = slice(start, start + 128)
            place = slice(group * width + start, group * width + start + 128)
            products[:, place] = (x_in[:, place].astype(F32) * returned[:, lanes]).astype(BF16)
        summed = dot(jnp.ones((16, length), BF16), state_in[group] * out_low)
        own = row - GROUP * group == lane
        dots = dots + jnp.sum(jnp.where(own, summed, 0.0), axis=1, keepdims=True)
    inner_b = dot(products[...], selector[...]).T[:heads, :]
    cumul, step = cumul_in[...], step_in[...]
    w = jnp.exp(cumul[:, length - 1 :] - cumul) * inner_b
    q, r = q_in[...], r_in[...]
    inside = jnp.sum(step * w, axis=1, keepdims=True)
    end = inside + jnp.exp(cumul[:, length - 1 :]) * dots[:heads]
    last = lax.broadcasted_iota(jnp.int32, (heads, length), 1) == length - 1
    grad_cumul = q - step * (r + w) + jnp.where(last, end, 0.0)
    grad_log = dot_split(grad_cumul, triangle(length, False).astype(BF16))
    grad_dt[...] = (r + w + rate[...] * grad_log) * dt_slope[...]


def grad_x_body(
    at,
    base,
    bc,
    step_in,
    cumul_in,
    partial,
    slope,
    taps,
    halo,
    out_in,
    grad_x,
    ext,
):
    length, width = partial.shape
    weights = block_weights(step_in[...], cumul_in[...])
    returned = dot(bc[0], out_in[0])
    for head in range(width // 128):
        lanes = slice(head * 128, head * 128 + 128)
        weight = weights[:, head : head + 1]
        ext[0:length, :] = (partial[:, lanes] + weight * returned[:, lanes]) * slope[:, lanes]
        ext[length : length + 3, :] = jnp.where(place_bit(base, 6) == 1, 0.0, halo[:, lanes])
        total = taps[0:1, lanes] * ext[3 : 3 + length, :]
        for k in range(1, 4):
            total = total + taps[k : k + 1, lanes] * ext[3 - k : 3 - k + length, :]
        grad_x[:, lanes] = total.astype(BF16)


def bc_back_body(at, place, grad_pre, halo, taps, kept, sent, ext, total):
    length, half = grad_pre.shape[1], kept.shape[1]
    for j in range(2):
        ext[0:length, :] = grad_pre[j]
        rim = halo[:, 128 * j : 128 * j + 128]
        ext[length : length + 3, :] = jnp.where(place_bit(place, 6) == 1, 0.0, rim)
        summed = taps[j, 0:1, :] * ext[3 : 3 + length, :]
        for k in range(1, 4):
            summed = summed + taps[j, k : k + 1, :] * ext[3 - k : 3 - k + length, :]
        total[...] = summed
        kept[j] = total[pl.ds(pl.multiple_of(place_bit(place, 3) * half, half), half), :]
        sent[j] = total[pl.ds(pl.multiple_of((1 - place_bit(place, 3)) * half, half), half), :]


def bc_half_body(at, place, mine, taken, kept, sent, total):
    half = kept.shape[1]
    for j in range(2):
        total[...] = mine[j] + taken[j]
        kept[j] = total[pl.ds(pl.multiple_of(place_bit(place, 4) * half, half), half), :]
        sent[j] = total[pl.ds(pl.multiple_of((1 - place_bit(place, 4)) * half, half), half), :]


def bc_last_body(at, _, mine, taken, out):
    out[...] = (mine[...] + taken[...]).astype(BF16)


def conv_back(extended, weights):
    length = extended.shape[-2] - 3
    summed = weights[..., 0, :][..., None, :] * extended[..., 3 : 3 + length, :]
    for k in range(1, 4):
        summed = (
            summed
            + weights[..., k, :][..., None, :] * extended[..., 3 - k : 3 - k + length, :]
        )
    return summed


def shards(
    x_input,
    z_input,
    bc_input,
    dt_raw,
    dt_bias,
    a_log,
    d_skip,
    conv_x,
    convolution_bc_taps,
    rescale_factor,
    grad_out,
):
    length, channels = x_input.shape
    heads = dt_raw.shape[0]
    groups = heads // GROUP
    width = GROUP * 128
    count, parts = lax.axis_size("seq"), lax.axis_size("head")
    inner = channels * parts
    own = lax.axis_index("seq")
    split = count == 8 and groups == 4
    own_half = groups // 2 if split else groups
    bit = lambda value, place: lax.shift_right_logical(value, place) & 1
    along_head = lax.axis_index("head")
    base = bit(own, 0) * own_half if split else own * 0
    ends = (own == 0).astype(jnp.int32), (own == count - 1).astype(jnp.int32)
    for place, value in enumerate(
        (bit(own, 2), bit(own, 1), bit(own, 0), bit(along_head, 1), bit(along_head, 0), *ends)
    ):
        base = base | lax.shift_left(value, 8 + place)
    base = base.astype(jnp.int32)[None]

    whole = lambda *shape: ((shape, lambda g, b: (0,) * len(shape)),)
    wide_at = lambda off: (Groups("wide", (length, width), off, groups),)
    rows_at = lambda off: (Groups("heads", (GROUP, length), off, groups),)
    lanes_at = lambda n, off: (Groups("wide", (n, width), off, groups),)
    slot = (Groups("slots", (1, length, width), 0, groups),)
    full = lambda array: (array,) + whole(*array.shape)
    half_width = own_half * width
    half_heads = own_half * GROUP
    half = lambda n: (Groups("half", (n, width), 0, groups),)
    half_rows = (Groups("half heads", (GROUP, length), 0, groups),)
    window_at = lambda n, off: (Groups("window", (n, width), off, groups),)
    halves = [own_half, 0] if split else [0]
    rest = halves[0]

    gain = rescale_factor[None, :]
    f32 = lambda *shape: (shape, F32)
    low = lambda *shape: (shape, BF16)

    step, cumul, rate, dt_slope, rows, rim, bc_rows, bc_taps = call(
        steps_body,
        [
            f32(heads, length) + whole(heads, length),
            f32(heads, length) + whole(heads, length),
            f32(heads, length) + whole(heads, length),
            f32(heads, length) + whole(heads, length),
            f32(2, channels) + whole(2, channels),
            low(3, channels + 256) + whole(3, channels + 256),
            low(2, length, 128) + whole(2, length, 128),
            f32(2, 4, 128) + whole(2, 4, 128),
        ],
        [
            full(in_hbm(dt_raw)),
            full(in_hbm(dt_bias[None, :])),
            full(in_hbm(a_log[None, :])),
            full(in_hbm(d_skip[None, :])),
            (in_hbm(x_input), ((16, channels), lambda g, b: (length // 16 - 1, 0))),
            full(in_hbm(bc_input)),
            full(in_hbm(convolution_bc_taps)),
        ],
        base=base,
    )
    rim_sent = rim
    rim = lax.ppermute(rim, "seq", [(i, (i + 1) % count) for i in range(count)])
    if split:
        swap = lambda block, bit: lax.ppermute(
            block, "seq", [(i, i ^ bit) for i in range(count)]
        )
        total = rows[0:1]
        total_core = swap(total, 1)
        chip_total = total + total_core
        total_across = swap(chip_total, 2)
        table = f32(16, channels) + whole(16, channels)
        ahead, behind = call(
            weights_body,
            [table, table],
            [full(rows), full(total_core), full(total_across)],
            base=base,
            )

    def passed(locals_, reverse, beside):
        if split:
            local_sent, local = locals_[rest], locals_[0]
            weights = behind if reverse else ahead
            return scan_blocks(base, groups, weights, local, local_sent, reverse, beside)
        local = locals_[0]
        for work in beside:
            work(local)
        return gather_blocks(rows[0:1], local, reverse)

    x_low, slope, local = {}, {}, {}
    ready = rim_sent
    for off in halves:
        outs = [
            low(length, half_width) + half(length),
            f32(length, half_width) + half(length),
            low(16, half_width) + half(16),
            f32(4, half_width) + half(4),
        ]
        if off == rest:
            x_all, taps_all = in_hbm(x_input), in_hbm(conv_x)
            ins = [(x_all,) + wide_at(off), (taps_all,) + lanes_at(4, off)]
            scratch = [pltpu.VMEM((length + 8, 128), F32)]
            if split:
                ins += [(x_all, None), (taps_all, None)]
                outs += [
                    low(length, half_width) + whole(length, half_width),
                    f32(4, half_width) + whole(4, half_width),
                ]
                scratch += [pltpu.SemaphoreType.DMA((2,))]
            x_low[off], slope[off], x_top, taps, *fetched = call(
                functools.partial(conv_body, split),
                outs,
                ins,
                base=base,
                grid=own_half,
                scratch=scratch,
                after=[ready],
            )
        else:
            x_low[off], slope[off], x_top, taps = call(
                functools.partial(conv_body, False),
                outs,
                [(fetched[0],) + half(length), (fetched[1],) + half(4)],
                base=base,
                loop=own_half,
                scratch=[pltpu.VMEM((length + 8, 128), F32)],
                after=[ready],
            )
        first = off == rest
        top = (Groups("top", (16, width), 0, groups),)
        ins = [
            (x_low[off],) + half(length),
            (x_top,) + half(16),
            (rim,) + lanes_at(3, off),
            (taps,) + half(4),
            (step,) + rows_at(off),
            (cumul,) + rows_at(off),
        ]
        outs = [
            f32(length, half_width) + top,
            low(length, half_width) + top,
            low(own_half, length, width) + slot,
        ]
        scratch = [pltpu.VMEM((24, width), F32)]
        if first:
            ins += [
                full(bc_rows),
                (rim, ((3, 256), lambda g, b: (0, channels // 256))),
                full(bc_taps),
            ]
            outs += [
                low(2, length, 128) + whole(2, length, 128),
                f32(2, length, 128) + whole(2, length, 128),
                f32(length, length) + whole(length, length),
                f32(128, length) + whole(128, length),
            ]
            scratch += [pltpu.VMEM((length + 8, 128), F32)]
        else:
            ins += [full(b_turned)]
        result = call(
            functools.partial(state_body, first),
            outs,
            ins,
            base=base,
            loop=own_half,
            scratch=scratch,
            carry=[slope[off]],
            place={0: 1},
            flops=2 * length * 128 * half_width,
        )
        if first:
            bc, bc_slope, gram, b_turned = result[3:]
        slope[off], x_low[off], local[off] = result[:3]
        ready = local[off]

    inside, gate, gate_slope, scaled, scaled_gate = {}, {}, {}, {}, {}

    def mix_inside(off, ready):
        inside[off], token = call(
            inner_body,
            [f32(length, half_width) + half(length)],
            [
                full(gram),
                (step,) + rows_at(off),
                (cumul,) + rows_at(off),
                (x_low[off],) + half(length),
                (rows,) + lanes_at(2, off),
            ],
            base=base,
            loop=own_half,
            after=[ready],
            token=True,
            flops=2 * length * 128 * half_width,
        )
        return token

    def gates(off, ready):
        gate[off], gate_slope[off], scaled[off], scaled_gate[off], token = call(
            gate_body,
            [f32(length, half_width) + half(length)] * 4,
            [
                (z_input,) + wide_at(off),
                (grad_out,) + wide_at(off),
                (gain,) + lanes_at(1, off),
            ],
            base=base,
            loop=own_half,
            after=[ready],
            token=True,
        )
        return token

    def mix_second(ready):
        return mix_inside(rest, ready) if split else ready

    def mix_third(ready):
        return [], [gates(off, ready) for off in reversed(halves)]

    states = passed(local, False, (functools.partial(mix_inside, 0), mix_second, mix_third))
    states = dict(zip((0, rest), states))
    mixed, sums = {}, jnp.zeros((8, length), F32)
    two_scales = [pltpu.VMEM((length, 128), F32), pltpu.VMEM((length, 128), F32)]
    for off in reversed(halves):
        mixed[off], sums = call(
            mix_body,
            [f32(length, half_width) + half(length), f32(8, length) + whole(8, length)],
            [
                (inside[off],) + half(length),
                (bc, ((1, length, 128), lambda g, b: (1, 0, 0))),
                (cumul,) + rows_at(off),
                (states[off],) + slot,
                (gate[off],) + half(length),
                (scaled_gate[off],) + half(length),
                full(sums),
            ],
            base=base,
            loop=own_half,
            scratch=two_scales,
            flops=2 * length * 128 * half_width,
        )
    turn_head = lambda block, bit: lax.ppermute(
        block, "head", [(i, i ^ bit) for i in range(parts)]
    )
    weighted_x, lifted_c, squared = {}, {}, {}
    for off in halves:
        weighted_x[off], lifted_c[off] = call(
            lift_body,
            [low(length, half_width) + half(length), low(length, half_width) + half(length)],
            [
                full(bc),
                (step,) + rows_at(off),
                (cumul,) + rows_at(off),
                (x_low[off],) + half(length),
            ],
            base=base,
            loop=own_half,
            scratch=[pltpu.VMEM((128, length), F32)],
            after=[sums],
        )
        (squared[off],) = call(
            square_body,
            [f32(length, half_width) + half(length)],
            [(mixed[off],) + half(length), (gate[off],) + half(length)],
            base=base,
            loop=own_half,
        )
    if parts == 4:
        sums = sums + turn_head(sums, 1)
        all_sums = [sums, turn_head(sums, 2)]
    else:
        all_sums = [lax.psum(sums, "head")]
    grad_mixed, local_back = {}, {}
    for off in halves:
        grad_mixed[off], local_back[off] = call(
            functools.partial(grad_mixed_body, inner, len(all_sums)),
            [low(length, half_width) + half(length), low(own_half, length, width) + slot],
            [full(part) for part in all_sums]
            + [
                (squared[off],) + half(length),
                (scaled_gate[off],) + half(length),
                (lifted_c[off],) + half(length),
            ],
            base=base,
            loop=own_half,
            scratch=two_scales,
            flops=2 * length * 128 * half_width,
        )

    partial, q_rows, r_rows = {}, {}, {}
    carried = {"sums": jnp.zeros((2, length, 128), F32), "z": [], "dt": [], "x": []}

    def back_inside(off, ready):
        partial[off], q_rows[off], r_rows[off], carried["sums"], token = call(
            functools.partial(inner_back_body, off == rest),
            [
                f32(length, half_width) + half(length),
                f32(half_heads, length) + half_rows,
                f32(half_heads, length) + half_rows,
                f32(2, length, 128) + whole(2, length, 128),
            ],
            [
                full(gram),
                full(bc),
                (step,) + rows_at(off),
                (cumul,) + rows_at(off),
                (x_low[off],) + half(length),
                (grad_mixed[off],) + half(length),
                (states[off],) + slot,
                (rows,) + lanes_at(2, off),
                full(carried["sums"]),
            ],
            base=base,
            loop=own_half,
            scratch=[pltpu.VMEM((length, length), F32), pltpu.VMEM((length, 128), F32)],
            after=[ready],
            token=True,
            flops=6 * length * 128 * half_width,
        )
        return token

    def back_gates(off, ready):
        grad_z, token = call(
            functools.partial(grad_z_body, inner, len(all_sums)),
            [low(length, channels) + window_at(length, off)],
            [full(part) for part in all_sums]
            + [
                (mixed[off],) + half(length),
                (gate[off],) + half(length),
                (gate_slope[off],) + half(length),
                (scaled[off],) + half(length),
            ],
            base=base,
            loop=own_half,
            scratch=two_scales,
            carry=carried["z"],
            after=[ready],
            token=True,
        )
        carried["z"] = [grad_z]
        carried["z_token"] = token
        return token

    def back_second(ready):
        return back_gates(0, ready)

    def back_third(ready):
        if not split:
            return [], []
        token = back_inside(rest, ready)
        return [token], [back_gates(rest, token)]

    backs = passed(local_back, True, (functools.partial(back_inside, 0), back_second, back_third))
    backs = dict(zip((0, rest), backs))

    def make_grad_dt(off, after):
        table = (Groups("heads", (half_heads, length), off, groups, own_half),)
        window = (Groups("window heads", (half_heads, length), off, groups, own_half),)
        grad_dt, token = call(
            grad_dt_body,
            [f32(heads, length) + window],
            [
                full(bc),
                (rate,) + table,
                (dt_slope,) + table,
                (step,) + table,
                (cumul,) + table,
                full(q_rows[off]),
                full(r_rows[off]),
                full(x_low[off]),
                full(states[off]),
                full(backs[off]),
            ],
            base=base,
            scratch=[pltpu.VMEM((half_width, 128), BF16), pltpu.VMEM((length, half_width), BF16)],
            carry=carried["dt"],
            after=after,
            token=True,
            flops=4 * length * 128 * half_width,
        )
        carried["dt"] = [grad_dt]
        return token

    def make_grad_x(off, after):
        grad_x, token = call(
            grad_x_body,
            [low(length, channels) + window_at(length, off)],
            [
                full(bc),
                (step,) + rows_at(off),
                (cumul,) + rows_at(off),
                (partial[off],) + half(length),
                (slope[off],) + half(length),
                (conv_x,) + lanes_at(4, off),
                (rim_back,) + lanes_at(3, off),
                (backs[off],) + slot,
            ],
            base=base,
            loop=own_half,
            scratch=[pltpu.VMEM((length + 8, 128), F32)],
            carry=carried["x"],
            after=after,
            token=True,
            flops=2 * length * 128 * half_width,
        )
        carried["x"] = [grad_x]
        return token

    def make_rim(off, before, after):
        last = off == rest
        if last:
            outs = [
                f32(3, channels + 256) + whole(3, channels + 256),
                f32(2, length, 128) + whole(2, length, 128),
            ]
        else:
            outs = [f32(3, half_width) + whole(3, half_width), f32(length, 128) + whole(length, 128)]
        return call(
            functools.partial(rim_body, last),
            outs,
            [
                full(bc),
                (step,) + rows_at(off),
                (cumul,) + rows_at(off),
                (weighted_x[off],) + half(length),
                (partial[off],) + half(length),
                (slope[off],) + half(length),
                (backs[off],) + slot,
            ]
            + [full(array) for array in before],
            base=base,
            loop=own_half,
            scratch=[pltpu.VMEM((length, 128), F32)] if last else [],
            after=after,
            flops=2 * length * 128 * half_width,
        )

    if split:
        before = make_rim(0, [], [])
    else:
        before = [jnp.zeros((3, channels), F32), jnp.zeros((length, 128), F32)]
    rim_back, grad_bc_pre = make_rim(rest, [*before, carried["sums"], bc_slope], [])
    rim_back = lax.ppermute(rim_back, "seq", [(i, (i - 1) % count) for i in range(count)])
    dt_token = make_grad_dt(rest, [grad_bc_pre])
    if parts == 4:
        piece = lambda rows: f32(2, rows, 128) + whole(2, rows, 128)
        kept, sent = call(
            bc_back_body,
            [piece(length // 2), piece(length // 2)],
            [
                full(grad_bc_pre),
                (rim_back, ((3, 256), lambda g, b: (0, channels // 256))),
                full(bc_taps),
            ],
            base=base,
            scratch=[pltpu.VMEM((length + 8, 128), F32), pltpu.VMEM((length, 128), F32)],
            after=[dt_token],
        )
        taken = turn_head(sent, 2)
        x_tokens = [make_grad_x(0, [sent])]
        if split:
            x_tokens = [make_grad_dt(0, x_tokens)]
        kept, sent = call(
            bc_half_body,
            [piece(length // 4), piece(length // 4)],
            [full(kept), full(taken)],
            base=base,
            scratch=[pltpu.VMEM((length // 2, 128), F32)],
            after=x_tokens,
        )
        taken = turn_head(sent, 1)
        x_tokens = [make_grad_x(rest, [sent])] if split else []
        (grad_bc,) = call(
            bc_last_body,
            [low(2, length // 4, 128) + whole(2, length // 4, 128)],
            [full(kept), full(taken)],
            base=base,
            after=x_tokens,
        )
    else:
        if split:
            make_grad_dt(0, [])
        for off in halves:
            make_grad_x(off, [])
        bc_halo = jnp.moveaxis(rim_back[:, channels:].reshape(3, 2, 128), 1, 0)
        bc_halo = jnp.where(own == count - 1, 0.0, bc_halo)
        bc_sum = conv_back(jnp.concatenate([grad_bc_pre, bc_halo], axis=1), convolution_bc_taps)
        share = length // parts
        bc_sum = lax.psum(bc_sum, "head")
        grad_bc = lax.dynamic_slice_in_dim(bc_sum, along_head * share, share, 1).astype(BF16)
    return (carried["x"][0], carried["z"][0], grad_bc, carried["dt"][0])


def solution(mesh):
    return jax.shard_map(
        shards,
        mesh=mesh,
        in_specs=(
            P("seq", "head"),
            P("seq", "head"),
            P(None, "seq", None),
            P("head", "seq"),
            P("head"),
            P("head"),
            P("head"),
            P(None, "head"),
            P(),
            P("head"),
            P("seq", "head"),
        ),
        out_specs=(
            P("seq", "head"),
            P("seq", "head"),
            P(None, ("seq", "head"), None),
            P("head", "seq"),
        ),
        check_vma=False,
    )
```

```python
import functools

import jax
import jax.numpy as jnp
from jax import lax
from jax.experimental import pallas as pl
from jax.experimental.pallas import tpu as pltpu
from jax.sharding import PartitionSpec as P

EPS = 1e-05
GROUP = 8
F32 = jnp.float32
BF16 = jnp.bfloat16
VMEM_BYTES = 16 * 2**20


def sigmoid(value):
    return 0.5 + 0.5 * jnp.tanh(0.5 * value)


def dot(a, b):
    return jnp.dot(a, b, preferred_element_type=F32)


def dot_split(a, b):
    high = a.astype(BF16)
    rest = a - high.astype(F32)
    middle = rest.astype(BF16)
    low = (rest - middle.astype(F32)).astype(BF16)
    return dot(high, b) + (dot(middle, b) + dot(low, b))


def dot_rows(a, b):
    return lax.dot_general(a, b, (((1,), (1,)), ((), ())), preferred_element_type=F32)


def dot_columns(a, b):
    return lax.dot_general(a, b, (((0,), (0,)), ((), ())), preferred_element_type=F32)


def triangle(length, upper):
    first = lax.broadcasted_iota(jnp.int32, (length, length), 0)
    second = lax.broadcasted_iota(jnp.int32, (length, length), 1)
    return first <= second if upper else first >= second


def columns_of(rows):
    return rows.T


class Groups:
    def __init__(self, kind, block, off, groups, size=1):
        self.kind, self.block, self.off, self.groups = kind, block, off, groups
        self.size = size
        self.by_rows = kind.endswith("heads")

    def turn(self, group, base):
        first = self.off + first_group(base)
        return lax.rem(group * self.size + first, self.groups) // self.size

    def place(self, index):
        return (index, 0) if self.by_rows else (0, index)

    def spec(self):
        if self.kind == "slots":
            return pl.BlockSpec(self.block, lambda g, b: (g, 0, 0))
        if self.kind.startswith("half"):
            return pl.BlockSpec(self.block, lambda g, b: self.place(g))
        return pl.BlockSpec(self.block, lambda g, b: self.place(self.turn(g, b)))

    def whole(self, shape, count):
        if self.kind.startswith("window"):
            block = list(self.block)
            block[0 if self.by_rows else 1] *= count
            return pl.BlockSpec(
                tuple(block), lambda g, b: self.place(self.turn(0, b) // count)
            )
        if self.kind == "top":
            shape = (self.block[0], count * self.block[1])
        return pl.BlockSpec(shape, lambda g, b: (0,) * len(shape))

    def view(self, ref, group, base):
        if self.kind == "slots":
            return ref.at[pl.ds(group, 1)]
        if self.kind in ("wide", "heads"):
            group = self.turn(group, base)
        size = self.block[0 if self.by_rows else 1]
        span = pl.ds(pl.multiple_of(jnp.int32(group) * size, size), size)
        return ref.at[span] if self.by_rows else ref.at[:, span]


def call(
    body,
    outs,
    ins,
    *,
    base,
    grid=1,
    loop=1,
    scratch=(),
    after=(),
    carry=(),
    place=None,
    token=False,
    flops=0,
):
    aliases = {1 + len(ins) + len(after) + i: i for i in range(len(carry))}
    for read, written in (place or {}).items():
        aliases[1 + read] = written
    after = list(after) + list(carry)
    outs = list(outs)
    if token:
        outs.append(((8, 128), F32, ((8, 128), lambda *_: (0, 0))))

    def spec(shape, block):
        if block is None:
            return pl.BlockSpec(memory_space=pl.ANY)
        if not isinstance(block, Groups):
            return pl.BlockSpec(*block)
        return block.whole(shape, loop) if grid == 1 else block.spec()

    in_specs = [spec(array.shape, block) for array, block in ins]
    in_specs += [pl.BlockSpec(memory_space=pl.ANY) for _ in after]
    out_specs = [spec(shape, block) for shape, _, block in outs]
    out_shape = [jax.ShapeDtypeStruct(shape, dtype) for shape, dtype, _ in outs]
    arrays = [array for array, _ in ins]
    moved = sum(a.size * a.dtype.itemsize for a in arrays + out_shape)
    blocks = [block for _, block in ins] + [block for _, _, block in outs]

    def ordered(where, *refs):
        taken, rest = refs[: len(ins)], refs[len(ins) + len(after) :]
        results, extra = rest[: len(outs)], rest[len(outs) :]
        if token:
            results[-1][...] = jnp.zeros((8, 128), F32)

        def step(group, _):
            views = [
                block.view(ref, group, where) if isinstance(block, Groups) else ref
                for ref, block in zip(taken + results, blocks)
            ]
            if token:
                views = views[:-1]
            body((group, loop), where, *views, *extra)
            return 0

        if grid > 1:
            views = taken + (results[:-1] if token else results)
            body((pl.program_id(0), grid), where, *views, *extra)
        elif loop > 1:
            lax.fori_loop(0, loop, step, 0)
        else:
            step(0, 0)

    return pl.pallas_call(
        ordered,
        out_shape=out_shape,
        grid_spec=pltpu.PrefetchScalarGridSpec(
            num_scalar_prefetch=1,
            grid=(grid,),
            in_specs=in_specs,
            out_specs=out_specs,
            scratch_shapes=list(scratch),
        ),
        input_output_aliases=aliases,
        cost_estimate=pl.CostEstimate(flops=flops, bytes_accessed=moved, transcendentals=0),
        compiler_params=pltpu.CompilerParams(vmem_limit_bytes=VMEM_BYTES),
    )(base, *arrays, *after)


def in_hbm(array):
    return pltpu.with_memory_space_constraint(array, pltpu.HBM)


def column_of(row):
    count = row.shape[1]
    first = lax.broadcasted_iota(jnp.int32, (count, count), 0)
    second = lax.broadcasted_iota(jnp.int32, (count, count), 1)
    return jnp.sum(jnp.where(first == second, row, 0.0), axis=1, keepdims=True)


def steps_body(
    at,
    base,
    raw,
    bias,
    log_rate,
    skip,
    x_tail,
    bc_in,
    bc_taps,
    step_out,
    cumul_out,
    rate_out,
    slope_out,
    rows_out,
    rim_out,
    bc_in_out,
    bc_taps_out,
):
    bc_in_out[...] = bc_in[...]
    bc_taps_out[...] = bc_taps[...]
    heads, length = raw.shape
    channels = x_tail.shape[1]
    rim_out[:, 0:channels] = x_tail[...].astype(F32)[13:16, :].astype(BF16)
    for j in range(2):
        start = channels + 128 * j
        rim_out[:, start : start + 128] = bc_in[j, length - 16 :].astype(F32)[13:16, :].astype(BF16)
    shifted = raw[...] + column_of(bias[...])
    step = jnp.maximum(shifted, 0.0) + jnp.log1p(jnp.exp(-jnp.abs(shifted)))
    rate = jnp.broadcast_to(-jnp.exp(column_of(log_rate[...])), step.shape)
    cumul = dot_split(rate * step, triangle(length, True).astype(BF16))
    step_out[...] = step
    cumul_out[...] = cumul
    rate_out[...] = rate
    slope_out[...] = sigmoid(shifted)
    skips = column_of(skip[...])
    for head in range(heads):
        lanes = slice(head * 128, head * 128 + 128)
        rows_out[0:1, lanes] = jnp.broadcast_to(cumul[head : head + 1, length - 1 :], (1, 128))
        rows_out[1:2, lanes] = jnp.broadcast_to(skips[head : head + 1, :], (1, 128))


def pick(test, yes, no):
    return jnp.where(test, yes, no)


def first_group(place):
    return place[0] & 255


def place_bit(place, index):
    return lax.shift_right_logical(place[0], 8 + index) & 1


def weights_body(at, place, own, core, across, beyond, *outs):
    t0, t1 = own[0:1, :], core[...]
    e0, e1, own_chip, ex = jnp.exp(t0), jnp.exp(t1), jnp.exp(t0 + t1), jnp.exp(across[...] + beyond[...])
    one = jnp.ones_like(e0)
    zero = jnp.zeros_like(e0)
    bits = [place_bit(place, i) for i in range(3)]
    x_first = bits[2] == 0
    for out, reverse in zip(outs, (False, True)):
        y, x, c = ((1 - bit if reverse else bit) == 1 for bit in bits)
        either = jnp.logical_or(x, y)
        scale = pick(jnp.logical_or(x_first, either), one, ex)
        rows = [pick(c, one, e1), pick(c, e0, one)]
        rows += [rows[0] * scale, rows[1] * scale]
        rows += [
            pick(x_first, pick(x, one, ex), pick(jnp.logical_and(x, y), zero, one)),
            pick(x_first, pick(x, own_chip, one), pick(y, pick(x, one, own_chip), zero)),
        ]
        a = pick(x_first, pick(x, one, zero), pick(y, pick(x, ex, one), zero))
        b = pick(x_first, pick(y, pick(x, ex, one), zero), pick(either, one, zero))
        into, send = pick(c, e1, one), pick(c, one, e0)
        rows += [into * a, into * b, pick(c, one, zero)]
        rows += [send * a, send * b, pick(c, zero, one)]
        for index, row in enumerate(rows):
            out[index : index + 1, :] = row


def combine(base, groups, weights, outs, after=(), slots_of=None, at=0, carry=()):
    arrays, columns = [], []
    for slots in outs:
        for column, terms in slots:
            if column not in columns:
                columns.append(column)
            for _, (array, slot) in terms:
                if not any(array is a and slot == s for a, s in arrays):
                    arrays.append((array, slot))
    place = lambda array, slot: [
        i for i, (a, s) in enumerate(arrays) if a is array and s == slot
    ][0]
    plan = [
        [
            (columns.index(column), [(row, place(*source)) for row, source in terms])
            for column, terms in slots
        ]
        for slots in outs
    ]

    def body(at, base, *refs):
        rows, values = refs[: len(columns)], refs[len(columns) : len(columns) + len(arrays)]
        results = refs[len(columns) + len(arrays) :]
        width = rows[0].shape[1]
        for result, slots in zip(results, plan):
            for slot, (column, terms) in enumerate(slots):
                for start in range(0, width, 256):
                    lanes = slice(start, start + 256)
                    total = None
                    for row, index in terms:
                        term = rows[column][row : row + 1, lanes] * values[index][
                            0, :, lanes
                        ].astype(F32)
                        total = term if total is None else total + term
                    result[slot, :, lanes] = total.astype(BF16)

    length, width = arrays[0][0].shape[1:]
    block = lambda slot, count: ((count, length, width), lambda g, b: (slot, 0, 0))
    ins = [
        (
            weights,
            (
                (weights.shape[0], width),
                lambda g, b, column=column: (0, lax.rem(first_group(b) + column, groups)),
            ),
        )
        for column in columns
    ]
    ins += [(array, block(slot, 1)) for array, slot in arrays]
    results = [
        ((slots_of or len(slots), length, width), BF16, block(at, len(slots))) for slots in outs
    ]
    return call(body, results, ins, base=base, after=after, carry=carry)


def scan_blocks(base, groups, weights, local, local_sent, reverse, beside):
    count = lax.axis_size("seq")

    def swap(block, bits):
        route = [(i, i ^ bits[i % 2]) for i in range(count)]
        return lax.ppermute(block, "seq", route)

    def merge(slot, *plans, **places):
        outs = [[(slot, list(zip(rows, sources)))] for rows, sources in plans]
        return combine(base, groups, weights, outs, **places)

    taken = swap(local_sent, (1, 1))
    chips, first_taken, sent, second_taken = [], [], [], []
    for slot in range(2):
        both = ((local, slot), (taken, slot))
        chip, chip_sent = merge(slot, ((0, 1), both), ((2, 3), both))
        chips.append(chip)
        first_taken.append(swap(chip_sent, (2, 4)))
    after = [beside[0](chips[1])]
    for slot in range(2):
        sources = ((chips[slot], 0), (first_taken[slot], 0))
        (block,) = merge(slot, ((4, 5), sources), after=after)
        sent.append(block)
        second_taken.append(swap(block, (4, 2)))
        if slot == 0:
            after = [beside[1](block)]
    after = beside[2](sent[1])
    carry = []
    for slot in range(2):
        sources = ((first_taken[slot], 0), (second_taken[slot], 0))
        mine, handed = merge(
            slot,
            ((6, 7, 8), (*sources, (taken, slot))),
            ((9, 10, 11), (*sources, (local, slot))),
            after=after[slot],
            slots_of=2,
            at=slot,
            carry=carry,
        )
        carry = [mine, handed]
    return mine, swap(handed, (1, 1))


def gather_blocks(totals, local, reverse):
    table = lax.all_gather(totals, "seq", axis=0, tiled=True)
    blocks = lax.all_gather(local[None], "seq", axis=0, tiled=True)
    own = lax.axis_index("seq")
    order = jnp.arange(table.shape[0], dtype=jnp.int32)
    if reverse:
        inside = (order[None, :] > own) & (order[None, :] < order[:, None])
        selected = order > own
    else:
        inside = (order[None, :] > order[:, None]) & (order[None, :] < own)
        selected = order < own
    exponent = jnp.sum(jnp.where(inside[:, :, None], table[None], 0.0), axis=1)
    factor = jnp.where(selected[:, None], jnp.exp(exponent), 0.0)
    factor = factor.reshape(factor.shape[0], local.shape[0], 1, local.shape[2])
    state = jnp.sum(factor * blocks.astype(F32), axis=0).astype(BF16)
    return state, state


def conv_body(fetch, at, base, x_in, taps, *refs):
    length, width = x_in.shape
    group, groups = at
    if fetch:
        x_all, taps_all, x_out, slope_out, top_out, taps_out, x_mine, taps_mine, ext, sems = refs
        lanes = pl.ds(pl.multiple_of(first_group(base) * width, 128), x_mine.shape[1])
        copies = [
            pltpu.make_async_copy(x_all.at[:, lanes], x_mine, sems.at[0]),
            pltpu.make_async_copy(taps_all.at[:, lanes], taps_mine, sems.at[1]),
        ]

        @pl.when(group == 0)
        def _():
            for copy in copies:
                copy.start()

    else:
        x_out, slope_out, top_out, taps_out, ext = refs
    top_out[...] = x_in[0:16, :]
    taps_out[...] = taps[...]
    ext[0:8, :] = jnp.zeros((8, 128), F32)
    for start in range(0, width, 128):
        lanes = slice(start, start + 128)
        ext[8 : 8 + length, :] = x_in[:, lanes].astype(F32)
        pre = taps[0:1, lanes] * ext[5 : 5 + length, :]
        for k in range(1, 4):
            pre = pre + taps[k : k + 1, lanes] * ext[5 + k : 5 + k + length, :]
        sigma = sigmoid(pre)
        x_out[:, lanes] = (pre * sigma).astype(BF16)
        slope_out[:, lanes] = sigma * (1.0 + pre * (1.0 - sigma))
    if fetch:

        @pl.when(group == groups - 1)
        def _():
            for copy in copies:
                copy.wait()


def state_body(first, at, base, x_low, x_top, x_halo, taps, step_in, cumul_in, *refs):
    length, width = x_low.shape
    if first:
        bc_in, bc_halo, bc_taps, slope_out, x_out, state_out = refs[:6]
        bc_out, bc_slope_out, gram_out, b_turned, ext, bc_ext = refs[6:]

        @pl.when(at[0] == 0)
        def _():
            for j in range(2):
                halo = bc_halo[:, j * 128 : j * 128 + 128].astype(F32)
                bc_ext[5:8, :] = jnp.where(place_bit(base, 5) == 1, 0.0, halo)
                bc_ext[8 : 8 + length, :] = bc_in[j].astype(F32)
                pre = bc_taps[j, 0:1, :] * bc_ext[5 : 5 + length, :]
                for k in range(1, 4):
                    pre = pre + bc_taps[j, k : k + 1, :] * bc_ext[5 + k : 5 + k + length, :]
                sigma = sigmoid(pre)
                bc_out[j] = (pre * sigma).astype(BF16)
                bc_slope_out[j] = sigma * (1.0 + pre * (1.0 - sigma))
            b_turned[...] = bc_out[0].astype(F32).T
            gram_out[...] = jnp.where(
                triangle(length, False), dot_rows(bc_out[1], bc_out[0]), 0.0
            )

    else:
        b_turned, slope_out, x_out, state_out, ext = refs

    top = x_top.shape[0]
    ext[5:8, :] = jnp.where(place_bit(base, 5) == 1, 0.0, x_halo[...].astype(F32))
    ext[8 : 8 + top, :] = x_top[...].astype(F32)
    tail_step = jnp.exp(cumul_in[:, length - 1 :] - cumul_in[...]) * step_in[...]
    for head in range(width // 128):
        lanes = slice(head * 128, head * 128 + 128)
        pre = taps[0:1, lanes] * ext[5 : 5 + top, lanes]
        for k in range(1, 4):
            pre = pre + taps[k : k + 1, lanes] * ext[5 + k : 5 + k + top, lanes]
        sigma = sigmoid(pre)
        x_rows = (pre * sigma).astype(BF16)
        x_out[:, lanes] = x_rows
        slope_out[:, lanes] = sigma * (1.0 + pre * (1.0 - sigma))
        x_head = jnp.concatenate([x_rows, x_low[top:, lanes]], axis=0)
        weighted = (b_turned[...] * tail_step[head : head + 1, :]).astype(BF16)
        state_out[0, :, lanes] = dot(weighted, x_head).astype(BF16)


def inner_body(at, base, gram, step_in, cumul_in, x_in, rows, mixed_out):
    cumul = cumul_in[...]
    cumul_columns = columns_of(cumul)
    for head in range(x_in.shape[1] // 128):
        lanes = slice(head * 128, head * 128 + 128)
        row = cumul[head : head + 1, :]
        decay = jnp.exp(jnp.minimum(cumul_columns[:, head : head + 1] - row, 0.0))
        mixer = (gram[...] * decay * step_in[head : head + 1, :]).astype(BF16)
        x_head = x_in[:, lanes]
        mixed_out[:, lanes] = dot(mixer, x_head) + rows[1:2, lanes] * x_head.astype(F32)


def gate_body(
    at, base, z_in, grad_in, gain, gate_out, gate_slope_out, scaled_out, scaled_gate_out
):
    for start in range(0, z_in.shape[1], 128):
        lanes = slice(start, start + 128)
        z = z_in[:, lanes].astype(F32)
        sigma = sigmoid(z)
        gate = z * sigma
        scaled = grad_in[:, lanes].astype(F32) * gain[:, lanes]
        gate_out[:, lanes] = gate
        gate_slope_out[:, lanes] = sigma * (1.0 + z * (1.0 - sigma))
        scaled_out[:, lanes] = scaled
        scaled_gate_out[:, lanes] = scaled * gate


def lift_body(at, base, bc, step_in, cumul_in, x_in, weighted_x, lifted_out, c_turned):
    @pl.when(at[0] == 0)
    def _():
        c_turned[...] = bc[1].astype(F32).T

    weights = block_weights(step_in[...], cumul_in[...])
    lifted = jnp.exp(cumul_in[...])
    for head in range(x_in.shape[1] // 128):
        lanes = slice(head * 128, head * 128 + 128)
        weight = weights[:, head : head + 1]
        weighted_x[:, lanes] = (weight * x_in[:, lanes].astype(F32)).astype(BF16)
        lifted_out[:, lanes] = (c_turned[...] * lifted[head : head + 1, :]).astype(BF16)


def mix_body(
    at, base, mixed_in, c_rows, cumul_in, state, gate_in, scaled_in, sums_in, *outs
):
    mixed_out, sums_out, squares, products = outs
    group, groups = at

    @pl.when(group == 0)
    def _():
        squares[...] = jnp.zeros_like(squares)
        products[...] = jnp.zeros_like(products)

    carried = dot(c_rows[0], state[0])
    lifted = jnp.exp(columns_of(cumul_in[...]))
    square, product = squares[...], products[...]
    for head in range(mixed_in.shape[1] // 128):
        lanes = slice(head * 128, head * 128 + 128)
        mixed = mixed_in[:, lanes] + lifted[:, head : head + 1] * carried[:, lanes]
        mixed_out[:, lanes] = mixed
        gated = mixed * gate_in[:, lanes]
        square = square + gated * gated
        product = product + mixed * scaled_in[:, lanes]
    squares[...] = square
    products[...] = product

    @pl.when(group == groups - 1)
    def _():
        sums_out[...] = sums_in[...]
        sums_out[0:1, :] += jnp.sum(squares[...].T, axis=0, keepdims=True)
        sums_out[1:2, :] += jnp.sum(products[...].T, axis=0, keepdims=True)


def square_body(at, base, mixed_in, gate_in, squared):
    for start in range(0, mixed_in.shape[1], 128):
        lanes = slice(start, start + 128)
        gate = gate_in[:, lanes]
        squared[:, lanes] = mixed_in[:, lanes] * gate * gate


def norm_scales(at, inner, sums, alpha, beta):
    @pl.when(at[0] == 0)
    def _():
        total = sums[0][...]
        for part in sums[1:]:
            total = total + part[...]
        inv_rms = lax.rsqrt(total[0:1, :] / inner + EPS)
        mean_dot = inv_rms * total[1:2, :] / inner
        alpha[...] = jnp.broadcast_to(inv_rms, alpha.shape).T
        beta[...] = jnp.broadcast_to(inv_rms * inv_rms * mean_dot, beta.shape).T


def grad_mixed_body(inner, parts, at, base, *refs):
    sums = refs[:parts]
    squared, scaled_in, lifted_c, grad_mixed, state_out, alpha, beta = refs[parts:]
    norm_scales(at, inner, sums, alpha, beta)
    for start in range(0, squared.shape[1], 128):
        lanes = slice(start, start + 128)
        low = (alpha[...] * scaled_in[:, lanes] - beta[...] * squared[:, lanes]).astype(BF16)
        grad_mixed[:, lanes] = low
        state_out[0, :, lanes] = dot(lifted_c[:, lanes], low).astype(BF16)


def grad_z_body(inner, parts, at, base, *refs):
    sums = refs[:parts]
    mixed_in, gate_in, gate_slope_in, scaled_in, grad_z, alpha, beta = refs[parts:]
    norm_scales(at, inner, sums, alpha, beta)
    for start in range(0, mixed_in.shape[1], 128):
        lanes = slice(start, start + 128)
        mixed = mixed_in[:, lanes]
        grad_gated = alpha[...] * scaled_in[:, lanes] - beta[...] * (mixed * gate_in[:, lanes])
        grad_z[:, lanes] = (grad_gated * (mixed * gate_slope_in[:, lanes])).astype(BF16)


def inner_back_body(
    last,
    at,
    base,
    gram,
    bc,
    step_in,
    cumul_in,
    x_in,
    grad_in,
    state_in,
    rows,
    sums_in,
    grad_x,
    q_out,
    r_out,
    bc_out,
    z_sum,
    c_sum,
):
    group, groups = at
    length = x_in.shape[0]

    @pl.when(group == 0)
    def _():
        z_sum[...] = sums_in[0]
        c_sum[...] = sums_in[1]

    cumul = cumul_in[...]
    cumul_columns = columns_of(cumul)
    lifted = jnp.exp(cumul_columns)
    state = state_in[0]
    c_rows = bc[1].astype(F32)
    lane = lax.broadcasted_iota(jnp.int32, (length, 128), 1)
    q_columns = jnp.zeros((length, 128), F32)
    for head in range(x_in.shape[1] // 128):
        lanes = slice(head * 128, head * 128 + 128)
        step = step_in[head : head + 1, :]
        decay = jnp.exp(
            jnp.minimum(cumul_columns[:, head : head + 1] - cumul[head : head + 1, :], 0.0)
        )
        gram_decay = gram[...] * decay
        mixer = (gram_decay * step).astype(BF16)
        x_head, grad_head = x_in[:, lanes], grad_in[:, lanes]
        product = dot_rows(grad_head, x_head)
        z_sum[...] += product * decay * step
        gram_grad = product * gram_decay
        r_out[head : head + 1, :] = jnp.sum(gram_grad, axis=0, keepdims=True)
        handed = lifted[:, head : head + 1] * dot_rows(grad_head, state[:, lanes])
        c_sum[...] += handed
        q = jnp.sum(gram_grad * step + c_rows * handed, axis=1, keepdims=True)
        q_columns = jnp.where(lane == head, q, q_columns)
        grad_x[:, lanes] = dot_columns(mixer, grad_head) + rows[1:2, lanes] * grad_head.astype(F32)
    q_out[...] = q_columns.T[:GROUP, :]

    @pl.when(group == groups - 1)
    def _():
        if last:
            summed = jnp.where(triangle(length, False), z_sum[...], 0.0)
            bc_out[0] = dot_split(summed.T, bc[1])
            bc_out[1] = c_sum[...] + dot_split(summed, bc[0])
        else:
            bc_out[0] = z_sum[...]
            bc_out[1] = c_sum[...]


def block_weights(step, cumul):
    return columns_of(jnp.exp(cumul[:, cumul.shape[1] - 1 :] - cumul) * step)


def rim_body(last, at, base, bc, step_in, cumul_in, weighted_x, partial, slope, out_in, *refs):
    group, groups = at
    width = weighted_x.shape[1]
    if last:
        rows_before, b_before, bc_partial, bc_slope, rim_low, bc_out, b_sum, rim_out = refs
    else:
        rim_out, b_sum = refs

    @pl.when(group == 0)
    def _():
        b_sum[...] = b_before[...] if last else jnp.zeros_like(b_sum)

    out_low = out_in[0]
    b_sum[...] += dot_rows(weighted_x[...], out_low)
    weights = block_weights(step_in[...], cumul_in[...])[0:8, :]
    returned = dot(bc[0][0:16, :], out_low)[0:8, :]
    start = group
    if last:
        count = rim_out.shape[1] // width
        start = lax.rem(group + count - groups + first_group(base), count)
    for head in range(width // 128):
        lanes = slice(head * 128, head * 128 + 128)
        weight = weights[:, head : head + 1]
        rows = (partial[0:8, lanes] + weight * returned[:, lanes]) * slope[0:8, lanes]
        place = pl.multiple_of(jnp.int32(start) * width + head * 128, 128)
        rim_out[:, pl.ds(place, 128)] = rows[0:3, :]

    if last:

        @pl.when(group == groups - 1)
        def _():
            before = rows_before.shape[1]
            if before < rim_out.shape[1] - 256:
                place = pl.multiple_of(first_group(base) * width, 128)
                rim_out[:, pl.ds(place, before)] = rows_before[...]
            bc_out[0] = (b_sum[...] + bc_partial[0]) * bc_slope[0]
            bc_out[1] = bc_partial[1] * bc_slope[1]
            for j in range(2):
                lanes = rim_out.shape[1] - 256 + 128 * j
                rim_out[:, lanes : lanes + 128] = bc_out[j, 0:3, :]
            rim_low[...] = rim_out[...].astype(BF16)


def grad_dt_body(
    at,
    base,
    bc,
    rate,
    dt_slope,
    step_in,
    cumul_in,
    q_in,
    r_in,
    x_in,
    state_in,
    out_in,
    grad_dt,
    selector,
    products,
):
    heads, length = q_in.shape
    width = state_in.shape[2]
    row = lax.broadcasted_iota(jnp.int32, selector.shape, 0)
    lane = lax.broadcasted_iota(jnp.int32, selector.shape, 1)
    selector[...] = (lax.shift_right_logical(row, 7) == lane).astype(BF16)
    row = lax.broadcasted_iota(jnp.int32, (16, width), 0)
    lane = lax.shift_right_logical(lax.broadcasted_iota(jnp.int32, (16, width), 1), 7)
    dots = jnp.zeros((16, 1), F32)
    for group in range(state_in.shape[0]):
        out_low = out_in[group]
        returned = dot(bc[0], out_low)
        for start in range(0, width, 128):
            lanes = slice(start, start + 128)
            place = slice(group * width + start, group * width + start + 128)
            products[:, place] = (x_in[:, place].astype(F32) * returned[:, lanes]).astype(BF16)
        summed = dot(jnp.ones((16, length), BF16), state_in[group] * out_low)
        own = row - GROUP * group == lane
        dots = dots + jnp.sum(jnp.where(own, summed, 0.0), axis=1, keepdims=True)
    inner_b = dot(products[...], selector[...]).T[:heads, :]
    cumul, step = cumul_in[...], step_in[...]
    w = jnp.exp(cumul[:, length - 1 :] - cumul) * inner_b
    q, r = q_in[...], r_in[...]
    inside = jnp.sum(step * w, axis=1, keepdims=True)
    end = inside + jnp.exp(cumul[:, length - 1 :]) * dots[:heads]
    last = lax.broadcasted_iota(jnp.int32, (heads, length), 1) == length - 1
    grad_cumul = q - step * (r + w) + jnp.where(last, end, 0.0)
    grad_log = dot_split(grad_cumul, triangle(length, False).astype(BF16))
    grad_dt[...] = (r + w + rate[...] * grad_log) * dt_slope[...]


def grad_x_body(
    at,
    base,
    bc,
    step_in,
    cumul_in,
    partial,
    slope,
    taps,
    halo,
    out_in,
    grad_x,
    ext,
):
    length, width = partial.shape
    weights = block_weights(step_in[...], cumul_in[...])
    returned = dot(bc[0], out_in[0])
    rim = jnp.where(place_bit(base, 6) == 1, 0.0, halo[...].astype(F32))
    for head in range(width // 128):
        lanes = slice(head * 128, head * 128 + 128)
        weight = weights[:, head : head + 1]
        ext[0:length, :] = (partial[:, lanes] + weight * returned[:, lanes]) * slope[:, lanes]
        ext[length : length + 3, :] = rim[:, lanes]
        total = taps[0:1, lanes] * ext[3 : 3 + length, :]
        for k in range(1, 4):
            total = total + taps[k : k + 1, lanes] * ext[3 - k : 3 - k + length, :]
        grad_x[:, lanes] = total.astype(BF16)


def bc_back_body(at, place, grad_pre, halo, taps, kept, sent, ext, total):
    length, half = grad_pre.shape[1], kept.shape[1]
    rims = jnp.where(place_bit(place, 6) == 1, 0.0, halo[...].astype(F32))
    for j in range(2):
        ext[0:length, :] = grad_pre[j]
        ext[length : length + 3, :] = rims[:, 128 * j : 128 * j + 128]
        summed = taps[j, 0:1, :] * ext[3 : 3 + length, :]
        for k in range(1, 4):
            summed = summed + taps[j, k : k + 1, :] * ext[3 - k : 3 - k + length, :]
        total[...] = summed
        kept[j] = total[pl.ds(pl.multiple_of(place_bit(place, 3) * half, half), half), :]
        sent[j] = total[pl.ds(pl.multiple_of((1 - place_bit(place, 3)) * half, half), half), :].astype(BF16)


def bc_half_body(at, place, mine, taken, kept, sent, total):
    half = kept.shape[1]
    for j in range(2):
        total[...] = mine[j] + taken[j].astype(F32)
        kept[j] = total[pl.ds(pl.multiple_of(place_bit(place, 4) * half, half), half), :]
        sent[j] = total[pl.ds(pl.multiple_of((1 - place_bit(place, 4)) * half, half), half), :].astype(BF16)


def bc_last_body(at, _, mine, taken, out):
    out[...] = (mine[...] + taken[...].astype(F32)).astype(BF16)


def conv_back(extended, weights):
    length = extended.shape[-2] - 3
    summed = weights[..., 0, :][..., None, :] * extended[..., 3 : 3 + length, :]
    for k in range(1, 4):
        summed = (
            summed
            + weights[..., k, :][..., None, :] * extended[..., 3 - k : 3 - k + length, :]
        )
    return summed


def shards(
    x_input,
    z_input,
    bc_input,
    dt_raw,
    dt_bias,
    a_log,
    d_skip,
    conv_x,
    convolution_bc_taps,
    rescale_factor,
    grad_out,
):
    length, channels = x_input.shape
    heads = dt_raw.shape[0]
    groups = heads // GROUP
    width = GROUP * 128
    count, parts = lax.axis_size("seq"), lax.axis_size("head")
    inner = channels * parts
    own = lax.axis_index("seq")
    split = count == 8 and groups == 4
    own_half = groups // 2 if split else groups
    bit = lambda value, place: lax.shift_right_logical(value, place) & 1
    along_head = lax.axis_index("head")
    base = bit(own, 0) * own_half if split else own * 0
    ends = (own == 0).astype(jnp.int32), (own == count - 1).astype(jnp.int32)
    for place, value in enumerate(
        (bit(own, 2), bit(own, 1), bit(own, 0), bit(along_head, 1), bit(along_head, 0), *ends)
    ):
        base = base | lax.shift_left(value, 8 + place)
    base = base.astype(jnp.int32)[None]

    whole = lambda *shape: ((shape, lambda g, b: (0,) * len(shape)),)
    wide_at = lambda off: (Groups("wide", (length, width), off, groups),)
    rows_at = lambda off: (Groups("heads", (GROUP, length), off, groups),)
    lanes_at = lambda n, off: (Groups("wide", (n, width), off, groups),)
    slot = (Groups("slots", (1, length, width), 0, groups),)
    full = lambda array: (array,) + whole(*array.shape)
    half_width = own_half * width
    half_heads = own_half * GROUP
    half = lambda n: (Groups("half", (n, width), 0, groups),)
    half_rows = (Groups("half heads", (GROUP, length), 0, groups),)
    window_at = lambda n, off: (Groups("window", (n, width), off, groups),)
    halves = [own_half, 0] if split else [0]
    rest = halves[0]

    gain = rescale_factor[None, :]
    f32 = lambda *shape: (shape, F32)
    low = lambda *shape: (shape, BF16)

    step, cumul, rate, dt_slope, rows, rim, bc_rows, bc_taps = call(
        steps_body,
        [
            f32(heads, length) + whole(heads, length),
            f32(heads, length) + whole(heads, length),
            f32(heads, length) + whole(heads, length),
            f32(heads, length) + whole(heads, length),
            f32(2, channels) + whole(2, channels),
            low(3, channels + 256) + whole(3, channels + 256),
            low(2, length, 128) + whole(2, length, 128),
            f32(2, 4, 128) + whole(2, 4, 128),
        ],
        [
            full(in_hbm(dt_raw)),
            full(in_hbm(dt_bias[None, :])),
            full(in_hbm(a_log[None, :])),
            full(in_hbm(d_skip[None, :])),
            (in_hbm(x_input), ((16, channels), lambda g, b: (length // 16 - 1, 0))),
            full(in_hbm(bc_input)),
            full(in_hbm(convolution_bc_taps)),
        ],
        base=base,
    )
    rim_sent = rim
    rim = lax.ppermute(rim, "seq", [(i, (i + 1) % count) for i in range(count)])
    if split:
        swap = lambda block, bit: lax.ppermute(
            block, "seq", [(i, i ^ bit) for i in range(count)]
        )
        total = rows[0:1]
        total_core, total_across = swap(total, 1), swap(total, 2)
        total_beyond = swap(total_across, 1)
        table = f32(16, channels) + whole(16, channels)
        ahead, behind = call(
            weights_body,
            [table, table],
            [full(rows), full(total_core), full(total_across), full(total_beyond)],
            base=base,
            )

    def passed(locals_, reverse, beside):
        if split:
            local_sent, local = locals_[rest], locals_[0]
            weights = behind if reverse else ahead
            return scan_blocks(base, groups, weights, local, local_sent, reverse, beside)
        local = locals_[0]
        for work in beside:
            work(local)
        return gather_blocks(rows[0:1], local, reverse)

    x_low, slope, local = {}, {}, {}
    ready = rim_sent
    for off in halves:
        outs = [
            low(length, half_width) + half(length),
            f32(length, half_width) + half(length),
            low(16, half_width) + half(16),
            f32(4, half_width) + half(4),
        ]
        if off == rest:
            x_all, taps_all = in_hbm(x_input), in_hbm(conv_x)
            ins = [(x_all,) + wide_at(off), (taps_all,) + lanes_at(4, off)]
            scratch = [pltpu.VMEM((length + 8, 128), F32)]
            if split:
                ins += [(x_all, None), (taps_all, None)]
                outs += [
                    low(length, half_width) + whole(length, half_width),
                    f32(4, half_width) + whole(4, half_width),
                ]
                scratch += [pltpu.SemaphoreType.DMA((2,))]
            x_low[off], slope[off], x_top, taps, *fetched = call(
                functools.partial(conv_body, split),
                outs,
                ins,
                base=base,
                grid=own_half,
                scratch=scratch,
                after=[ready],
            )
        else:
            x_low[off], slope[off], x_top, taps = call(
                functools.partial(conv_body, False),
                outs,
                [(fetched[0],) + half(length), (fetched[1],) + half(4)],
                base=base,
                loop=own_half,
                scratch=[pltpu.VMEM((length + 8, 128), F32)],
                after=[ready],
            )
        first = off == rest
        top = (Groups("top", (16, width), 0, groups),)
        ins = [
            (x_low[off],) + half(length),
            (x_top,) + half(16),
            (rim,) + lanes_at(3, off),
            (taps,) + half(4),
            (step,) + rows_at(off),
            (cumul,) + rows_at(off),
        ]
        outs = [
            f32(length, half_width) + top,
            low(length, half_width) + top,
            low(own_half, length, width) + slot,
        ]
        scratch = [pltpu.VMEM((24, width), F32)]
        if first:
            ins += [
                full(bc_rows),
                (rim, ((3, 256), lambda g, b: (0, channels // 256))),
                full(bc_taps),
            ]
            outs += [
                low(2, length, 128) + whole(2, length, 128),
                f32(2, length, 128) + whole(2, length, 128),
                f32(length, length) + whole(length, length),
                f32(128, length) + whole(128, length),
            ]
            scratch += [pltpu.VMEM((length + 8, 128), F32)]
        else:
            ins += [full(b_turned)]
        result = call(
            functools.partial(state_body, first),
            outs,
            ins,
            base=base,
            loop=own_half,
            scratch=scratch,
            carry=[slope[off]],
            place={0: 1},
            flops=2 * length * 128 * half_width,
        )
        if first:
            bc, bc_slope, gram, b_turned = result[3:]
        slope[off], x_low[off], local[off] = result[:3]
        ready = local[off]

    inside, gate, gate_slope, scaled, scaled_gate = {}, {}, {}, {}, {}

    def mix_inside(off, ready):
        inside[off], token = call(
            inner_body,
            [f32(length, half_width) + half(length)],
            [
                full(gram),
                (step,) + rows_at(off),
                (cumul,) + rows_at(off),
                (x_low[off],) + half(length),
                (rows,) + lanes_at(2, off),
            ],
            base=base,
            loop=own_half,
            after=[ready],
            token=True,
            flops=2 * length * 128 * half_width,
        )
        return token

    def gates(off, ready):
        gate[off], gate_slope[off], scaled[off], scaled_gate[off], token = call(
            gate_body,
            [f32(length, half_width) + half(length)] * 4,
            [
                (z_input,) + wide_at(off),
                (grad_out,) + wide_at(off),
                (gain,) + lanes_at(1, off),
            ],
            base=base,
            loop=own_half,
            after=[ready],
            token=True,
        )
        return token

    def mix_second(ready):
        return mix_inside(rest, ready) if split else ready

    def mix_third(ready):
        return [], [gates(off, ready) for off in reversed(halves)]

    states = passed(local, False, (functools.partial(mix_inside, 0), mix_second, mix_third))
    states = dict(zip((0, rest), states))
    mixed, sums = {}, jnp.zeros((8, length), F32)
    two_scales = [pltpu.VMEM((length, 128), F32), pltpu.VMEM((length, 128), F32)]
    for off in reversed(halves):
        mixed[off], sums = call(
            mix_body,
            [f32(length, half_width) + half(length), f32(8, length) + whole(8, length)],
            [
                (inside[off],) + half(length),
                (bc, ((1, length, 128), lambda g, b: (1, 0, 0))),
                (cumul,) + rows_at(off),
                (states[off],) + slot,
                (gate[off],) + half(length),
                (scaled_gate[off],) + half(length),
                full(sums),
            ],
            base=base,
            loop=own_half,
            scratch=two_scales,
            flops=2 * length * 128 * half_width,
        )
    turn_head = lambda block, bit: lax.ppermute(
        block, "head", [(i, i ^ bit) for i in range(parts)]
    )
    weighted_x, lifted_c, squared = {}, {}, {}
    for off in halves:
        weighted_x[off], lifted_c[off] = call(
            lift_body,
            [low(length, half_width) + half(length), low(length, half_width) + half(length)],
            [
                full(bc),
                (step,) + rows_at(off),
                (cumul,) + rows_at(off),
                (x_low[off],) + half(length),
            ],
            base=base,
            loop=own_half,
            scratch=[pltpu.VMEM((128, length), F32)],
            after=[sums],
        )
        (squared[off],) = call(
            square_body,
            [f32(length, half_width) + half(length)],
            [(mixed[off],) + half(length), (gate[off],) + half(length)],
            base=base,
            loop=own_half,
        )
    if parts == 4:
        sums = sums + turn_head(sums, 1)
        all_sums = [sums, turn_head(sums, 2)]
    else:
        all_sums = [lax.psum(sums, "head")]
    grad_mixed, local_back = {}, {}
    for off in halves:
        grad_mixed[off], local_back[off] = call(
            functools.partial(grad_mixed_body, inner, len(all_sums)),
            [low(length, half_width) + half(length), low(own_half, length, width) + slot],
            [full(part) for part in all_sums]
            + [
                (squared[off],) + half(length),
                (scaled_gate[off],) + half(length),
                (lifted_c[off],) + half(length),
            ],
            base=base,
            loop=own_half,
            scratch=two_scales,
            flops=2 * length * 128 * half_width,
        )

    partial, q_rows, r_rows = {}, {}, {}
    carried = {"sums": jnp.zeros((2, length, 128), F32), "z": [], "dt": [], "x": []}

    def back_inside(off, ready):
        partial[off], q_rows[off], r_rows[off], carried["sums"], token = call(
            functools.partial(inner_back_body, off == rest),
            [
                f32(length, half_width) + half(length),
                f32(half_heads, length) + half_rows,
                f32(half_heads, length) + half_rows,
                f32(2, length, 128) + whole(2, length, 128),
            ],
            [
                full(gram),
                full(bc),
                (step,) + rows_at(off),
                (cumul,) + rows_at(off),
                (x_low[off],) + half(length),
                (grad_mixed[off],) + half(length),
                (states[off],) + slot,
                (rows,) + lanes_at(2, off),
                full(carried["sums"]),
            ],
            base=base,
            loop=own_half,
            scratch=[pltpu.VMEM((length, length), F32), pltpu.VMEM((length, 128), F32)],
            after=[ready],
            token=True,
            flops=6 * length * 128 * half_width,
        )
        return token

    def back_gates(off, ready):
        grad_z, token = call(
            functools.partial(grad_z_body, inner, len(all_sums)),
            [low(length, channels) + window_at(length, off)],
            [full(part) for part in all_sums]
            + [
                (mixed[off],) + half(length),
                (gate[off],) + half(length),
                (gate_slope[off],) + half(length),
                (scaled[off],) + half(length),
            ],
            base=base,
            loop=own_half,
            scratch=two_scales,
            carry=carried["z"],
            after=[ready],
            token=True,
        )
        carried["z"] = [grad_z]
        carried["z_token"] = token
        return token

    def back_second(ready):
        return back_gates(0, ready)

    def back_third(ready):
        if not split:
            return [], []
        token = back_inside(rest, ready)
        return [token], [back_gates(rest, token)]

    backs = passed(local_back, True, (functools.partial(back_inside, 0), back_second, back_third))
    backs = dict(zip((0, rest), backs))

    def make_grad_dt(off, after):
        table = (Groups("heads", (half_heads, length), off, groups, own_half),)
        window = (Groups("window heads", (half_heads, length), off, groups, own_half),)
        grad_dt, token = call(
            grad_dt_body,
            [f32(heads, length) + window],
            [
                full(bc),
                (rate,) + table,
                (dt_slope,) + table,
                (step,) + table,
                (cumul,) + table,
                full(q_rows[off]),
                full(r_rows[off]),
                full(x_low[off]),
                full(states[off]),
                full(backs[off]),
            ],
            base=base,
            scratch=[pltpu.VMEM((half_width, 128), BF16), pltpu.VMEM((length, half_width), BF16)],
            carry=carried["dt"],
            after=after,
            token=True,
            flops=4 * length * 128 * half_width,
        )
        carried["dt"] = [grad_dt]
        return token

    def make_grad_x(off, after):
        grad_x, token = call(
            grad_x_body,
            [low(length, channels) + window_at(length, off)],
            [
                full(bc),
                (step,) + rows_at(off),
                (cumul,) + rows_at(off),
                (partial[off],) + half(length),
                (slope[off],) + half(length),
                (conv_x,) + lanes_at(4, off),
                (rim_back,) + lanes_at(3, off),
                (backs[off],) + slot,
            ],
            base=base,
            loop=own_half,
            scratch=[pltpu.VMEM((length + 8, 128), F32)],
            carry=carried["x"],
            after=after,
            token=True,
            flops=2 * length * 128 * half_width,
        )
        carried["x"] = [grad_x]
        return token

    def make_rim(off, before, after):
        last = off == rest
        if last:
            outs = [
                low(3, channels + 256) + whole(3, channels + 256),
                f32(2, length, 128) + whole(2, length, 128),
            ]
            scratch = [pltpu.VMEM((length, 128), F32), pltpu.VMEM((3, channels + 256), F32)]
        else:
            scratch = []
            outs = [f32(3, half_width) + whole(3, half_width), f32(length, 128) + whole(length, 128)]
        return call(
            functools.partial(rim_body, last),
            outs,
            [
                full(bc),
                (step,) + rows_at(off),
                (cumul,) + rows_at(off),
                (weighted_x[off],) + half(length),
                (partial[off],) + half(length),
                (slope[off],) + half(length),
                (backs[off],) + slot,
            ]
            + [full(array) for array in before],
            base=base,
            loop=own_half,
            scratch=scratch,
            after=after,
            flops=2 * length * 128 * half_width,
        )

    if split:
        before = make_rim(0, [], [])
    else:
        before = [jnp.zeros((3, channels), F32), jnp.zeros((length, 128), F32)]
    rim_back, grad_bc_pre = make_rim(rest, [*before, carried["sums"], bc_slope], [])
    rim_back = lax.ppermute(rim_back, "seq", [(i, (i - 1) % count) for i in range(count)])
    dt_token = make_grad_dt(rest, [grad_bc_pre])
    if parts == 4:
        piece = lambda rows: f32(2, rows, 128) + whole(2, rows, 128)
        piece_low = lambda rows: low(2, rows, 128) + whole(2, rows, 128)
        kept, sent = call(
            bc_back_body,
            [piece(length // 2), piece_low(length // 2)],
            [
                full(grad_bc_pre),
                (rim_back, ((3, 256), lambda g, b: (0, channels // 256))),
                full(bc_taps),
            ],
            base=base,
            scratch=[pltpu.VMEM((length + 8, 128), F32), pltpu.VMEM((length, 128), F32)],
            after=[dt_token],
        )
        taken = turn_head(sent, 2)
        x_tokens = [make_grad_x(0, [sent])]
        if split:
            x_tokens = [make_grad_dt(0, x_tokens)]
        kept, sent = call(
            bc_half_body,
            [piece(length // 4), piece_low(length // 4)],
            [full(kept), full(taken)],
            base=base,
            scratch=[pltpu.VMEM((length // 2, 128), F32)],
            after=x_tokens,
        )
        taken = turn_head(sent, 1)
        x_tokens = [make_grad_x(rest, [sent])] if split else []
        (grad_bc,) = call(
            bc_last_body,
            [piece_low(length // 4)],
            [full(kept), full(taken)],
            base=base,
            after=x_tokens,
        )
    else:
        if split:
            make_grad_dt(0, [])
        for off in halves:
            make_grad_x(off, [])
        bc_halo = jnp.moveaxis(rim_back[:, channels:].reshape(3, 2, 128), 1, 0)
        bc_halo = jnp.where(own == count - 1, 0.0, bc_halo.astype(F32))
        bc_sum = conv_back(jnp.concatenate([grad_bc_pre, bc_halo], axis=1), convolution_bc_taps)
        share = length // parts
        bc_sum = lax.psum(bc_sum, "head")
        grad_bc = lax.dynamic_slice_in_dim(bc_sum, along_head * share, share, 1).astype(BF16)
    return (carried["x"][0], carried["z"][0], grad_bc, carried["dt"][0])


def solution(mesh):
    return jax.shard_map(
        shards,
        mesh=mesh,
        in_specs=(
            P("seq", "head"),
            P("seq", "head"),
            P(None, "seq", None),
            P("head", "seq"),
            P("head"),
            P("head"),
            P("head"),
            P(None, "head"),
            P(),
            P("head"),
            P("seq", "head"),
        ),
        out_specs=(
            P("seq", "head"),
            P("seq", "head"),
            P(None, ("seq", "head"), None),
            P("head", "seq"),
        ),
        check_vma=False,
    )
```

```python
import functools

import jax
import jax.numpy as jnp
from jax import lax
from jax.experimental import pallas as pl
from jax.experimental.pallas import tpu as pltpu
from jax.sharding import PartitionSpec as P

EPS = 1e-05
GROUP = 8
F32 = jnp.float32
BF16 = jnp.bfloat16
VMEM_BYTES = 16 * 2**20


def sigmoid(value):
    return 0.5 + 0.5 * jnp.tanh(0.5 * value)


def dot(a, b):
    return jnp.dot(a, b, preferred_element_type=F32)


def dot_split(a, b):
    high = a.astype(BF16)
    rest = a - high.astype(F32)
    middle = rest.astype(BF16)
    low = (rest - middle.astype(F32)).astype(BF16)
    return dot(high, b) + (dot(middle, b) + dot(low, b))


def dot_rows(a, b):
    return lax.dot_general(a, b, (((1,), (1,)), ((), ())), preferred_element_type=F32)


def dot_columns(a, b):
    return lax.dot_general(a, b, (((0,), (0,)), ((), ())), preferred_element_type=F32)


def triangle(length, upper):
    first = lax.broadcasted_iota(jnp.int32, (length, length), 0)
    second = lax.broadcasted_iota(jnp.int32, (length, length), 1)
    return first <= second if upper else first >= second


def columns_of(rows):
    return rows.T


class Groups:
    def __init__(self, kind, block, off, groups, size=1):
        self.kind, self.block, self.off, self.groups = kind, block, off, groups
        self.size = size
        self.by_rows = kind.endswith("heads")

    def turn(self, group, base):
        first = self.off + first_group(base)
        return lax.rem(group * self.size + first, self.groups) // self.size

    def place(self, index):
        return (index, 0) if self.by_rows else (0, index)

    def spec(self):
        if self.kind == "slots":
            return pl.BlockSpec(self.block, lambda g, b: (g, 0, 0))
        if self.kind.startswith("half"):
            return pl.BlockSpec(self.block, lambda g, b: self.place(g))
        return pl.BlockSpec(self.block, lambda g, b: self.place(self.turn(g, b)))

    def whole(self, shape, count):
        if self.kind.startswith("window"):
            block = list(self.block)
            block[0 if self.by_rows else 1] *= count
            return pl.BlockSpec(
                tuple(block), lambda g, b: self.place(self.turn(0, b) // count)
            )
        if self.kind == "top":
            shape = (self.block[0], count * self.block[1])
        return pl.BlockSpec(shape, lambda g, b: (0,) * len(shape))

    def view(self, ref, group, base):
        if self.kind == "slots":
            return ref.at[pl.ds(group, 1)]
        if self.kind in ("wide", "heads"):
            group = self.turn(group, base)
        size = self.block[0 if self.by_rows else 1]
        span = pl.ds(pl.multiple_of(jnp.int32(group) * size, size), size)
        return ref.at[span] if self.by_rows else ref.at[:, span]


def call(
    body,
    outs,
    ins,
    *,
    base,
    grid=1,
    loop=1,
    scratch=(),
    after=(),
    carry=(),
    place=None,
    token=False,
    flops=0,
):
    aliases = {1 + len(ins) + len(after) + i: i for i in range(len(carry))}
    for read, written in (place or {}).items():
        aliases[1 + read] = written
    after = list(after) + list(carry)
    outs = list(outs)
    if token:
        outs.append(((8, 128), F32, ((8, 128), lambda *_: (0, 0))))

    def spec(shape, block):
        if block is None:
            return pl.BlockSpec(memory_space=pl.ANY)
        if not isinstance(block, Groups):
            return pl.BlockSpec(*block)
        return block.whole(shape, loop) if grid == 1 else block.spec()

    in_specs = [spec(array.shape, block) for array, block in ins]
    in_specs += [pl.BlockSpec(memory_space=pl.ANY) for _ in after]
    out_specs = [spec(shape, block) for shape, _, block in outs]
    out_shape = [jax.ShapeDtypeStruct(shape, dtype) for shape, dtype, _ in outs]
    arrays = [array for array, _ in ins]
    moved = sum(a.size * a.dtype.itemsize for a in arrays + out_shape)
    blocks = [block for _, block in ins] + [block for _, _, block in outs]

    def ordered(where, *refs):
        taken, rest = refs[: len(ins)], refs[len(ins) + len(after) :]
        results, extra = rest[: len(outs)], rest[len(outs) :]
        if token:
            results[-1][...] = jnp.zeros((8, 128), F32)

        def step(group, _):
            views = [
                block.view(ref, group, where) if isinstance(block, Groups) else ref
                for ref, block in zip(taken + results, blocks)
            ]
            if token:
                views = views[:-1]
            body((group, loop), where, *views, *extra)
            return 0

        if grid > 1:
            views = taken + (results[:-1] if token else results)
            body((pl.program_id(0), grid), where, *views, *extra)
        elif loop > 1:
            lax.fori_loop(0, loop, step, 0)
        else:
            step(0, 0)

    return pl.pallas_call(
        ordered,
        out_shape=out_shape,
        grid_spec=pltpu.PrefetchScalarGridSpec(
            num_scalar_prefetch=1,
            grid=(grid,),
            in_specs=in_specs,
            out_specs=out_specs,
            scratch_shapes=list(scratch),
        ),
        input_output_aliases=aliases,
        cost_estimate=pl.CostEstimate(flops=flops, bytes_accessed=moved, transcendentals=0),
        compiler_params=pltpu.CompilerParams(vmem_limit_bytes=VMEM_BYTES),
    )(base, *arrays, *after)


def in_hbm(array):
    return pltpu.with_memory_space_constraint(array, pltpu.HBM)


def column_of(row):
    count = row.shape[1]
    first = lax.broadcasted_iota(jnp.int32, (count, count), 0)
    second = lax.broadcasted_iota(jnp.int32, (count, count), 1)
    return jnp.sum(jnp.where(first == second, row, 0.0), axis=1, keepdims=True)


def steps_body(
    at,
    base,
    raw,
    bias,
    log_rate,
    skip,
    x_tail,
    bc_in,
    bc_taps,
    step_out,
    cumul_out,
    rate_out,
    slope_out,
    rows_out,
    rim_out,
    bc_in_out,
    bc_taps_out,
):
    bc_in_out[...] = bc_in[...]
    bc_taps_out[...] = bc_taps[...]
    heads, length = raw.shape
    channels = x_tail.shape[1]
    rim_out[:, 0:channels] = x_tail[...].astype(F32)[13:16, :].astype(BF16)
    for j in range(2):
        start = channels + 128 * j
        rim_out[:, start : start + 128] = bc_in[j, length - 16 :].astype(F32)[13:16, :].astype(BF16)
    shifted = raw[...] + column_of(bias[...])
    step = jnp.maximum(shifted, 0.0) + jnp.log1p(jnp.exp(-jnp.abs(shifted)))
    rate = jnp.broadcast_to(-jnp.exp(column_of(log_rate[...])), step.shape)
    cumul = dot_split(rate * step, triangle(length, True).astype(BF16))
    step_out[...] = step
    cumul_out[...] = cumul
    rate_out[...] = rate
    slope_out[...] = sigmoid(shifted)
    skips = column_of(skip[...])
    for head in range(heads):
        lanes = slice(head * 128, head * 128 + 128)
        rows_out[0:1, lanes] = jnp.broadcast_to(cumul[head : head + 1, length - 1 :], (1, 128))
        rows_out[1:2, lanes] = jnp.broadcast_to(skips[head : head + 1, :], (1, 128))


def pick(test, yes, no):
    return jnp.where(test, yes, no)


def first_group(place):
    return place[0] & 255


def place_bit(place, index):
    return lax.shift_right_logical(place[0], 8 + index) & 1


def weights_body(at, place, own, core, across, beyond, *outs):
    t0, t1 = own[0:1, :], core[...]
    e0, e1, own_chip, ex = jnp.exp(t0), jnp.exp(t1), jnp.exp(t0 + t1), jnp.exp(across[...] + beyond[...])
    one = jnp.ones_like(e0)
    zero = jnp.zeros_like(e0)
    bits = [place_bit(place, i) for i in range(3)]
    x_first = bits[2] == 0
    for out, reverse in zip(outs, (False, True)):
        y, x, c = ((1 - bit if reverse else bit) == 1 for bit in bits)
        either = jnp.logical_or(x, y)
        scale = pick(jnp.logical_or(x_first, either), one, ex)
        rows = [pick(c, one, e1), pick(c, e0, one)]
        rows += [rows[0] * scale, rows[1] * scale]
        rows += [
            pick(x_first, pick(x, one, ex), pick(jnp.logical_and(x, y), zero, one)),
            pick(x_first, pick(x, own_chip, one), pick(y, pick(x, one, own_chip), zero)),
        ]
        a = pick(x_first, pick(x, one, zero), pick(y, pick(x, ex, one), zero))
        b = pick(x_first, pick(y, pick(x, ex, one), zero), pick(either, one, zero))
        into, send = pick(c, e1, one), pick(c, one, e0)
        rows += [into * a, into * b, pick(c, one, zero)]
        rows += [send * a, send * b, pick(c, zero, one)]
        for index, row in enumerate(rows):
            out[index : index + 1, :] = row


def combine(base, groups, weights, outs, after=(), slots_of=None, at=0, carry=()):
    arrays, columns = [], []
    for slots in outs:
        for column, terms in slots:
            if column not in columns:
                columns.append(column)
            for _, (array, slot) in terms:
                if not any(array is a and slot == s for a, s in arrays):
                    arrays.append((array, slot))
    place = lambda array, slot: [
        i for i, (a, s) in enumerate(arrays) if a is array and s == slot
    ][0]
    plan = [
        [
            (columns.index(column), [(row, place(*source)) for row, source in terms])
            for column, terms in slots
        ]
        for slots in outs
    ]

    def body(at, base, *refs):
        rows, values = refs[: len(columns)], refs[len(columns) : len(columns) + len(arrays)]
        results = refs[len(columns) + len(arrays) :]
        width = rows[0].shape[1]
        for result, slots in zip(results, plan):
            for slot, (column, terms) in enumerate(slots):
                for start in range(0, width, 256):
                    lanes = slice(start, start + 256)
                    total = None
                    for row, index in terms:
                        term = rows[column][row : row + 1, lanes] * values[index][
                            0, :, lanes
                        ].astype(F32)
                        total = term if total is None else total + term
                    result[slot, :, lanes] = total.astype(BF16)

    length, width = arrays[0][0].shape[1:]
    block = lambda slot, count: ((count, length, width), lambda g, b: (slot, 0, 0))
    ins = [
        (
            weights,
            (
                (weights.shape[0], width),
                lambda g, b, column=column: (0, lax.rem(first_group(b) + column, groups)),
            ),
        )
        for column in columns
    ]
    ins += [(array, block(slot, 1)) for array, slot in arrays]
    results = [
        ((slots_of or len(slots), length, width), BF16, block(at, len(slots))) for slots in outs
    ]
    return call(body, results, ins, base=base, after=after, carry=carry)


def scan_blocks(base, groups, weights, local, local_sent, reverse, beside):
    count = lax.axis_size("seq")

    def swap(block, bits):
        route = [(i, i ^ bits[i % 2]) for i in range(count)]
        return lax.ppermute(block, "seq", route)

    def merge(slot, *plans, **places):
        outs = [[(slot, list(zip(rows, sources)))] for rows, sources in plans]
        return combine(base, groups, weights, outs, **places)

    taken = swap(local_sent, (1, 1))
    chips, first_taken, sent, second_taken = [], [], [], []
    for slot in range(2):
        both = ((local, slot), (taken, slot))
        chip, chip_sent = merge(slot, ((0, 1), both), ((2, 3), both))
        chips.append(chip)
        first_taken.append(swap(chip_sent, (2, 4)))
    after = [beside[0](chips[1])]
    for slot in range(2):
        sources = ((chips[slot], 0), (first_taken[slot], 0))
        (block,) = merge(slot, ((4, 5), sources), after=after)
        sent.append(block)
        second_taken.append(swap(block, (4, 2)))
        if slot == 0:
            after = [beside[1](block)]
    after = beside[2](sent[1])
    carry = []
    for slot in range(2):
        sources = ((first_taken[slot], 0), (second_taken[slot], 0))
        mine, handed = merge(
            slot,
            ((6, 7, 8), (*sources, (taken, slot))),
            ((9, 10, 11), (*sources, (local, slot))),
            after=after[slot],
            slots_of=2,
            at=slot,
            carry=carry,
        )
        carry = [mine, handed]
    return mine, swap(handed, (1, 1))


def gather_blocks(totals, local, reverse):
    table = lax.all_gather(totals, "seq", axis=0, tiled=True)
    blocks = lax.all_gather(local[None], "seq", axis=0, tiled=True)
    own = lax.axis_index("seq")
    order = jnp.arange(table.shape[0], dtype=jnp.int32)
    if reverse:
        inside = (order[None, :] > own) & (order[None, :] < order[:, None])
        selected = order > own
    else:
        inside = (order[None, :] > order[:, None]) & (order[None, :] < own)
        selected = order < own
    exponent = jnp.sum(jnp.where(inside[:, :, None], table[None], 0.0), axis=1)
    factor = jnp.where(selected[:, None], jnp.exp(exponent), 0.0)
    factor = factor.reshape(factor.shape[0], local.shape[0], 1, local.shape[2])
    state = jnp.sum(factor * blocks.astype(F32), axis=0).astype(BF16)
    return state, state


def conv_body(fetch, at, base, x_in, taps, *refs):
    length, width = x_in.shape
    group, groups = at
    if fetch:
        x_all, taps_all, x_out, slope_out, top_out, taps_out, x_mine, taps_mine, ext, sems = refs
        lanes = pl.ds(pl.multiple_of(first_group(base) * width, 128), x_mine.shape[1])
        copies = [
            pltpu.make_async_copy(x_all.at[:, lanes], x_mine, sems.at[0]),
            pltpu.make_async_copy(taps_all.at[:, lanes], taps_mine, sems.at[1]),
        ]

        @pl.when(group == 0)
        def _():
            for copy in copies:
                copy.start()

    else:
        x_out, slope_out, top_out, taps_out, ext = refs
    top_out[...] = x_in[0:16, :]
    taps_out[...] = taps[...]
    ext[0:8, :] = jnp.zeros((8, 128), F32)
    for start in range(0, width, 128):
        lanes = slice(start, start + 128)
        ext[8 : 8 + length, :] = x_in[:, lanes].astype(F32)
        pre = taps[0:1, lanes] * ext[5 : 5 + length, :]
        for k in range(1, 4):
            pre = pre + taps[k : k + 1, lanes] * ext[5 + k : 5 + k + length, :]
        sigma = sigmoid(pre)
        x_out[:, lanes] = (pre * sigma).astype(BF16)
        slope_out[:, lanes] = sigma * (1.0 + pre * (1.0 - sigma))
    if fetch:

        @pl.when(group == groups - 1)
        def _():
            for copy in copies:
                copy.wait()


def state_body(first, at, base, x_low, x_top, x_halo, taps, step_in, cumul_in, *refs):
    length, width = x_low.shape
    if first:
        bc_in, bc_halo, bc_taps, slope_out, x_out, state_out = refs[:6]
        bc_out, bc_slope_out, gram_out, b_turned, ext, bc_ext = refs[6:]

        @pl.when(at[0] == 0)
        def _():
            for j in range(2):
                halo = bc_halo[:, j * 128 : j * 128 + 128].astype(F32)
                bc_ext[5:8, :] = jnp.where(place_bit(base, 5) == 1, 0.0, halo)
                bc_ext[8 : 8 + length, :] = bc_in[j].astype(F32)
                pre = bc_taps[j, 0:1, :] * bc_ext[5 : 5 + length, :]
                for k in range(1, 4):
                    pre = pre + bc_taps[j, k : k + 1, :] * bc_ext[5 + k : 5 + k + length, :]
                sigma = sigmoid(pre)
                bc_out[j] = (pre * sigma).astype(BF16)
                bc_slope_out[j] = sigma * (1.0 + pre * (1.0 - sigma))
            b_turned[...] = bc_out[0].astype(F32).T
            gram_out[...] = jnp.where(
                triangle(length, False), dot_rows(bc_out[1], bc_out[0]), 0.0
            )

    else:
        b_turned, slope_out, x_out, state_out, ext = refs

    top = x_top.shape[0]
    ext[5:8, :] = jnp.where(place_bit(base, 5) == 1, 0.0, x_halo[...].astype(F32))
    ext[8 : 8 + top, :] = x_top[...].astype(F32)
    tail_step = jnp.exp(cumul_in[:, length - 1 :] - cumul_in[...]) * step_in[...]
    for head in range(width // 128):
        lanes = slice(head * 128, head * 128 + 128)
        pre = taps[0:1, lanes] * ext[5 : 5 + top, lanes]
        for k in range(1, 4):
            pre = pre + taps[k : k + 1, lanes] * ext[5 + k : 5 + k + top, lanes]
        sigma = sigmoid(pre)
        x_rows = (pre * sigma).astype(BF16)
        x_out[:, lanes] = x_rows
        slope_out[:, lanes] = sigma * (1.0 + pre * (1.0 - sigma))
        x_head = jnp.concatenate([x_rows, x_low[top:, lanes]], axis=0)
        weighted = (b_turned[...] * tail_step[head : head + 1, :]).astype(BF16)
        state_out[0, :, lanes] = dot(weighted, x_head).astype(BF16)


def inner_body(at, base, gram, step_in, cumul_in, x_in, rows, mixed_out):
    cumul = cumul_in[...]
    cumul_columns = columns_of(cumul)
    for head in range(x_in.shape[1] // 128):
        lanes = slice(head * 128, head * 128 + 128)
        row = cumul[head : head + 1, :]
        decay = jnp.exp(jnp.minimum(cumul_columns[:, head : head + 1] - row, 0.0))
        mixer = (gram[...] * decay * step_in[head : head + 1, :]).astype(BF16)
        x_head = x_in[:, lanes]
        mixed_out[:, lanes] = dot(mixer, x_head) + rows[1:2, lanes] * x_head.astype(F32)


def gate_body(
    at, base, z_in, grad_in, gain, gate_out, gate_slope_out, scaled_out, scaled_gate_out
):
    for start in range(0, z_in.shape[1], 128):
        lanes = slice(start, start + 128)
        z = z_in[:, lanes].astype(F32)
        sigma = sigmoid(z)
        gate = z * sigma
        scaled = grad_in[:, lanes].astype(F32) * gain[:, lanes]
        gate_out[:, lanes] = gate
        gate_slope_out[:, lanes] = sigma * (1.0 + z * (1.0 - sigma))
        scaled_out[:, lanes] = scaled
        scaled_gate_out[:, lanes] = scaled * gate


def lift_body(at, base, bc, step_in, cumul_in, x_in, weighted_x, lifted_out, c_turned):
    @pl.when(at[0] == 0)
    def _():
        c_turned[...] = bc[1].astype(F32).T

    weights = block_weights(step_in[...], cumul_in[...])
    lifted = jnp.exp(cumul_in[...])
    for head in range(x_in.shape[1] // 128):
        lanes = slice(head * 128, head * 128 + 128)
        weight = weights[:, head : head + 1]
        weighted_x[:, lanes] = (weight * x_in[:, lanes].astype(F32)).astype(BF16)
        lifted_out[:, lanes] = (c_turned[...] * lifted[head : head + 1, :]).astype(BF16)


def mix_body(
    at, base, mixed_in, c_rows, cumul_in, state, gate_in, scaled_in, sums_in, *outs
):
    mixed_out, sums_out, squares, products = outs
    group, groups = at

    @pl.when(group == 0)
    def _():
        squares[...] = jnp.zeros_like(squares)
        products[...] = jnp.zeros_like(products)

    carried = dot(c_rows[0], state[0])
    lifted = jnp.exp(columns_of(cumul_in[...]))
    square, product = squares[...], products[...]
    for head in range(mixed_in.shape[1] // 128):
        lanes = slice(head * 128, head * 128 + 128)
        mixed = mixed_in[:, lanes] + lifted[:, head : head + 1] * carried[:, lanes]
        mixed_out[:, lanes] = mixed
        gated = mixed * gate_in[:, lanes]
        square = square + gated * gated
        product = product + mixed * scaled_in[:, lanes]
    squares[...] = square
    products[...] = product

    @pl.when(group == groups - 1)
    def _():
        sums_out[...] = sums_in[...]
        sums_out[0:1, :] += jnp.sum(squares[...].T, axis=0, keepdims=True)
        sums_out[1:2, :] += jnp.sum(products[...].T, axis=0, keepdims=True)


def square_body(at, base, mixed_in, gate_in, squared):
    for start in range(0, mixed_in.shape[1], 128):
        lanes = slice(start, start + 128)
        gate = gate_in[:, lanes]
        squared[:, lanes] = mixed_in[:, lanes] * gate * gate


def norm_scales(at, inner, sums, alpha, beta):
    @pl.when(at[0] == 0)
    def _():
        total = sums[0][...]
        for part in sums[1:]:
            total = total + part[...]
        inv_rms = lax.rsqrt(total[0:1, :] / inner + EPS)
        mean_dot = inv_rms * total[1:2, :] / inner
        alpha[...] = jnp.broadcast_to(inv_rms, alpha.shape).T
        beta[...] = jnp.broadcast_to(inv_rms * inv_rms * mean_dot, beta.shape).T


def grad_mixed_body(inner, parts, at, base, *refs):
    sums = refs[:parts]
    squared, scaled_in, lifted_c, grad_mixed, state_out, alpha, beta = refs[parts:]
    norm_scales(at, inner, sums, alpha, beta)
    for start in range(0, squared.shape[1], 128):
        lanes = slice(start, start + 128)
        low = (alpha[...] * scaled_in[:, lanes] - beta[...] * squared[:, lanes]).astype(BF16)
        grad_mixed[:, lanes] = low
        state_out[0, :, lanes] = dot(lifted_c[:, lanes], low).astype(BF16)


def grad_z_body(inner, parts, at, base, *refs):
    sums = refs[:parts]
    mixed_in, gate_in, gate_slope_in, scaled_in, grad_z, alpha, beta = refs[parts:]
    norm_scales(at, inner, sums, alpha, beta)
    for start in range(0, mixed_in.shape[1], 128):
        lanes = slice(start, start + 128)
        mixed = mixed_in[:, lanes]
        grad_gated = alpha[...] * scaled_in[:, lanes] - beta[...] * (mixed * gate_in[:, lanes])
        grad_z[:, lanes] = (grad_gated * (mixed * gate_slope_in[:, lanes])).astype(BF16)


def inner_back_body(
    last,
    at,
    base,
    gram,
    bc,
    step_in,
    cumul_in,
    x_in,
    grad_in,
    state_in,
    rows,
    sums_in,
    grad_x,
    q_out,
    r_out,
    bc_out,
    z_sum,
    c_sum,
):
    group, groups = at
    length = x_in.shape[0]

    @pl.when(group == 0)
    def _():
        z_sum[...] = sums_in[0]
        c_sum[...] = sums_in[1]

    cumul = cumul_in[...]
    cumul_columns = columns_of(cumul)
    lifted = jnp.exp(cumul_columns)
    state = state_in[0]
    c_rows = bc[1].astype(F32)
    lane = lax.broadcasted_iota(jnp.int32, (length, 128), 1)
    q_columns = jnp.zeros((length, 128), F32)
    for head in range(x_in.shape[1] // 128):
        lanes = slice(head * 128, head * 128 + 128)
        step = step_in[head : head + 1, :]
        decay = jnp.exp(
            jnp.minimum(cumul_columns[:, head : head + 1] - cumul[head : head + 1, :], 0.0)
        )
        gram_decay = gram[...] * decay
        mixer = (gram_decay * step).astype(BF16)
        x_head, grad_head = x_in[:, lanes], grad_in[:, lanes]
        product = dot_rows(grad_head, x_head)
        z_sum[...] += product * decay * step
        gram_grad = product * gram_decay
        r_out[head : head + 1, :] = jnp.sum(gram_grad, axis=0, keepdims=True)
        handed = lifted[:, head : head + 1] * dot_rows(grad_head, state[:, lanes])
        c_sum[...] += handed
        q = jnp.sum(gram_grad * step + c_rows * handed, axis=1, keepdims=True)
        q_columns = jnp.where(lane == head, q, q_columns)
        grad_x[:, lanes] = dot_columns(mixer, grad_head) + rows[1:2, lanes] * grad_head.astype(F32)
    q_out[...] = q_columns.T[:GROUP, :]

    @pl.when(group == groups - 1)
    def _():
        if last:
            summed = jnp.where(triangle(length, False), z_sum[...], 0.0)
            bc_out[0] = dot_split(summed.T, bc[1])
            bc_out[1] = c_sum[...] + dot_split(summed, bc[0])
        else:
            bc_out[0] = z_sum[...]
            bc_out[1] = c_sum[...]


def block_weights(step, cumul):
    return columns_of(jnp.exp(cumul[:, cumul.shape[1] - 1 :] - cumul) * step)


def rim_body(last, at, base, bc, step_in, cumul_in, weighted_x, partial, slope, out_in, *refs):
    group, groups = at
    width = weighted_x.shape[1]
    if last:
        rows_before, b_before, bc_partial, bc_slope, rim_low, bc_out, b_sum, rim_out = refs
    else:
        rim_out, b_sum = refs

    @pl.when(group == 0)
    def _():
        b_sum[...] = b_before[...] if last else jnp.zeros_like(b_sum)

    out_low = out_in[0]
    b_sum[...] += dot_rows(weighted_x[...], out_low)
    weights = block_weights(step_in[...], cumul_in[...])[0:8, :]
    returned = dot(bc[0][0:16, :], out_low)[0:8, :]
    start = group
    if last:
        count = rim_out.shape[1] // width
        start = lax.rem(group + count - groups + first_group(base), count)
    for head in range(width // 128):
        lanes = slice(head * 128, head * 128 + 128)
        weight = weights[:, head : head + 1]
        rows = (partial[0:8, lanes] + weight * returned[:, lanes]) * slope[0:8, lanes]
        place = pl.multiple_of(jnp.int32(start) * width + head * 128, 128)
        rim_out[:, pl.ds(place, 128)] = rows[0:3, :]

    if last:

        @pl.when(group == groups - 1)
        def _():
            before = rows_before.shape[1]
            if before < rim_out.shape[1] - 256:
                place = pl.multiple_of(first_group(base) * width, 128)
                rim_out[:, pl.ds(place, before)] = rows_before[...]
            bc_out[0] = (b_sum[...] + bc_partial[0]) * bc_slope[0]
            bc_out[1] = bc_partial[1] * bc_slope[1]
            for j in range(2):
                lanes = rim_out.shape[1] - 256 + 128 * j
                rim_out[:, lanes : lanes + 128] = bc_out[j, 0:3, :]
            rim_low[...] = rim_out[...].astype(BF16)


def grad_dt_body(
    at,
    base,
    bc,
    rate,
    dt_slope,
    step_in,
    cumul_in,
    q_in,
    r_in,
    x_in,
    state_in,
    out_in,
    grad_dt,
    selector,
    products,
):
    heads, length = q_in.shape
    width = state_in.shape[2]
    row = lax.broadcasted_iota(jnp.int32, selector.shape, 0)
    lane = lax.broadcasted_iota(jnp.int32, selector.shape, 1)
    selector[...] = (lax.shift_right_logical(row, 7) == lane).astype(BF16)
    row = lax.broadcasted_iota(jnp.int32, (16, width), 0)
    lane = lax.shift_right_logical(lax.broadcasted_iota(jnp.int32, (16, width), 1), 7)
    dots = jnp.zeros((16, 1), F32)
    for group in range(state_in.shape[0]):
        out_low = out_in[group]
        returned = dot(bc[0], out_low)
        for start in range(0, width, 128):
            lanes = slice(start, start + 128)
            place = slice(group * width + start, group * width + start + 128)
            products[:, place] = (x_in[:, place].astype(F32) * returned[:, lanes]).astype(BF16)
        summed = dot(jnp.ones((16, length), BF16), state_in[group] * out_low)
        own = row - GROUP * group == lane
        dots = dots + jnp.sum(jnp.where(own, summed, 0.0), axis=1, keepdims=True)
    inner_b = dot(products[...], selector[...]).T[:heads, :]
    cumul, step = cumul_in[...], step_in[...]
    w = jnp.exp(cumul[:, length - 1 :] - cumul) * inner_b
    q, r = q_in[...], r_in[...]
    inside = jnp.sum(step * w, axis=1, keepdims=True)
    end = inside + jnp.exp(cumul[:, length - 1 :]) * dots[:heads]
    last = lax.broadcasted_iota(jnp.int32, (heads, length), 1) == length - 1
    grad_cumul = q - step * (r + w) + jnp.where(last, end, 0.0)
    grad_log = dot_split(grad_cumul, triangle(length, False).astype(BF16))
    grad_dt[...] = (r + w + rate[...] * grad_log) * dt_slope[...]


def grad_x_body(
    at,
    base,
    bc,
    step_in,
    cumul_in,
    partial,
    slope,
    taps,
    halo,
    out_in,
    grad_x,
    ext,
):
    length, width = partial.shape
    weights = block_weights(step_in[...], cumul_in[...])
    returned = dot(bc[0], out_in[0])
    rim = jnp.where(place_bit(base, 6) == 1, 0.0, halo[...].astype(F32))
    for head in range(width // 128):
        lanes = slice(head * 128, head * 128 + 128)
        weight = weights[:, head : head + 1]
        ext[0:length, :] = (partial[:, lanes] + weight * returned[:, lanes]) * slope[:, lanes]
        ext[length : length + 3, :] = rim[:, lanes]
        total = taps[0:1, lanes] * ext[3 : 3 + length, :]
        for k in range(1, 4):
            total = total + taps[k : k + 1, lanes] * ext[3 - k : 3 - k + length, :]
        grad_x[:, lanes] = total.astype(BF16)


def bc_back_body(at, place, grad_pre, halo, taps, kept, sent, ext, total):
    length, half = grad_pre.shape[1], kept.shape[1]
    rims = jnp.where(place_bit(place, 6) == 1, 0.0, halo[...].astype(F32))
    for j in range(2):
        ext[0:length, :] = grad_pre[j]
        ext[length : length + 3, :] = rims[:, 128 * j : 128 * j + 128]
        summed = taps[j, 0:1, :] * ext[3 : 3 + length, :]
        for k in range(1, 4):
            summed = summed + taps[j, k : k + 1, :] * ext[3 - k : 3 - k + length, :]
        total[...] = summed
        kept[j] = total[pl.ds(pl.multiple_of(place_bit(place, 3) * half, half), half), :]
        sent[j] = total[pl.ds(pl.multiple_of((1 - place_bit(place, 3)) * half, half), half), :].astype(BF16)


def bc_half_body(at, place, mine, taken, kept, sent, total):
    half = kept.shape[1]
    for j in range(2):
        total[...] = mine[j] + taken[j].astype(F32)
        kept[j] = total[pl.ds(pl.multiple_of(place_bit(place, 4) * half, half), half), :]
        sent[j] = total[pl.ds(pl.multiple_of((1 - place_bit(place, 4)) * half, half), half), :].astype(BF16)


def bc_last_body(at, _, mine, taken, out):
    out[...] = (mine[...] + taken[...].astype(F32)).astype(BF16)


def conv_back(extended, weights):
    length = extended.shape[-2] - 3
    summed = weights[..., 0, :][..., None, :] * extended[..., 3 : 3 + length, :]
    for k in range(1, 4):
        summed = (
            summed
            + weights[..., k, :][..., None, :] * extended[..., 3 - k : 3 - k + length, :]
        )
    return summed


def shards(
    x_input,
    z_input,
    bc_input,
    dt_raw,
    dt_bias,
    a_log,
    d_skip,
    conv_x,
    convolution_bc_taps,
    rescale_factor,
    grad_out,
):
    length, channels = x_input.shape
    heads = dt_raw.shape[0]
    groups = heads // GROUP
    width = GROUP * 128
    count, parts = lax.axis_size("seq"), lax.axis_size("head")
    inner = channels * parts
    own = lax.axis_index("seq")
    split = count == 8 and groups == 4
    own_half = groups // 2 if split else groups
    bit = lambda value, place: lax.shift_right_logical(value, place) & 1
    along_head = lax.axis_index("head")
    base = bit(own, 0) * own_half if split else own * 0
    ends = (own == 0).astype(jnp.int32), (own == count - 1).astype(jnp.int32)
    for place, value in enumerate(
        (bit(own, 2), bit(own, 1), bit(own, 0), bit(along_head, 1), bit(along_head, 0), *ends)
    ):
        base = base | lax.shift_left(value, 8 + place)
    base = base.astype(jnp.int32)[None]

    whole = lambda *shape: ((shape, lambda g, b: (0,) * len(shape)),)
    wide_at = lambda off: (Groups("wide", (length, width), off, groups),)
    rows_at = lambda off: (Groups("heads", (GROUP, length), off, groups),)
    lanes_at = lambda n, off: (Groups("wide", (n, width), off, groups),)
    slot = (Groups("slots", (1, length, width), 0, groups),)
    full = lambda array: (array,) + whole(*array.shape)
    half_width = own_half * width
    half_heads = own_half * GROUP
    half = lambda n: (Groups("half", (n, width), 0, groups),)
    half_rows = (Groups("half heads", (GROUP, length), 0, groups),)
    window_at = lambda n, off: (Groups("window", (n, width), off, groups),)
    halves = [own_half, 0] if split else [0]
    rest = halves[0]

    gain = rescale_factor[None, :]
    f32 = lambda *shape: (shape, F32)
    low = lambda *shape: (shape, BF16)

    step, cumul, rate, dt_slope, rows, rim, bc_rows, bc_taps = call(
        steps_body,
        [
            f32(heads, length) + whole(heads, length),
            f32(heads, length) + whole(heads, length),
            f32(heads, length) + whole(heads, length),
            f32(heads, length) + whole(heads, length),
            f32(2, channels) + whole(2, channels),
            low(3, channels + 256) + whole(3, channels + 256),
            low(2, length, 128) + whole(2, length, 128),
            f32(2, 4, 128) + whole(2, 4, 128),
        ],
        [
            full(in_hbm(dt_raw)),
            full(in_hbm(dt_bias[None, :])),
            full(in_hbm(a_log[None, :])),
            full(in_hbm(d_skip[None, :])),
            (in_hbm(x_input), ((16, channels), lambda g, b: (length // 16 - 1, 0))),
            full(in_hbm(bc_input)),
            full(in_hbm(convolution_bc_taps)),
        ],
        base=base,
    )
    rim_sent = rim
    rim = lax.ppermute(rim, "seq", [(i, (i + 1) % count) for i in range(count)])
    if split:
        swap = lambda block, bit: lax.ppermute(
            block, "seq", [(i, i ^ bit) for i in range(count)]
        )
        total = rows[0:1]
        total_core, total_across = swap(total, 1), swap(total, 2)
        total_beyond = swap(total_across, 1)
        table = f32(16, channels) + whole(16, channels)
        ahead, behind = call(
            weights_body,
            [table, table],
            [full(rows), full(total_core), full(total_across), full(total_beyond)],
            base=base,
            )

    def passed(locals_, reverse, beside):
        if split:
            local_sent, local = locals_[rest], locals_[0]
            weights = behind if reverse else ahead
            return scan_blocks(base, groups, weights, local, local_sent, reverse, beside)
        local = locals_[0]
        for work in beside:
            work(local)
        return gather_blocks(rows[0:1], local, reverse)

    x_low, slope, local = {}, {}, {}
    ready = rim_sent
    for off in halves:
        outs = [
            low(length, half_width) + half(length),
            f32(length, half_width) + half(length),
            low(16, half_width) + half(16),
            f32(4, half_width) + half(4),
        ]
        if off == rest:
            x_all, taps_all = in_hbm(x_input), in_hbm(conv_x)
            ins = [(x_all,) + wide_at(off), (taps_all,) + lanes_at(4, off)]
            scratch = [pltpu.VMEM((length + 8, 128), F32)]
            if split:
                ins += [(x_all, None), (taps_all, None)]
                outs += [
                    low(length, half_width) + whole(length, half_width),
                    f32(4, half_width) + whole(4, half_width),
                ]
                scratch += [pltpu.SemaphoreType.DMA((2,))]
            x_low[off], slope[off], x_top, taps, *fetched = call(
                functools.partial(conv_body, split),
                outs,
                ins,
                base=base,
                grid=own_half,
                scratch=scratch,
                after=[ready],
            )
        else:
            x_low[off], slope[off], x_top, taps = call(
                functools.partial(conv_body, False),
                outs,
                [(fetched[0],) + half(length), (fetched[1],) + half(4)],
                base=base,
                loop=own_half,
                scratch=[pltpu.VMEM((length + 8, 128), F32)],
                after=[ready],
            )
        first = off == rest
        top = (Groups("top", (16, width), 0, groups),)
        ins = [
            (x_low[off],) + half(length),
            (x_top,) + half(16),
            (rim,) + lanes_at(3, off),
            (taps,) + half(4),
            (step,) + rows_at(off),
            (cumul,) + rows_at(off),
        ]
        outs = [
            f32(length, half_width) + top,
            low(length, half_width) + top,
            low(own_half, length, width) + slot,
        ]
        scratch = [pltpu.VMEM((24, width), F32)]
        if first:
            ins += [
                full(bc_rows),
                (rim, ((3, 256), lambda g, b: (0, channels // 256))),
                full(bc_taps),
            ]
            outs += [
                low(2, length, 128) + whole(2, length, 128),
                f32(2, length, 128) + whole(2, length, 128),
                f32(length, length) + whole(length, length),
                f32(128, length) + whole(128, length),
            ]
            scratch += [pltpu.VMEM((length + 8, 128), F32)]
        else:
            ins += [full(b_turned)]
        result = call(
            functools.partial(state_body, first),
            outs,
            ins,
            base=base,
            loop=own_half,
            scratch=scratch,
            after=[total_across] if split and first else [],
            carry=[slope[off]],
            place={0: 1},
            flops=2 * length * 128 * half_width,
        )
        if first:
            bc, bc_slope, gram, b_turned = result[3:]
        slope[off], x_low[off], local[off] = result[:3]
        ready = local[off]

    inside, gate, gate_slope, scaled, scaled_gate = {}, {}, {}, {}, {}

    def mix_inside(off, ready):
        inside[off], token = call(
            inner_body,
            [f32(length, half_width) + half(length)],
            [
                full(gram),
                (step,) + rows_at(off),
                (cumul,) + rows_at(off),
                (x_low[off],) + half(length),
                (rows,) + lanes_at(2, off),
            ],
            base=base,
            loop=own_half,
            after=[ready],
            token=True,
            flops=2 * length * 128 * half_width,
        )
        return token

    def gates(off, ready):
        gate[off], gate_slope[off], scaled[off], scaled_gate[off], token = call(
            gate_body,
            [f32(length, half_width) + half(length)] * 4,
            [
                (z_input,) + wide_at(off),
                (grad_out,) + wide_at(off),
                (gain,) + lanes_at(1, off),
            ],
            base=base,
            loop=own_half,
            after=[ready],
            token=True,
        )
        return token

    def mix_second(ready):
        return mix_inside(rest, ready) if split else ready

    def mix_third(ready):
        return [], [gates(off, ready) for off in reversed(halves)]

    states = passed(local, False, (functools.partial(mix_inside, 0), mix_second, mix_third))
    states = dict(zip((0, rest), states))
    mixed, sums = {}, jnp.zeros((8, length), F32)
    two_scales = [pltpu.VMEM((length, 128), F32), pltpu.VMEM((length, 128), F32)]
    for off in reversed(halves):
        mixed[off], sums = call(
            mix_body,
            [f32(length, half_width) + half(length), f32(8, length) + whole(8, length)],
            [
                (inside[off],) + half(length),
                (bc, ((1, length, 128), lambda g, b: (1, 0, 0))),
                (cumul,) + rows_at(off),
                (states[off],) + slot,
                (gate[off],) + half(length),
                (scaled_gate[off],) + half(length),
                full(sums),
            ],
            base=base,
            loop=own_half,
            scratch=two_scales,
            flops=2 * length * 128 * half_width,
        )
    turn_head = lambda block, bit: lax.ppermute(
        block, "head", [(i, i ^ bit) for i in range(parts)]
    )
    weighted_x, lifted_c, squared = {}, {}, {}
    for off in halves:
        weighted_x[off], lifted_c[off] = call(
            lift_body,
            [low(length, half_width) + half(length), low(length, half_width) + half(length)],
            [
                full(bc),
                (step,) + rows_at(off),
                (cumul,) + rows_at(off),
                (x_low[off],) + half(length),
            ],
            base=base,
            loop=own_half,
            scratch=[pltpu.VMEM((128, length), F32)],
            after=[sums],
        )
        (squared[off],) = call(
            square_body,
            [f32(length, half_width) + half(length)],
            [(mixed[off],) + half(length), (gate[off],) + half(length)],
            base=base,
            loop=own_half,
        )
    if parts == 4:
        sums = sums + turn_head(sums, 1)
        all_sums = [sums, turn_head(sums, 2)]
    else:
        all_sums = [lax.psum(sums, "head")]
    grad_mixed, local_back = {}, {}
    for off in halves:
        grad_mixed[off], local_back[off] = call(
            functools.partial(grad_mixed_body, inner, len(all_sums)),
            [low(length, half_width) + half(length), low(own_half, length, width) + slot],
            [full(part) for part in all_sums]
            + [
                (squared[off],) + half(length),
                (scaled_gate[off],) + half(length),
                (lifted_c[off],) + half(length),
            ],
            base=base,
            loop=own_half,
            scratch=two_scales,
            flops=2 * length * 128 * half_width,
        )

    partial, q_rows, r_rows = {}, {}, {}
    carried = {"sums": jnp.zeros((2, length, 128), F32), "z": [], "dt": [], "x": []}

    def back_inside(off, ready):
        partial[off], q_rows[off], r_rows[off], carried["sums"], token = call(
            functools.partial(inner_back_body, off == rest),
            [
                f32(length, half_width) + half(length),
                f32(half_heads, length) + half_rows,
                f32(half_heads, length) + half_rows,
                f32(2, length, 128) + whole(2, length, 128),
            ],
            [
                full(gram),
                full(bc),
                (step,) + rows_at(off),
                (cumul,) + rows_at(off),
                (x_low[off],) + half(length),
                (grad_mixed[off],) + half(length),
                (states[off],) + slot,
                (rows,) + lanes_at(2, off),
                full(carried["sums"]),
            ],
            base=base,
            loop=own_half,
            scratch=[pltpu.VMEM((length, length), F32), pltpu.VMEM((length, 128), F32)],
            after=[ready],
            token=True,
            flops=6 * length * 128 * half_width,
        )
        return token

    def back_gates(off, ready):
        grad_z, token = call(
            functools.partial(grad_z_body, inner, len(all_sums)),
            [low(length, channels) + window_at(length, off)],
            [full(part) for part in all_sums]
            + [
                (mixed[off],) + half(length),
                (gate[off],) + half(length),
                (gate_slope[off],) + half(length),
                (scaled[off],) + half(length),
            ],
            base=base,
            loop=own_half,
            scratch=two_scales,
            carry=carried["z"],
            after=[ready],
            token=True,
        )
        carried["z"] = [grad_z]
        carried["z_token"] = token
        return token

    def back_second(ready):
        return back_gates(0, ready)

    def back_third(ready):
        if not split:
            return [], []
        token = back_inside(rest, ready)
        return [token], [back_gates(rest, token)]

    backs = passed(local_back, True, (functools.partial(back_inside, 0), back_second, back_third))
    backs = dict(zip((0, rest), backs))

    def make_grad_dt(off, after):
        table = (Groups("heads", (half_heads, length), off, groups, own_half),)
        window = (Groups("window heads", (half_heads, length), off, groups, own_half),)
        grad_dt, token = call(
            grad_dt_body,
            [f32(heads, length) + window],
            [
                full(bc),
                (rate,) + table,
                (dt_slope,) + table,
                (step,) + table,
                (cumul,) + table,
                full(q_rows[off]),
                full(r_rows[off]),
                full(x_low[off]),
                full(states[off]),
                full(backs[off]),
            ],
            base=base,
            scratch=[pltpu.VMEM((half_width, 128), BF16), pltpu.VMEM((length, half_width), BF16)],
            carry=carried["dt"],
            after=after,
            token=True,
            flops=4 * length * 128 * half_width,
        )
        carried["dt"] = [grad_dt]
        return token

    def make_grad_x(off, after):
        grad_x, token = call(
            grad_x_body,
            [low(length, channels) + window_at(length, off)],
            [
                full(bc),
                (step,) + rows_at(off),
                (cumul,) + rows_at(off),
                (partial[off],) + half(length),
                (slope[off],) + half(length),
                (conv_x,) + lanes_at(4, off),
                (rim_back,) + lanes_at(3, off),
                (backs[off],) + slot,
            ],
            base=base,
            loop=own_half,
            scratch=[pltpu.VMEM((length + 8, 128), F32)],
            carry=carried["x"],
            after=after,
            token=True,
            flops=2 * length * 128 * half_width,
        )
        carried["x"] = [grad_x]
        return token

    def make_rim(off, before, after):
        last = off == rest
        if last:
            outs = [
                low(3, channels + 256) + whole(3, channels + 256),
                f32(2, length, 128) + whole(2, length, 128),
            ]
            scratch = [pltpu.VMEM((length, 128), F32), pltpu.VMEM((3, channels + 256), F32)]
        else:
            scratch = []
            outs = [f32(3, half_width) + whole(3, half_width), f32(length, 128) + whole(length, 128)]
        return call(
            functools.partial(rim_body, last),
            outs,
            [
                full(bc),
                (step,) + rows_at(off),
                (cumul,) + rows_at(off),
                (weighted_x[off],) + half(length),
                (partial[off],) + half(length),
                (slope[off],) + half(length),
                (backs[off],) + slot,
            ]
            + [full(array) for array in before],
            base=base,
            loop=own_half,
            scratch=scratch,
            after=after,
            flops=2 * length * 128 * half_width,
        )

    if split:
        before = make_rim(0, [], [])
    else:
        before = [jnp.zeros((3, channels), F32), jnp.zeros((length, 128), F32)]
    rim_back, grad_bc_pre = make_rim(rest, [*before, carried["sums"], bc_slope], [])
    rim_back = lax.ppermute(rim_back, "seq", [(i, (i - 1) % count) for i in range(count)])
    dt_token = make_grad_dt(rest, [grad_bc_pre])
    if parts == 4:
        piece = lambda rows: f32(2, rows, 128) + whole(2, rows, 128)
        piece_low = lambda rows: low(2, rows, 128) + whole(2, rows, 128)
        kept, sent = call(
            bc_back_body,
            [piece(length // 2), piece_low(length // 2)],
            [
                full(grad_bc_pre),
                (rim_back, ((3, 256), lambda g, b: (0, channels // 256))),
                full(bc_taps),
            ],
            base=base,
            scratch=[pltpu.VMEM((length + 8, 128), F32), pltpu.VMEM((length, 128), F32)],
            after=[dt_token],
        )
        taken = turn_head(sent, 2)
        x_tokens = [make_grad_x(0, [sent])]
        if split:
            x_tokens = [make_grad_dt(0, x_tokens)]
        kept, sent = call(
            bc_half_body,
            [piece(length // 4), piece_low(length // 4)],
            [full(kept), full(taken)],
            base=base,
            scratch=[pltpu.VMEM((length // 2, 128), F32)],
            after=x_tokens,
        )
        taken = turn_head(sent, 1)
        x_tokens = [make_grad_x(rest, [sent])] if split else []
        (grad_bc,) = call(
            bc_last_body,
            [piece_low(length // 4)],
            [full(kept), full(taken)],
            base=base,
            after=x_tokens,
        )
    else:
        if split:
            make_grad_dt(0, [])
        for off in halves:
            make_grad_x(off, [])
        bc_halo = jnp.moveaxis(rim_back[:, channels:].reshape(3, 2, 128), 1, 0)
        bc_halo = jnp.where(own == count - 1, 0.0, bc_halo.astype(F32))
        bc_sum = conv_back(jnp.concatenate([grad_bc_pre, bc_halo], axis=1), convolution_bc_taps)
        share = length // parts
        bc_sum = lax.psum(bc_sum, "head")
        grad_bc = lax.dynamic_slice_in_dim(bc_sum, along_head * share, share, 1).astype(BF16)
    return (carried["x"][0], carried["z"][0], grad_bc, carried["dt"][0])


def solution(mesh):
    return jax.shard_map(
        shards,
        mesh=mesh,
        in_specs=(
            P("seq", "head"),
            P("seq", "head"),
            P(None, "seq", None),
            P("head", "seq"),
            P("head"),
            P("head"),
            P("head"),
            P(None, "head"),
            P(),
            P("head"),
            P("seq", "head"),
        ),
        out_specs=(
            P("seq", "head"),
            P("seq", "head"),
            P(None, ("seq", "head"), None),
            P("head", "seq"),
        ),
        check_vma=False,
    )
```

```python
import functools

import jax
import jax.numpy as jnp
from jax import lax
from jax.experimental import pallas as pl
from jax.experimental.pallas import tpu as pltpu
from jax.sharding import PartitionSpec as P

EPS = 1e-05
GROUP = 8
F32 = jnp.float32
BF16 = jnp.bfloat16
VMEM_BYTES = 16 * 2**20


def sigmoid(value):
    return 0.5 + 0.5 * jnp.tanh(0.5 * value)


def dot(a, b):
    return jnp.dot(a, b, preferred_element_type=F32)


def dot_split(a, b):
    high = a.astype(BF16)
    rest = a - high.astype(F32)
    middle = rest.astype(BF16)
    low = (rest - middle.astype(F32)).astype(BF16)
    return dot(high, b) + (dot(middle, b) + dot(low, b))


def dot_rows(a, b):
    return lax.dot_general(a, b, (((1,), (1,)), ((), ())), preferred_element_type=F32)


def dot_columns(a, b):
    return lax.dot_general(a, b, (((0,), (0,)), ((), ())), preferred_element_type=F32)


def triangle(length, upper):
    first = lax.broadcasted_iota(jnp.int32, (length, length), 0)
    second = lax.broadcasted_iota(jnp.int32, (length, length), 1)
    return first <= second if upper else first >= second


def columns_of(rows):
    return rows.T


class Groups:
    def __init__(self, kind, block, off, groups, size=1):
        self.kind, self.block, self.off, self.groups = kind, block, off, groups
        self.size = size
        self.by_rows = kind.endswith("heads")

    def turn(self, group, base):
        first = self.off + first_group(base)
        return lax.rem(group * self.size + first, self.groups) // self.size

    def place(self, index):
        return (index, 0) if self.by_rows else (0, index)

    def spec(self):
        if self.kind == "slots":
            return pl.BlockSpec(self.block, lambda g, b: (g, 0, 0))
        if self.kind.startswith("half"):
            return pl.BlockSpec(self.block, lambda g, b: self.place(g))
        return pl.BlockSpec(self.block, lambda g, b: self.place(self.turn(g, b)))

    def whole(self, shape, count):
        if self.kind.startswith("window"):
            block = list(self.block)
            block[0 if self.by_rows else 1] *= count
            return pl.BlockSpec(
                tuple(block), lambda g, b: self.place(self.turn(0, b) // count)
            )
        if self.kind == "top":
            shape = (self.block[0], count * self.block[1])
        return pl.BlockSpec(shape, lambda g, b: (0,) * len(shape))

    def view(self, ref, group, base):
        if self.kind == "slots":
            return ref.at[pl.ds(group, 1)]
        if self.kind in ("wide", "heads"):
            group = self.turn(group, base)
        size = self.block[0 if self.by_rows else 1]
        span = pl.ds(pl.multiple_of(jnp.int32(group) * size, size), size)
        return ref.at[span] if self.by_rows else ref.at[:, span]


def call(
    body,
    outs,
    ins,
    *,
    base,
    grid=1,
    loop=1,
    scratch=(),
    after=(),
    carry=(),
    place=None,
    token=False,
    flops=0,
):
    aliases = {1 + len(ins) + len(after) + i: i for i in range(len(carry))}
    for read, written in (place or {}).items():
        aliases[1 + read] = written
    after = list(after) + list(carry)
    outs = list(outs)
    if token:
        outs.append(((8, 128), F32, ((8, 128), lambda *_: (0, 0))))

    def spec(shape, block):
        if block is None:
            return pl.BlockSpec(memory_space=pl.ANY)
        if not isinstance(block, Groups):
            return pl.BlockSpec(*block)
        return block.whole(shape, loop) if grid == 1 else block.spec()

    in_specs = [spec(array.shape, block) for array, block in ins]
    in_specs += [pl.BlockSpec(memory_space=pl.ANY) for _ in after]
    out_specs = [spec(shape, block) for shape, _, block in outs]
    out_shape = [jax.ShapeDtypeStruct(shape, dtype) for shape, dtype, _ in outs]
    arrays = [array for array, _ in ins]
    moved = sum(a.size * a.dtype.itemsize for a in arrays + out_shape)
    blocks = [block for _, block in ins] + [block for _, _, block in outs]

    def ordered(where, *refs):
        taken, rest = refs[: len(ins)], refs[len(ins) + len(after) :]
        results, extra = rest[: len(outs)], rest[len(outs) :]
        if token:
            results[-1][...] = jnp.zeros((8, 128), F32)

        def step(group, _):
            views = [
                block.view(ref, group, where) if isinstance(block, Groups) else ref
                for ref, block in zip(taken + results, blocks)
            ]
            if token:
                views = views[:-1]
            body((group, loop), where, *views, *extra)
            return 0

        if grid > 1:
            views = taken + (results[:-1] if token else results)
            body((pl.program_id(0), grid), where, *views, *extra)
        elif loop > 1:
            lax.fori_loop(0, loop, step, 0)
        else:
            step(0, 0)

    return pl.pallas_call(
        ordered,
        out_shape=out_shape,
        grid_spec=pltpu.PrefetchScalarGridSpec(
            num_scalar_prefetch=1,
            grid=(grid,),
            in_specs=in_specs,
            out_specs=out_specs,
            scratch_shapes=list(scratch),
        ),
        input_output_aliases=aliases,
        cost_estimate=pl.CostEstimate(flops=flops, bytes_accessed=moved, transcendentals=0),
        compiler_params=pltpu.CompilerParams(vmem_limit_bytes=VMEM_BYTES),
    )(base, *arrays, *after)


def in_hbm(array):
    return pltpu.with_memory_space_constraint(array, pltpu.HBM)


def column_of(row):
    count = row.shape[1]
    first = lax.broadcasted_iota(jnp.int32, (count, count), 0)
    second = lax.broadcasted_iota(jnp.int32, (count, count), 1)
    return jnp.sum(jnp.where(first == second, row, 0.0), axis=1, keepdims=True)


def steps_body(
    at,
    base,
    raw,
    bias,
    log_rate,
    skip,
    x_tail,
    bc_in,
    bc_taps,
    step_out,
    cumul_out,
    rate_out,
    slope_out,
    rows_out,
    rim_out,
    bc_in_out,
    bc_taps_out,
):
    bc_in_out[...] = bc_in[...]
    bc_taps_out[...] = bc_taps[...]
    heads, length = raw.shape
    channels = x_tail.shape[1]
    rim_out[:, 0:channels] = x_tail[...].astype(F32)[13:16, :].astype(BF16)
    for j in range(2):
        start = channels + 128 * j
        rim_out[:, start : start + 128] = bc_in[j, length - 16 :].astype(F32)[13:16, :].astype(BF16)
    shifted = raw[...] + column_of(bias[...])
    step = jnp.maximum(shifted, 0.0) + jnp.log1p(jnp.exp(-jnp.abs(shifted)))
    rate = jnp.broadcast_to(-jnp.exp(column_of(log_rate[...])), step.shape)
    cumul = dot_split(rate * step, triangle(length, True).astype(BF16))
    step_out[...] = step
    cumul_out[...] = cumul
    rate_out[...] = rate
    slope_out[...] = sigmoid(shifted)
    skips = column_of(skip[...])
    for head in range(heads):
        lanes = slice(head * 128, head * 128 + 128)
        rows_out[0:1, lanes] = jnp.broadcast_to(cumul[head : head + 1, length - 1 :], (1, 128))
        rows_out[1:2, lanes] = jnp.broadcast_to(skips[head : head + 1, :], (1, 128))


def pick(test, yes, no):
    return jnp.where(test, yes, no)


def first_group(place):
    return place[0] & 255


def place_bit(place, index):
    return lax.shift_right_logical(place[0], 8 + index) & 1


def weights_body(at, place, own, core, across, beyond, *outs):
    t0, t1 = own[0:1, :], core[...]
    e0, e1, own_chip, ex = jnp.exp(t0), jnp.exp(t1), jnp.exp(t0 + t1), jnp.exp(across[...] + beyond[...])
    one = jnp.ones_like(e0)
    zero = jnp.zeros_like(e0)
    bits = [place_bit(place, i) for i in range(3)]
    x_first = bits[2] == 0
    for out, reverse in zip(outs, (False, True)):
        y, x, c = ((1 - bit if reverse else bit) == 1 for bit in bits)
        either = jnp.logical_or(x, y)
        scale = pick(jnp.logical_or(x_first, either), one, ex)
        rows = [pick(c, one, e1), pick(c, e0, one)]
        rows += [rows[0] * scale, rows[1] * scale]
        rows += [
            pick(x_first, pick(x, one, ex), pick(jnp.logical_and(x, y), zero, one)),
            pick(x_first, pick(x, own_chip, one), pick(y, pick(x, one, own_chip), zero)),
        ]
        a = pick(x_first, pick(x, one, zero), pick(y, pick(x, ex, one), zero))
        b = pick(x_first, pick(y, pick(x, ex, one), zero), pick(either, one, zero))
        into, send = pick(c, e1, one), pick(c, one, e0)
        rows += [into * a, into * b, pick(c, one, zero)]
        rows += [send * a, send * b, pick(c, zero, one)]
        for index, row in enumerate(rows):
            out[index : index + 1, :] = row


def combine(base, groups, weights, outs, after=(), slots_of=None, at=0, carry=()):
    arrays, columns = [], []
    for slots in outs:
        for column, terms in slots:
            if column not in columns:
                columns.append(column)
            for _, (array, slot) in terms:
                if not any(array is a and slot == s for a, s in arrays):
                    arrays.append((array, slot))
    place = lambda array, slot: [
        i for i, (a, s) in enumerate(arrays) if a is array and s == slot
    ][0]
    plan = [
        [
            (columns.index(column), [(row, place(*source)) for row, source in terms])
            for column, terms in slots
        ]
        for slots in outs
    ]

    def body(at, base, *refs):
        rows, values = refs[: len(columns)], refs[len(columns) : len(columns) + len(arrays)]
        results = refs[len(columns) + len(arrays) :]
        width = rows[0].shape[1]
        for result, slots in zip(results, plan):
            for slot, (column, terms) in enumerate(slots):
                for start in range(0, width, 256):
                    lanes = slice(start, start + 256)
                    total = None
                    for row, index in terms:
                        term = rows[column][row : row + 1, lanes] * values[index][
                            0, :, lanes
                        ].astype(F32)
                        total = term if total is None else total + term
                    result[slot, :, lanes] = total.astype(BF16)

    length, width = arrays[0][0].shape[1:]
    block = lambda slot, count: ((count, length, width), lambda g, b: (slot, 0, 0))
    ins = [
        (
            weights,
            (
                (weights.shape[0], width),
                lambda g, b, column=column: (0, lax.rem(first_group(b) + column, groups)),
            ),
        )
        for column in columns
    ]
    ins += [(array, block(slot, 1)) for array, slot in arrays]
    results = [
        ((slots_of or len(slots), length, width), BF16, block(at, len(slots))) for slots in outs
    ]
    return call(body, results, ins, base=base, after=after, carry=carry)


def scan_blocks(base, groups, weights, local, local_sent, reverse, beside):
    count = lax.axis_size("seq")

    def swap(block, bits):
        route = [(i, i ^ bits[i % 2]) for i in range(count)]
        return lax.ppermute(block, "seq", route)

    def merge(slot, *plans, **places):
        outs = [[(slot, list(zip(rows, sources)))] for rows, sources in plans]
        return combine(base, groups, weights, outs, **places)

    taken = swap(local_sent, (1, 1))
    chips, first_taken, sent, second_taken = [], [], [], []
    for slot in range(2):
        both = ((local, slot), (taken, slot))
        chip, chip_sent = merge(slot, ((0, 1), both), ((2, 3), both))
        chips.append(chip)
        first_taken.append(swap(chip_sent, (2, 4)))
    after = [beside[0](chips[1])]
    for slot in range(2):
        sources = ((chips[slot], 0), (first_taken[slot], 0))
        (block,) = merge(slot, ((4, 5), sources), after=after)
        sent.append(block)
        second_taken.append(swap(block, (4, 2)))
        if slot == 0:
            after = [beside[1](block)]
    after = beside[2](sent[1])
    carry = []
    for slot in range(2):
        sources = ((first_taken[slot], 0), (second_taken[slot], 0))
        mine, handed = merge(
            slot,
            ((6, 7, 8), (*sources, (taken, slot))),
            ((9, 10, 11), (*sources, (local, slot))),
            after=after[slot],
            slots_of=2,
            at=slot,
            carry=carry,
        )
        carry = [mine, handed]
    return mine, swap(handed, (1, 1))


def gather_blocks(totals, local, reverse):
    table = lax.all_gather(totals, "seq", axis=0, tiled=True)
    blocks = lax.all_gather(local[None], "seq", axis=0, tiled=True)
    own = lax.axis_index("seq")
    order = jnp.arange(table.shape[0], dtype=jnp.int32)
    if reverse:
        inside = (order[None, :] > own) & (order[None, :] < order[:, None])
        selected = order > own
    else:
        inside = (order[None, :] > order[:, None]) & (order[None, :] < own)
        selected = order < own
    exponent = jnp.sum(jnp.where(inside[:, :, None], table[None], 0.0), axis=1)
    factor = jnp.where(selected[:, None], jnp.exp(exponent), 0.0)
    factor = factor.reshape(factor.shape[0], local.shape[0], 1, local.shape[2])
    state = jnp.sum(factor * blocks.astype(F32), axis=0).astype(BF16)
    return state, state


def conv_body(fetch, at, base, x_in, taps, *refs):
    length, width = x_in.shape
    group, groups = at
    if fetch:
        x_all, taps_all, x_out, slope_out, top_out, taps_out, x_mine, taps_mine, ext, sems = refs
        lanes = pl.ds(pl.multiple_of(first_group(base) * width, 128), x_mine.shape[1])
        copies = [
            pltpu.make_async_copy(x_all.at[:, lanes], x_mine, sems.at[0]),
            pltpu.make_async_copy(taps_all.at[:, lanes], taps_mine, sems.at[1]),
        ]

        @pl.when(group == 0)
        def _():
            for copy in copies:
                copy.start()

    else:
        x_out, slope_out, top_out, taps_out, ext = refs
    top_out[...] = x_in[0:16, :]
    taps_out[...] = taps[...]
    ext[0:8, :] = jnp.zeros((8, 128), F32)
    for start in range(0, width, 128):
        lanes = slice(start, start + 128)
        ext[8 : 8 + length, :] = x_in[:, lanes].astype(F32)
        pre = taps[0:1, lanes] * ext[5 : 5 + length, :]
        for k in range(1, 4):
            pre = pre + taps[k : k + 1, lanes] * ext[5 + k : 5 + k + length, :]
        sigma = sigmoid(pre)
        x_out[:, lanes] = (pre * sigma).astype(BF16)
        slope_out[:, lanes] = sigma * (1.0 + pre * (1.0 - sigma))
    if fetch:

        @pl.when(group == groups - 1)
        def _():
            for copy in copies:
                copy.wait()


def state_body(first, at, base, x_low, x_top, x_halo, taps, step_in, cumul_in, *refs):
    length, width = x_low.shape
    if first:
        bc_in, bc_halo, bc_taps, slope_out, x_out, state_out = refs[:6]
        bc_out, bc_slope_out, gram_out, b_turned, ext, bc_ext = refs[6:]

        @pl.when(at[0] == 0)
        def _():
            for j in range(2):
                halo = bc_halo[:, j * 128 : j * 128 + 128].astype(F32)
                bc_ext[5:8, :] = jnp.where(place_bit(base, 5) == 1, 0.0, halo)
                bc_ext[8 : 8 + length, :] = bc_in[j].astype(F32)
                pre = bc_taps[j, 0:1, :] * bc_ext[5 : 5 + length, :]
                for k in range(1, 4):
                    pre = pre + bc_taps[j, k : k + 1, :] * bc_ext[5 + k : 5 + k + length, :]
                sigma = sigmoid(pre)
                bc_out[j] = (pre * sigma).astype(BF16)
                bc_slope_out[j] = sigma * (1.0 + pre * (1.0 - sigma))
            b_turned[...] = bc_out[0].astype(F32).T
            gram_out[...] = jnp.where(
                triangle(length, False), dot_rows(bc_out[1], bc_out[0]), 0.0
            )

    else:
        b_turned, slope_out, x_out, state_out, ext = refs

    top = x_top.shape[0]
    ext[5:8, :] = jnp.where(place_bit(base, 5) == 1, 0.0, x_halo[...].astype(F32))
    ext[8 : 8 + top, :] = x_top[...].astype(F32)
    tail_step = jnp.exp(cumul_in[:, length - 1 :] - cumul_in[...]) * step_in[...]
    for head in range(width // 128):
        lanes = slice(head * 128, head * 128 + 128)
        pre = taps[0:1, lanes] * ext[5 : 5 + top, lanes]
        for k in range(1, 4):
            pre = pre + taps[k : k + 1, lanes] * ext[5 + k : 5 + k + top, lanes]
        sigma = sigmoid(pre)
        x_rows = (pre * sigma).astype(BF16)
        x_out[:, lanes] = x_rows
        slope_out[:, lanes] = sigma * (1.0 + pre * (1.0 - sigma))
        x_head = jnp.concatenate([x_rows, x_low[top:, lanes]], axis=0)
        weighted = (b_turned[...] * tail_step[head : head + 1, :]).astype(BF16)
        state_out[0, :, lanes] = dot(weighted, x_head).astype(BF16)


def inner_body(at, base, gram, step_in, cumul_in, x_in, rows, mixed_out):
    cumul = cumul_in[...]
    cumul_columns = columns_of(cumul)
    for head in range(x_in.shape[1] // 128):
        lanes = slice(head * 128, head * 128 + 128)
        row = cumul[head : head + 1, :]
        decay = jnp.exp(jnp.minimum(cumul_columns[:, head : head + 1] - row, 0.0))
        mixer = (gram[...] * decay * step_in[head : head + 1, :]).astype(BF16)
        x_head = x_in[:, lanes]
        mixed_out[:, lanes] = dot(mixer, x_head) + rows[1:2, lanes] * x_head.astype(F32)


def gate_body(
    at, base, z_in, grad_in, gain, gate_out, gate_slope_out, scaled_out, scaled_gate_out
):
    for start in range(0, z_in.shape[1], 128):
        lanes = slice(start, start + 128)
        z = z_in[:, lanes].astype(F32)
        sigma = sigmoid(z)
        gate = z * sigma
        scaled = grad_in[:, lanes].astype(F32) * gain[:, lanes]
        gate_out[:, lanes] = gate
        gate_slope_out[:, lanes] = sigma * (1.0 + z * (1.0 - sigma))
        scaled_out[:, lanes] = scaled
        scaled_gate_out[:, lanes] = scaled * gate


def lift_body(at, base, bc, step_in, cumul_in, x_in, weighted_x, lifted_out, c_turned):
    @pl.when(at[0] == 0)
    def _():
        c_turned[...] = bc[1].astype(F32).T

    weights = block_weights(step_in[...], cumul_in[...])
    lifted = jnp.exp(cumul_in[...])
    for head in range(x_in.shape[1] // 128):
        lanes = slice(head * 128, head * 128 + 128)
        weight = weights[:, head : head + 1]
        weighted_x[:, lanes] = (weight * x_in[:, lanes].astype(F32)).astype(BF16)
        lifted_out[:, lanes] = (c_turned[...] * lifted[head : head + 1, :]).astype(BF16)


def mix_body(
    at, base, mixed_in, c_rows, cumul_in, state, gate_in, scaled_in, sums_in, *outs
):
    mixed_out, sums_out, squares, products = outs
    group, groups = at

    @pl.when(group == 0)
    def _():
        squares[...] = jnp.zeros_like(squares)
        products[...] = jnp.zeros_like(products)

    carried = dot(c_rows[0], state[0])
    lifted = jnp.exp(columns_of(cumul_in[...]))
    square, product = squares[...], products[...]
    for head in range(mixed_in.shape[1] // 128):
        lanes = slice(head * 128, head * 128 + 128)
        mixed = mixed_in[:, lanes] + lifted[:, head : head + 1] * carried[:, lanes]
        mixed_out[:, lanes] = mixed
        gated = mixed * gate_in[:, lanes]
        square = square + gated * gated
        product = product + mixed * scaled_in[:, lanes]
    squares[...] = square
    products[...] = product

    @pl.when(group == groups - 1)
    def _():
        sums_out[...] = sums_in[...]
        sums_out[0:1, :] += jnp.sum(squares[...].T, axis=0, keepdims=True)
        sums_out[1:2, :] += jnp.sum(products[...].T, axis=0, keepdims=True)


def square_body(at, base, mixed_in, gate_in, squared):
    for start in range(0, mixed_in.shape[1], 128):
        lanes = slice(start, start + 128)
        gate = gate_in[:, lanes]
        squared[:, lanes] = mixed_in[:, lanes] * gate * gate


def norm_scales(at, inner, sums, alpha, beta):
    @pl.when(at[0] == 0)
    def _():
        total = sums[0][...]
        for part in sums[1:]:
            total = total + part[...]
        inv_rms = lax.rsqrt(total[0:1, :] / inner + EPS)
        mean_dot = inv_rms * total[1:2, :] / inner
        alpha[...] = jnp.broadcast_to(inv_rms, alpha.shape).T
        beta[...] = jnp.broadcast_to(inv_rms * inv_rms * mean_dot, beta.shape).T


def grad_mixed_body(inner, parts, at, base, *refs):
    sums = refs[:parts]
    squared, scaled_in, lifted_c, grad_mixed, state_out, alpha, beta = refs[parts:]
    norm_scales(at, inner, sums, alpha, beta)
    for start in range(0, squared.shape[1], 128):
        lanes = slice(start, start + 128)
        low = (alpha[...] * scaled_in[:, lanes] - beta[...] * squared[:, lanes]).astype(BF16)
        grad_mixed[:, lanes] = low
        state_out[0, :, lanes] = dot(lifted_c[:, lanes], low).astype(BF16)


def grad_z_body(inner, parts, at, base, *refs):
    sums = refs[:parts]
    mixed_in, gate_in, gate_slope_in, scaled_in, grad_z, alpha, beta = refs[parts:]
    norm_scales(at, inner, sums, alpha, beta)
    for start in range(0, mixed_in.shape[1], 128):
        lanes = slice(start, start + 128)
        mixed = mixed_in[:, lanes]
        grad_gated = alpha[...] * scaled_in[:, lanes] - beta[...] * (mixed * gate_in[:, lanes])
        grad_z[:, lanes] = (grad_gated * (mixed * gate_slope_in[:, lanes])).astype(BF16)


def inner_back_body(
    last,
    at,
    base,
    gram,
    bc,
    step_in,
    cumul_in,
    x_in,
    grad_in,
    state_in,
    rows,
    sums_in,
    grad_x,
    q_out,
    r_out,
    bc_out,
    z_sum,
    c_sum,
):
    group, groups = at
    length = x_in.shape[0]

    @pl.when(group == 0)
    def _():
        z_sum[...] = sums_in[0]
        c_sum[...] = sums_in[1]

    cumul = cumul_in[...]
    cumul_columns = columns_of(cumul)
    lifted = jnp.exp(cumul_columns)
    state = state_in[0]
    c_rows = bc[1].astype(F32)
    lane = lax.broadcasted_iota(jnp.int32, (length, 128), 1)
    q_columns = jnp.zeros((length, 128), F32)
    for head in range(x_in.shape[1] // 128):
        lanes = slice(head * 128, head * 128 + 128)
        step = step_in[head : head + 1, :]
        decay = jnp.exp(
            jnp.minimum(cumul_columns[:, head : head + 1] - cumul[head : head + 1, :], 0.0)
        )
        gram_decay = gram[...] * decay
        mixer = (gram_decay * step).astype(BF16)
        x_head, grad_head = x_in[:, lanes], grad_in[:, lanes]
        product = dot_rows(grad_head, x_head)
        z_sum[...] += product * decay * step
        gram_grad = product * gram_decay
        r_out[head : head + 1, :] = jnp.sum(gram_grad, axis=0, keepdims=True)
        handed = lifted[:, head : head + 1] * dot_rows(grad_head, state[:, lanes])
        c_sum[...] += handed
        q = jnp.sum(gram_grad * step + c_rows * handed, axis=1, keepdims=True)
        q_columns = jnp.where(lane == head, q, q_columns)
        grad_x[:, lanes] = dot_columns(mixer, grad_head) + rows[1:2, lanes] * grad_head.astype(F32)
    q_out[...] = q_columns.T[:GROUP, :]

    @pl.when(group == groups - 1)
    def _():
        if last:
            summed = jnp.where(triangle(length, False), z_sum[...], 0.0)
            bc_out[0] = dot_split(summed.T, bc[1])
            bc_out[1] = c_sum[...] + dot_split(summed, bc[0])
        else:
            bc_out[0] = z_sum[...]
            bc_out[1] = c_sum[...]


def block_weights(step, cumul):
    return columns_of(jnp.exp(cumul[:, cumul.shape[1] - 1 :] - cumul) * step)


def rim_body(last, at, base, bc, step_in, cumul_in, weighted_x, partial, slope, out_in, *refs):
    group, groups = at
    width = weighted_x.shape[1]
    if last:
        rows_before, b_before, bc_partial, bc_slope, rim_low, bc_out, b_sum, rim_out = refs
    else:
        rim_out, b_sum = refs

    @pl.when(group == 0)
    def _():
        b_sum[...] = b_before[...] if last else jnp.zeros_like(b_sum)

    out_low = out_in[0]
    b_sum[...] += dot_rows(weighted_x[...], out_low)
    weights = block_weights(step_in[...], cumul_in[...])[0:8, :]
    returned = dot(bc[0][0:16, :], out_low)[0:8, :]
    start = group
    if last:
        count = rim_out.shape[1] // width
        start = lax.rem(group + count - groups + first_group(base), count)
    for head in range(width // 128):
        lanes = slice(head * 128, head * 128 + 128)
        weight = weights[:, head : head + 1]
        rows = (partial[0:8, lanes] + weight * returned[:, lanes]) * slope[0:8, lanes]
        place = pl.multiple_of(jnp.int32(start) * width + head * 128, 128)
        rim_out[:, pl.ds(place, 128)] = rows[0:3, :]

    if last:

        @pl.when(group == groups - 1)
        def _():
            before = rows_before.shape[1]
            if before < rim_out.shape[1] - 256:
                place = pl.multiple_of(first_group(base) * width, 128)
                rim_out[:, pl.ds(place, before)] = rows_before[...]
            bc_out[0] = (b_sum[...] + bc_partial[0]) * bc_slope[0]
            bc_out[1] = bc_partial[1] * bc_slope[1]
            for j in range(2):
                lanes = rim_out.shape[1] - 256 + 128 * j
                rim_out[:, lanes : lanes + 128] = bc_out[j, 0:3, :]
            rim_low[...] = rim_out[...].astype(BF16)


def grad_dt_body(
    at,
    base,
    bc,
    rate,
    dt_slope,
    step_in,
    cumul_in,
    q_in,
    r_in,
    x_in,
    state_in,
    out_in,
    grad_dt,
    selector,
    products,
):
    heads, length = q_in.shape
    width = state_in.shape[2]
    row = lax.broadcasted_iota(jnp.int32, selector.shape, 0)
    lane = lax.broadcasted_iota(jnp.int32, selector.shape, 1)
    selector[...] = (lax.shift_right_logical(row, 7) == lane).astype(BF16)
    row = lax.broadcasted_iota(jnp.int32, (16, width), 0)
    lane = lax.shift_right_logical(lax.broadcasted_iota(jnp.int32, (16, width), 1), 7)
    dots = jnp.zeros((16, 1), F32)
    for group in range(state_in.shape[0]):
        out_low = out_in[group]
        returned = dot(bc[0], out_low)
        for start in range(0, width, 128):
            lanes = slice(start, start + 128)
            place = slice(group * width + start, group * width + start + 128)
            products[:, place] = (x_in[:, place].astype(F32) * returned[:, lanes]).astype(BF16)
        summed = dot(jnp.ones((16, length), BF16), state_in[group] * out_low)
        own = row - GROUP * group == lane
        dots = dots + jnp.sum(jnp.where(own, summed, 0.0), axis=1, keepdims=True)
    inner_b = dot(products[...], selector[...]).T[:heads, :]
    cumul, step = cumul_in[...], step_in[...]
    w = jnp.exp(cumul[:, length - 1 :] - cumul) * inner_b
    q, r = q_in[...], r_in[...]
    inside = jnp.sum(step * w, axis=1, keepdims=True)
    end = inside + jnp.exp(cumul[:, length - 1 :]) * dots[:heads]
    last = lax.broadcasted_iota(jnp.int32, (heads, length), 1) == length - 1
    grad_cumul = q - step * (r + w) + jnp.where(last, end, 0.0)
    grad_log = dot_split(grad_cumul, triangle(length, False).astype(BF16))
    grad_dt[...] = (r + w + rate[...] * grad_log) * dt_slope[...]


def grad_x_body(
    at,
    base,
    bc,
    step_in,
    cumul_in,
    partial,
    slope,
    taps,
    halo,
    out_in,
    grad_x,
    ext,
):
    length, width = partial.shape
    weights = block_weights(step_in[...], cumul_in[...])
    returned = dot(bc[0], out_in[0])
    rim = jnp.where(place_bit(base, 6) == 1, 0.0, halo[...].astype(F32))
    for head in range(width // 128):
        lanes = slice(head * 128, head * 128 + 128)
        weight = weights[:, head : head + 1]
        ext[0:length, :] = (partial[:, lanes] + weight * returned[:, lanes]) * slope[:, lanes]
        ext[length : length + 3, :] = rim[:, lanes]
        total = taps[0:1, lanes] * ext[3 : 3 + length, :]
        for k in range(1, 4):
            total = total + taps[k : k + 1, lanes] * ext[3 - k : 3 - k + length, :]
        grad_x[:, lanes] = total.astype(BF16)


def bc_back_body(at, place, grad_pre, halo, taps, kept, sent, ext, total):
    length, half = grad_pre.shape[1], kept.shape[1]
    rims = jnp.where(place_bit(place, 6) == 1, 0.0, halo[...].astype(F32))
    for j in range(2):
        ext[0:length, :] = grad_pre[j]
        ext[length : length + 3, :] = rims[:, 128 * j : 128 * j + 128]
        summed = taps[j, 0:1, :] * ext[3 : 3 + length, :]
        for k in range(1, 4):
            summed = summed + taps[j, k : k + 1, :] * ext[3 - k : 3 - k + length, :]
        total[...] = summed
        kept[j] = total[pl.ds(pl.multiple_of(place_bit(place, 3) * half, half), half), :]
        sent[j] = total[pl.ds(pl.multiple_of((1 - place_bit(place, 3)) * half, half), half), :].astype(BF16)


def bc_half_body(at, place, mine, taken, kept, sent, total):
    half = kept.shape[1]
    for j in range(2):
        total[...] = mine[j] + taken[j].astype(F32)
        kept[j] = total[pl.ds(pl.multiple_of(place_bit(place, 4) * half, half), half), :]
        sent[j] = total[pl.ds(pl.multiple_of((1 - place_bit(place, 4)) * half, half), half), :].astype(BF16)


def bc_last_body(at, _, mine, taken, out):
    out[...] = (mine[...] + taken[...].astype(F32)).astype(BF16)


def conv_back(extended, weights):
    length = extended.shape[-2] - 3
    summed = weights[..., 0, :][..., None, :] * extended[..., 3 : 3 + length, :]
    for k in range(1, 4):
        summed = (
            summed
            + weights[..., k, :][..., None, :] * extended[..., 3 - k : 3 - k + length, :]
        )
    return summed


def shards(
    x_input,
    z_input,
    bc_input,
    dt_raw,
    dt_bias,
    a_log,
    d_skip,
    conv_x,
    convolution_bc_taps,
    rescale_factor,
    grad_out,
):
    length, channels = x_input.shape
    heads = dt_raw.shape[0]
    groups = heads // GROUP
    width = GROUP * 128
    count, parts = lax.axis_size("seq"), lax.axis_size("head")
    inner = channels * parts
    own = lax.axis_index("seq")
    split = count == 8 and groups == 4
    own_half = groups // 2 if split else groups
    bit = lambda value, place: lax.shift_right_logical(value, place) & 1
    along_head = lax.axis_index("head")
    base = bit(own, 0) * own_half if split else own * 0
    ends = (own == 0).astype(jnp.int32), (own == count - 1).astype(jnp.int32)
    for place, value in enumerate(
        (bit(own, 2), bit(own, 1), bit(own, 0), bit(along_head, 1), bit(along_head, 0), *ends)
    ):
        base = base | lax.shift_left(value, 8 + place)
    base = base.astype(jnp.int32)[None]

    whole = lambda *shape: ((shape, lambda g, b: (0,) * len(shape)),)
    wide_at = lambda off: (Groups("wide", (length, width), off, groups),)
    rows_at = lambda off: (Groups("heads", (GROUP, length), off, groups),)
    lanes_at = lambda n, off: (Groups("wide", (n, width), off, groups),)
    slot = (Groups("slots", (1, length, width), 0, groups),)
    full = lambda array: (array,) + whole(*array.shape)
    half_width = own_half * width
    half_heads = own_half * GROUP
    half = lambda n: (Groups("half", (n, width), 0, groups),)
    half_rows = (Groups("half heads", (GROUP, length), 0, groups),)
    window_at = lambda n, off: (Groups("window", (n, width), off, groups),)
    halves = [own_half, 0] if split else [0]
    rest = halves[0]

    gain = rescale_factor[None, :]
    f32 = lambda *shape: (shape, F32)
    low = lambda *shape: (shape, BF16)

    step, cumul, rate, dt_slope, rows, rim, bc_rows, bc_taps = call(
        steps_body,
        [
            f32(heads, length) + whole(heads, length),
            f32(heads, length) + whole(heads, length),
            f32(heads, length) + whole(heads, length),
            f32(heads, length) + whole(heads, length),
            f32(2, channels) + whole(2, channels),
            low(3, channels + 256) + whole(3, channels + 256),
            low(2, length, 128) + whole(2, length, 128),
            f32(2, 4, 128) + whole(2, 4, 128),
        ],
        [
            full(in_hbm(dt_raw)),
            full(in_hbm(dt_bias[None, :])),
            full(in_hbm(a_log[None, :])),
            full(in_hbm(d_skip[None, :])),
            (in_hbm(x_input), ((16, channels), lambda g, b: (length // 16 - 1, 0))),
            full(in_hbm(bc_input)),
            full(in_hbm(convolution_bc_taps)),
        ],
        base=base,
    )
    rim_sent = rim
    rim = lax.ppermute(rim, "seq", [(i, (i + 1) % count) for i in range(count)])
    if split:
        swap = lambda block, bit: lax.ppermute(
            block, "seq", [(i, i ^ bit) for i in range(count)]
        )
        total = rows[0:1]
        total_core, total_across = swap(total, 1), swap(total, 2)
        total_beyond = swap(total_across, 1)
        table = f32(16, channels) + whole(16, channels)
        ahead, behind = call(
            weights_body,
            [table, table],
            [full(rows), full(total_core), full(total_across), full(total_beyond)],
            base=base,
            )

    def passed(locals_, reverse, beside):
        if split:
            local_sent, local = locals_[rest], locals_[0]
            weights = behind if reverse else ahead
            return scan_blocks(base, groups, weights, local, local_sent, reverse, beside)
        local = locals_[0]
        for work in beside:
            work(local)
        return gather_blocks(rows[0:1], local, reverse)

    x_low, slope, local = {}, {}, {}
    ready = rim_sent
    for off in halves:
        outs = [
            low(length, half_width) + half(length),
            f32(length, half_width) + half(length),
            low(16, half_width) + half(16),
            f32(4, half_width) + half(4),
        ]
        if off == rest:
            x_all, taps_all = in_hbm(x_input), in_hbm(conv_x)
            ins = [(x_all,) + wide_at(off), (taps_all,) + lanes_at(4, off)]
            scratch = [pltpu.VMEM((length + 8, 128), F32)]
            if split:
                ins += [(x_all, None), (taps_all, None)]
                outs += [
                    low(length, half_width) + whole(length, half_width),
                    f32(4, half_width) + whole(4, half_width),
                ]
                scratch += [pltpu.SemaphoreType.DMA((2,))]
            x_low[off], slope[off], x_top, taps, *fetched = call(
                functools.partial(conv_body, split),
                outs,
                ins,
                base=base,
                grid=own_half,
                scratch=scratch,
                after=[ready],
            )
        else:
            x_low[off], slope[off], x_top, taps = call(
                functools.partial(conv_body, False),
                outs,
                [(fetched[0],) + half(length), (fetched[1],) + half(4)],
                base=base,
                loop=own_half,
                scratch=[pltpu.VMEM((length + 8, 128), F32)],
                after=[ready],
            )
        first = off == rest
        top = (Groups("top", (16, width), 0, groups),)
        ins = [
            (x_low[off],) + half(length),
            (x_top,) + half(16),
            (rim,) + lanes_at(3, off),
            (taps,) + half(4),
            (step,) + rows_at(off),
            (cumul,) + rows_at(off),
        ]
        outs = [
            f32(length, half_width) + top,
            low(length, half_width) + top,
            low(own_half, length, width) + slot,
        ]
        scratch = [pltpu.VMEM((24, width), F32)]
        if first:
            ins += [
                full(bc_rows),
                (rim, ((3, 256), lambda g, b: (0, channels // 256))),
                full(bc_taps),
            ]
            outs += [
                low(2, length, 128) + whole(2, length, 128),
                f32(2, length, 128) + whole(2, length, 128),
                f32(length, length) + whole(length, length),
                f32(128, length) + whole(128, length),
            ]
            scratch += [pltpu.VMEM((length + 8, 128), F32)]
        else:
            ins += [full(b_turned)]
        result = call(
            functools.partial(state_body, first),
            outs,
            ins,
            base=base,
            loop=own_half,
            scratch=scratch,
            after=[total_across] if split and first else [],
            carry=[slope[off]],
            place={0: 1},
            flops=2 * length * 128 * half_width,
        )
        if first:
            bc, bc_slope, gram, b_turned = result[3:]
        slope[off], x_low[off], local[off] = result[:3]
        ready = local[off]

    inside, gate, gate_slope, scaled, scaled_gate = {}, {}, {}, {}, {}

    def mix_inside(off, ready):
        inside[off], token = call(
            inner_body,
            [f32(length, half_width) + half(length)],
            [
                full(gram),
                (step,) + rows_at(off),
                (cumul,) + rows_at(off),
                (x_low[off],) + half(length),
                (rows,) + lanes_at(2, off),
            ],
            base=base,
            loop=own_half,
            after=[ready],
            token=True,
            flops=2 * length * 128 * half_width,
        )
        return token

    def gates(off, ready):
        gate[off], gate_slope[off], scaled[off], scaled_gate[off], token = call(
            gate_body,
            [f32(length, half_width) + half(length)] * 4,
            [
                (z_input,) + wide_at(off),
                (grad_out,) + wide_at(off),
                (gain,) + lanes_at(1, off),
            ],
            base=base,
            loop=own_half,
            after=[ready],
            token=True,
        )
        return token

    def mix_second(ready):
        return mix_inside(rest, ready) if split else ready

    def mix_third(ready):
        return [], [gates(off, ready) for off in reversed(halves)]

    states = passed(local, False, (functools.partial(mix_inside, 0), mix_second, mix_third))
    states = dict(zip((0, rest), states))
    mixed, sums = {}, jnp.zeros((8, length), F32)
    two_scales = [pltpu.VMEM((length, 128), F32), pltpu.VMEM((length, 128), F32)]
    for off in reversed(halves):
        mixed[off], sums = call(
            mix_body,
            [f32(length, half_width) + half(length), f32(8, length) + whole(8, length)],
            [
                (inside[off],) + half(length),
                (bc, ((1, length, 128), lambda g, b: (1, 0, 0))),
                (cumul,) + rows_at(off),
                (states[off],) + slot,
                (gate[off],) + half(length),
                (scaled_gate[off],) + half(length),
                full(sums),
            ],
            base=base,
            loop=own_half,
            scratch=two_scales,
            flops=2 * length * 128 * half_width,
        )
    turn_head = lambda block, bit: lax.ppermute(
        block, "head", [(i, i ^ bit) for i in range(parts)]
    )
    weighted_x, lifted_c, squared = {}, {}, {}
    for off in halves:
        weighted_x[off], lifted_c[off] = call(
            lift_body,
            [low(length, half_width) + half(length), low(length, half_width) + half(length)],
            [
                full(bc),
                (step,) + rows_at(off),
                (cumul,) + rows_at(off),
                (x_low[off],) + half(length),
            ],
            base=base,
            loop=own_half,
            scratch=[pltpu.VMEM((128, length), F32)],
            after=[sums],
        )
        (squared[off],) = call(
            square_body,
            [f32(length, half_width) + half(length)],
            [(mixed[off],) + half(length), (gate[off],) + half(length)],
            base=base,
            loop=own_half,
        )
    if parts == 4:
        sums = sums + turn_head(sums, 1)
        all_sums = [sums, turn_head(sums, 2)]
    else:
        all_sums = [lax.psum(sums, "head")]
    grad_mixed, local_back = {}, {}
    for off in halves:
        grad_mixed[off], local_back[off] = call(
            functools.partial(grad_mixed_body, inner, len(all_sums)),
            [low(length, half_width) + half(length), low(own_half, length, width) + slot],
            [full(part) for part in all_sums]
            + [
                (squared[off],) + half(length),
                (scaled_gate[off],) + half(length),
                (lifted_c[off],) + half(length),
            ],
            base=base,
            loop=own_half,
            scratch=two_scales,
            flops=2 * length * 128 * half_width,
        )

    partial, q_rows, r_rows = {}, {}, {}
    carried = {"sums": jnp.zeros((2, length, 128), F32), "z": [], "dt": [], "x": []}

    def back_inside(off, ready):
        partial[off], q_rows[off], r_rows[off], carried["sums"], token = call(
            functools.partial(inner_back_body, off == rest),
            [
                f32(length, half_width) + half(length),
                f32(half_heads, length) + half_rows,
                f32(half_heads, length) + half_rows,
                f32(2, length, 128) + whole(2, length, 128),
            ],
            [
                full(gram),
                full(bc),
                (step,) + rows_at(off),
                (cumul,) + rows_at(off),
                (x_low[off],) + half(length),
                (grad_mixed[off],) + half(length),
                (states[off],) + slot,
                (rows,) + lanes_at(2, off),
                full(carried["sums"]),
            ],
            base=base,
            loop=own_half,
            scratch=[pltpu.VMEM((length, length), F32), pltpu.VMEM((length, 128), F32)],
            after=[ready],
            token=True,
            flops=6 * length * 128 * half_width,
        )
        return token

    def back_gates(off, ready):
        grad_z, token = call(
            functools.partial(grad_z_body, inner, len(all_sums)),
            [low(length, channels) + window_at(length, off)],
            [full(part) for part in all_sums]
            + [
                (mixed[off],) + half(length),
                (gate[off],) + half(length),
                (gate_slope[off],) + half(length),
                (scaled[off],) + half(length),
            ],
            base=base,
            loop=own_half,
            scratch=two_scales,
            carry=carried["z"],
            after=[ready],
            token=True,
        )
        carried["z"] = [grad_z]
        carried["z_token"] = token
        return token

    def back_second(ready):
        return back_gates(0, ready)

    def back_third(ready):
        if not split:
            return [], []
        token = back_inside(rest, ready)
        return [token], [back_gates(rest, token)]

    backs = passed(local_back, True, (functools.partial(back_inside, 0), back_second, back_third))
    backs = dict(zip((0, rest), backs))

    def make_grad_dt(off, after):
        table = (Groups("heads", (half_heads, length), off, groups, own_half),)
        window = (Groups("window heads", (half_heads, length), off, groups, own_half),)
        grad_dt, token = call(
            grad_dt_body,
            [f32(heads, length) + window],
            [
                full(bc),
                (rate,) + table,
                (dt_slope,) + table,
                (step,) + table,
                (cumul,) + table,
                full(q_rows[off]),
                full(r_rows[off]),
                full(x_low[off]),
                full(states[off]),
                full(backs[off]),
            ],
            base=base,
            scratch=[pltpu.VMEM((half_width, 128), BF16), pltpu.VMEM((length, half_width), BF16)],
            carry=carried["dt"],
            after=after,
            token=True,
            flops=4 * length * 128 * half_width,
        )
        carried["dt"] = [grad_dt]
        return token

    def make_grad_x(off, after):
        grad_x, token = call(
            grad_x_body,
            [low(length, channels) + window_at(length, off)],
            [
                full(bc),
                (step,) + rows_at(off),
                (cumul,) + rows_at(off),
                (partial[off],) + half(length),
                (slope[off],) + half(length),
                (conv_x,) + lanes_at(4, off),
                (rim_back,) + lanes_at(3, off),
                (backs[off],) + slot,
            ],
            base=base,
            loop=own_half,
            scratch=[pltpu.VMEM((length + 8, 128), F32)],
            carry=carried["x"],
            after=after,
            token=True,
            flops=2 * length * 128 * half_width,
        )
        carried["x"] = [grad_x]
        return token

    def make_rim(off, before, after):
        last = off == rest
        if last:
            outs = [
                low(3, channels + 256) + whole(3, channels + 256),
                f32(2, length, 128) + whole(2, length, 128),
            ]
            scratch = [pltpu.VMEM((length, 128), F32), pltpu.VMEM((3, channels + 256), F32)]
        else:
            scratch = []
            outs = [f32(3, half_width) + whole(3, half_width), f32(length, 128) + whole(length, 128)]
        return call(
            functools.partial(rim_body, last),
            outs,
            [
                full(bc),
                (step,) + rows_at(off),
                (cumul,) + rows_at(off),
                (weighted_x[off],) + half(length),
                (partial[off],) + half(length),
                (slope[off],) + half(length),
                (backs[off],) + slot,
            ]
            + [full(array) for array in before],
            base=base,
            loop=own_half,
            scratch=scratch,
            after=after,
            flops=2 * length * 128 * half_width,
        )

    if split:
        before = make_rim(0, [], [])
    else:
        before = [jnp.zeros((3, channels), F32), jnp.zeros((length, 128), F32)]
    rim_back, grad_bc_pre = make_rim(rest, [*before, carried["sums"], bc_slope], [])
    rim_back = lax.ppermute(rim_back, "seq", [(i, (i - 1) % count) for i in range(count)])
    dt_token = make_grad_dt(rest, [grad_bc_pre])
    if split:
        dt_token = make_grad_dt(0, [dt_token])
    if parts == 4:
        piece = lambda rows: f32(2, rows, 128) + whole(2, rows, 128)
        piece_low = lambda rows: low(2, rows, 128) + whole(2, rows, 128)
        kept, sent = call(
            bc_back_body,
            [piece(length // 2), piece_low(length // 2)],
            [
                full(grad_bc_pre),
                (rim_back, ((3, 256), lambda g, b: (0, channels // 256))),
                full(bc_taps),
            ],
            base=base,
            scratch=[pltpu.VMEM((length + 8, 128), F32), pltpu.VMEM((length, 128), F32)],
            after=[dt_token],
        )
        taken = turn_head(sent, 2)
        x_tokens = [make_grad_x(0, [sent])]
        kept, sent = call(
            bc_half_body,
            [piece(length // 4), piece_low(length // 4)],
            [full(kept), full(taken)],
            base=base,
            scratch=[pltpu.VMEM((length // 2, 128), F32)],
            after=x_tokens,
        )
        taken = turn_head(sent, 1)
        x_tokens = [make_grad_x(rest, [sent])] if split else []
        (grad_bc,) = call(
            bc_last_body,
            [piece_low(length // 4)],
            [full(kept), full(taken)],
            base=base,
            after=x_tokens,
        )
    else:
        for off in halves:
            make_grad_x(off, [])
        bc_halo = jnp.moveaxis(rim_back[:, channels:].reshape(3, 2, 128), 1, 0)
        bc_halo = jnp.where(own == count - 1, 0.0, bc_halo.astype(F32))
        bc_sum = conv_back(jnp.concatenate([grad_bc_pre, bc_halo], axis=1), convolution_bc_taps)
        share = length // parts
        bc_sum = lax.psum(bc_sum, "head")
        grad_bc = lax.dynamic_slice_in_dim(bc_sum, along_head * share, share, 1).astype(BF16)
    return (carried["x"][0], carried["z"][0], grad_bc, carried["dt"][0])


def solution(mesh):
    return jax.shard_map(
        shards,
        mesh=mesh,
        in_specs=(
            P("seq", "head"),
            P("seq", "head"),
            P(None, "seq", None),
            P("head", "seq"),
            P("head"),
            P("head"),
            P("head"),
            P(None, "head"),
            P(),
            P("head"),
            P("seq", "head"),
        ),
        out_specs=(
            P("seq", "head"),
            P("seq", "head"),
            P(None, ("seq", "head"), None),
            P("head", "seq"),
        ),
        check_vma=False,
    )
```
